32 devices in a mesh: expert: 16 (over z, y, x), tensor: 2 (over core).
Axes of the slice: x: 2, y: 2, z: 4, core: 2. Of those that a mesh axis runs over, the one named last changes fastest.
Arguments:
- first_half: bfloat16 [2048, 2048], P('expert', 'tensor'), may hold values from -6 to 6
- second_half: bfloat16 [2048, 2048], P('expert', 'tensor'), may hold values from -1.5 to 1.5
- first_grad: bfloat16 [2048, 2048], P('expert', 'tensor'), may hold values from -1.5 to 1.5
- second_grad: bfloat16 [2048, 2048], P('expert', 'tensor'), may hold values from -6 to 6
- expert_ids: int32 [2048, 6], P('expert'), may hold values from 0 to 15, as said below
- gate_weights: bfloat16 [2048, 6], P('expert'), may hold values from 0.049804688 to 0.5
- expert_in: bfloat16 [16, 2, 1408, 2048], P('expert', None, 'tensor'), may hold values from -0.125 to 0.125
- expert_out: bfloat16 [16, 1408, 2048], P('expert', 'tensor'), may hold values from -0.15625 to 0.15625
Outputs:
- restored: bfloat16 [2048, 2048], P('expert', 'tensor')
- carried_grad: bfloat16 [2048, 2048], P('expert', 'tensor')
- gate_grad: float32 [2048, 6], P('expert')
- grad_in: bfloat16 [16, 2, 1408, 2048], P('expert', None, 'tensor')
- grad_out: bfloat16 [16, 1408, 2048], P('expert', 'tensor')
The draws below stay inside these ranges and needn't reach their ends.
Inputs may be any that keep to these rules, and one draw needn't show every extreme that they name: `expert_ids`: each token names 6 different experts. In the rows of one index of expert (128 tokens) each expert is named by at least 40 and at most 56 tokens, and one expert is named by exactly 56 tokens of every index of expert.
All inputs are finite; a program needn't handle non-finite values.
Results may differ from the reference program's by a relative error of at most 0.02.
Values may be sent and summed in bfloat16 or wider, within the bound.
No kernel may reach another device: no remote copies, remote signals or barrier semaphores. Data moves between devices by JAX's collectives and lax.ppermute only.
A program may use at most 128 MiB of HBM per device.

```python
import math
import jax
import jax.numpy as jnp
from jax import lax

D = 2048
HID = 1408
TOP = 6
TOK_DEV = 128
EXPERTS = 16
TOKENS = 2048
CAP = 56
N_TENSOR = 2


def route_block(key, hot):
    first_key, second_key, third_key = jax.random.split(key, 3)
    order = jax.random.permutation(first_key, EXPERTS).astype(jnp.int32)
    order = jnp.where(order == hot, order[0], order)
    order = order.at[0].set(hot)
    unit = CAP // 7
    share = jax.random.randint(second_key, (EXPERTS // 2,), 0, 2 * unit + 1).astype(jnp.int32)
    share = jnp.where(jnp.arange(EXPERTS // 2) == 0, 0, share)
    removal = jnp.stack([share, 2 * unit - share], axis=1).reshape(EXPERTS)
    loads = CAP - removal
    bounds = jnp.cumsum(loads)
    places = jnp.arange(TOK_DEV * TOP, dtype=jnp.int32)
    ranked = jnp.sum((places[:, None] >= bounds[None, :]).astype(jnp.int32), axis=1)
    sequence = order[ranked]
    layout = sequence.reshape(TOP, TOK_DEV).T
    shuffle = jax.random.permutation(third_key, TOK_DEV)
    return layout[shuffle]


def draw_expert_ids(key, part):
    hot = jax.random.randint(jax.random.fold_in(key, 7), (), 0, EXPERTS).astype(jnp.int32)
    keys = jax.random.split(jax.random.fold_in(key, 11), TOKENS // TOK_DEV)
    blocks = jax.vmap(lambda item: route_block(item, hot))(keys)
    return blocks.reshape(TOKENS, TOP).astype(jnp.int32)


def block_levels(stream_key, dims, pieces, least, high):
    loudness, own = 1.0, jax.random.fold_in(stream_key, 6)
    for axis_at, shards_of in pieces:
        heights = jnp.exp(jax.random.uniform(jax.random.fold_in(own, axis_at), (shards_of,), jnp.float32, least / len(pieces), high / len(pieces)))
        loudness = loudness * jnp.repeat(heights, dims[axis_at] // shards_of).reshape([-1 if axis == axis_at else 1 for axis in range(len(dims))])
    return loudness


def scatter_about(rng, shape, scale, limit, pieces=(), kind=jnp.bfloat16):
    gain = block_levels(rng, shape, pieces, -0.22, 0.18) if pieces else 1.0
    values = jax.random.normal(rng, shape, jnp.float32) * scale * gain
    return jnp.minimum(jnp.maximum(values, -limit), limit).astype(kind)


def setup_inputs(seed: int = 0) -> dict:
    streams_of = jax.random.split(jax.random.key(seed), 9)
    first_half = scatter_about(streams_of[0], (TOKENS, D), 1.0, 6.0, ((0, 16), (1, 2)))
    second_half = scatter_about(streams_of[1], (TOKENS, D), 0.25, 1.5, ((0, 16), (1, 2)))
    first_grad = scatter_about(streams_of[2], (TOKENS, D), 0.25, 1.5, ((0, 16), (1, 2)))
    second_grad = scatter_about(streams_of[3], (TOKENS, D), 1.0, 6.0, ((0, 16), (1, 2)))
    expert_ids = draw_expert_ids(jax.random.fold_in(streams_of[8], 71), 0)
    gate_weights = jnp.clip(jnp.exp(math.log(0.5) - 2.306499 * jax.random.uniform(streams_of[5], (TOKENS, TOP), jnp.float32) ** block_levels(streams_of[5], (TOKENS, TOP), ((0, 16),), -0.2, 0.2)), 0.049804688, 0.5).astype(jnp.bfloat16)
    expert_in = scatter_about(streams_of[6], (EXPERTS, 2, HID, D), D ** -0.5, 0.125, ((0, 16), (2, 2)))
    expert_out = scatter_about(streams_of[7], (EXPERTS, HID, D), HID ** -0.5, 0.15625, ((0, 16), (1, 2)))
    return {"first_half": first_half, "second_half": second_half, "first_grad": first_grad, "second_grad": second_grad, "expert_ids": expert_ids, "gate_weights": gate_weights, "expert_in": expert_in, "expert_out": expert_out}


def settle(values):
    return lax.optimization_barrier(values.astype(jnp.bfloat16)).astype(jnp.float32)


def reference(first_half, second_half, first_grad, second_grad, expert_ids, gate_weights, expert_in, expert_out):
    blocks = TOKENS // TOK_DEV
    routes = expert_ids.reshape(blocks, TOK_DEV * TOP)
    onehot = (routes[:, :, None] == jnp.arange(EXPERTS, dtype=jnp.int32)[None, None, :]).astype(jnp.int32)
    before = jnp.cumsum(onehot, axis=1) - onehot
    slot_index = jnp.sum(before * onehot, axis=2).reshape(-1).astype(jnp.int32)
    flat = expert_ids.reshape(-1).astype(jnp.int32)
    count = TOKENS * TOP
    route_ids = jnp.arange(count, dtype=jnp.int32)
    source = route_ids // (TOK_DEV * TOP)
    position = flat * (blocks * CAP) + source * CAP + slot_index
    slot_route = jnp.full((EXPERTS * blocks * CAP,), count, jnp.int32).at[position].set(route_ids)
    slot_route = slot_route.reshape(EXPERTS, blocks * CAP)
    route_token = jnp.concatenate([route_ids // TOP, jnp.full((1,), TOKENS, jnp.int32)])
    gate_pad = jnp.concatenate([gate_weights.reshape(-1), jnp.zeros((1,), jnp.bfloat16)])
    first_pad = jnp.concatenate([first_half, jnp.zeros((1, D), jnp.bfloat16)], axis=0)
    cot_pad = jnp.concatenate([second_grad, jnp.zeros((1, D), jnp.bfloat16)], axis=0)
    width = HID // N_TENSOR

    def one_expert(carry, inputs):
        out_acc, dx_acc, gate_acc = carry
        picked, weights_in, weights_out = inputs
        token_rows = route_token[picked]
        slot_rows = first_pad[token_rows]
        slot_cots = cot_pad[token_rows]
        slot_gates = gate_pad[picked].astype(jnp.float32)
        scaled = (slot_gates[:, None] * slot_cots.astype(jnp.float32)).astype(jnp.bfloat16)
        out_sum = jnp.zeros((slot_rows.shape[0], D), jnp.float32)
        dx_sum = jnp.zeros((slot_rows.shape[0], D), jnp.float32)
        gate_sum = jnp.zeros((slot_rows.shape[0],), jnp.float32)
        grads_in = []
        grads_out = []
        for group in range(N_TENSOR):
            w_gate = weights_in[0][group * width:(group + 1) * width, :]
            w_up = weights_in[1][group * width:(group + 1) * width, :]
            w_down = weights_out[group * width:(group + 1) * width, :]
            gate_pre = jnp.dot(slot_rows, w_gate.T, preferred_element_type=jnp.float32)
            up_pre = jnp.dot(slot_rows, w_up.T, preferred_element_type=jnp.float32)
            sigma = jax.nn.sigmoid(gate_pre)
            active = gate_pre * sigma
            hidden = (active * up_pre).astype(jnp.bfloat16)
            part_out = jnp.dot(hidden, w_down, preferred_element_type=jnp.float32)
            out_sum = out_sum + settle(part_out)
            gate_sum = gate_sum + settle(jnp.sum(slot_cots.astype(jnp.float32) * part_out, axis=1))
            hidden_grad = jnp.dot(scaled, w_down.T, preferred_element_type=jnp.float32)
            gate_pre_grad = (hidden_grad * up_pre * sigma * (1.0 + gate_pre * (1.0 - sigma))).astype(jnp.bfloat16)
            up_grad = (hidden_grad * active).astype(jnp.bfloat16)
            input_piece = jnp.dot(gate_pre_grad, w_gate, preferred_element_type=jnp.float32) + jnp.dot(up_grad, w_up, preferred_element_type=jnp.float32)
            dx_sum = dx_sum + settle(input_piece)
            grads_in.append(jnp.stack([jnp.dot(gate_pre_grad.T, slot_rows, preferred_element_type=jnp.float32), jnp.dot(up_grad.T, slot_rows, preferred_element_type=jnp.float32)]).astype(jnp.bfloat16))
            grads_out.append(jnp.dot(hidden.T, scaled, preferred_element_type=jnp.float32).astype(jnp.bfloat16))
        out_acc = out_acc.at[token_rows].add(slot_gates[:, None] * out_sum)
        dx_acc = dx_acc.at[token_rows].add(dx_sum)
        gate_acc = gate_acc.at[picked].add(gate_sum)
        return (out_acc, dx_acc, gate_acc), (jnp.concatenate(grads_in, axis=1), jnp.concatenate(grads_out, axis=0))

    start = (jnp.zeros((TOKENS + 1, D), jnp.float32), jnp.zeros((TOKENS + 1, D), jnp.float32), jnp.zeros((count + 1,), jnp.float32))
    (out_acc, dx_acc, gate_acc), (grad_in, grad_out) = lax.scan(one_expert, start, (slot_route, expert_in, expert_out))
    restored = (second_half.astype(jnp.float32) - out_acc[:TOKENS]).astype(jnp.bfloat16)
    carried_grad = (first_grad.astype(jnp.float32) + dx_acc[:TOKENS]).astype(jnp.bfloat16)
    gate_grad = gate_acc[:count].reshape(TOKENS, TOP)
    return restored, carried_grad, gate_grad, grad_in, grad_out
```

```python
import functools

import jax
import jax.numpy as jnp
from jax import lax
from jax.experimental import pallas as pl
from jax.experimental.pallas import tpu as pltpu
from jax.sharding import PartitionSpec as P

PLANE = 4
TAIL = 16
VMEM_LIMIT = 56 * 1024 * 1024
F32 = jnp.float32
BF16 = jnp.bfloat16


def dot_nn(a, b):
    return lax.dot_general(a, b, (((1,), (0,)), ((), ())), preferred_element_type=F32)


def dot_nt(a, b):
    return lax.dot_general(a, b, (((1,), (1,)), ((), ())), preferred_element_type=F32)


def dot_tn(a, b):
    return lax.dot_general(a, b, (((0,), (0,)), ((), ())), preferred_element_type=F32)


def iota(shape, axis):
    return lax.broadcasted_iota(jnp.int32, shape, axis)


def call(kernel, outs, args, specs, scratch=(), out_specs=None, flops=0, name=None):
    vmem = pl.BlockSpec(memory_space=pltpu.VMEM)
    nbytes = sum(a.size * a.dtype.itemsize for a in args) + sum(
        o.size * o.dtype.itemsize for o in outs
    )
    return pl.pallas_call(
        kernel,
        out_shape=outs,
        in_specs=specs,
        out_specs=out_specs if out_specs is not None else [vmem] * len(outs),
        scratch_shapes=list(scratch),
        compiler_params=pltpu.CompilerParams(vmem_limit_bytes=VMEM_LIMIT),
        cost_estimate=pl.CostEstimate(flops=flops, bytes_accessed=nbytes, transcendentals=0),
        name=name,
    )(*args)


def route_kernel(info, meta, metat, sel, selt, *, zn, pn, tokens, picks, cap):
    rows = zn * cap
    base, inner = info[0], info[1]
    partner_r = iota((8, 1), 0)
    partner_c = iota((1, 8), 1)
    experts_r = jnp.where(partner_r < pn, base + (partner_r ^ inner), -2).astype(F32)
    experts_c = jnp.where(partner_c < pn, base + (partner_c ^ inner), -2).astype(F32)
    earlier_r = (iota((tokens, tokens), 0) < iota((tokens, tokens), 1)).astype(F32).astype(BF16)
    earlier_c = (iota((tokens, tokens), 1) < iota((tokens, tokens), 0)).astype(F32).astype(BF16)
    slot_r = iota((rows, tokens), 0).astype(F32)
    slot_c = iota((tokens, pn * rows), 1).astype(F32)
    for s in range(zn):
        here = slice(s * tokens, (s + 1) * tokens)
        ids_r = meta[0:8, here]
        ids_c = metat[here, 0:8]
        named_r = jnp.zeros((8, tokens), F32)
        named_c = jnp.zeros((tokens, 8), F32)
        for k in range(picks):
            named_r += (ids_r[k : k + 1, :] == experts_r).astype(F32)
            named_c += (ids_c[:, k : k + 1] == experts_c).astype(F32)
        dest_r = dot_nn(named_r.astype(BF16), earlier_r) + s * cap
        dest_c = dot_nn(earlier_c, named_c.astype(BF16)) + s * cap
        dest_r = jnp.where(named_r > 0, dest_r, -1.0)
        dest_c = jnp.where(named_c > 0, dest_c + rows * partner_c.astype(F32), -1.0)
        picked = jnp.zeros((tokens, pn * rows), F32)
        for q in range(pn):
            sel[q * rows : (q + 1) * rows, here] = (
                (slot_r == dest_r[q : q + 1, :]).astype(F32).astype(BF16)
            )
            picked += (slot_c == dest_c[:, q : q + 1]).astype(F32)
        selt[here, :] = picked.astype(BF16)


def pack_kernel(info, meta, sel, *refs, zn, pn, tokens, picks, rows, gates):
    sources, outs, whole = refs[:zn], refs[zn : zn + pn], refs[zn + pn]
    base, inner = info[0], info[1]
    for s in range(zn):
        whole[s * tokens : (s + 1) * tokens, :] = sources[s][...]
    for q in range(pn):
        chosen = sel[q * rows : (q + 1) * rows, :]
        outs[q][0:rows, :] = dot_nn(chosen, whole[...]).astype(BF16)
        if gates:
            expert = (base + (inner ^ q)).astype(F32)
            gate = jnp.zeros((1, zn * tokens), F32)
            for k in range(picks):
                gate += jnp.where(meta[k : k + 1, :] == expert, meta[8 + k : 9 + k, :], 0.0)
            gate = jnp.broadcast_to(gate, (TAIL, zn * tokens)).astype(BF16)
            outs[q][rows : rows + TAIL, :] = jnp.zeros((TAIL, outs[q].shape[1]), BF16)
            outs[q][rows : rows + TAIL, 0:rows] = dot_nt(gate, chosen).astype(BF16)


def combine_kernel(info, meta, sel, selt, *refs, zn, pn, tokens, rows, gates):
    sources, outs, whole = refs[:pn], refs[pn : pn + zn], refs[pn + zn]
    base, inner = info[0], info[1]
    for q in range(pn):
        whole[q * rows : (q + 1) * rows, :] = sources[q][0:rows, :]
    for s in range(zn):
        here = slice(s * tokens, (s + 1) * tokens)
        outs[s][0:tokens, :] = dot_nn(selt[here, :], whole[...]).astype(BF16)
    if gates:
        total = jnp.zeros((8, zn * tokens), F32)
        for q in range(pn):
            expert = (base + (inner ^ q)).astype(F32)
            row = sources[q][rows : rows + TAIL, 0:rows]
            spread = dot_nn(row, sel[q * rows : (q + 1) * rows, :])
            total += jnp.where(meta[0:8, :] == expert, spread[0:8, :], 0.0)
        total = jnp.concatenate([total, jnp.zeros((TAIL - 8, zn * tokens), F32)], axis=0)
        total = total.astype(BF16)
        for s in range(zn):
            outs[s][tokens : tokens + TAIL, :] = jnp.zeros((TAIL, outs[s].shape[1]), BF16)
            outs[s][tokens : tokens + TAIL, 0:tokens] = total[:, s * tokens : (s + 1) * tokens]


def column_block(info, j, nt, cols):
    block = lax.rem(info[2] - j + nt, nt)
    return pl.ds(pl.multiple_of(block * cols, 128), cols)


def forward_kernel(info, *refs, nt, pn, rows, cols):
    n = nt * pn
    xs, win, wout = refs[:n], refs[n], refs[n + 1]
    outs = refs[n + 2 : 2 * n + 2]
    hs, hid, a1, a2, wg, wu, wd, sems = refs[2 * n + 2 :]
    copies = []
    for j in range(nt):
        at = column_block(info, j, nt, cols)
        copies.append(pltpu.make_async_copy(win.at[0, 0, :, at], wg.at[j], sems.at[0, j]))
        copies.append(pltpu.make_async_copy(win.at[0, 1, :, at], wu.at[j], sems.at[1, j]))
    for j in range(nt):
        at = column_block(info, j, nt, cols)
        copies.append(pltpu.make_async_copy(wout.at[0, :, at], wd.at[j], sems.at[2, j]))
    for copy in copies:
        copy.start()
    for copy in copies[: 2 * nt]:
        copy.wait()
    same = iota((rows, rows), 0) == iota((rows, rows), 1)
    for q in range(pn):
        here = slice(q * rows, (q + 1) * rows)
        gate = xs[q][rows : rows + TAIL, 0:rows].astype(F32)[0:1, :]
        gate = jnp.sum(jnp.where(same, gate, 0.0), axis=1, keepdims=True)
        pre = [xs[j * pn + q][0:rows, :] for j in range(nt)]
        g = dot_nt(pre[0], wg[0])
        u = dot_nt(pre[0], wu[0])
        for j in range(1, nt):
            g += dot_nt(pre[j], wg[j])
            u += dot_nt(pre[j], wu[j])
        sigma = jax.nn.sigmoid(g)
        active = g * sigma
        hidden = active * u
        scaled = (gate * hidden).astype(BF16)
        hs[here, :] = scaled
        hid[here, :] = hidden.astype(BF16)
        a1[here, :] = (gate * (u * sigma * (1.0 + g * (1.0 - sigma)))).astype(BF16)
        a2[here, :] = (gate * active).astype(BF16)
        if q == 0:
            for copy in copies[2 * nt :]:
                copy.wait()
        for j in range(nt):
            outs[j * pn + q][...] = dot_nn(scaled, wd[(nt - j) % nt]).astype(BF16)


def backward_kernel(info, *refs, nt, pn, rows, cols):
    n = nt * pn
    cs, win, wout, hid, a1, a2 = refs[:n], *refs[n : n + 5]
    outs = refs[n + 5 : 2 * n + 5]
    gg, ug, wg, wu, wd, sems = refs[2 * n + 5 :]
    copies = []
    for j in range(nt):
        at = column_block(info, j, nt, cols)
        copies.append(pltpu.make_async_copy(wout.at[0, :, at], wd.at[j], sems.at[2, j]))
    for j in range(nt):
        at = column_block(info, j, nt, cols)
        copies.append(pltpu.make_async_copy(win.at[0, 0, :, at], wg.at[j], sems.at[0, j]))
        copies.append(pltpu.make_async_copy(win.at[0, 1, :, at], wu.at[j], sems.at[1, j]))
    for copy in copies:
        copy.start()
    for copy in copies[:nt]:
        copy.wait()
    same = iota((rows, rows), 0) == iota((rows, rows), 1)
    for q in range(pn):
        here = slice(q * rows, (q + 1) * rows)
        grad = dot_nt(cs[q][...], wd[0])
        for j in range(1, nt):
            grad += dot_nt(cs[j * pn + q][...], wd[j])
        piece = jnp.sum(grad * hid[here, :].astype(F32), axis=1, keepdims=True)
        piece = jnp.sum(jnp.where(same, piece, 0.0), axis=0, keepdims=True)
        piece = jnp.broadcast_to(piece, (TAIL, rows)).astype(BF16)
        gate_grad = (grad * a1[here, :].astype(F32)).astype(BF16)
        up_grad = (grad * a2[here, :].astype(F32)).astype(BF16)
        gg[here, :] = gate_grad
        ug[here, :] = up_grad
        if q == 0:
            for copy in copies[nt:]:
                copy.wait()
        for j in range(nt):
            out = outs[j * pn + q]
            w = (nt - j) % nt
            out[0:rows, :] = (dot_nn(gate_grad, wg[w]) + dot_nn(up_grad, wu[w])).astype(BF16)
            out[rows : rows + TAIL, :] = jnp.zeros((TAIL, cols), BF16)
            out[rows : rows + TAIL, 0:rows] = piece


def weights_kernel(info, *refs, nt, pn, rows, cols):
    n = nt * pn
    xs, cs, gg, ug, hs = refs[:n], refs[n : 2 * n], *refs[2 * n : 2 * n + 3]
    gin, gout, whole, stage, sems = refs[2 * n + 3 :]
    copies = []
    for j in range(nt):
        at = column_block(info, j, nt, cols)
        for q in range(pn):
            whole[0, q * rows : (q + 1) * rows, :] = xs[j * pn + q][0:rows, :]
            whole[1, q * rows : (q + 1) * rows, :] = cs[j * pn + q][...]
        for w, (left, right, out) in enumerate(
            ((gg, 0, gin.at[0, 0, :, at]), (ug, 0, gin.at[0, 1, :, at]), (hs, 1, gout.at[0, :, at]))
        ):
            stage[j, w] = dot_tn(left[...], whole[right]).astype(BF16)
            copy = pltpu.make_async_copy(stage.at[j, w], out, sems.at[j, w])
            copy.start()
            copies.append(copy)
    for copy in copies:
        copy.wait()


def body(
    first_half,
    second_half,
    first_grad,
    second_grad,
    expert_ids,
    gate_weights,
    expert_in,
    expert_out,
):
    tokens, picks = expert_ids.shape
    groups = lax.axis_size("expert")
    nt = lax.axis_size("tensor")
    pn = PLANE
    zn = groups // pn
    cap = tokens * picks * 7 // (6 * groups)
    rows = zn * cap
    cols = first_half.shape[1]
    hid_n = expert_out.shape[1]
    width = expert_out.shape[2]
    me = lax.axis_index("expert")
    info = jnp.stack(
        [(me // pn) * pn, me % pn, lax.axis_index("tensor")]
    ).astype(jnp.int32)

    smem = pl.BlockSpec(memory_space=pltpu.SMEM)
    vmem = pl.BlockSpec(memory_space=pltpu.VMEM)
    hbm = pl.BlockSpec(memory_space=pl.ANY)

    def outer_send(value, s):
        if s % zn == 0:
            return value
        return lax.ppermute(
            value,
            "expert",
            [(e, ((e // pn + s) % zn) * pn + e % pn) for e in range(groups)],
        )

    def inner_send(value, q):
        if q == 0:
            return value
        return lax.ppermute(value, "expert", [(e, e ^ q) for e in range(groups)])

    def tensor_send(value, j):
        if j == 0:
            return value
        return lax.ppermute(value, "tensor", [(c, (c + j) % nt) for c in range(nt)])

    def shape(*dims, dtype=BF16):
        return jax.ShapeDtypeStruct(dims, dtype)

    ids8 = jnp.full((8, tokens), -1.0, F32).at[:picks].set(expert_ids.T.astype(F32))
    gates8 = jnp.zeros((8, tokens), F32).at[:picks].set(gate_weights.T.astype(F32))
    own = jnp.concatenate([ids8, gates8], axis=0)
    x_parts = [outer_send(first_half, s) for s in range(zn)]
    meta = jnp.concatenate([outer_send(own, s) for s in range(zn)], axis=1)
    sel, selt = call(
        functools.partial(route_kernel, zn=zn, pn=pn, tokens=tokens, picks=picks, cap=cap),
        [shape(pn * rows, zn * tokens), shape(zn * tokens, pn * rows)],
        [info, meta, meta.T],
        [smem, vmem, vmem],
        name="route",
    )

    def pack(parts, gates):
        height = rows + TAIL if gates else rows
        return call(
            functools.partial(
                pack_kernel, zn=zn, pn=pn, tokens=tokens, picks=picks, rows=rows, gates=gates
            ),
            [shape(height, cols)] * pn,
            [info, meta, sel, *parts],
            [smem] + [vmem] * (2 + zn),
            scratch=[pltpu.VMEM((zn * tokens, cols), BF16)],
            flops=2 * pn * rows * zn * tokens * cols,
            name="pack_gates" if gates else "pack",
        )

    def combine(parts, gates):
        height = tokens + TAIL if gates else tokens
        return call(
            functools.partial(
                combine_kernel, zn=zn, pn=pn, tokens=tokens, rows=rows, gates=gates
            ),
            [shape(height, cols)] * zn,
            [info, meta, sel, selt, *parts],
            [smem] + [vmem] * (3 + pn),
            scratch=[pltpu.VMEM((pn * rows, cols), BF16)],
            flops=2 * pn * rows * zn * tokens * cols,
            name="combine_gates" if gates else "combine",
        )

    def dispatch(parts, gates):
        mine = [inner_send(piece, q) for q, piece in enumerate(pack(parts, gates))]
        return [tensor_send(piece, j) for j in range(nt) for piece in mine]

    def collect(pieces, gates):
        summed = []
        for q in range(pn):
            total = pieces[q].astype(F32)
            for j in range(1, nt):
                total += tensor_send(pieces[j * pn + q], j).astype(F32)
            summed.append(inner_send(total.astype(BF16), q))
        return [outer_send(part, -s) for s, part in enumerate(combine(summed, gates))]

    slots = pn * rows
    work = 2 * slots * hid_n * width
    weight_scratch = [pltpu.VMEM((nt, hid_n, cols), BF16)] * 3 + [
        pltpu.SemaphoreType.DMA((3, nt))
    ]

    xs = dispatch(x_parts, True)
    grad_whole, *_ = lax.optimization_barrier((second_grad, *x_parts))
    c_parts = [outer_send(grad_whole, s) for s in range(zn)]
    cs = dispatch(c_parts, False)

    forward = call(
        functools.partial(forward_kernel, nt=nt, pn=pn, rows=rows, cols=cols),
        [shape(rows, cols)] * (nt * pn) + [shape(slots, hid_n)] * 4,
        [info, *xs, expert_in, expert_out],
        [smem] + [vmem] * (nt * pn) + [hbm, hbm],
        scratch=weight_scratch,
        flops=3 * work,
        name="expert_forward",
    )
    out_parts = collect(forward[: nt * pn], False)
    hs, hid, a1, a2 = forward[nt * pn :]
    backward = call(
        functools.partial(backward_kernel, nt=nt, pn=pn, rows=rows, cols=cols),
        [shape(rows + TAIL, cols)] * (nt * pn) + [shape(slots, hid_n)] * 2,
        [info, *cs, expert_in, expert_out, hid, a1, a2],
        [smem] + [vmem] * (nt * pn) + [hbm, hbm] + [vmem] * 3,
        scratch=weight_scratch,
        flops=3 * work,
        name="expert_backward",
    )
    grad_parts = collect(backward[: nt * pn], True)
    gg, ug = backward[nt * pn :]
    grad_in, grad_out = call(
        functools.partial(weights_kernel, nt=nt, pn=pn, rows=rows, cols=cols),
        [shape(*expert_in.shape), shape(*expert_out.shape)],
        [info, *xs, *cs, gg, ug, hs],
        [smem] + [vmem] * (2 * nt * pn + 3),
        out_specs=[hbm, hbm],
        scratch=[
            pltpu.VMEM((2, slots, cols), BF16),
            pltpu.VMEM((nt, 3, hid_n, cols), BF16),
            pltpu.SemaphoreType.DMA((nt, 3)),
        ],
        flops=3 * work,
        name="expert_weights",
    )

    branch = sum(part.astype(F32) for part in out_parts)
    input_sum = sum(part[:tokens].astype(F32) for part in grad_parts)
    gate_sum = sum(part[tokens : tokens + picks, :tokens].astype(F32) for part in grad_parts)
    restored = (second_half.astype(F32) - branch).astype(BF16)
    carried_grad = (first_grad.astype(F32) + input_sum).astype(BF16)
    return (restored, carried_grad, gate_sum.T, grad_in, grad_out)


def solution(mesh):
    in_specs = (
        P("expert", "tensor"),
        P("expert", "tensor"),
        P("expert", "tensor"),
        P("expert", "tensor"),
        P("expert", None),
        P("expert", None),
        P("expert", None, "tensor", None),
        P("expert", "tensor", None),
    )
    out_specs = (
        P("expert", "tensor"),
        P("expert", "tensor"),
        P("expert", None),
        P("expert", None, "tensor", None),
        P("expert", "tensor", None),
    )
    return jax.shard_map(body, mesh=mesh, in_specs=in_specs, out_specs=out_specs, check_vma=False)
```

```python
import functools

import jax
import jax.numpy as jnp
from jax import lax
from jax.experimental import pallas as pl
from jax.experimental.pallas import tpu as pltpu
from jax.sharding import PartitionSpec as P

PLANE = 4
CHUNKS = 2
TAIL = 16
VMEM_LIMIT = 56 * 1024 * 1024
F32 = jnp.float32
BF16 = jnp.bfloat16


def dot_nn(a, b):
    return lax.dot_general(a, b, (((1,), (0,)), ((), ())), preferred_element_type=F32)


def dot_nt(a, b):
    return lax.dot_general(a, b, (((1,), (1,)), ((), ())), preferred_element_type=F32)


def dot_tn(a, b):
    return lax.dot_general(a, b, (((0,), (0,)), ((), ())), preferred_element_type=F32)


def iota(shape, axis):
    return lax.broadcasted_iota(jnp.int32, shape, axis)


SMEM = pl.BlockSpec(memory_space=pltpu.SMEM)
VMEM = pl.BlockSpec(memory_space=pltpu.VMEM)
HBM = pl.BlockSpec(memory_space=pl.ANY)


def call(kernel, outs, args, specs, out_specs=None, scratch=(), flops=0, name=None):
    nbytes = sum(a.size * a.dtype.itemsize for a in (*args, *outs))
    return pl.pallas_call(
        kernel,
        out_shape=outs,
        in_specs=specs,
        out_specs=out_specs if out_specs is not None else [VMEM] * len(outs),
        scratch_shapes=list(scratch),
        compiler_params=pltpu.CompilerParams(vmem_limit_bytes=VMEM_LIMIT),
        cost_estimate=pl.CostEstimate(flops=flops, bytes_accessed=nbytes, transcendentals=0),
        name=name,
    )(*args)


def shape(*dims, dtype=BF16):
    return jax.ShapeDtypeStruct(dims, dtype)


def earlier(tokens):
    return (iota((tokens, tokens), 0) < iota((tokens, tokens), 1)).astype(F32).astype(BF16)


def select_kernel(info, meta, *sels, zn, pn, tokens, picks, cap):
    zc = zn // CHUNKS
    rows = zc * cap
    partner = iota((8, 1), 0)
    experts = jnp.where(partner < pn, info[0] + (partner ^ info[1]), -2).astype(F32)
    before = earlier(tokens)
    slot = iota((rows, tokens), 0).astype(F32)
    for s in range(zn):
        g, local = divmod(s, zc)
        source = lax.rem(info[3] - s + zn, zn) * pn + info[1]
        ids = meta[source]
        named = jnp.zeros((8, tokens), F32)
        for k in range(picks):
            named += (ids[k : k + 1, :] == experts).astype(F32)
        dest = dot_nn(named.astype(BF16), before) + local * cap
        dest = jnp.where(named > 0, dest, -1.0)
        for q in range(pn):
            sels[g][q * rows : (q + 1) * rows, local * tokens : (local + 1) * tokens] = (
                (slot == dest[q : q + 1, :]).astype(F32).astype(BF16)
            )


def route_kernel(info, meta, *refs, zn, pn, tokens, picks, cap):
    zc = zn // CHUNKS
    rows = zc * cap
    ones, gated, (ids_out, gate_out) = refs[:CHUNKS], refs[CHUNKS : 2 * CHUNKS], refs[-2:]
    partner = iota((1, 8), 1)
    experts = jnp.where(partner < pn, info[0] + (partner ^ info[1]), -2).astype(F32)
    after = (iota((tokens, tokens), 1) < iota((tokens, tokens), 0)).astype(F32).astype(BF16)
    before = earlier(tokens)
    eye = (iota((16, 16), 0) == iota((16, 16), 1)).astype(F32).astype(BF16)
    lane = iota((tokens, pn * rows), 1).astype(F32)
    slot = iota((rows, tokens), 0).astype(F32)
    own = (info[0] + info[1]).astype(F32)
    for s in range(zn):
        g, local = divmod(s, zc)
        here = slice(local * tokens, (local + 1) * tokens)
        outer = lax.rem(info[3] - s + zn, zn) * pn
        rowed = meta[outer + info[1]]
        ids_out[:, s * tokens : (s + 1) * tokens] = rowed[0:8, :]
        columned = dot_tn(rowed.astype(BF16), eye)
        named = jnp.zeros((tokens, 8), F32)
        gate = jnp.zeros((tokens, 8), F32)
        for k in range(picks):
            match = (columned[:, k : k + 1] == experts).astype(F32)
            named += match
            gate += match * columned[:, 8 + k : 9 + k]
        dest = dot_nn(after, named.astype(BF16)) + local * cap
        dest = jnp.where(named > 0, dest + rows * partner.astype(F32), -1.0)
        picked = jnp.zeros((tokens, pn * rows), F32)
        weighed = jnp.zeros((tokens, pn * rows), F32)
        for q in range(pn):
            match = lane == dest[:, q : q + 1]
            picked += match.astype(F32)
            weighed += jnp.where(match, gate[:, q : q + 1], 0.0)
        ones[g][here, :] = picked.astype(BF16)
        gated[g][here, :] = weighed.astype(BF16)
    for g in range(CHUNKS):
        for q in range(pn):
            column = jnp.zeros((rows, 1), F32)
            for local in range(zc):
                s = g * zc + local
                outer = lax.rem(info[3] - s + zn, zn) * pn
                rowed = meta[outer + (info[1] ^ q)]
                match = (rowed[0:8, :] == own).astype(F32)
                named = jnp.sum(match[0:picks, :], axis=0, keepdims=True)
                gate = jnp.sum(match[0:picks, :] * rowed[8 : 8 + picks, :], axis=0, keepdims=True)
                many = jnp.broadcast_to(named, (8, tokens)).astype(BF16)
                dest = dot_nn(many, before)[0:1, :] + local * cap
                dest = jnp.where(named > 0, dest, -1.0)
                column += jnp.sum(
                    jnp.where(slot == dest, gate, 0.0), axis=1, keepdims=True
                )
            gate_out[(g * pn + q) * rows : (g * pn + q + 1) * rows, :] = column


def pack_kernel(sel, *refs, zc, pn, tokens, rows):
    sources, outs, whole = refs[:zc], refs[zc : zc + pn], refs[zc + pn]
    for s in range(zc):
        whole[s * tokens : (s + 1) * tokens, :] = sources[s][...]
    for q in range(pn):
        outs[q][...] = dot_nn(sel[q * rows : (q + 1) * rows, :], whole[...]).astype(BF16)


def add_kernel(first, second, *outs, pn, rows, tail):
    for q in range(pn):
        here = slice(q * rows, (q + 1) * rows)
        outs[q][0:rows, :] = (first[here, :].astype(F32) + second[here, :].astype(F32)).astype(BF16)
    if tail:
        here = slice(pn * rows, pn * rows + TAIL)
        total = (first[here, :].astype(F32) + second[here, :].astype(F32)).astype(BF16)
        for q in range(pn):
            outs[q][rows : rows + TAIL, :] = total


def combine_kernel(chosen, *refs, zc, pn, tokens, rows):
    sources, outs, whole = refs[:pn], refs[pn : pn + zc], refs[pn + zc]
    for q in range(pn):
        whole[q * rows : (q + 1) * rows, :] = sources[q][0:rows, :]
    for s in range(zc):
        outs[s][...] = dot_nn(chosen[s * tokens : (s + 1) * tokens, :], whole[...]).astype(BF16)


def combine_far_kernel(info, ids, *refs, zc, pn, tokens, rows):
    sels, chosen, sources = refs[:CHUNKS], refs[CHUNKS], refs[CHUNKS + 1 : CHUNKS + 1 + pn]
    *outs, gate_out, whole = refs[CHUNKS + 1 + pn :]
    for q in range(pn):
        whole[q * rows : (q + 1) * rows, :] = sources[q][0:rows, :]
    gate_out[...] = jnp.zeros(gate_out.shape, BF16)
    for g in range(CHUNKS):
        span = slice(g * zc * tokens, (g + 1) * zc * tokens)
        total = jnp.zeros((8, zc * tokens), F32)
        for q in range(pn):
            expert = (info[0] + (info[1] ^ q)).astype(F32)
            row = g * pn + q
            values = sources[q][rows : rows + TAIL, 0:rows].astype(F32)[row : row + 1, :]
            values = jnp.broadcast_to(values, (8, rows)).astype(BF16)
            spread = dot_nn(values, sels[g][q * rows : (q + 1) * rows, :])
            total += jnp.where(ids[:, span] == expert, spread, 0.0)
        total = jnp.concatenate([total, jnp.zeros((TAIL - 8, zc * tokens), F32)], axis=0)
        gate_out[:, span] = total.astype(BF16)
    for s in range(zc):
        part = dot_nn(chosen[s * tokens : (s + 1) * tokens, :], whole[...]).astype(BF16)
        outs[s][0:tokens, :] = part
        at = (CHUNKS - 1) * zc + s
        outs[s][tokens : tokens + TAIL, :] = jnp.zeros((TAIL, part.shape[1]), BF16)
        outs[s][tokens : tokens + TAIL, 0:tokens] = gate_out[:, at * tokens : (at + 1) * tokens]


def combine_near_kernel(gates, chosen, *refs, zc, pn, tokens, rows, first):
    sources, outs, whole = refs[:pn], refs[pn : pn + zc], refs[pn + zc]
    for q in range(pn):
        whole[q * rows : (q + 1) * rows, :] = sources[q][0:rows, :]
    for s in range(zc):
        part = dot_nn(chosen[s * tokens : (s + 1) * tokens, :], whole[...]).astype(BF16)
        outs[s][0:tokens, :] = part
        at = first + s
        outs[s][tokens : tokens + TAIL, :] = jnp.zeros((TAIL, part.shape[1]), BF16)
        outs[s][tokens : tokens + TAIL, 0:tokens] = gates[:, at * tokens : (at + 1) * tokens]


class Loads:
    def __init__(self, sems):
        self.sems, self.copies, self.waited = sems, {}, set()

    def add(self, key, source, target):
        self.copies[key] = pltpu.make_async_copy(source, target, self.sems.at[len(self.copies)])
        self.copies[key].start()

    def need(self, *keys):
        for key in keys:
            if key not in self.waited:
                self.waited.add(key)
                self.copies[key].wait()

    def finish(self):
        self.need(*self.copies)


def column_block(info, j, nt, cols):
    block = lax.rem(info[2] - j + nt, nt)
    return pl.ds(pl.multiple_of(block * cols, 128), cols)


def forward_kernel(info, *refs, nt, rows, cols):
    n = nt * CHUNKS
    xs, win, wout = refs[:n], refs[n], refs[n + 1]
    outs, hid, a1, a2 = refs[n + 2 : 2 * n + 2], *refs[2 * n + 2 : 2 * n + 5]
    x, wg, wu, wd, stage, in_sems, out_sems = refs[2 * n + 5 :]
    loads, stores = Loads(in_sems), Loads(out_sems)
    for j in range(nt):
        at = column_block(info, j, nt, cols)
        loads.add(("x", 0, j), xs[j], x.at[0, j])
        loads.add(("g", j), win.at[0, 0, :, at], wg.at[j])
        loads.add(("u", j), win.at[0, 1, :, at], wu.at[j])
    for g in range(1, CHUNKS):
        for j in range(nt):
            loads.add(("x", g, j), xs[g * nt + j], x.at[g, j])
    for j in range(nt):
        loads.add(("d", j), wout.at[0, :, column_block(info, j, nt, cols)], wd.at[j])
    for g in range(CHUNKS):
        here = slice(g * rows, (g + 1) * rows)
        loads.need(("x", g, 0), ("g", 0))
        gate = dot_nt(x[g, 0], wg[0])
        loads.need(("u", 0))
        up = dot_nt(x[g, 0], wu[0])
        for j in range(1, nt):
            loads.need(("x", g, j), ("g", j), ("u", j))
            gate += dot_nt(x[g, j], wg[j])
            up += dot_nt(x[g, j], wu[j])
        sigma = jax.nn.sigmoid(gate)
        active = gate * sigma
        hidden = (active * up).astype(BF16)
        hid[here, :] = hidden
        a1[here, :] = (up * sigma * (1.0 + gate * (1.0 - sigma))).astype(BF16)
        a2[here, :] = active.astype(BF16)
        for j in reversed(range(nt)):
            w = (nt - j) % nt
            loads.need(("d", w))
            stage[g, j] = dot_nn(hidden, wd[w]).astype(BF16)
            stores.add((g, j), stage.at[g, j], outs[g * nt + j])
    loads.finish()
    stores.finish()


def backward_kernel(info, *refs, nt, pn, rows, cols):
    n = nt * CHUNKS
    cs, win, wout, hid, a1, a2, gates = refs[:n], *refs[n : n + 6]
    outs, gg, ug, hs = refs[n + 6 : 2 * n + 6], *refs[2 * n + 6 : 2 * n + 9]
    c, h, b1, b2, wg, wu, wd, stage, in_sems, out_sems = refs[2 * n + 9 :]
    loads, stores = Loads(in_sems), Loads(out_sems)
    for j in range(nt):
        at = column_block(info, j, nt, cols)
        loads.add(("c", 0, j), cs[j], c.at[0, j])
        loads.add(("d", j), wout.at[0, :, at], wd.at[j])
    for key, source, target in (("h", hid, h), ("1", a1, b1), ("2", a2, b2)):
        loads.add(key, source, target)
    for j in range(nt):
        at = column_block(info, j, nt, cols)
        loads.add(("g", j), win.at[0, 0, :, at], wg.at[j])
        loads.add(("u", j), win.at[0, 1, :, at], wu.at[j])
    for g in range(1, CHUNKS):
        for j in range(nt):
            loads.add(("c", g, j), cs[g * nt + j], c.at[g, j])
    piece_rows = rows // pn
    same = iota((piece_rows, piece_rows), 0) == iota((piece_rows, piece_rows), 1)
    tail_row = iota((TAIL, piece_rows), 0)
    tail = jnp.zeros((TAIL, piece_rows), F32)
    for g in range(CHUNKS):
        here = slice(g * rows, (g + 1) * rows)
        loads.need(("c", g, 0), ("d", 0))
        grad = dot_nt(c[g, 0], wd[0])
        for j in range(1, nt):
            loads.need(("c", g, j), ("d", j))
            grad += dot_nt(c[g, j], wd[j])
        loads.need("h", "1", "2")
        hidden = h[here, :].astype(F32)
        piece = jnp.sum(grad * hidden, axis=1, keepdims=True)
        for q in range(pn):
            part = piece[q * piece_rows : (q + 1) * piece_rows, :]
            part = jnp.sum(jnp.where(same, part, 0.0), axis=0, keepdims=True)
            tail += jnp.where(tail_row == g * pn + q, part, 0.0)
        gate = gates[here, :]
        grad = gate * grad
        hs[here, :] = (gate * hidden).astype(BF16)
        gate_grad = (grad * b1[here, :].astype(F32)).astype(BF16)
        up_grad = (grad * b2[here, :].astype(F32)).astype(BF16)
        gg[here, :] = gate_grad
        ug[here, :] = up_grad
        for j in reversed(range(nt)):
            w = (nt - j) % nt
            loads.need(("g", w), ("u", w))
            part = dot_nn(gate_grad, wg[w]) + dot_nn(up_grad, wu[w])
            stage[g, j, 0:rows, :] = part.astype(BF16)
            if g == CHUNKS - 1:
                stage[g, j, rows : rows + TAIL, :] = jnp.zeros((TAIL, cols), BF16)
                stage[g, j, rows : rows + TAIL, 0:piece_rows] = tail.astype(BF16)
                stores.add((g, j), stage.at[g, j], outs[g * nt + j])
            else:
                stores.add((g, j), stage.at[g, j, pl.ds(0, rows)], outs[g * nt + j])
    loads.finish()
    stores.finish()


def weights_kernel(info, *refs, nt, rows, cols):
    n = nt * CHUNKS
    xs, cs, lefts = refs[:n], refs[n : 2 * n], refs[2 * n : 2 * n + 3]
    gin, gout, left, right, stage, in_sems, out_sems = refs[2 * n + 3 :]
    loads, stores = Loads(in_sems), Loads(out_sems)
    order = ((0, 0, xs), (1, 0, xs), (2, 1, cs))
    for w, side, sources in order:
        loads.add(("l", w), lefts[w], left.at[w])
        if w == 1:
            continue
        for j in range(nt):
            for g in range(CHUNKS):
                target = right.at[side, j, pl.ds(g * rows, rows)]
                loads.add((side, j, g), sources[g * nt + j], target)
    for w, side, _ in order:
        loads.need(("l", w))
        for j in range(nt):
            loads.need(*((side, j, g) for g in range(CHUNKS)))
            at = column_block(info, j, nt, cols)
            stage[j, w] = dot_tn(left[w], right[side, j]).astype(BF16)
            target = gout.at[0, :, at] if w == 2 else gin.at[0, w, :, at]
            stores.add((j, w), stage.at[j, w], target)
    loads.finish()
    stores.finish()


def body(
    first_half,
    second_half,
    first_grad,
    second_grad,
    expert_ids,
    gate_weights,
    expert_in,
    expert_out,
):
    tokens, picks = expert_ids.shape
    groups = lax.axis_size("expert")
    nt = lax.axis_size("tensor")
    pn = PLANE
    zn = groups // pn
    zc = zn // CHUNKS
    cap = tokens * picks * 7 // (6 * groups)
    rows = zc * cap
    chunk = pn * rows
    slots = CHUNKS * chunk
    cols = first_half.shape[1]
    hid_n = expert_out.shape[1]
    width = expert_out.shape[2]
    me = lax.axis_index("expert")
    info = jnp.stack([(me // pn) * pn, me % pn, lax.axis_index("tensor"), me // pn]).astype(jnp.int32)

    def outer_send(value, s):
        if s % zn == 0:
            return value
        return lax.ppermute(
            value, "expert", [(e, ((e // pn + s) % zn) * pn + e % pn) for e in range(groups)]
        )

    def inner_send(value, q):
        if q == 0:
            return value
        return lax.ppermute(value, "expert", [(e, e ^ q) for e in range(groups)])

    def tensor_send(value, j):
        if j == 0:
            return value
        return lax.ppermute(value, "tensor", [(c, (c + j) % nt) for c in range(nt)])

    fixed = dict(zn=zn, pn=pn, tokens=tokens, picks=picks, cap=cap)
    near = dict(zc=zc, pn=pn, tokens=tokens, rows=rows)

    own = jnp.concatenate(
        [
            jnp.pad(expert_ids.T.astype(F32), ((0, 8 - picks), (0, 0)), constant_values=-1.0),
            jnp.pad(gate_weights.T.astype(F32), ((0, 8 - picks), (0, 0))),
        ],
        axis=0,
    )
    x_parts = [outer_send(first_half, s) for s in range(zn)]
    meta = lax.all_gather(own, "expert")
    sels = call(
        functools.partial(select_kernel, **fixed),
        [shape(chunk, zc * tokens)] * CHUNKS,
        [info, meta],
        [SMEM, VMEM],
        name="select",
    )
    routed = call(
        functools.partial(route_kernel, **fixed),
        [shape(zc * tokens, chunk)] * (2 * CHUNKS)
        + [shape(8, zn * tokens, dtype=F32), shape(slots, 1, dtype=F32)],
        [info, meta],
        [SMEM, VMEM],
        name="route",
    )
    ones, gated, (ids, gates) = routed[:CHUNKS], routed[CHUNKS : 2 * CHUNKS], routed[-2:]

    def dispatch(parts):
        arrays = []
        for g in range(CHUNKS):
            pieces = call(
                functools.partial(pack_kernel, **near),
                [shape(rows, cols)] * pn,
                [sels[g], *parts[g * zc : (g + 1) * zc]],
                [VMEM] * (1 + zc),
                scratch=[pltpu.VMEM((zc * tokens, cols), BF16)],
                flops=2 * chunk * zc * tokens * cols,
                name="pack",
            )
            mine = jnp.concatenate([inner_send(piece, q) for q, piece in enumerate(pieces)], axis=0)
            arrays += [tensor_send(mine, j) for j in range(nt)]
        return arrays

    def collect(g, arrays, tail):
        height = rows + TAIL if tail else rows
        total = arrays[0]
        for j in range(1, nt):
            pieces = call(
                functools.partial(add_kernel, pn=pn, rows=rows, tail=tail),
                [shape(height, cols)] * pn,
                [total, tensor_send(arrays[j], j)],
                [VMEM] * 2,
                name="add",
            )
            if j < nt - 1:
                total = jnp.concatenate(
                    [piece[:rows] for piece in pieces] + ([pieces[0][rows:]] if tail else []), axis=0
                )
        return [inner_send(piece, q) for q, piece in enumerate(pieces)]

    def combine(g, pieces):
        parts = call(
            functools.partial(combine_kernel, **near),
            [shape(tokens, cols)] * zc,
            [gated[g], *pieces],
            [VMEM] * (1 + pn),
            scratch=[pltpu.VMEM((chunk, cols), BF16)],
            flops=2 * chunk * zc * tokens * cols,
            name="combine",
        )
        return [outer_send(part, -(g * zc + s)) for s, part in enumerate(parts)]

    work = 2 * slots * hid_n * width
    weights = [pltpu.VMEM((nt, hid_n, cols), BF16)] * 3
    last = CHUNKS - 1

    xs = dispatch(x_parts)
    grad_whole, *_ = lax.optimization_barrier((second_grad, *x_parts[1:]))
    cs = dispatch([outer_send(grad_whole, s) for s in range(zn)])

    forward = call(
        functools.partial(forward_kernel, nt=nt, rows=chunk, cols=cols),
        [shape(chunk, cols)] * (nt * CHUNKS) + [shape(slots, hid_n)] * 3,
        [info, *xs, expert_in, expert_out],
        [SMEM] + [HBM] * (nt * CHUNKS + 2),
        out_specs=[HBM] * (nt * CHUNKS) + [VMEM] * 3,
        scratch=[pltpu.VMEM((CHUNKS, nt, chunk, cols), BF16)]
        + weights
        + [
            pltpu.VMEM((CHUNKS, nt, chunk, cols), BF16),
            pltpu.SemaphoreType.DMA((3 * nt + CHUNKS * nt,)),
            pltpu.SemaphoreType.DMA((CHUNKS * nt,)),
        ],
        flops=3 * work,
        name="expert_forward",
    )
    outs, (hid, a1, a2) = forward[: nt * CHUNKS], forward[nt * CHUNKS :]
    out_parts = {}
    for g in reversed(range(CHUNKS)):
        out_parts[g] = combine(g, collect(g, outs[g * nt : (g + 1) * nt], False))

    backward = call(
        functools.partial(backward_kernel, nt=nt, pn=pn, rows=chunk, cols=cols),
        [
            shape(chunk + (TAIL if g == last else 0), cols)
            for g in range(CHUNKS)
            for _ in range(nt)
        ]
        + [shape(slots, hid_n)] * 3,
        [info, *cs, expert_in, expert_out, hid, a1, a2, gates],
        [SMEM] + [HBM] * (nt * CHUNKS + 5) + [VMEM],
        out_specs=[HBM] * (nt * CHUNKS) + [VMEM] * 3,
        scratch=[pltpu.VMEM((CHUNKS, nt, chunk, cols), BF16)]
        + [pltpu.VMEM((slots, hid_n), BF16)] * 3
        + weights
        + [
            pltpu.VMEM((CHUNKS, nt, chunk + TAIL, cols), BF16),
            pltpu.SemaphoreType.DMA((3 * nt + CHUNKS * nt + 3,)),
            pltpu.SemaphoreType.DMA((CHUNKS * nt,)),
        ],
        flops=3 * work,
        name="expert_backward",
    )
    grads, (gg, ug, hs) = backward[: nt * CHUNKS], backward[nt * CHUNKS :]
    grad_parts = {}
    pieces = collect(last, grads[last * nt :], True)
    *parts, gate_parts = call(
        functools.partial(combine_far_kernel, **near),
        [shape(tokens + TAIL, cols)] * zc + [shape(TAIL, zn * tokens)],
        [info, ids, *sels, ones[last], *pieces],
        [SMEM] + [VMEM] * (2 + CHUNKS + pn),
        scratch=[pltpu.VMEM((chunk, cols), BF16)],
        flops=2 * chunk * zc * tokens * cols,
        name="combine_far",
    )
    grad_parts[last] = [outer_send(part, -(last * zc + s)) for s, part in enumerate(parts)]
    for g in reversed(range(last)):
        parts = call(
            functools.partial(combine_near_kernel, **near, first=g * zc),
            [shape(tokens + TAIL, cols)] * zc,
            [gate_parts, ones[g], *collect(g, grads[g * nt : (g + 1) * nt], False)],
            [VMEM] * (2 + pn),
            scratch=[pltpu.VMEM((chunk, cols), BF16)],
            flops=2 * chunk * zc * tokens * cols,
            name="combine_near",
        )
        grad_parts[g] = [outer_send(part, -(g * zc + s)) for s, part in enumerate(parts)]

    grad_in, grad_out = call(
        functools.partial(weights_kernel, nt=nt, rows=chunk, cols=cols),
        [shape(*expert_in.shape), shape(*expert_out.shape)],
        [info, *xs, *cs, gg, ug, hs],
        [SMEM] + [HBM] * (2 * nt * CHUNKS + 3),
        out_specs=[HBM, HBM],
        scratch=[
            pltpu.VMEM((3, slots, hid_n), BF16),
            pltpu.VMEM((2, nt, slots, cols), BF16),
            pltpu.VMEM((nt, 3, hid_n, cols), BF16),
            pltpu.SemaphoreType.DMA((3 + 2 * nt * CHUNKS,)),
            pltpu.SemaphoreType.DMA((3 * nt,)),
        ],
        flops=3 * work,
        name="expert_weights",
    )

    out_all = [part for g in range(CHUNKS) for part in out_parts[g]]
    grad_all = [part for g in range(CHUNKS) for part in grad_parts[g]]
    branch = sum(part.astype(F32) for part in out_all)
    input_sum = sum(part[:tokens].astype(F32) for part in grad_all)
    gate_sum = sum(part[tokens : tokens + picks, :tokens].astype(F32) for part in grad_all)
    restored = (second_half.astype(F32) - branch).astype(BF16)
    carried_grad = (first_grad.astype(F32) + input_sum).astype(BF16)
    return (restored, carried_grad, gate_sum.T, grad_in, grad_out)


def solution(mesh):
    in_specs = (
        P("expert", "tensor"),
        P("expert", "tensor"),
        P("expert", "tensor"),
        P("expert", "tensor"),
        P("expert", None),
        P("expert", None),
        P("expert", None, "tensor", None),
        P("expert", "tensor", None),
    )
    out_specs = (
        P("expert", "tensor"),
        P("expert", "tensor"),
        P("expert", None),
        P("expert", None, "tensor", None),
        P("expert", "tensor", None),
    )
    return jax.shard_map(body, mesh=mesh, in_specs=in_specs, out_specs=out_specs, check_vma=False)
```

```python
import functools

import jax
import jax.numpy as jnp
from jax import lax
from jax.experimental import pallas as pl
from jax.experimental.pallas import tpu as pltpu
from jax.sharding import PartitionSpec as P

PLANE = 4
TAIL = 16
VMEM_LIMIT = 56 * 1024 * 1024
F32 = jnp.float32
BF16 = jnp.bfloat16


def dot_nn(a, b):
    return lax.dot_general(a, b, (((1,), (0,)), ((), ())), preferred_element_type=F32)


def dot_nt(a, b):
    return lax.dot_general(a, b, (((1,), (1,)), ((), ())), preferred_element_type=F32)


def dot_tn(a, b):
    return lax.dot_general(a, b, (((0,), (0,)), ((), ())), preferred_element_type=F32)


def iota(shape, axis):
    return lax.broadcasted_iota(jnp.int32, shape, axis)


SMEM = pl.BlockSpec(memory_space=pltpu.SMEM)
VMEM = pl.BlockSpec(memory_space=pltpu.VMEM)
HBM = pl.BlockSpec(memory_space=pl.ANY)


def call(kernel, outs, args, specs, out_specs=None, scratch=(), flops=0, name=None):
    nbytes = sum(a.size * a.dtype.itemsize for a in (*args, *outs))
    return pl.pallas_call(
        kernel,
        out_shape=outs,
        in_specs=specs,
        out_specs=out_specs if out_specs is not None else [VMEM] * len(outs),
        scratch_shapes=list(scratch),
        compiler_params=pltpu.CompilerParams(vmem_limit_bytes=VMEM_LIMIT),
        cost_estimate=pl.CostEstimate(flops=flops, bytes_accessed=nbytes, transcendentals=0),
        name=name,
    )(*args)


def shape(*dims, dtype=BF16):
    return jax.ShapeDtypeStruct(dims, dtype)


def select_kernel(info, meta, sel, *, zn, pn, tokens, picks, cap):
    rows = zn * cap
    expert = iota((8, 1), 0)
    experts = jnp.where(expert < pn, info[0] + expert, -2).astype(F32)
    before = (iota((tokens, tokens), 0) < iota((tokens, tokens), 1)).astype(F32).astype(BF16)
    slot = iota((rows, tokens), 0).astype(F32)
    for s in range(zn):
        here = slice(s * tokens, (s + 1) * tokens)
        ids = meta[0:8, here]
        named = jnp.zeros((8, tokens), F32)
        for k in range(picks):
            named += (ids[k : k + 1, :] == experts).astype(F32)
        dest = dot_nn(named.astype(BF16), before) + s * cap
        dest = jnp.where(named > 0, dest, -1.0)
        for q in range(pn):
            sel[q * rows : (q + 1) * rows, here] = (
                (slot == dest[q : q + 1, :]).astype(F32).astype(BF16)
            )


def route_kernel(info, meta, ones, gated, *, zn, pn, tokens, picks, cap):
    rows = zn * cap
    expert = iota((1, 8), 1)
    experts = jnp.where(expert < pn, info[0] + expert, -2).astype(F32)
    after = (iota((tokens, tokens), 1) < iota((tokens, tokens), 0)).astype(F32).astype(BF16)
    eye = (iota((16, 16), 0) == iota((16, 16), 1)).astype(F32).astype(BF16)
    lane = iota((tokens, pn * rows), 1).astype(F32)
    for s in range(zn):
        here = slice(s * tokens, (s + 1) * tokens)
        columned = dot_tn(meta[:, here].astype(BF16), eye)
        named = jnp.zeros((tokens, 8), F32)
        gate = jnp.zeros((tokens, 8), F32)
        for k in range(picks):
            match = (columned[:, k : k + 1] == experts).astype(F32)
            named += match
            gate += match * columned[:, 8 + k : 9 + k]
        dest = dot_nn(after, named.astype(BF16)) + s * cap
        dest = jnp.where(named > 0, dest + rows * expert.astype(F32), -1.0)
        picked = jnp.zeros((tokens, pn * rows), F32)
        weighed = jnp.zeros((tokens, pn * rows), F32)
        for q in range(pn):
            match = lane == dest[:, q : q + 1]
            picked += match.astype(F32)
            weighed += jnp.where(match, gate[:, q : q + 1], 0.0)
        ones[here, :] = picked.astype(BF16)
        gated[here, :] = weighed.astype(BF16)


def pack_kernel(info, meta, sel, *refs, zn, pn, tokens, picks, rows, gates):
    sources, out, whole = refs[:zn], refs[zn], refs[zn + 1]
    for s in range(zn):
        whole[s * tokens : (s + 1) * tokens, :] = sources[s][...]
    for q in range(pn):
        chosen = sel[q * rows : (q + 1) * rows, :]
        out[q, 0:rows, :] = dot_nn(chosen, whole[...]).astype(BF16)
        if gates:
            expert = (info[0] + q).astype(F32)
            gate = jnp.zeros((1, zn * tokens), F32)
            for k in range(picks):
                gate += jnp.where(meta[k : k + 1, :] == expert, meta[8 + k : 9 + k, :], 0.0)
            gate = jnp.broadcast_to(gate, (TAIL, zn * tokens)).astype(BF16)
            out[q, rows : rows + TAIL, :] = jnp.zeros((TAIL, out.shape[2]), BF16)
            out[q, rows : rows + TAIL, 0:rows] = dot_nt(gate, chosen).astype(BF16)


def combine_kernel(info, meta, sel, chosen, back, *outs, zn, pn, tokens, rows, gates):
    cols = back.shape[2]
    whole = back[:, 0:rows, :].reshape(pn * rows, cols)
    if gates:
        total = jnp.zeros((8, zn * tokens), F32)
        for q in range(pn):
            expert = (info[0] + q).astype(F32)
            row = back[q, rows : rows + TAIL, 0:rows]
            spread = dot_nn(row, sel[q * rows : (q + 1) * rows, :])
            total += jnp.where(meta[0:8, :] == expert, spread[0:8, :], 0.0)
        total = jnp.concatenate([total, jnp.zeros((TAIL - 8, zn * tokens), F32)], axis=0)
        total = total.astype(BF16)
    for s in range(zn):
        here = slice(s * tokens, (s + 1) * tokens)
        outs[s][0:tokens, :] = dot_nn(chosen[here, :], whole).astype(BF16)
        if gates:
            outs[s][tokens : tokens + TAIL, :] = jnp.zeros((TAIL, cols), BF16)
            outs[s][tokens : tokens + TAIL, 0:tokens] = total[:, here]


class Loads:
    def __init__(self, sems):
        self.sems, self.copies, self.waited = sems, {}, set()

    def add(self, key, source, target):
        self.copies[key] = pltpu.make_async_copy(source, target, self.sems.at[len(self.copies)])
        self.copies[key].start()

    def need(self, *keys):
        for key in keys:
            if key not in self.waited:
                self.waited.add(key)
                self.copies[key].wait()

    def finish(self):
        self.need(*self.copies)


def column_block(info, j, nt, cols):
    block = lax.rem(info[2] - j + nt, nt)
    return pl.ds(pl.multiple_of(block * cols, 128), cols)


def load_weights(loads, info, win, wout, wg, wu, wd, nt, cols, kinds):
    for kind in kinds:
        for j in range(nt):
            at = column_block(info, j, nt, cols)
            to = pl.ds(j * cols, cols)
            if kind == "g":
                loads.add(("g", j), win.at[0, 0, :, at], wg.at[:, to])
            elif kind == "u":
                loads.add(("u", j), win.at[0, 1, :, at], wu.at[:, to])
            else:
                loads.add(("d", j), wout.at[0, :, at], wd.at[:, to])


def forward_kernel(info, *refs, nt, pn, rows, cols):
    xs, win, wout = refs[:nt], refs[nt], refs[nt + 1]
    outs, hid, a1, a2 = refs[nt + 2 : 2 * nt + 2], *refs[2 * nt + 2 : 2 * nt + 5]
    x, wg, wu, wd, stage, in_sems, out_sems = refs[2 * nt + 5 :]
    loads, stores = Loads(in_sems), Loads(out_sems)
    every = range(nt)

    def load_rows(g):
        for j in every:
            for q in (2 * g, 2 * g + 1):
                target = x.at[pl.ds(q * rows, rows), pl.ds(j * cols, cols)]
                loads.add(("x", j, q), xs[j].at[q], target)

    load_rows(0)
    load_weights(loads, info, win, wout, wg, wu, wd, nt, cols, "gu")
    for g in range(1, pn // 2):
        load_rows(g)
    load_weights(loads, info, win, wout, wg, wu, wd, nt, cols, "d")
    for g in range(pn // 2):
        here = slice(2 * g * rows, 2 * (g + 1) * rows)
        loads.need(*(("x", j, q) for j in every for q in (2 * g, 2 * g + 1)))
        loads.need(*(("g", j) for j in every))
        gate = dot_nt(x[here, :], wg[...])
        loads.need(*(("u", j) for j in every))
        up = dot_nt(x[here, :], wu[...])
        sigma = jax.nn.sigmoid(gate)
        active = gate * sigma
        hidden = (active * up).astype(BF16)
        hid[here, :] = hidden
        a1[here, :] = (up * sigma * (1.0 + gate * (1.0 - sigma))).astype(BF16)
        a2[here, :] = active.astype(BF16)
        loads.need(*(("d", j) for j in every))
        part = dot_nn(hidden, wd[...]).astype(BF16)
        for j in every:
            w = (nt - j) % nt
            stage[j, 2 * g : 2 * g + 2] = part[:, w * cols : (w + 1) * cols].reshape(2, rows, cols)
            span = pl.ds(2 * g, 2)
            stores.add((g, j), stage.at[j, span], outs[j].at[span])
    loads.finish()
    stores.finish()


def backward_kernel(info, *refs, nt, pn, rows, cols):
    cs, win, wout, hid, a1, a2 = refs[:nt], *refs[nt : nt + 5]
    outs, gg, ug, hs = refs[nt + 5 : 2 * nt + 5], *refs[2 * nt + 5 : 2 * nt + 8]
    c, tails, h, b1, b2, wg, wu, wd, stage, in_sems, out_sems = refs[2 * nt + 8 :]
    loads, stores = Loads(in_sems), Loads(out_sems)
    every = range(nt)

    def load_rows(g):
        for j in every:
            for q in (2 * g, 2 * g + 1):
                target = c.at[pl.ds(q * rows, rows), pl.ds(j * cols, cols)]
                loads.add(("c", j, q), cs[j].at[q, pl.ds(0, rows)], target)

    load_rows(0)
    load_weights(loads, info, win, wout, wg, wu, wd, nt, cols, "d")
    loads.add("t", cs[0].at[:, pl.ds(rows, TAIL)], tails)
    for key, source, target in (("h", hid, h), ("1", a1, b1), ("2", a2, b2)):
        loads.add(key, source, target)
    load_weights(loads, info, win, wout, wg, wu, wd, nt, cols, "gu")
    for g in range(1, pn // 2):
        load_rows(g)
    same = iota((rows, rows), 0) == iota((rows, rows), 1)
    for g in range(pn // 2):
        here = slice(2 * g * rows, 2 * (g + 1) * rows)
        both = (2 * g, 2 * g + 1)
        loads.need(*(("c", j, q) for j in every for q in both), *(("d", j) for j in every))
        grad = dot_nt(c[here, :], wd[...])
        loads.need("t", "h", "1", "2")
        hidden = h[here, :].astype(F32)
        piece = jnp.sum(grad * hidden, axis=1, keepdims=True)
        gates = []
        for at, q in enumerate(both):
            row = tails[q, :, 0:rows].astype(F32)[0:1, :]
            gates.append(jnp.sum(jnp.where(same, row, 0.0), axis=1, keepdims=True))
            part = piece[at * rows : (at + 1) * rows, :]
            part = jnp.sum(jnp.where(same, part, 0.0), axis=0, keepdims=True)
            part = jnp.broadcast_to(part, (TAIL, rows)).astype(BF16)
            for j in every:
                stage[j, q, rows : rows + TAIL, :] = jnp.zeros((TAIL, cols), BF16)
                stage[j, q, rows : rows + TAIL, 0:rows] = part
        gate = jnp.concatenate(gates, axis=0)
        grad = gate * grad
        hs[here, :] = (gate * hidden).astype(BF16)
        gate_grad = (grad * b1[here, :].astype(F32)).astype(BF16)
        up_grad = (grad * b2[here, :].astype(F32)).astype(BF16)
        gg[here, :] = gate_grad
        ug[here, :] = up_grad
        loads.need(*((k, j) for k in "gu" for j in every))
        part = (dot_nn(gate_grad, wg[...]) + dot_nn(up_grad, wu[...])).astype(BF16)
        for j in every:
            w = (nt - j) % nt
            block = part[:, w * cols : (w + 1) * cols].reshape(2, rows, cols)
            stage[j, 2 * g : 2 * g + 2, 0:rows, :] = block
            span = pl.ds(2 * g, 2)
            stores.add((g, j), stage.at[j, span], outs[j].at[span])
    loads.finish()
    stores.finish()


def weights_kernel(info, *refs, nt, pn, rows, cols):
    xs, cs, lefts = refs[:nt], refs[nt : 2 * nt], refs[2 * nt : 2 * nt + 3]
    gin, gout, left, right, stage, in_sems, out_sems = refs[2 * nt + 3 :]
    loads, stores = Loads(in_sems), Loads(out_sems)
    order = ((0, 0, xs), (1, 0, xs), (2, 1, cs))
    for w, side, sources in order:
        loads.add(("l", w), lefts[w], left.at[w])
        if w == 1:
            continue
        for j in range(nt):
            for q in range(pn):
                target = right.at[side, j, pl.ds(q * rows, rows)]
                loads.add((side, j, q), sources[j].at[q, pl.ds(0, rows)], target)
    for w, side, _ in order:
        loads.need(("l", w))
        for j in range(nt):
            loads.need(*((side, j, q) for q in range(pn)))
            at = column_block(info, j, nt, cols)
            stage[j, w] = dot_tn(left[w], right[side, j]).astype(BF16)
            target = gout.at[0, :, at] if w == 2 else gin.at[0, w, :, at]
            stores.add((j, w), stage.at[j, w], target)
    loads.finish()
    stores.finish()


def after(value, *others):
    return lax.optimization_barrier((value, *others))[0]


def body(
    first_half,
    second_half,
    first_grad,
    second_grad,
    expert_ids,
    gate_weights,
    expert_in,
    expert_out,
):
    tokens, picks = expert_ids.shape
    groups = lax.axis_size("expert")
    nt = lax.axis_size("tensor")
    pn = PLANE
    zn = groups // pn
    cap = tokens * picks * 7 // (6 * groups)
    rows = zn * cap
    slots = pn * rows
    cols = first_half.shape[1]
    hid_n = expert_out.shape[1]
    width = expert_out.shape[2]
    me = lax.axis_index("expert")
    info = jnp.stack([(me // pn) * pn, me % pn, lax.axis_index("tensor")]).astype(jnp.int32)

    def outer_send(value, s):
        if s % zn == 0:
            return value
        return lax.ppermute(
            value, "expert", [(e, ((e // pn + s) % zn) * pn + e % pn) for e in range(groups)]
        )

    def inner_exchange(value):
        planes = [[z * pn + q for q in range(pn)] for z in range(zn)]
        return lax.all_to_all(
            value, "expert", split_axis=0, concat_axis=0, axis_index_groups=planes, tiled=True
        )

    def tensor_send(value, j):
        if j == 0:
            return value
        return lax.ppermute(value, "tensor", [(c, (c + j) % nt) for c in range(nt)])

    fixed = dict(zn=zn, pn=pn, tokens=tokens)

    own = jnp.concatenate(
        [
            jnp.pad(expert_ids.T.astype(F32), ((0, 8 - picks), (0, 0)), constant_values=-1.0),
            jnp.pad(gate_weights.T.astype(F32), ((0, 8 - picks), (0, 0))),
        ],
        axis=0,
    )
    meta = jnp.concatenate([outer_send(own, s) for s in range(zn)], axis=1)
    sel = call(
        functools.partial(select_kernel, **fixed, picks=picks, cap=cap),
        [shape(slots, zn * tokens)],
        [info, meta],
        [SMEM, VMEM],
        name="select",
    )[0]
    late = zn // 2
    x_parts = [
        outer_send(after(first_half, sel) if s == late else first_half, s) for s in range(zn)
    ]

    def pack(parts, gates):
        return call(
            functools.partial(pack_kernel, **fixed, picks=picks, rows=rows, gates=gates),
            [shape(pn, rows + TAIL if gates else rows, cols)],
            [info, meta, sel, *parts],
            [SMEM] + [VMEM] * (2 + zn),
            scratch=[pltpu.VMEM((zn * tokens, cols), BF16)],
            flops=2 * slots * zn * tokens * cols,
            name="pack_gates" if gates else "pack",
        )[0]

    def combine(chosen, back, gates):
        parts = call(
            functools.partial(combine_kernel, **fixed, rows=rows, gates=gates),
            [shape(tokens + TAIL if gates else tokens, cols)] * zn,
            [info, meta, sel, chosen, back],
            [SMEM] + [VMEM] * 4,
            flops=2 * slots * zn * tokens * cols,
            name="combine_gates" if gates else "combine",
        )
        return [outer_send(part, -s) for s, part in enumerate(parts)]

    def core_sum(parts):
        total = parts[0].astype(F32)
        for j in range(1, nt):
            total += tensor_send(parts[j], j).astype(F32)
        return total.astype(BF16)

    work = 2 * slots * hid_n * width
    weights = [pltpu.VMEM((hid_n, nt * cols), BF16)] * 3
    sizes = dict(nt=nt, pn=pn, rows=rows, cols=cols)

    x_packed = pack(x_parts, False)
    x_here = inner_exchange(x_packed)
    xs = [tensor_send(x_here, j) for j in range(nt)]
    grad_whole = after(second_grad, *x_parts[1:])
    c_parts = [outer_send(grad_whole, s) for s in range(zn)]
    ones, gated = call(
        functools.partial(route_kernel, **fixed, picks=picks, cap=cap),
        [shape(zn * tokens, slots)] * 2,
        [info, after(meta, x_packed)],
        [SMEM, VMEM],
        name="route",
    )
    c_packed = pack(c_parts, True)
    c_here = inner_exchange(c_packed)

    forward = call(
        functools.partial(forward_kernel, **sizes),
        [shape(pn, rows, cols)] * nt + [shape(slots, hid_n)] * 3,
        [info, *xs, expert_in, expert_out],
        [SMEM] + [HBM] * (nt + 2),
        out_specs=[HBM] * nt + [VMEM] * 3,
        scratch=[pltpu.VMEM((slots, nt * cols), BF16)]
        + weights
        + [
            pltpu.VMEM((nt, pn, rows, cols), BF16),
            pltpu.SemaphoreType.DMA(((3 + pn) * nt,)),
            pltpu.SemaphoreType.DMA((pn // 2 * nt,)),
        ],
        flops=3 * work,
        name="expert_forward",
    )
    outs, (hid, a1, a2) = forward[:nt], forward[nt:]
    c_here = after(c_here, hid)
    cs = [tensor_send(c_here, j) for j in range(nt)]
    out_here = core_sum(outs)
    out_back = inner_exchange(out_here)

    backward = call(
        functools.partial(backward_kernel, **sizes),
        [shape(pn, rows + TAIL, cols)] * nt + [shape(slots, hid_n)] * 3,
        [info, *cs, expert_in, expert_out, after(hid, out_here), a1, a2],
        [SMEM] + [HBM] * (nt + 5),
        out_specs=[HBM] * nt + [VMEM] * 3,
        scratch=[pltpu.VMEM((slots, nt * cols), BF16), pltpu.VMEM((pn, TAIL, cols), BF16)]
        + [pltpu.VMEM((slots, hid_n), BF16)] * 3
        + weights
        + [
            pltpu.VMEM((nt, pn, rows + TAIL, cols), BF16),
            pltpu.SemaphoreType.DMA(((3 + pn) * nt + 4,)),
            pltpu.SemaphoreType.DMA((pn // 2 * nt,)),
        ],
        flops=3 * work,
        name="expert_backward",
    )
    grads, (gg, ug, hs) = backward[:nt], backward[nt:]
    dx_here = core_sum(grads)
    dx_back = inner_exchange(dx_here)
    out_parts = combine(gated, out_back, False)
    grad_parts = combine(ones, dx_back, True)

    grad_in, grad_out = call(
        functools.partial(weights_kernel, **sizes),
        [shape(*expert_in.shape), shape(*expert_out.shape)],
        [info, *xs, *cs, gg, ug, after(hs, dx_here)],
        [SMEM] + [HBM] * (2 * nt + 3),
        out_specs=[HBM, HBM],
        scratch=[
            pltpu.VMEM((3, slots, hid_n), BF16),
            pltpu.VMEM((2, nt, slots, cols), BF16),
            pltpu.VMEM((nt, 3, hid_n, cols), BF16),
            pltpu.SemaphoreType.DMA((3 + 2 * nt * pn,)),
            pltpu.SemaphoreType.DMA((3 * nt,)),
        ],
        flops=3 * work,
        name="expert_weights",
    )

    branch = sum(part.astype(F32) for part in out_parts)
    input_sum = sum(part[:tokens].astype(F32) for part in grad_parts)
    gate_sum = sum(part[tokens : tokens + picks, :tokens].astype(F32) for part in grad_parts)
    restored = (second_half.astype(F32) - branch).astype(BF16)
    carried_grad = (first_grad.astype(F32) + input_sum).astype(BF16)
    return (restored, carried_grad, gate_sum.T, grad_in, grad_out)


def solution(mesh):
    in_specs = (
        P("expert", "tensor"),
        P("expert", "tensor"),
        P("expert", "tensor"),
        P("expert", "tensor"),
        P("expert", None),
        P("expert", None),
        P("expert", None, "tensor", None),
        P("expert", "tensor", None),
    )
    out_specs = (
        P("expert", "tensor"),
        P("expert", "tensor"),
        P("expert", None),
        P("expert", None, "tensor", None),
        P("expert", "tensor", None),
    )
    return jax.shard_map(body, mesh=mesh, in_specs=in_specs, out_specs=out_specs, check_vma=False)
```

```python
import functools

import jax
import jax.numpy as jnp
from jax import lax
from jax.experimental import pallas as pl
from jax.experimental.pallas import tpu as pltpu
from jax.sharding import PartitionSpec as P

PLANE = 4
TAIL = 16
VMEM_LIMIT = 56 * 1024 * 1024
F32 = jnp.float32
BF16 = jnp.bfloat16


def dot_nn(a, b):
    return lax.dot_general(a, b, (((1,), (0,)), ((), ())), preferred_element_type=F32)


def dot_nt(a, b):
    return lax.dot_general(a, b, (((1,), (1,)), ((), ())), preferred_element_type=F32)


def dot_tn(a, b):
    return lax.dot_general(a, b, (((0,), (0,)), ((), ())), preferred_element_type=F32)


def iota(shape, axis):
    return lax.broadcasted_iota(jnp.int32, shape, axis)


SMEM = pl.BlockSpec(memory_space=pltpu.SMEM)
VMEM = pl.BlockSpec(memory_space=pltpu.VMEM)
HBM = pl.BlockSpec(memory_space=pl.ANY)


def call(kernel, outs, args, specs, out_specs=None, scratch=(), name=None):
    return pl.pallas_call(
        kernel,
        out_shape=outs,
        in_specs=specs,
        out_specs=out_specs if out_specs is not None else [VMEM] * len(outs),
        scratch_shapes=list(scratch),
        compiler_params=pltpu.CompilerParams(vmem_limit_bytes=VMEM_LIMIT),
        cost_estimate=pl.CostEstimate(flops=1024, bytes_accessed=1024, transcendentals=0),
        name=name,
    )(*args)


def shape(*dims, dtype=BF16):
    return jax.ShapeDtypeStruct(dims, dtype)


def outer_meta(info, meta, s, zn):
    return meta[lax.rem(info[3] - s + zn, zn)]


def select_kernel(info, meta, sel, *, zn, pn, tokens, picks, cap):
    rows = zn * cap
    partner = iota((8, 1), 0)
    experts = jnp.where(partner < pn, info[0] + (partner ^ info[1]), -2).astype(F32)
    before = (iota((tokens, tokens), 0) < iota((tokens, tokens), 1)).astype(F32).astype(BF16)
    slot = iota((rows, tokens), 0).astype(F32)
    for s in range(zn):
        here = slice(s * tokens, (s + 1) * tokens)
        ids = outer_meta(info, meta, s, zn)
        named = jnp.zeros((8, tokens), F32)
        for k in range(picks):
            named += (ids[k : k + 1, :] == experts).astype(F32)
        dest = dot_nn(named.astype(BF16), before) + s * cap
        dest = jnp.where(named > 0, dest, -1.0)
        for q in range(pn):
            sel[q * rows : (q + 1) * rows, here] = (
                (slot == dest[q : q + 1, :]).astype(F32).astype(BF16)
            )


def route_kernel(info, meta, ones, gated, *, zn, pn, tokens, picks, cap):
    rows = zn * cap
    partner = iota((1, 8), 1)
    experts = jnp.where(partner < pn, info[0] + (partner ^ info[1]), -2).astype(F32)
    after = (iota((tokens, tokens), 1) < iota((tokens, tokens), 0)).astype(F32).astype(BF16)
    eye = (iota((16, 16), 0) == iota((16, 16), 1)).astype(F32).astype(BF16)
    lane = iota((tokens, pn * rows), 1).astype(F32)
    for s in range(zn):
        here = slice(s * tokens, (s + 1) * tokens)
        columned = dot_tn(outer_meta(info, meta, s, zn).astype(BF16), eye)
        named = jnp.zeros((tokens, 8), F32)
        gate = jnp.zeros((tokens, 8), F32)
        for k in range(picks):
            match = (columned[:, k : k + 1] == experts).astype(F32)
            named += match
            gate += match * columned[:, 8 + k : 9 + k]
        dest = dot_nn(after, named.astype(BF16)) + s * cap
        dest = jnp.where(named > 0, dest + rows * partner.astype(F32), -1.0)
        picked = jnp.zeros((tokens, pn * rows), F32)
        weighed = jnp.zeros((tokens, pn * rows), F32)
        for q in range(pn):
            match = lane == dest[:, q : q + 1]
            picked += match.astype(F32)
            weighed += jnp.where(match, gate[:, q : q + 1], 0.0)
        ones[here, :] = picked.astype(BF16)
        gated[here, :] = weighed.astype(BF16)


def pack_kernel(info, meta, sel, *refs, zn, pn, tokens, picks, rows, gates):
    sources, outs, whole = refs[:zn], refs[zn : zn + pn], refs[zn + pn]
    for s in range(zn):
        whole[s * tokens : (s + 1) * tokens, :] = sources[s][...]
    for q in range(pn):
        chosen = sel[q * rows : (q + 1) * rows, :]
        out = outs[q]
        out[0:rows, :] = dot_nn(chosen, whole[...]).astype(BF16)
        if gates:
            expert = (info[0] + (info[1] ^ q)).astype(F32)
            tail = jnp.zeros((TAIL, rows), F32)
            for s in range(zn):
                known = outer_meta(info, meta, s, zn)
                gate = jnp.zeros((1, tokens), F32)
                for k in range(picks):
                    gate += jnp.where(known[k : k + 1, :] == expert, known[8 + k : 9 + k, :], 0.0)
                gate = jnp.broadcast_to(gate, (TAIL, tokens)).astype(BF16)
                tail += dot_nt(gate, chosen[:, s * tokens : (s + 1) * tokens])
            out[rows : rows + TAIL, :] = jnp.zeros((TAIL, out.shape[1]), BF16)
            out[rows : rows + TAIL, 0:rows] = tail.astype(BF16)


def combine_kernel(info, meta, sel, chosen, *refs, zn, pn, tokens, rows, gates):
    backs, outs, whole = refs[:pn], refs[pn : pn + zn], refs[pn + zn]
    cols = whole.shape[1]
    for q in range(pn):
        whole[q * rows : (q + 1) * rows, :] = backs[q][0:rows, :]
    if gates:
        spreads = []
        for q in range(pn):
            row = backs[q][rows : rows + TAIL, 0:rows]
            spreads.append(dot_nn(row, sel[q * rows : (q + 1) * rows, :])[0:8, :])
    for s in range(zn):
        here = slice(s * tokens, (s + 1) * tokens)
        outs[s][0:tokens, :] = dot_nn(chosen[here, :], whole[...]).astype(BF16)
        if gates:
            outs[s][tokens : tokens + TAIL, :] = jnp.zeros((TAIL, cols), BF16)
            ids = outer_meta(info, meta, s, zn)[0:8, :]
            total = jnp.zeros((8, tokens), F32)
            for q in range(pn):
                expert = (info[0] + (info[1] ^ q)).astype(F32)
                total += jnp.where(ids == expert, spreads[q][:, here], 0.0)
            total = jnp.concatenate([total, jnp.zeros((TAIL - 8, tokens), F32)], axis=0)
            outs[s][tokens : tokens + TAIL, 0:tokens] = total.astype(BF16)


class Loads:
    def __init__(self, sems):
        self.sems, self.copies, self.waited = sems, {}, set()

    def add(self, key, source, target):
        self.copies[key] = pltpu.make_async_copy(source, target, self.sems.at[len(self.copies)])
        self.copies[key].start()

    def need(self, *keys):
        for key in keys:
            if key not in self.waited:
                self.waited.add(key)
                self.copies[key].wait()

    def finish(self):
        self.need(*self.copies)


def column_block(info, j, nt, cols):
    block = lax.rem(info[2] - j + nt, nt)
    return pl.ds(pl.multiple_of(block * cols, 128), cols)


def load_weight(loads, info, kind, source, target, blocks, nt, cols):
    for at, j in enumerate(blocks):
        block = source.at[:, column_block(info, j, nt, cols)]
        loads.add((kind, j), block, target.at[:, pl.ds(at * cols, cols)])


def by_core(refs, nt, pn):
    return [refs[j * pn : (j + 1) * pn] for j in range(nt)]


def load_rows(loads, sources, target, group, rows, cols):
    for j, pieces in enumerate(sources):
        for q in group:
            to = target.at[pl.ds(q * rows, rows), pl.ds(j * cols, cols)]
            loads.add(("r", j, q), pieces[q].at[pl.ds(0, rows)], to)


def forward_kernel(info, *refs, nt, pn, rows, cols):
    xs, refs = by_core(refs, nt, pn), refs[nt * pn :]
    win, wout, outs, refs = refs[0], refs[1], refs[2 : nt + 1], refs[nt + 1 :]
    hid, a1, a2, x, wg, wu, wd, stage, in_sems, out_sems = refs
    loads, stores = Loads(in_sems), Loads(out_sems)
    every, others = range(nt), [(nt - j) % nt for j in range(1, nt)]
    groups = [(2 * g, 2 * g + 1) for g in range(pn // 2)]
    load_rows(loads, xs, x, groups[0], rows, cols)
    load_weight(loads, info, "g", win.at[0, 0], wg, every, nt, cols)
    load_weight(loads, info, "u", win.at[0, 1], wu, every, nt, cols)
    for group in groups[1:]:
        load_rows(loads, xs, x, group, rows, cols)
    load_weight(loads, info, "d", wout.at[0], wd, others, nt, cols)
    for g, group in enumerate(groups):
        here = slice(2 * g * rows, 2 * (g + 1) * rows)
        loads.need(*(("r", j, q) for j in every for q in group), *(("g", j) for j in every))
        gate = dot_nt(x[here, :], wg[...])
        loads.need(*(("u", j) for j in every))
        up = dot_nt(x[here, :], wu[...])
        sigma = jax.nn.sigmoid(gate)
        active = gate * sigma
        hidden = (active * up).astype(BF16)
        hid[here, :] = hidden
        a1[here, :] = (up * sigma * (1.0 + gate * (1.0 - sigma))).astype(BF16)
        a2[here, :] = active.astype(BF16)
        loads.need(*(("d", j) for j in others))
        part = dot_nn(hidden, wd[...]).astype(BF16)
        span = pl.ds(2 * g, 2)
        for j in range(nt - 1):
            stage[j, 2 * g : 2 * g + 2] = part[:, j * cols : (j + 1) * cols].reshape(2, rows, cols)
            stores.add((g, j), stage.at[j, span], outs[j].at[span])
    loads.finish()
    stores.finish()


def output_kernel(info, *refs, nt, pn, rows, cols):
    hid, recvs, wout, outs = refs[0], refs[1:nt], refs[nt], refs[nt + 1 : nt + 1 + pn]
    h, got, wd, stage, in_sems, out_sems = refs[nt + 1 + pn :]
    loads, stores = Loads(in_sems), Loads(out_sems)
    loads.add("h", hid, h)
    load_weight(loads, info, "d", wout.at[0], wd, (0,), nt, cols)
    for j in range(nt - 1):
        for g in range(pn // 2):
            span = pl.ds(2 * g, 2)
            loads.add(("r", j, g), recvs[j].at[span], got.at[j, span])
    for g in range(pn // 2):
        here = slice(2 * g * rows, 2 * (g + 1) * rows)
        loads.need("h", ("d", 0))
        part = dot_nn(h[here, :], wd[...])
        for j in range(nt - 1):
            loads.need(("r", j, g))
            part += got[j, 2 * g : 2 * g + 2].reshape(2 * rows, cols).astype(F32)
        stage[2 * g : 2 * g + 2] = part.astype(BF16).reshape(2, rows, cols)
        for q in (2 * g, 2 * g + 1):
            stores.add(q, stage.at[q], outs[q])
    loads.finish()
    stores.finish()


def backward_kernel(info, *refs, nt, pn, rows, cols):
    cs, refs = by_core(refs, nt, pn), refs[nt * pn :]
    (win, wout, hid, a1, a2), refs = refs[:5], refs[5:]
    outs, (own_tails, gg, ug, hs), refs = refs[: nt - 1], refs[nt - 1 : nt + 3], refs[nt + 3 :]
    c, tails, h, b1, b2, wg, wu, wd, stage, in_sems, out_sems = refs
    loads, stores = Loads(in_sems), Loads(out_sems)
    every, others = range(nt), [(nt - j) % nt for j in range(1, nt)]
    groups = [(2 * g, 2 * g + 1) for g in range(pn // 2)]
    load_rows(loads, cs, c, groups[0], rows, cols)
    load_weight(loads, info, "d", wout.at[0], wd, every, nt, cols)
    for q in range(pn):
        loads.add(("t", q), cs[0][q].at[pl.ds(rows, TAIL)], tails.at[q])
    for key, source, target in (("h", hid, h), ("1", a1, b1), ("2", a2, b2)):
        loads.add(key, source, target)
    load_weight(loads, info, "g", win.at[0, 0], wg, others, nt, cols)
    load_weight(loads, info, "u", win.at[0, 1], wu, others, nt, cols)
    for group in groups[1:]:
        load_rows(loads, cs, c, group, rows, cols)
    same = iota((rows, rows), 0) == iota((rows, rows), 1)
    for g, group in enumerate(groups):
        here = slice(2 * g * rows, 2 * (g + 1) * rows)
        loads.need(*(("r", j, q) for j in every for q in group), *(("d", j) for j in every))
        grad = dot_nt(c[here, :], wd[...])
        loads.need("h", "1", "2", *(("t", q) for q in group))
        hidden = h[here, :].astype(F32)
        piece = jnp.sum(grad * hidden, axis=1, keepdims=True)
        gates = []
        for at, q in enumerate(group):
            row = tails[q, :, 0:rows].astype(F32)[0:1, :]
            gates.append(jnp.sum(jnp.where(same, row, 0.0), axis=1, keepdims=True))
            part = piece[at * rows : (at + 1) * rows, :]
            part = jnp.sum(jnp.where(same, part, 0.0), axis=0, keepdims=True)
            part = jnp.broadcast_to(part, (TAIL, rows)).astype(BF16)
            own_tails[q] = jnp.zeros((TAIL, cols), BF16)
            own_tails[q, :, 0:rows] = part
            for j in range(nt - 1):
                stage[j, q, rows : rows + TAIL, :] = jnp.zeros((TAIL, cols), BF16)
                stage[j, q, rows : rows + TAIL, 0:rows] = part
        gate = jnp.concatenate(gates, axis=0)
        grad = gate * grad
        hs[here, :] = (gate * hidden).astype(BF16)
        gate_grad = (grad * b1[here, :].astype(F32)).astype(BF16)
        up_grad = (grad * b2[here, :].astype(F32)).astype(BF16)
        gg[here, :] = gate_grad
        ug[here, :] = up_grad
        loads.need(*((k, j) for k in "gu" for j in others))
        part = (dot_nn(gate_grad, wg[...]) + dot_nn(up_grad, wu[...])).astype(BF16)
        span = pl.ds(2 * g, 2)
        for j in range(nt - 1):
            block = part[:, j * cols : (j + 1) * cols].reshape(2, rows, cols)
            stage[j, 2 * g : 2 * g + 2, 0:rows, :] = block
            stores.add((g, j), stage.at[j, span], outs[j].at[span])
    loads.finish()
    stores.finish()


def input_kernel(info, *refs, nt, pn, rows, cols):
    gg, ug, own_tails, recvs, win = *refs[:3], refs[3 : nt + 2], refs[nt + 2]
    outs, refs = refs[nt + 3 : nt + 3 + pn], refs[nt + 3 + pn :]
    left, got, wg, wu, stage, in_sems, out_sems = refs
    loads, stores = Loads(in_sems), Loads(out_sems)
    loads.add("gg", gg, left.at[0])
    load_weight(loads, info, "g", win.at[0, 0], wg, (0,), nt, cols)
    loads.add("ug", ug, left.at[1])
    load_weight(loads, info, "u", win.at[0, 1], wu, (0,), nt, cols)
    for j in range(nt - 1):
        for g in range(pn // 2):
            span = pl.ds(2 * g, 2)
            loads.add(("r", j, g), recvs[j].at[span], got.at[j, span])
    for g in range(pn // 2):
        here = slice(2 * g * rows, 2 * (g + 1) * rows)
        both = slice(2 * g, 2 * g + 2)
        loads.need("gg", ("g", 0))
        part = dot_nn(left[0, here, :], wg[...])
        loads.need("ug", ("u", 0))
        part += dot_nn(left[1, here, :], wu[...])
        tail = own_tails[both].astype(F32)
        for j in range(nt - 1):
            loads.need(("r", j, g))
            part += got[j, both, 0:rows, :].reshape(2 * rows, cols).astype(F32)
            tail += got[j, both, rows : rows + TAIL, :].astype(F32)
        stage[both, 0:rows, :] = part.astype(BF16).reshape(2, rows, cols)
        stage[both, rows : rows + TAIL, :] = tail.astype(BF16)
        for q in (2 * g, 2 * g + 1):
            stores.add(q, stage.at[q], outs[q])
    loads.finish()
    stores.finish()


def weights_kernel(info, *refs, nt, pn, rows, cols):
    n = nt * pn
    xs, cs, lefts = by_core(refs, nt, pn), by_core(refs[n:], nt, pn), refs[2 * n : 2 * n + 3]
    gin, gout, left, right, stage, in_sems, out_sems = refs[2 * n + 3 :]
    loads, stores = Loads(in_sems), Loads(out_sems)
    order = ((0, 0, xs), (1, 0, xs), (2, 1, cs))
    for w, side, sources in order:
        loads.add(("l", w), lefts[w], left.at[w])
        if w == 1:
            continue
        for j in range(nt):
            for q in range(pn):
                target = right.at[side, j, pl.ds(q * rows, rows)]
                loads.add((side, j, q), sources[j][q].at[pl.ds(0, rows)], target)
    for w, side, _ in order:
        loads.need(("l", w))
        for j in range(nt):
            loads.need(*((side, j, q) for q in range(pn)))
            at = column_block(info, j, nt, cols)
            stage[j, w] = dot_tn(left[w], right[side, j]).astype(BF16)
            target = gout.at[0, :, at] if w == 2 else gin.at[0, w, :, at]
            stores.add((j, w), stage.at[j, w], target)
    loads.finish()
    stores.finish()


def after(value, *others):
    return lax.optimization_barrier((value, *others))[0]


def body(
    first_half,
    second_half,
    first_grad,
    second_grad,
    expert_ids,
    gate_weights,
    expert_in,
    expert_out,
):
    tokens, picks = expert_ids.shape
    groups = lax.axis_size("expert")
    nt = lax.axis_size("tensor")
    pn = PLANE
    zn = groups // pn
    cap = tokens * picks * 7 // (6 * groups)
    rows = zn * cap
    slots = pn * rows
    cols = first_half.shape[1]
    hid_n = expert_out.shape[1]
    me = lax.axis_index("expert")
    info = jnp.stack([(me // pn) * pn, me % pn, lax.axis_index("tensor"), me // pn]).astype(jnp.int32)

    def outer_send(value, s):
        if s % zn == 0:
            return value
        return lax.ppermute(
            value, "expert", [(e, ((e // pn + s) % zn) * pn + e % pn) for e in range(groups)]
        )

    def inner_send(value, q):
        if q == 0:
            return value
        return lax.ppermute(value, "expert", [(e, e ^ q) for e in range(groups)])

    def inner_exchange(pieces):
        return [inner_send(piece, q) for q, piece in enumerate(pieces)]

    def tensor_send(value, j):
        if j == 0:
            return value
        return lax.ppermute(value, "tensor", [(c, (c + j) % nt) for c in range(nt)])

    fixed = dict(zn=zn, pn=pn, tokens=tokens)

    own = jnp.concatenate(
        [
            jnp.pad(expert_ids.T.astype(F32), ((0, 8 - picks), (0, 0)), constant_values=-1.0),
            jnp.pad(gate_weights.T.astype(F32), ((0, 8 - picks), (0, 0))),
        ],
        axis=0,
    )
    columns = [[z * pn + q for z in range(zn)] for q in range(pn)]
    meta = lax.all_to_all(
        jnp.broadcast_to(own[None], (zn,) + own.shape),
        "expert",
        split_axis=0,
        concat_axis=0,
        axis_index_groups=columns,
        tiled=True,
    )
    sel = call(
        functools.partial(select_kernel, **fixed, picks=picks, cap=cap),
        [shape(slots, zn * tokens)],
        [info, meta],
        [SMEM, VMEM],
        name="select",
    )[0]
    x_parts = [outer_send(first_half, s) for s in range(zn)]

    def pack(sel, parts, gates):
        return call(
            functools.partial(pack_kernel, **fixed, picks=picks, rows=rows, gates=gates),
            [shape(rows + TAIL if gates else rows, cols)] * pn,
            [info, meta, sel, *parts],
            [SMEM] + [VMEM] * (2 + zn),
            scratch=[pltpu.VMEM((zn * tokens, cols), BF16)],
                name="pack_gates" if gates else "pack",
        )

    def combine(chosen, backs, gates):
        parts = call(
            functools.partial(combine_kernel, **fixed, rows=rows, gates=gates),
            [shape(tokens + TAIL if gates else tokens, cols)] * zn,
            [info, meta, sel, chosen, *backs],
            [SMEM] + [VMEM] * (3 + pn),
            scratch=[pltpu.VMEM((slots, cols), BF16)],
                name="combine_gates" if gates else "combine",
        )
        return [outer_send(part, -s) for s, part in enumerate(parts)]

    sizes = dict(nt=nt, pn=pn, rows=rows, cols=cols)

    x_packed = pack(sel, x_parts, False)
    x_here = inner_exchange(x_packed)
    xs = [tensor_send(piece, j) for j in range(nt) for piece in x_here]
    grad_whole = after(second_grad, *x_parts[1:])
    c_parts = [outer_send(grad_whole, s) for s in range(zn)]
    ones, gated = call(
        functools.partial(route_kernel, **fixed, picks=picks, cap=cap),
        [shape(zn * tokens, slots)] * 2,
        [info, after(meta, *x_packed)],
        [SMEM, VMEM],
        name="route",
    )
    c_packed = pack(after(sel, ones), c_parts, True)
    c_here = inner_exchange(c_packed)

    dma = pltpu.SemaphoreType.DMA
    forward = call(
        functools.partial(forward_kernel, **sizes),
        [shape(pn, rows, cols)] * (nt - 1) + [shape(slots, hid_n)] * 3,
        [after(info, *c_packed), *xs, expert_in, expert_out],
        [SMEM] + [HBM] * (nt * pn + 2),
        out_specs=[HBM] * (nt - 1) + [VMEM] * 3,
        scratch=[pltpu.VMEM((slots, nt * cols), BF16)]
        + [pltpu.VMEM((hid_n, nt * cols), BF16)] * 2
        + [pltpu.VMEM((hid_n, (nt - 1) * cols), BF16)]
        + [pltpu.VMEM((nt - 1, pn, rows, cols), BF16), dma(((3 + pn) * nt - 1,))]
        + [dma((pn // 2 * (nt - 1),))],
        name="expert_forward",
    )
    outs, (hid, a1, a2) = forward[: nt - 1], forward[nt - 1 :]
    outs = [after(part, *c_here) for part in outs]
    c_here = [after(piece, hid) for piece in c_here]
    cs = [tensor_send(piece, j) for j in range(nt) for piece in c_here]
    out_here = call(
        functools.partial(output_kernel, **sizes),
        [shape(rows, cols)] * pn,
        [info, hid, *(tensor_send(out, j + 1) for j, out in enumerate(outs)), expert_out],
        [SMEM] + [HBM] * (nt + 1),
        out_specs=[HBM] * pn,
        scratch=[pltpu.VMEM((slots, hid_n), BF16), pltpu.VMEM((nt - 1, pn, rows, cols), BF16)]
        + [pltpu.VMEM((hid_n, cols), BF16), pltpu.VMEM((pn, rows, cols), BF16)]
        + [dma((2 + pn // 2 * (nt - 1),)), dma((pn,))],
        name="expert_output",
    )
    out_back = inner_exchange(out_here)

    backward = call(
        functools.partial(backward_kernel, **sizes),
        [shape(pn, rows + TAIL, cols)] * (nt - 1)
        + [shape(pn, TAIL, cols)]
        + [shape(slots, hid_n)] * 3,
        [info, *cs, expert_in, expert_out, after(hid, *out_here), a1, a2],
        [SMEM] + [HBM] * (nt * pn + 5),
        out_specs=[HBM] * (nt - 1) + [VMEM] * 4,
        scratch=[pltpu.VMEM((slots, nt * cols), BF16), pltpu.VMEM((pn, TAIL, cols), BF16)]
        + [pltpu.VMEM((slots, hid_n), BF16)] * 3
        + [pltpu.VMEM((hid_n, (nt - 1) * cols), BF16)] * 2
        + [pltpu.VMEM((hid_n, nt * cols), BF16)]
        + [pltpu.VMEM((nt - 1, pn, rows + TAIL, cols), BF16), dma(((3 + pn) * nt + 1 + pn,))]
        + [dma((pn // 2 * (nt - 1),))],
        name="expert_backward",
    )
    grads, (tails, gg, ug, hs) = backward[: nt - 1], backward[nt - 1 :]
    grads = [after(part, *out_back) for part in grads]
    dx_here = call(
        functools.partial(input_kernel, **sizes),
        [shape(rows + TAIL, cols)] * pn,
        [info, gg, ug, tails, *(tensor_send(part, j + 1) for j, part in enumerate(grads)), expert_in],
        [SMEM] + [HBM] * 2 + [VMEM] + [HBM] * nt,
        out_specs=[HBM] * pn,
        scratch=[pltpu.VMEM((2, slots, hid_n), BF16)]
        + [pltpu.VMEM((nt - 1, pn, rows + TAIL, cols), BF16)]
        + [pltpu.VMEM((hid_n, cols), BF16)] * 2
        + [pltpu.VMEM((pn, rows + TAIL, cols), BF16)]
        + [dma((4 + pn // 2 * (nt - 1),)), dma((pn,))],
        name="expert_input",
    )
    dx_back = inner_exchange(dx_here)
    out_parts = combine(gated, out_back, False)
    grad_parts = combine(ones, dx_back, True)

    grad_in, grad_out = call(
        functools.partial(weights_kernel, **sizes),
        [shape(*expert_in.shape), shape(*expert_out.shape)],
        [info, *xs, *cs, gg, ug, after(hs, *dx_here)],
        [SMEM] + [HBM] * (2 * nt * pn + 3),
        out_specs=[HBM, HBM],
        scratch=[
            pltpu.VMEM((3, slots, hid_n), BF16),
            pltpu.VMEM((2, nt, slots, cols), BF16),
            pltpu.VMEM((nt, 3, hid_n, cols), BF16),
            pltpu.SemaphoreType.DMA((3 + 2 * nt * pn,)),
            pltpu.SemaphoreType.DMA((3 * nt,)),
        ],
        name="expert_weights",
    )

    branch = sum(part.astype(F32) for part in out_parts)
    input_sum = sum(part[:tokens].astype(F32) for part in grad_parts)
    gate_sum = sum(part[tokens : tokens + picks, :tokens].astype(F32) for part in grad_parts)
    restored = (second_half.astype(F32) - branch).astype(BF16)
    carried_grad = (first_grad.astype(F32) + input_sum).astype(BF16)
    return (restored, carried_grad, gate_sum.T, grad_in, grad_out)


def solution(mesh):
    in_specs = (
        P("expert", "tensor"),
        P("expert", "tensor"),
        P("expert", "tensor"),
        P("expert", "tensor"),
        P("expert", None),
        P("expert", None),
        P("expert", None, "tensor", None),
        P("expert", "tensor", None),
    )
    out_specs = (
        P("expert", "tensor"),
        P("expert", "tensor"),
        P("expert", None),
        P("expert", None, "tensor", None),
        P("expert", "tensor", None),
    )
    return jax.shard_map(body, mesh=mesh, in_specs=in_specs, out_specs=out_specs, check_vma=False)
```

```python
import functools

import jax
import jax.numpy as jnp
from jax import lax
from jax.experimental import pallas as pl
from jax.experimental.pallas import tpu as pltpu
from jax.sharding import PartitionSpec as P

PLANE = 4
CHUNKS = 1
TAIL = 16
VMEM_LIMIT = 60 * 1024 * 1024
F32 = jnp.float32
BF16 = jnp.bfloat16


def dot_nn(a, b):
    return lax.dot_general(a, b, (((1,), (0,)), ((), ())), preferred_element_type=F32)


def dot_nt(a, b):
    return lax.dot_general(a, b, (((1,), (1,)), ((), ())), preferred_element_type=F32)


def dot_tn(a, b):
    return lax.dot_general(a, b, (((0,), (0,)), ((), ())), preferred_element_type=F32)


def iota(shape, axis):
    return lax.broadcasted_iota(jnp.int32, shape, axis)


SMEM = pl.BlockSpec(memory_space=pltpu.SMEM)
VMEM = pl.BlockSpec(memory_space=pltpu.VMEM)
HBM = pl.BlockSpec(memory_space=pl.ANY)


def call(kernel, outs, args, specs, out_specs=None, scratch=(), name=None):
    return pl.pallas_call(
        kernel,
        out_shape=outs,
        in_specs=specs,
        out_specs=out_specs if out_specs is not None else [VMEM] * len(outs),
        scratch_shapes=list(scratch),
        compiler_params=pltpu.CompilerParams(vmem_limit_bytes=VMEM_LIMIT),
        cost_estimate=pl.CostEstimate(flops=1024, bytes_accessed=1024, transcendentals=0),
        name=name,
    )(*args)


def shape(*dims, dtype=BF16):
    return jax.ShapeDtypeStruct(dims, dtype)


def outer_meta(info, meta, s, zn):
    return meta[lax.rem(info[3] - s + zn, zn)]


def select_kernel(info, meta, *sels, zn, pn, tokens, picks, cap):
    zc = zn // CHUNKS
    rows = zc * cap
    partner = iota((8, 1), 0)
    experts = jnp.where(partner < pn, info[0] + (partner ^ info[1]), -2).astype(F32)
    before = (iota((tokens, tokens), 0) < iota((tokens, tokens), 1)).astype(F32).astype(BF16)
    slot = iota((rows, tokens), 0).astype(F32)
    for s in range(zn):
        g, local = divmod(s, zc)
        ids = outer_meta(info, meta, s, zn)
        named = jnp.zeros((8, tokens), F32)
        for k in range(picks):
            named += (ids[k : k + 1, :] == experts).astype(F32)
        dest = dot_nn(named.astype(BF16), before) + local * cap
        dest = jnp.where(named > 0, dest, -1.0)
        for q in range(pn):
            sels[g][q * rows : (q + 1) * rows, local * tokens : (local + 1) * tokens] = (
                (slot == dest[q : q + 1, :]).astype(F32).astype(BF16)
            )


def route_kernel(info, meta, ones, *, zn, pn, tokens, picks, cap):
    rows = zn * cap
    partner = iota((1, 8), 1)
    experts = jnp.where(partner < pn, info[0] + (partner ^ info[1]), -2).astype(F32)
    after = (iota((tokens, tokens), 1) < iota((tokens, tokens), 0)).astype(F32).astype(BF16)
    eye = (iota((16, 16), 0) == iota((16, 16), 1)).astype(F32).astype(BF16)
    lane = iota((tokens, pn * rows), 1).astype(F32)
    for s in range(zn):
        here = slice(s * tokens, (s + 1) * tokens)
        columned = dot_tn(outer_meta(info, meta, s, zn).astype(BF16), eye)
        named = jnp.zeros((tokens, 8), F32)
        for k in range(picks):
            named += (columned[:, k : k + 1] == experts).astype(F32)
        dest = dot_nn(after, named.astype(BF16)) + s * cap
        dest = jnp.where(named > 0, dest + rows * partner.astype(F32), -1.0)
        picked = jnp.zeros((tokens, pn * rows), F32)
        for q in range(pn):
            picked += (lane == dest[:, q : q + 1]).astype(F32)
        ones[here, :] = picked.astype(BF16)


def tail_lanes(rows):
    return -(-rows // 128) * 128


class Loads:
    def __init__(self, sems):
        self.sems, self.copies, self.waited = sems, {}, set()

    def add(self, key, source, target):
        self.copies[key] = pltpu.make_async_copy(source, target, self.sems.at[len(self.copies)])
        self.copies[key].start()

    def need(self, *keys):
        for key in keys:
            if key not in self.waited:
                self.waited.add(key)
                self.copies[key].wait()

    def finish(self):
        self.need(*self.copies)


def pack_kernel(info, sel, source, *refs, zn, pn, tokens, rows):
    outs, whole, sems = refs[:pn], refs[-2], refs[-1]
    loads = Loads(sems)
    for s in range(zn):
        place = lax.rem(info[3] - s + zn, zn)
        loads.add(s, source.at[place], whole.at[pl.ds(s * tokens, tokens)])
    loads.finish()
    for q in range(pn):
        outs[q][...] = dot_nn(sel[q * rows : (q + 1) * rows, :], whole[...]).astype(BF16)


def pack_gates_kernel(info, meta, *refs, zn, pn, tokens, picks, rows):
    zc = zn // CHUNKS
    sels, sources = refs[:CHUNKS], refs[CHUNKS : CHUNKS + zc]
    outs, whole, sems = refs[CHUNKS + zc : CHUNKS + zc + pn], refs[-2], refs[-1]
    loads = Loads(sems)
    for s in range(zc):
        loads.add(s, sources[s], whole.at[pl.ds(s * tokens, tokens)])
    for q in range(pn):
        expert = (info[0] + (info[1] ^ q)).astype(F32)
        outs[q][rows : rows + TAIL, :] = jnp.zeros((TAIL, outs[q].shape[1]), BF16)
        for g in range(CHUNKS):
            tail = jnp.zeros((TAIL, rows), F32)
            for local in range(zc):
                known = outer_meta(info, meta, g * zc + local, zn)
                gate = jnp.zeros((1, tokens), F32)
                for k in range(picks):
                    gate += jnp.where(known[k : k + 1, :] == expert, known[8 + k : 9 + k, :], 0.0)
                gate = jnp.broadcast_to(gate, (TAIL, tokens)).astype(BF16)
                here = slice(local * tokens, (local + 1) * tokens)
                tail += dot_nt(gate, sels[g][q * rows : (q + 1) * rows, here])
            at = g * tail_lanes(rows)
            outs[q][rows : rows + TAIL, at : at + rows] = tail.astype(BF16)
    loads.finish()
    for q in range(pn):
        chosen = sels[0][q * rows : (q + 1) * rows, :]
        outs[q][0:rows, :] = dot_nn(chosen, whole[...]).astype(BF16)


def combine_kernel(info, meta, *refs, zn, pn, tokens, rows, gates):
    zc, part_rows = zn // CHUNKS, rows // CHUNKS
    sels, chosen, backs = refs[:CHUNKS], refs[CHUNKS], refs[CHUNKS + 1 : CHUNKS + 1 + pn]
    outs, (whole, tails, sems) = refs[CHUNKS + 1 + pn : -3], refs[-3:]
    cols = whole.shape[1]
    loads = Loads(sems)
    for q in range(pn):
        if gates:
            loads.add(("t", q), backs[q].at[pl.ds(rows, TAIL)], tails.at[q])
        loads.add(q, backs[q].at[pl.ds(0, rows)], whole.at[pl.ds(q * rows, rows)])
    totals = {}
    if gates:
        loads.need(*(("t", q) for q in range(pn)))
        for g in range(CHUNKS):
            spreads = []
            for q in range(pn):
                at = g * tail_lanes(part_rows)
                row = tails[q, :, at : at + part_rows]
                spreads.append(dot_nn(row, sels[g][q * part_rows : (q + 1) * part_rows, :])[0:8, :])
            for local in range(zc):
                ids = outer_meta(info, meta, g * zc + local, zn)[0:8, :]
                total = jnp.zeros((8, tokens), F32)
                for q in range(pn):
                    expert = (info[0] + (info[1] ^ q)).astype(F32)
                    spread = spreads[q][:, local * tokens : (local + 1) * tokens]
                    total += jnp.where(ids == expert, spread, 0.0)
                totals[g * zc + local] = jnp.concatenate(
                    [total, jnp.zeros((TAIL - 8, tokens), F32)], axis=0
                ).astype(BF16)
    loads.finish()
    for s in range(zn):
        here = slice(s * tokens, (s + 1) * tokens)
        part = dot_nn(chosen[here, :], whole[...]).astype(BF16)
        if not gates:
            outs[0][lax.rem(info[3] - s + zn, zn)] = part
        else:
            outs[s][0:tokens, :] = part
            outs[s][tokens : tokens + TAIL, :] = jnp.zeros((TAIL, cols), BF16)
            outs[s][tokens : tokens + TAIL, 0:tokens] = totals[s]


def column_block(info, j, nt, cols):
    block = lax.rem(info[2] - j + nt, nt)
    return pl.ds(pl.multiple_of(block * cols, 128), cols)


def load_weight(loads, info, kind, source, target, blocks, nt, cols):
    for at, j in enumerate(blocks):
        block = source.at[:, column_block(info, j, nt, cols)]
        loads.add((kind, j), block, target.at[:, pl.ds(at * cols, cols)])


def by_core(refs, nt, pn):
    return [refs[j * pn : (j + 1) * pn] for j in range(nt)]


def load_chunk(loads, sources, target, g, pn, rows, cols):
    for j, pieces in enumerate(sources):
        for q in range(pn):
            to = target.at[pl.ds((g * pn + q) * rows, rows), pl.ds(j * cols, cols)]
            loads.add(("r", g, j, q), pieces[g * pn + q].at[pl.ds(0, rows)], to)


def halves(pn):
    units = [(g, q) for g in range(CHUNKS) for q in range(pn)]
    return units[: len(units) // 2], units[len(units) // 2 :]


def forward_kernel(info, *refs, nt, pn, rows, cols):
    n = CHUNKS * pn
    xs, refs = by_core(refs, nt, n), refs[nt * n :]
    (win, wout), outs, refs = refs[:2], by_core(refs[2:], nt, pn), refs[2 + nt * pn :]
    hs, hid, a1, a2, x, tails, wg, wu, wd, stage, in_sems, out_sems = refs
    loads, stores = Loads(in_sems), Loads(out_sems)
    every = range(nt)
    load_chunk(loads, xs, x, 0, pn, rows, cols)
    load_weight(loads, info, "g", win.at[0, 0], wg, every, nt, cols)
    load_weight(loads, info, "u", win.at[0, 1], wu, every, nt, cols)
    for q in range(pn):
        loads.add(("t", q), xs[0][q].at[pl.ds(rows, TAIL)], tails.at[q])
    for g in range(1, CHUNKS):
        load_chunk(loads, xs, x, g, pn, rows, cols)
    load_weight(loads, info, "d", wout.at[0], wd, every, nt, cols)
    same = iota((rows, rows), 0) == iota((rows, rows), 1)
    tail_step = tail_lanes(rows)
    for b, units in enumerate(halves(pn)):
        here = slice(b * len(units) * rows, (b + 1) * len(units) * rows)
        loads.need(*(("r", g, j, q) for j in every for g, q in units))
        loads.need(*(("g", j) for j in every))
        gate = dot_nt(x[here, :], wg[...])
        loads.need(*(("u", j) for j in every), *(("t", q) for q in range(pn)))
        up = dot_nt(x[here, :], wu[...])
        columns = []
        for g, q in units:
            row = tails[q, :, g * tail_step : g * tail_step + rows].astype(F32)[0:1, :]
            columns.append(jnp.sum(jnp.where(same, row, 0.0), axis=1, keepdims=True))
        weight = jnp.concatenate(columns, axis=0)
        sigma = jax.nn.sigmoid(gate)
        active = gate * sigma
        hidden = active * up
        scaled = (weight * hidden).astype(BF16)
        hs[here, :] = scaled
        hid[here, :] = hidden.astype(BF16)
        a1[here, :] = (weight * (up * sigma * (1.0 + gate * (1.0 - sigma)))).astype(BF16)
        a2[here, :] = (weight * active).astype(BF16)
        loads.need(*(("d", j) for j in every))
        part = dot_nn(scaled, wd[...]).astype(BF16)
        for j in reversed(every):
            w = (nt - j) % nt
            for u, (g, q) in enumerate(units):
                block = part[u * rows : (u + 1) * rows, w * cols : (w + 1) * cols]
                stage[j, q, g * rows : (g + 1) * rows, :] = block
                if g == CHUNKS - 1:
                    stores.add((j, q), stage.at[j, q], outs[j][q])
    loads.finish()
    stores.finish()


def backward_kernel(info, *refs, nt, pn, rows, cols):
    n = CHUNKS * pn
    cs, refs = by_core(refs, nt, n), refs[nt * n :]
    (win, wout, hid, a1, a2), outs, refs = refs[:5], by_core(refs[5:], nt, pn), refs[5 + nt * pn :]
    gg, ug, c, h, b1, b2, wg, wu, wd, stage, in_sems, out_sems = refs
    loads, stores = Loads(in_sems), Loads(out_sems)
    every = range(nt)
    load_chunk(loads, cs, c, 0, pn, rows, cols)
    load_weight(loads, info, "d", wout.at[0], wd, every, nt, cols)
    for key, source, target in (("h", hid, h), ("1", a1, b1), ("2", a2, b2)):
        loads.add(key, source, target)
    load_weight(loads, info, "g", win.at[0, 0], wg, every, nt, cols)
    load_weight(loads, info, "u", win.at[0, 1], wu, every, nt, cols)
    for g in range(1, CHUNKS):
        load_chunk(loads, cs, c, g, pn, rows, cols)
    same = iota((rows, rows), 0) == iota((rows, rows), 1)
    tail_step = tail_lanes(rows)
    bottom = slice(CHUNKS * rows, CHUNKS * rows + TAIL)
    for b, units in enumerate(halves(pn)):
        here = slice(b * len(units) * rows, (b + 1) * len(units) * rows)
        loads.need(*(("r", g, j, q) for j in every for g, q in units))
        loads.need(*(("d", j) for j in every))
        grad = dot_nt(c[here, :], wd[...])
        loads.need("h", "1", "2")
        piece = jnp.sum(grad * h[here, :].astype(F32), axis=1, keepdims=True)
        gate_grad = (grad * b1[here, :].astype(F32)).astype(BF16)
        up_grad = (grad * b2[here, :].astype(F32)).astype(BF16)
        gg[here, :] = gate_grad
        ug[here, :] = up_grad
        for u, (g, q) in enumerate(units):
            part = piece[u * rows : (u + 1) * rows, :]
            part = jnp.sum(jnp.where(same, part, 0.0), axis=0, keepdims=True)
            part = jnp.broadcast_to(part, (TAIL, rows)).astype(BF16)
            for j in every:
                if g == 0:
                    stage[j, q, bottom, :] = jnp.zeros((TAIL, cols), BF16)
                stage[j, q, bottom, g * tail_step : g * tail_step + rows] = part
        loads.need(*((k, j) for k in "gu" for j in every))
        part = (dot_nn(gate_grad, wg[...]) + dot_nn(up_grad, wu[...])).astype(BF16)
        for j in reversed(every):
            w = (nt - j) % nt
            for u, (g, q) in enumerate(units):
                block = part[u * rows : (u + 1) * rows, w * cols : (w + 1) * cols]
                stage[j, q, g * rows : (g + 1) * rows, :] = block
                if g == CHUNKS - 1:
                    stores.add((j, q), stage.at[j, q], outs[j][q])
    loads.finish()
    stores.finish()


def weights_kernel(info, *refs, nt, pn, rows, cols):
    n = CHUNKS * pn
    xs, cs, refs = by_core(refs, nt, n), by_core(refs[nt * n :], nt, n), refs[2 * nt * n :]
    lefts, (gin, gout, left, right, stage, in_sems, out_sems) = refs[:3], refs[3:]
    loads, stores = Loads(in_sems), Loads(out_sems)
    order = ((0, 0, xs), (1, 0, xs), (2, 1, cs))
    for w, side, sources in order:
        loads.add(("l", w), lefts[w], left.at[w])
        if w == 1:
            continue
        for j in range(nt):
            for q in range(n):
                target = right.at[side, j, pl.ds(q * rows, rows)]
                loads.add((side, j, q), sources[j][q].at[pl.ds(0, rows)], target)
    for w, side, _ in order:
        loads.need(("l", w))
        for j in range(nt):
            loads.need(*((side, j, q) for q in range(n)))
            at = column_block(info, j, nt, cols)
            stage[j, w] = dot_tn(left[w], right[side, j]).astype(BF16)
            target = gout.at[0, :, at] if w == 2 else gin.at[0, w, :, at]
            stores.add((j, w), stage.at[j, w], target)
    loads.finish()
    stores.finish()


def after(value, *others):
    return lax.optimization_barrier((value, *others))[0]


def body(
    first_half,
    second_half,
    first_grad,
    second_grad,
    expert_ids,
    gate_weights,
    expert_in,
    expert_out,
):
    tokens, picks = expert_ids.shape
    groups = lax.axis_size("expert")
    nt = lax.axis_size("tensor")
    pn = PLANE
    zn = groups // pn
    cap = tokens * picks * 7 // (6 * groups)
    zc = zn // CHUNKS
    part_rows = zc * cap
    rows = CHUNKS * part_rows
    slots = pn * rows
    cols = first_half.shape[1]
    hid_n = expert_out.shape[1]
    me = lax.axis_index("expert")
    info = jnp.stack([(me // pn) * pn, me % pn, lax.axis_index("tensor"), me // pn]).astype(jnp.int32)

    def outer_send(value, s):
        if s % zn == 0:
            return value
        return lax.ppermute(
            value, "expert", [(e, ((e // pn + s) % zn) * pn + e % pn) for e in range(groups)]
        )

    def inner_send(value, q):
        if q == 0:
            return value
        return lax.ppermute(value, "expert", [(e, e ^ q) for e in range(groups)])

    def inner_exchange(pieces):
        return [inner_send(piece, q) for q, piece in enumerate(pieces)]

    def tensor_send(value, j):
        if j == 0:
            return value
        return lax.ppermute(value, "tensor", [(c, (c + j) % nt) for c in range(nt)])

    fixed = dict(zn=zn, pn=pn, tokens=tokens)

    own = jnp.concatenate(
        [
            jnp.pad(expert_ids.T.astype(F32), ((0, 8 - picks), (0, 0)), constant_values=-1.0),
            jnp.pad(gate_weights.T.astype(F32), ((0, 8 - picks), (0, 0))),
        ],
        axis=0,
    )
    columns = [[z * pn + q for z in range(zn)] for q in range(pn)]
    meta = lax.all_to_all(
        jnp.broadcast_to(own[None], (zn,) + own.shape),
        "expert",
        split_axis=0,
        concat_axis=0,
        axis_index_groups=columns,
        tiled=True,
    )
    sels = call(
        functools.partial(select_kernel, **fixed, picks=picks, cap=cap),
        [shape(pn * part_rows, zc * tokens)] * CHUNKS,
        [info, meta],
        [SMEM, VMEM],
        name="select",
    )
    dma = pltpu.SemaphoreType.DMA
    sizes = dict(nt=nt, pn=pn, rows=part_rows, cols=cols)

    def pack(gathered):
        return call(
            functools.partial(pack_kernel, **fixed, rows=part_rows),
            [shape(part_rows, cols)] * pn,
            [info, sels[0], gathered],
            [SMEM, VMEM, HBM],
            scratch=[pltpu.VMEM((zn * tokens, cols), BF16), dma((zn,))],
            name="pack",
        )

    def pack_gates(parts):
        return call(
            functools.partial(pack_gates_kernel, **fixed, picks=picks, rows=part_rows),
            [shape(part_rows + TAIL, cols)] * pn,
            [info, meta, *sels, *parts[:zc]],
            [SMEM] + [VMEM] * (1 + CHUNKS) + [HBM] * zc,
            scratch=[pltpu.VMEM((zc * tokens, cols), BF16), dma((zc,))],
            name="pack_gates",
        )

    def combine(backs, gates):
        parts = call(
            functools.partial(combine_kernel, **fixed, rows=rows, gates=gates),
            [shape(tokens + TAIL, cols)] * zn if gates else [shape(zn, tokens, cols)],
            [info, meta, *sels, chosen, *backs],
            [SMEM] + [VMEM] * (2 + CHUNKS) + [HBM] * pn,
            scratch=[pltpu.VMEM((slots, cols), BF16), pltpu.VMEM((pn, TAIL, cols), BF16)]
            + [dma((2 * pn,))],
            name="combine_gates" if gates else "combine",
        )
        if not gates:
            return lax.psum_scatter(
                parts[0], "expert", scatter_dimension=0, axis_index_groups=columns, tiled=False
            )
        return [outer_send(part, -s) for s, part in enumerate(parts)]

    def swapped(chunks):
        return [tensor_send(piece, j) for j in range(nt) for pieces in chunks for piece in pieces]

    def core_sum(arrays):
        sums = []
        for q in range(pn):
            total = arrays[q].astype(F32)
            for j in range(1, nt):
                total += tensor_send(arrays[j * pn + q], j).astype(F32)
            sums.append(total.astype(BF16))
        return sums

    x_parts = [outer_send(first_half, s) for s in range(zn)]
    x_packed = pack_gates(x_parts)
    x_here = inner_exchange(x_packed)
    gathered = lax.all_gather(
        after(second_grad, *x_parts[1:]), "expert", axis_index_groups=columns, tiled=False
    )
    chosen = call(
        functools.partial(route_kernel, **fixed, picks=picks, cap=cap),
        [shape(zn * tokens, slots)],
        [info, after(meta, *x_packed)],
        [SMEM, VMEM],
        name="route",
    )[0]
    c_packed = pack(after(gathered, chosen))
    c_here = inner_exchange(c_packed)

    xs = swapped((x_here,))
    pieces = nt * CHUNKS * pn
    forward = call(
        functools.partial(forward_kernel, **sizes),
        [shape(rows, cols)] * (nt * pn) + [shape(slots, hid_n)] * 4,
        [after(info, *c_packed), *xs, expert_in, expert_out],
        [SMEM] + [HBM] * (pieces + 2),
        out_specs=[HBM] * (nt * pn) + [VMEM] * 4,
        scratch=[pltpu.VMEM((slots, nt * cols), BF16), pltpu.VMEM((pn, TAIL, cols), BF16)]
        + [pltpu.VMEM((hid_n, nt * cols), BF16)] * 3
        + [pltpu.VMEM((nt, pn, rows, cols), BF16), dma((3 * nt + pieces + pn,))]
        + [dma((nt * pn,))],
        name="expert_forward",
    )
    outs, (hs, hid, a1, a2) = forward[: nt * pn], forward[nt * pn :]
    outs = [after(part, *c_here) for part in outs]
    cs = swapped(([after(piece, hid) for piece in c_here],))
    out_here = core_sum(outs)
    out_back = inner_exchange(out_here)

    backward = call(
        functools.partial(backward_kernel, **sizes),
        [shape(rows + TAIL, cols)] * (nt * pn) + [shape(slots, hid_n)] * 2,
        [info, *cs, expert_in, expert_out, after(hid, *out_here), a1, a2],
        [SMEM] + [HBM] * (pieces + 5),
        out_specs=[HBM] * (nt * pn) + [VMEM] * 2,
        scratch=[pltpu.VMEM((slots, nt * cols), BF16)]
        + [pltpu.VMEM((slots, hid_n), BF16)] * 3
        + [pltpu.VMEM((hid_n, nt * cols), BF16)] * 3
        + [pltpu.VMEM((nt, pn, rows + TAIL, cols), BF16), dma((3 * nt + pieces + 3,))]
        + [dma((nt * pn,))],
        name="expert_backward",
    )
    grads, (gg, ug) = backward[: nt * pn], backward[nt * pn :]
    dx_here = core_sum([after(part, *out_back) for part in grads])
    dx_back = inner_exchange(dx_here)
    branch = combine(out_back, False).astype(F32)
    grad_parts = combine(dx_back, True)

    grad_in, grad_out = call(
        functools.partial(weights_kernel, **sizes),
        [shape(*expert_in.shape), shape(*expert_out.shape)],
        [info, *xs, *cs, gg, ug, after(hs, *dx_here)],
        [SMEM] + [HBM] * (2 * pieces + 3),
        out_specs=[HBM, HBM],
        scratch=[
            pltpu.VMEM((3, slots, hid_n), BF16),
            pltpu.VMEM((2, nt, slots, cols), BF16),
            pltpu.VMEM((nt, 3, hid_n, cols), BF16),
            dma((3 + 2 * pieces,)),
            dma((3 * nt,)),
        ],
        name="expert_weights",
    )

    input_sum = sum(part[:tokens].astype(F32) for part in grad_parts)
    gate_sum = sum(part[tokens : tokens + picks, :tokens].astype(F32) for part in grad_parts)
    restored = (second_half.astype(F32) - branch).astype(BF16)
    carried_grad = (first_grad.astype(F32) + input_sum).astype(BF16)
    return (restored, carried_grad, gate_sum.T, grad_in, grad_out)


def solution(mesh):
    in_specs = (
        P("expert", "tensor"),
        P("expert", "tensor"),
        P("expert", "tensor"),
        P("expert", "tensor"),
        P("expert", None),
        P("expert", None),
        P("expert", None, "tensor", None),
        P("expert", "tensor", None),
    )
    out_specs = (
        P("expert", "tensor"),
        P("expert", "tensor"),
        P("expert", None),
        P("expert", None, "tensor", None),
        P("expert", "tensor", None),
    )
    return jax.shard_map(body, mesh=mesh, in_specs=in_specs, out_specs=out_specs, check_vma=False)
```

```python
import functools

import jax
import jax.numpy as jnp
from jax import lax
from jax.experimental import pallas as pl
from jax.experimental.pallas import tpu as pltpu
from jax.sharding import PartitionSpec as P

PLANE = 4
CHUNKS = 1
TAIL = 16
VMEM_LIMIT = 60 * 1024 * 1024
F32 = jnp.float32
BF16 = jnp.bfloat16


def dot_nn(a, b):
    return lax.dot_general(a, b, (((1,), (0,)), ((), ())), preferred_element_type=F32)


def dot_nt(a, b):
    return lax.dot_general(a, b, (((1,), (1,)), ((), ())), preferred_element_type=F32)


def dot_tn(a, b):
    return lax.dot_general(a, b, (((0,), (0,)), ((), ())), preferred_element_type=F32)


def iota(shape, axis):
    return lax.broadcasted_iota(jnp.int32, shape, axis)


SMEM = pl.BlockSpec(memory_space=pltpu.SMEM)
VMEM = pl.BlockSpec(memory_space=pltpu.VMEM)
HBM = pl.BlockSpec(memory_space=pl.ANY)


def call(kernel, outs, args, specs, out_specs=None, scratch=(), name=None):
    return pl.pallas_call(
        kernel,
        out_shape=outs,
        in_specs=specs,
        out_specs=out_specs if out_specs is not None else [VMEM] * len(outs),
        scratch_shapes=list(scratch),
        compiler_params=pltpu.CompilerParams(vmem_limit_bytes=VMEM_LIMIT),
        cost_estimate=pl.CostEstimate(flops=1024, bytes_accessed=1024, transcendentals=0),
        name=name,
    )(*args)


def shape(*dims, dtype=BF16):
    return jax.ShapeDtypeStruct(dims, dtype)


def outer_meta(info, meta, s, zn):
    return meta[lax.rem(info[3] - s + zn, zn)]


def select_kernel(info, meta, *sels, zn, pn, tokens, picks, cap):
    zc = zn // CHUNKS
    rows = zc * cap
    partner = iota((8, 1), 0)
    experts = jnp.where(partner < pn, info[0] + (partner ^ info[1]), -2).astype(F32)
    before = (iota((tokens, tokens), 0) < iota((tokens, tokens), 1)).astype(F32).astype(BF16)
    slot = iota((rows, tokens), 0).astype(F32)
    for s in range(zn):
        g, local = divmod(s, zc)
        ids = outer_meta(info, meta, s, zn)
        named = jnp.zeros((8, tokens), F32)
        for k in range(picks):
            named += (ids[k : k + 1, :] == experts).astype(F32)
        dest = dot_nn(named.astype(BF16), before) + local * cap
        dest = jnp.where(named > 0, dest, -1.0)
        for q in range(pn):
            sels[g][q * rows : (q + 1) * rows, local * tokens : (local + 1) * tokens] = (
                (slot == dest[q : q + 1, :]).astype(F32).astype(BF16)
            )


def route_kernel(info, meta, ones, *, zn, pn, tokens, picks, cap):
    rows = zn * cap
    partner = iota((1, 8), 1)
    experts = jnp.where(partner < pn, info[0] + (partner ^ info[1]), -2).astype(F32)
    after = (iota((tokens, tokens), 1) < iota((tokens, tokens), 0)).astype(F32).astype(BF16)
    eye = (iota((16, 16), 0) == iota((16, 16), 1)).astype(F32).astype(BF16)
    lane = iota((tokens, pn * rows), 1).astype(F32)
    for s in range(zn):
        here = slice(s * tokens, (s + 1) * tokens)
        columned = dot_tn(outer_meta(info, meta, s, zn).astype(BF16), eye)
        named = jnp.zeros((tokens, 8), F32)
        for k in range(picks):
            named += (columned[:, k : k + 1] == experts).astype(F32)
        dest = dot_nn(after, named.astype(BF16)) + s * cap
        dest = jnp.where(named > 0, dest + rows * partner.astype(F32), -1.0)
        picked = jnp.zeros((tokens, pn * rows), F32)
        for q in range(pn):
            picked += (lane == dest[:, q : q + 1]).astype(F32)
        ones[here, :] = picked.astype(BF16)


def tail_lanes(rows):
    return -(-rows // 128) * 128


class Loads:
    def __init__(self, sems):
        self.sems, self.copies, self.waited = sems, {}, set()

    def add(self, key, source, target):
        self.copies[key] = pltpu.make_async_copy(source, target, self.sems.at[len(self.copies)])
        self.copies[key].start()

    def need(self, *keys):
        for key in keys:
            if key not in self.waited:
                self.waited.add(key)
                self.copies[key].wait()

    def finish(self):
        self.need(*self.copies)


def pack_kernel(info, sel, source, *refs, zn, pn, tokens, rows):
    outs, whole, sems = refs[:pn], refs[-2], refs[-1]
    loads = Loads(sems)
    for s in range(zn):
        place = lax.rem(info[3] - s + zn, zn)
        loads.add(s, source.at[place], whole.at[pl.ds(s * tokens, tokens)])
    loads.finish()
    for q in range(pn):
        outs[q][...] = dot_nn(sel[q * rows : (q + 1) * rows, :], whole[...]).astype(BF16)


def pack_gates_kernel(info, meta, *refs, zn, pn, tokens, picks, rows):
    zc = zn // CHUNKS
    sels, sources = refs[:CHUNKS], refs[CHUNKS : CHUNKS + zc]
    outs, whole, sems = refs[CHUNKS + zc : CHUNKS + zc + pn], refs[-2], refs[-1]
    loads = Loads(sems)
    for s in range(zc):
        loads.add(s, sources[s], whole.at[pl.ds(s * tokens, tokens)])
    for q in range(pn):
        expert = (info[0] + (info[1] ^ q)).astype(F32)
        outs[q][rows : rows + TAIL, :] = jnp.zeros((TAIL, outs[q].shape[1]), BF16)
        for g in range(CHUNKS):
            tail = jnp.zeros((TAIL, rows), F32)
            for local in range(zc):
                known = outer_meta(info, meta, g * zc + local, zn)
                gate = jnp.zeros((1, tokens), F32)
                for k in range(picks):
                    gate += jnp.where(known[k : k + 1, :] == expert, known[8 + k : 9 + k, :], 0.0)
                gate = jnp.broadcast_to(gate, (TAIL, tokens)).astype(BF16)
                here = slice(local * tokens, (local + 1) * tokens)
                tail += dot_nt(gate, sels[g][q * rows : (q + 1) * rows, here])
            at = g * tail_lanes(rows)
            outs[q][rows : rows + TAIL, at : at + rows] = tail.astype(BF16)
    loads.finish()
    for q in range(pn):
        chosen = sels[0][q * rows : (q + 1) * rows, :]
        outs[q][0:rows, :] = dot_nn(chosen, whole[...]).astype(BF16)


def combine_kernel(info, meta, *refs, zn, pn, tokens, rows, gates):
    zc, part_rows = zn // CHUNKS, rows // CHUNKS
    sels, chosen, backs = refs[:CHUNKS], refs[CHUNKS], refs[CHUNKS + 1 : CHUNKS + 1 + pn]
    outs, (whole, tails, sems) = refs[CHUNKS + 1 + pn : -3], refs[-3:]
    cols = whole.shape[1]
    loads = Loads(sems)
    for q in range(pn):
        if gates:
            loads.add(("t", q), backs[q].at[pl.ds(rows, TAIL)], tails.at[q])
        loads.add(q, backs[q].at[pl.ds(0, rows)], whole.at[pl.ds(q * rows, rows)])
    totals = {}
    if gates:
        loads.need(*(("t", q) for q in range(pn)))
        for g in range(CHUNKS):
            spreads = []
            for q in range(pn):
                at = g * tail_lanes(part_rows)
                row = tails[q, :, at : at + part_rows]
                spreads.append(dot_nn(row, sels[g][q * part_rows : (q + 1) * part_rows, :])[0:8, :])
            for local in range(zc):
                ids = outer_meta(info, meta, g * zc + local, zn)[0:8, :]
                total = jnp.zeros((8, tokens), F32)
                for q in range(pn):
                    expert = (info[0] + (info[1] ^ q)).astype(F32)
                    spread = spreads[q][:, local * tokens : (local + 1) * tokens]
                    total += jnp.where(ids == expert, spread, 0.0)
                totals[g * zc + local] = jnp.concatenate(
                    [total, jnp.zeros((TAIL - 8, tokens), F32)], axis=0
                ).astype(BF16)
    loads.finish()
    for s in range(zn):
        here = slice(s * tokens, (s + 1) * tokens)
        outs[s][0:tokens, :] = dot_nn(chosen[here, :], whole[...]).astype(BF16)
        if gates:
            outs[s][tokens : tokens + TAIL, :] = jnp.zeros((TAIL, cols), BF16)
            outs[s][tokens : tokens + TAIL, 0:tokens] = totals[s]


def column_block(info, j, nt, cols):
    block = lax.rem(info[2] - j + nt, nt)
    return pl.ds(pl.multiple_of(block * cols, 128), cols)


def load_weight(loads, info, kind, source, target, blocks, nt, cols):
    for at, j in enumerate(blocks):
        block = source.at[:, column_block(info, j, nt, cols)]
        loads.add((kind, j), block, target.at[:, pl.ds(at * cols, cols)])


def by_core(refs, nt, pn):
    return [refs[j * pn : (j + 1) * pn] for j in range(nt)]


def load_chunk(loads, sources, target, g, pn, rows, cols):
    for j, pieces in enumerate(sources):
        for q in range(pn):
            to = target.at[pl.ds((g * pn + q) * rows, rows), pl.ds(j * cols, cols)]
            loads.add(("r", g, j, q), pieces[g * pn + q].at[pl.ds(0, rows)], to)


def halves(pn):
    units = [(g, q) for g in range(CHUNKS) for q in range(pn)]
    return units[: len(units) // 2], units[len(units) // 2 :]


def forward_kernel(info, *refs, nt, pn, rows, cols):
    n = CHUNKS * pn
    xs, refs = by_core(refs, nt, n), refs[nt * n :]
    (win, wout), outs, refs = refs[:2], by_core(refs[2:], nt, pn), refs[2 + nt * pn :]
    hs, hid, a1, a2, x, tails, wg, wu, wd, stage, in_sems, out_sems = refs
    loads, stores = Loads(in_sems), Loads(out_sems)
    every = range(nt)
    load_chunk(loads, xs, x, 0, pn, rows, cols)
    load_weight(loads, info, "g", win.at[0, 0], wg, every, nt, cols)
    load_weight(loads, info, "u", win.at[0, 1], wu, every, nt, cols)
    for q in range(pn):
        loads.add(("t", q), xs[0][q].at[pl.ds(rows, TAIL)], tails.at[q])
    for g in range(1, CHUNKS):
        load_chunk(loads, xs, x, g, pn, rows, cols)
    load_weight(loads, info, "d", wout.at[0], wd, every, nt, cols)
    same = iota((rows, rows), 0) == iota((rows, rows), 1)
    tail_step = tail_lanes(rows)
    for b, units in enumerate(halves(pn)):
        here = slice(b * len(units) * rows, (b + 1) * len(units) * rows)
        loads.need(*(("r", g, j, q) for j in every for g, q in units))
        loads.need(*(("g", j) for j in every))
        gate = dot_nt(x[here, :], wg[...])
        loads.need(*(("u", j) for j in every), *(("t", q) for q in range(pn)))
        up = dot_nt(x[here, :], wu[...])
        columns = []
        for g, q in units:
            row = tails[q, :, g * tail_step : g * tail_step + rows].astype(F32)[0:1, :]
            columns.append(jnp.sum(jnp.where(same, row, 0.0), axis=1, keepdims=True))
        weight = jnp.concatenate(columns, axis=0)
        sigma = jax.nn.sigmoid(gate)
        active = gate * sigma
        hidden = active * up
        scaled = (weight * hidden).astype(BF16)
        hs[here, :] = scaled
        hid[here, :] = hidden.astype(BF16)
        a1[here, :] = (weight * (up * sigma * (1.0 + gate * (1.0 - sigma)))).astype(BF16)
        a2[here, :] = (weight * active).astype(BF16)
        loads.need(*(("d", j) for j in every))
        part = dot_nn(scaled, wd[...]).astype(BF16)
        for j in reversed(every):
            w = (nt - j) % nt
            for u, (g, q) in enumerate(units):
                block = part[u * rows : (u + 1) * rows, w * cols : (w + 1) * cols]
                stage[j, q, g * rows : (g + 1) * rows, :] = block
                if g == CHUNKS - 1:
                    stores.add((j, q), stage.at[j, q], outs[j][q])
    loads.finish()
    stores.finish()


def backward_kernel(info, *refs, nt, pn, rows, cols):
    n = CHUNKS * pn
    cs, refs = by_core(refs, nt, n), refs[nt * n :]
    (win, wout, hid, a1, a2), outs, refs = refs[:5], by_core(refs[5:], nt, pn), refs[5 + nt * pn :]
    gg, ug, c, h, b1, b2, wg, wu, wd, stage, in_sems, out_sems = refs
    loads, stores = Loads(in_sems), Loads(out_sems)
    every = range(nt)
    load_chunk(loads, cs, c, 0, pn, rows, cols)
    load_weight(loads, info, "d", wout.at[0], wd, every, nt, cols)
    for key, source, target in (("h", hid, h), ("1", a1, b1), ("2", a2, b2)):
        loads.add(key, source, target)
    load_weight(loads, info, "g", win.at[0, 0], wg, every, nt, cols)
    load_weight(loads, info, "u", win.at[0, 1], wu, every, nt, cols)
    for g in range(1, CHUNKS):
        load_chunk(loads, cs, c, g, pn, rows, cols)
    same = iota((rows, rows), 0) == iota((rows, rows), 1)
    tail_step = tail_lanes(rows)
    bottom = slice(CHUNKS * rows, CHUNKS * rows + TAIL)
    for b, units in enumerate(halves(pn)):
        here = slice(b * len(units) * rows, (b + 1) * len(units) * rows)
        loads.need(*(("r", g, j, q) for j in every for g, q in units))
        loads.need(*(("d", j) for j in every))
        grad = dot_nt(c[here, :], wd[...])
        loads.need("h", "1", "2")
        piece = jnp.sum(grad * h[here, :].astype(F32), axis=1, keepdims=True)
        gate_grad = (grad * b1[here, :].astype(F32)).astype(BF16)
        up_grad = (grad * b2[here, :].astype(F32)).astype(BF16)
        gg[here, :] = gate_grad
        ug[here, :] = up_grad
        for u, (g, q) in enumerate(units):
            part = piece[u * rows : (u + 1) * rows, :]
            part = jnp.sum(jnp.where(same, part, 0.0), axis=0, keepdims=True)
            part = jnp.broadcast_to(part, (TAIL, rows)).astype(BF16)
            for j in every:
                if g == 0:
                    stage[j, q, bottom, :] = jnp.zeros((TAIL, cols), BF16)
                stage[j, q, bottom, g * tail_step : g * tail_step + rows] = part
        loads.need(*((k, j) for k in "gu" for j in every))
        part = (dot_nn(gate_grad, wg[...]) + dot_nn(up_grad, wu[...])).astype(BF16)
        for j in reversed(every):
            w = (nt - j) % nt
            for u, (g, q) in enumerate(units):
                block = part[u * rows : (u + 1) * rows, w * cols : (w + 1) * cols]
                stage[j, q, g * rows : (g + 1) * rows, :] = block
                if g == CHUNKS - 1:
                    stores.add((j, q), stage.at[j, q], outs[j][q])
    loads.finish()
    stores.finish()


def weights_kernel(info, *refs, nt, pn, rows, cols):
    n = CHUNKS * pn
    xs, cs, refs = by_core(refs, nt, n), by_core(refs[nt * n :], nt, n), refs[2 * nt * n :]
    lefts, (gin, gout, left, right, stage, in_sems, out_sems) = refs[:3], refs[3:]
    loads, stores = Loads(in_sems), Loads(out_sems)
    order = ((0, 0, xs), (1, 0, xs), (2, 1, cs))
    for w, side, sources in order:
        loads.add(("l", w), lefts[w], left.at[w])
        if w == 1:
            continue
        for j in range(nt):
            for q in range(n):
                target = right.at[side, j, pl.ds(q * rows, rows)]
                loads.add((side, j, q), sources[j][q].at[pl.ds(0, rows)], target)
    for w, side, _ in order:
        loads.need(("l", w))
        for j in range(nt):
            loads.need(*((side, j, q) for q in range(n)))
            at = column_block(info, j, nt, cols)
            stage[j, w] = dot_tn(left[w], right[side, j]).astype(BF16)
            target = gout.at[0, :, at] if w == 2 else gin.at[0, w, :, at]
            stores.add((j, w), stage.at[j, w], target)
    loads.finish()
    stores.finish()


def after(value, *others):
    return lax.optimization_barrier((value, *others))[0]


def body(
    first_half,
    second_half,
    first_grad,
    second_grad,
    expert_ids,
    gate_weights,
    expert_in,
    expert_out,
):
    tokens, picks = expert_ids.shape
    groups = lax.axis_size("expert")
    nt = lax.axis_size("tensor")
    pn = PLANE
    zn = groups // pn
    cap = tokens * picks * 7 // (6 * groups)
    zc = zn // CHUNKS
    part_rows = zc * cap
    rows = CHUNKS * part_rows
    slots = pn * rows
    cols = first_half.shape[1]
    hid_n = expert_out.shape[1]
    me = lax.axis_index("expert")
    info = jnp.stack([(me // pn) * pn, me % pn, lax.axis_index("tensor"), me // pn]).astype(jnp.int32)

    def outer_send(value, s):
        if s % zn == 0:
            return value
        return lax.ppermute(
            value, "expert", [(e, ((e // pn + s) % zn) * pn + e % pn) for e in range(groups)]
        )

    def inner_send(value, q):
        if q == 0:
            return value
        return lax.ppermute(value, "expert", [(e, e ^ q) for e in range(groups)])

    def inner_exchange(pieces):
        return [inner_send(piece, q) for q, piece in enumerate(pieces)]

    def tensor_send(value, j):
        if j == 0:
            return value
        return lax.ppermute(value, "tensor", [(c, (c + j) % nt) for c in range(nt)])

    fixed = dict(zn=zn, pn=pn, tokens=tokens)

    own = jnp.concatenate(
        [
            jnp.pad(expert_ids.T.astype(F32), ((0, 8 - picks), (0, 0)), constant_values=-1.0),
            jnp.pad(gate_weights.T.astype(F32), ((0, 8 - picks), (0, 0))),
        ],
        axis=0,
    )
    columns = [[z * pn + q for z in range(zn)] for q in range(pn)]
    meta = lax.all_to_all(
        jnp.broadcast_to(own[None], (zn,) + own.shape),
        "expert",
        split_axis=0,
        concat_axis=0,
        axis_index_groups=columns,
        tiled=True,
    )
    sels = call(
        functools.partial(select_kernel, **fixed, picks=picks, cap=cap),
        [shape(pn * part_rows, zc * tokens)] * CHUNKS,
        [info, meta],
        [SMEM, VMEM],
        name="select",
    )
    dma = pltpu.SemaphoreType.DMA
    sizes = dict(nt=nt, pn=pn, rows=part_rows, cols=cols)

    def pack(gathered):
        return call(
            functools.partial(pack_kernel, **fixed, rows=part_rows),
            [shape(part_rows, cols)] * pn,
            [info, sels[0], gathered],
            [SMEM, VMEM, HBM],
            scratch=[pltpu.VMEM((zn * tokens, cols), BF16), dma((zn,))],
            name="pack",
        )

    def pack_gates(parts):
        return call(
            functools.partial(pack_gates_kernel, **fixed, picks=picks, rows=part_rows),
            [shape(part_rows + TAIL, cols)] * pn,
            [info, meta, *sels, *parts[:zc]],
            [SMEM] + [VMEM] * (1 + CHUNKS) + [HBM] * zc,
            scratch=[pltpu.VMEM((zc * tokens, cols), BF16), dma((zc,))],
            name="pack_gates",
        )

    def combine(backs, gates):
        parts = call(
            functools.partial(combine_kernel, **fixed, rows=rows, gates=gates),
            [shape(tokens + TAIL if gates else tokens, cols)] * zn,
            [info, meta, *sels, chosen, *backs],
            [SMEM] + [VMEM] * (2 + CHUNKS) + [HBM] * pn,
            scratch=[pltpu.VMEM((slots, cols), BF16), pltpu.VMEM((pn, TAIL, cols), BF16)]
            + [dma((2 * pn,))],
            name="combine_gates" if gates else "combine",
        )
        return [outer_send(part, -s) for s, part in enumerate(parts)]

    def swapped(chunks):
        return [tensor_send(piece, j) for j in range(nt) for pieces in chunks for piece in pieces]

    def core_sum(arrays):
        sums = []
        for q in range(pn):
            total = arrays[q].astype(F32)
            for j in range(1, nt):
                total += tensor_send(arrays[j * pn + q], j).astype(F32)
            sums.append(total.astype(BF16))
        return sums

    x_parts = [outer_send(first_half if s < 2 else after(first_half, meta), s) for s in range(zn)]
    x_packed = pack_gates(x_parts)
    x_here = inner_exchange(x_packed)
    gathered = lax.all_gather(
        after(second_grad, *x_parts[1:]), "expert", axis_index_groups=columns, tiled=False
    )
    chosen = call(
        functools.partial(route_kernel, **fixed, picks=picks, cap=cap),
        [shape(zn * tokens, slots)],
        [info, after(meta, *x_packed)],
        [SMEM, VMEM],
        name="route",
    )[0]
    c_packed = pack(after(gathered, chosen))
    c_here = inner_exchange(c_packed)

    xs = swapped((x_here,))
    pieces = nt * CHUNKS * pn
    forward = call(
        functools.partial(forward_kernel, **sizes),
        [shape(rows, cols)] * (nt * pn) + [shape(slots, hid_n)] * 4,
        [after(info, *c_packed), *xs, expert_in, expert_out],
        [SMEM] + [HBM] * (pieces + 2),
        out_specs=[HBM] * (nt * pn) + [VMEM] * 4,
        scratch=[pltpu.VMEM((slots, nt * cols), BF16), pltpu.VMEM((pn, TAIL, cols), BF16)]
        + [pltpu.VMEM((hid_n, nt * cols), BF16)] * 3
        + [pltpu.VMEM((nt, pn, rows, cols), BF16), dma((3 * nt + pieces + pn,))]
        + [dma((nt * pn,))],
        name="expert_forward",
    )
    outs, (hs, hid, a1, a2) = forward[: nt * pn], forward[nt * pn :]
    outs = [after(part, *c_here) for part in outs]
    cs = swapped(([after(piece, hid) for piece in c_here],))
    out_here = core_sum(outs)
    out_back = inner_exchange(out_here)

    backward = call(
        functools.partial(backward_kernel, **sizes),
        [shape(rows + TAIL, cols)] * (nt * pn) + [shape(slots, hid_n)] * 2,
        [info, *cs, expert_in, expert_out, after(hid, *out_here), a1, a2],
        [SMEM] + [HBM] * (pieces + 5),
        out_specs=[HBM] * (nt * pn) + [VMEM] * 2,
        scratch=[pltpu.VMEM((slots, nt * cols), BF16)]
        + [pltpu.VMEM((slots, hid_n), BF16)] * 3
        + [pltpu.VMEM((hid_n, nt * cols), BF16)] * 3
        + [pltpu.VMEM((nt, pn, rows + TAIL, cols), BF16), dma((3 * nt + pieces + 3,))]
        + [dma((nt * pn,))],
        name="expert_backward",
    )
    grads, (gg, ug) = backward[: nt * pn], backward[nt * pn :]
    dx_here = core_sum([after(part, *out_back) for part in grads])
    dx_back = inner_exchange(dx_here)
    out_parts = combine([after(piece, *dx_here) for piece in out_back], False)
    grad_parts = combine(dx_back, True)

    grad_in, grad_out = call(
        functools.partial(weights_kernel, **sizes),
        [shape(*expert_in.shape), shape(*expert_out.shape)],
        [info, *xs, *cs, gg, ug, after(hs, *dx_here)],
        [SMEM] + [HBM] * (2 * pieces + 3),
        out_specs=[HBM, HBM],
        scratch=[
            pltpu.VMEM((3, slots, hid_n), BF16),
            pltpu.VMEM((2, nt, slots, cols), BF16),
            pltpu.VMEM((nt, 3, hid_n, cols), BF16),
            dma((3 + 2 * pieces,)),
            dma((3 * nt,)),
        ],
        name="expert_weights",
    )

    branch = sum(part.astype(F32) for part in out_parts)
    input_sum = sum(part[:tokens].astype(F32) for part in grad_parts)
    gate_sum = sum(part[tokens : tokens + picks, :tokens].astype(F32) for part in grad_parts)
    restored = (second_half.astype(F32) - branch).astype(BF16)
    carried_grad = (first_grad.astype(F32) + input_sum).astype(BF16)
    return (restored, carried_grad, gate_sum.T, grad_in, grad_out)


def solution(mesh):
    in_specs = (
        P("expert", "tensor"),
        P("expert", "tensor"),
        P("expert", "tensor"),
        P("expert", "tensor"),
        P("expert", None),
        P("expert", None),
        P("expert", None, "tensor", None),
        P("expert", "tensor", None),
    )
    out_specs = (
        P("expert", "tensor"),
        P("expert", "tensor"),
        P("expert", None),
        P("expert", None, "tensor", None),
        P("expert", "tensor", None),
    )
    return jax.shard_map(body, mesh=mesh, in_specs=in_specs, out_specs=out_specs, check_vma=False)
```

```python
import functools

import jax
import jax.numpy as jnp
from jax import lax
from jax.experimental import pallas as pl
from jax.experimental.pallas import tpu as pltpu
from jax.sharding import PartitionSpec as P

PLANE = 4
CHUNKS = 1
RETURNS = 2
TAIL = 16
VMEM_LIMIT = 62 * 1024 * 1024
F32 = jnp.float32
BF16 = jnp.bfloat16


def dot_nn(a, b):
    return lax.dot_general(a, b, (((1,), (0,)), ((), ())), preferred_element_type=F32)


def dot_nt(a, b):
    return lax.dot_general(a, b, (((1,), (1,)), ((), ())), preferred_element_type=F32)


def dot_tn(a, b):
    return lax.dot_general(a, b, (((0,), (0,)), ((), ())), preferred_element_type=F32)


def iota(shape, axis):
    return lax.broadcasted_iota(jnp.int32, shape, axis)


SMEM = pl.BlockSpec(memory_space=pltpu.SMEM)
VMEM = pl.BlockSpec(memory_space=pltpu.VMEM)
HBM = pl.BlockSpec(memory_space=pl.ANY)


def call(kernel, outs, args, specs, out_specs=None, scratch=(), name=None):
    return pl.pallas_call(
        kernel,
        out_shape=outs,
        in_specs=specs,
        out_specs=out_specs if out_specs is not None else [VMEM] * len(outs),
        scratch_shapes=list(scratch),
        compiler_params=pltpu.CompilerParams(vmem_limit_bytes=VMEM_LIMIT),
        cost_estimate=pl.CostEstimate(flops=1024, bytes_accessed=1024, transcendentals=0),
        name=name,
    )(*args)


def shape(*dims, dtype=BF16):
    return jax.ShapeDtypeStruct(dims, dtype)


def outer_meta(info, meta, s, zn):
    return meta[lax.rem(info[3] - s + zn, zn)]


def select_kernel(info, meta, *sels, zn, pn, tokens, picks, cap):
    zc = zn // CHUNKS
    rows = zc * cap
    partner = iota((8, 1), 0)
    experts = jnp.where(partner < pn, info[0] + (partner ^ info[1]), -2).astype(F32)
    before = (iota((tokens, tokens), 0) < iota((tokens, tokens), 1)).astype(F32).astype(BF16)
    slot = iota((rows, tokens), 0).astype(F32)
    for s in range(zn):
        g, local = divmod(s, zc)
        ids = outer_meta(info, meta, s, zn)
        named = jnp.zeros((8, tokens), F32)
        for k in range(picks):
            named += (ids[k : k + 1, :] == experts).astype(F32)
        dest = dot_nn(named.astype(BF16), before) + local * cap
        dest = jnp.where(named > 0, dest, -1.0)
        for q in range(pn):
            sels[g][q * rows : (q + 1) * rows, local * tokens : (local + 1) * tokens] = (
                (slot == dest[q : q + 1, :]).astype(F32).astype(BF16)
            )


def route_kernel(info, meta, *chosen, zn, pn, tokens, picks, cap):
    zr = zn // RETURNS
    rows = zr * cap
    partner = iota((1, 8), 1)
    experts = jnp.where(partner < pn, info[0] + (partner ^ info[1]), -2).astype(F32)
    after = (iota((tokens, tokens), 1) < iota((tokens, tokens), 0)).astype(F32).astype(BF16)
    eye = (iota((16, 16), 0) == iota((16, 16), 1)).astype(F32).astype(BF16)
    lane = iota((tokens, pn * rows), 1).astype(F32)
    for s in range(zn):
        g, local = divmod(s, zr)
        columned = dot_tn(outer_meta(info, meta, s, zn).astype(BF16), eye)
        named = jnp.zeros((tokens, 8), F32)
        for k in range(picks):
            named += (columned[:, k : k + 1] == experts).astype(F32)
        dest = dot_nn(after, named.astype(BF16)) + local * cap
        dest = jnp.where(named > 0, dest + rows * partner.astype(F32), -1.0)
        picked = jnp.zeros((tokens, pn * rows), F32)
        for q in range(pn):
            picked += (lane == dest[:, q : q + 1]).astype(F32)
        chosen[g][local * tokens : (local + 1) * tokens, :] = picked.astype(BF16)


def tail_lanes(rows):
    return -(-rows // 128) * 128


class Loads:
    def __init__(self, sems):
        self.sems, self.copies, self.waited = sems, {}, set()

    def add(self, key, source, target):
        self.copies[key] = pltpu.make_async_copy(source, target, self.sems.at[len(self.copies)])
        self.copies[key].start()

    def need(self, *keys):
        for key in keys:
            if key not in self.waited:
                self.waited.add(key)
                self.copies[key].wait()

    def finish(self):
        self.need(*self.copies)


def pack_kernel(info, sel, source, *refs, zn, pn, tokens, rows):
    outs, whole, sems = refs[:pn], refs[-2], refs[-1]
    loads = Loads(sems)
    for s in range(zn):
        place = lax.rem(info[3] - s + zn, zn)
        loads.add(s, source.at[place], whole.at[pl.ds(s * tokens, tokens)])
    loads.finish()
    for q in range(pn):
        outs[q][...] = dot_nn(sel[q * rows : (q + 1) * rows, :], whole[...]).astype(BF16)


def pack_gates_kernel(info, meta, *refs, zn, pn, tokens, picks, rows):
    zc = zn // CHUNKS
    sels, sources = refs[:CHUNKS], refs[CHUNKS : CHUNKS + zc]
    outs, whole, sems = refs[CHUNKS + zc : CHUNKS + zc + pn], refs[-2], refs[-1]
    loads = Loads(sems)
    for s in range(zc):
        loads.add(s, sources[s], whole.at[pl.ds(s * tokens, tokens)])
    for q in range(pn):
        expert = (info[0] + (info[1] ^ q)).astype(F32)
        outs[q][rows : rows + TAIL, :] = jnp.zeros((TAIL, outs[q].shape[1]), BF16)
        for g in range(CHUNKS):
            tail = jnp.zeros((TAIL, rows), F32)
            for local in range(zc):
                known = outer_meta(info, meta, g * zc + local, zn)
                gate = jnp.zeros((1, tokens), F32)
                for k in range(picks):
                    gate += jnp.where(known[k : k + 1, :] == expert, known[8 + k : 9 + k, :], 0.0)
                gate = jnp.broadcast_to(gate, (TAIL, tokens)).astype(BF16)
                here = slice(local * tokens, (local + 1) * tokens)
                tail += dot_nt(gate, sels[g][q * rows : (q + 1) * rows, here])
            at = g * tail_lanes(rows)
            outs[q][rows : rows + TAIL, at : at + rows] = tail.astype(BF16)
    loads.finish()
    for q in range(pn):
        chosen = sels[0][q * rows : (q + 1) * rows, :]
        outs[q][0:rows, :] = dot_nn(chosen, whole[...]).astype(BF16)


def combine_kernel(info, *refs, zn, pn, tokens, rows):
    zr = zn // RETURNS
    chosen, backs = refs[:RETURNS], refs[RETURNS : RETURNS + pn]
    out, whole, sems = refs[RETURNS + pn :]
    loads = Loads(sems)
    for g in range(RETURNS):
        for q in range(pn):
            to = whole.at[g, pl.ds(q * rows, rows)]
            loads.add((g, q), backs[q].at[pl.ds(g * rows, rows)], to)
    for g in range(RETURNS):
        loads.need(*((g, q) for q in range(pn)))
        part = dot_nn(chosen[g][...], whole[g]).astype(BF16)
        for local in range(zr):
            place = lax.rem(info[3] - (g * zr + local) + zn, zn)
            out[place] = part[local * tokens : (local + 1) * tokens, :]


def combine_far_kernel(info, meta, sel, chosen, *refs, zn, pn, tokens, rows):
    zr, slots = zn // RETURNS, RETURNS * rows
    backs, outs, (gates, whole, tails, sems) = refs[:pn], refs[pn:-4], refs[-4:]
    loads = Loads(sems)
    for q in range(pn):
        loads.add(("t", q), backs[q].at[pl.ds(rows, TAIL)], tails.at[q])
        loads.add(q, backs[q].at[pl.ds(0, rows)], whole.at[pl.ds(q * rows, rows)])
    spreads = []
    for q in range(pn):
        loads.need(("t", q))
        spreads.append(dot_nn(tails[q, :, 0:slots], sel[q * slots : (q + 1) * slots, :])[0:8, :])
    for s in range(zn):
        ids = outer_meta(info, meta, s, zn)[0:8, :]
        total = jnp.zeros((8, tokens), F32)
        for q in range(pn):
            expert = (info[0] + (info[1] ^ q)).astype(F32)
            total += jnp.where(ids == expert, spreads[q][:, s * tokens : (s + 1) * tokens], 0.0)
        total = jnp.concatenate([total, jnp.zeros((TAIL - 8, tokens), F32)], axis=0)
        gates[:, s * tokens : (s + 1) * tokens] = total.astype(BF16)
    loads.finish()
    finish_combine(chosen, whole, gates, outs, zn - zr, tokens)


def combine_near_kernel(gates, chosen, *refs, pn, tokens, rows):
    backs, outs, (whole, sems) = refs[:pn], refs[pn:-2], refs[-2:]
    loads = Loads(sems)
    for q in range(pn):
        loads.add(q, backs[q], whole.at[pl.ds(q * rows, rows)])
    loads.finish()
    finish_combine(chosen, whole, gates, outs, 0, tokens)


def finish_combine(chosen, whole, gates, outs, first, tokens):
    part = dot_nn(chosen[...], whole[...]).astype(BF16)
    for local, out in enumerate(outs):
        at = first + local
        out[0:tokens, :] = part[local * tokens : (local + 1) * tokens, :]
        out[tokens : tokens + TAIL, :] = jnp.zeros((TAIL, part.shape[1]), BF16)
        out[tokens : tokens + TAIL, 0:tokens] = gates[:, at * tokens : (at + 1) * tokens]


def column_block(info, j, nt, cols):
    block = lax.rem(info[2] - j + nt, nt)
    return pl.ds(pl.multiple_of(block * cols, 128), cols)


def load_weight(loads, info, kind, source, target, blocks, nt, cols):
    for at, j in enumerate(blocks):
        block = source.at[:, column_block(info, j, nt, cols)]
        loads.add((kind, j), block, target.at[:, pl.ds(at * cols, cols)])


def by_core(refs, nt, pn):
    return [refs[j * pn : (j + 1) * pn] for j in range(nt)]


def load_chunk(loads, sources, target, g, pn, rows, cols):
    for j, pieces in enumerate(sources):
        for q in range(pn):
            to = target.at[pl.ds((g * pn + q) * rows, rows), pl.ds(j * cols, cols)]
            loads.add(("r", g, j, q), pieces[g * pn + q].at[pl.ds(0, rows)], to)


def halves(pn):
    units = [(g, q) for g in range(CHUNKS) for q in range(pn)]
    return units[: len(units) // 2], units[len(units) // 2 :]


def forward_kernel(info, *refs, nt, pn, rows, cols):
    n = CHUNKS * pn
    xs, refs = by_core(refs, nt, n), refs[nt * n :]
    (win, wout), outs, refs = refs[:2], by_core(refs[2:], nt, pn), refs[2 + nt * pn :]
    hs, hid, a1, a2, x, tails, wg, wu, wd, stage, in_sems, out_sems = refs
    loads, stores = Loads(in_sems), Loads(out_sems)
    every = range(nt)
    load_chunk(loads, xs, x, 0, pn, rows, cols)
    load_weight(loads, info, "g", win.at[0, 0], wg, every, nt, cols)
    load_weight(loads, info, "u", win.at[0, 1], wu, every, nt, cols)
    for q in range(pn):
        loads.add(("t", q), xs[0][q].at[pl.ds(rows, TAIL)], tails.at[q])
    for g in range(1, CHUNKS):
        load_chunk(loads, xs, x, g, pn, rows, cols)
    load_weight(loads, info, "d", wout.at[0], wd, every, nt, cols)
    same = iota((rows, rows), 0) == iota((rows, rows), 1)
    tail_step = tail_lanes(rows)
    for b, units in enumerate(halves(pn)):
        here = slice(b * len(units) * rows, (b + 1) * len(units) * rows)
        loads.need(*(("r", g, j, q) for j in every for g, q in units))
        loads.need(*(("g", j) for j in every))
        gate = dot_nt(x[here, :], wg[...])
        loads.need(*(("u", j) for j in every), *(("t", q) for q in range(pn)))
        up = dot_nt(x[here, :], wu[...])
        columns = []
        for g, q in units:
            row = tails[q, :, g * tail_step : g * tail_step + rows].astype(F32)[0:1, :]
            columns.append(jnp.sum(jnp.where(same, row, 0.0), axis=1, keepdims=True))
        weight = jnp.concatenate(columns, axis=0)
        sigma = jax.nn.sigmoid(gate)
        active = gate * sigma
        hidden = active * up
        scaled = (weight * hidden).astype(BF16)
        hs[here, :] = scaled
        hid[here, :] = hidden.astype(BF16)
        a1[here, :] = (weight * (up * sigma * (1.0 + gate * (1.0 - sigma)))).astype(BF16)
        a2[here, :] = (weight * active).astype(BF16)
        loads.need(*(("d", j) for j in every))
        part = dot_nn(scaled, wd[...]).astype(BF16)
        for j in reversed(every):
            w = (nt - j) % nt
            for u, (g, q) in enumerate(units):
                block = part[u * rows : (u + 1) * rows, w * cols : (w + 1) * cols]
                stage[j, q, g * rows : (g + 1) * rows, :] = block
                if g == CHUNKS - 1:
                    stores.add((j, q), stage.at[j, q], outs[j][q])
    loads.finish()
    stores.finish()


def backward_kernel(info, *refs, nt, pn, rows, cols):
    n = CHUNKS * pn
    cs, refs = by_core(refs, nt, n), refs[nt * n :]
    (win, wout, hid, a1, a2), outs, refs = refs[:5], by_core(refs[5:], nt, pn), refs[5 + nt * pn :]
    gg, ug, c, h, b1, b2, wg, wu, wd, stage, in_sems, out_sems = refs
    loads, stores = Loads(in_sems), Loads(out_sems)
    every = range(nt)
    load_chunk(loads, cs, c, 0, pn, rows, cols)
    load_weight(loads, info, "d", wout.at[0], wd, every, nt, cols)
    for key, source, target in (("h", hid, h), ("1", a1, b1), ("2", a2, b2)):
        loads.add(key, source, target)
    load_weight(loads, info, "g", win.at[0, 0], wg, every, nt, cols)
    load_weight(loads, info, "u", win.at[0, 1], wu, every, nt, cols)
    for g in range(1, CHUNKS):
        load_chunk(loads, cs, c, g, pn, rows, cols)
    same = iota((rows, rows), 0) == iota((rows, rows), 1)
    tail_step = tail_lanes(rows)
    bottom = slice(CHUNKS * rows, CHUNKS * rows + TAIL)
    for b, units in enumerate(halves(pn)):
        here = slice(b * len(units) * rows, (b + 1) * len(units) * rows)
        loads.need(*(("r", g, j, q) for j in every for g, q in units))
        loads.need(*(("d", j) for j in every))
        grad = dot_nt(c[here, :], wd[...])
        loads.need("h", "1", "2")
        piece = jnp.sum(grad * h[here, :].astype(F32), axis=1, keepdims=True)
        gate_grad = (grad * b1[here, :].astype(F32)).astype(BF16)
        up_grad = (grad * b2[here, :].astype(F32)).astype(BF16)
        gg[here, :] = gate_grad
        ug[here, :] = up_grad
        for u, (g, q) in enumerate(units):
            part = piece[u * rows : (u + 1) * rows, :]
            part = jnp.sum(jnp.where(same, part, 0.0), axis=0, keepdims=True)
            part = jnp.broadcast_to(part, (TAIL, rows)).astype(BF16)
            for j in every:
                if g == 0:
                    stage[j, q, bottom, :] = jnp.zeros((TAIL, cols), BF16)
                stage[j, q, bottom, g * tail_step : g * tail_step + rows] = part
        loads.need(*((k, j) for k in "gu" for j in every))
        part = (dot_nn(gate_grad, wg[...]) + dot_nn(up_grad, wu[...])).astype(BF16)
        for j in reversed(every):
            w = (nt - j) % nt
            for u, (g, q) in enumerate(units):
                block = part[u * rows : (u + 1) * rows, w * cols : (w + 1) * cols]
                stage[j, q, g * rows : (g + 1) * rows, :] = block
                if g == CHUNKS - 1:
                    stores.add((j, q), stage.at[j, q], outs[j][q])
    loads.finish()
    stores.finish()


def weights_kernel(info, *refs, nt, pn, rows, cols):
    n = CHUNKS * pn
    xs, cs, refs = by_core(refs, nt, n), by_core(refs[nt * n :], nt, n), refs[2 * nt * n :]
    lefts, (gin, gout, left, right, stage, in_sems, out_sems) = refs[:3], refs[3:]
    loads, stores = Loads(in_sems), Loads(out_sems)
    order = ((0, 0, xs), (1, 0, xs), (2, 1, cs))
    for w, side, sources in order:
        loads.add(("l", w), lefts[w], left.at[w])
        if w == 1:
            continue
        for j in range(nt):
            for q in range(n):
                target = right.at[side, j, pl.ds(q * rows, rows)]
                loads.add((side, j, q), sources[j][q].at[pl.ds(0, rows)], target)
    for w, side, _ in order:
        loads.need(("l", w))
        for j in range(nt):
            loads.need(*((side, j, q) for q in range(n)))
            at = column_block(info, j, nt, cols)
            stage[j, w] = dot_tn(left[w], right[side, j]).astype(BF16)
            target = gout.at[0, :, at] if w == 2 else gin.at[0, w, :, at]
            stores.add((j, w), stage.at[j, w], target)
    loads.finish()
    stores.finish()


def after(value, *others):
    return lax.optimization_barrier((value, *others))[0]


def body(
    first_half,
    second_half,
    first_grad,
    second_grad,
    expert_ids,
    gate_weights,
    expert_in,
    expert_out,
):
    tokens, picks = expert_ids.shape
    groups = lax.axis_size("expert")
    nt = lax.axis_size("tensor")
    pn = PLANE
    zn = groups // pn
    cap = tokens * picks * 7 // (6 * groups)
    zc = zn // CHUNKS
    part_rows = zc * cap
    rows = CHUNKS * part_rows
    slots = pn * rows
    cols = first_half.shape[1]
    hid_n = expert_out.shape[1]
    me = lax.axis_index("expert")
    info = jnp.stack([(me // pn) * pn, me % pn, lax.axis_index("tensor"), me // pn]).astype(jnp.int32)

    def outer_send(value, s):
        if s % zn == 0:
            return value
        return lax.ppermute(
            value, "expert", [(e, ((e // pn + s) % zn) * pn + e % pn) for e in range(groups)]
        )

    def inner_send(value, q):
        if q == 0:
            return value
        return lax.ppermute(value, "expert", [(e, e ^ q) for e in range(groups)])

    def inner_exchange(pieces):
        return [inner_send(piece, q) for q, piece in enumerate(pieces)]

    def tensor_send(value, j):
        if j == 0:
            return value
        return lax.ppermute(value, "tensor", [(c, (c + j) % nt) for c in range(nt)])

    fixed = dict(zn=zn, pn=pn, tokens=tokens)

    own = jnp.concatenate(
        [
            jnp.pad(expert_ids.T.astype(F32), ((0, 8 - picks), (0, 0)), constant_values=-1.0),
            jnp.pad(gate_weights.T.astype(F32), ((0, 8 - picks), (0, 0))),
        ],
        axis=0,
    )
    columns = [[z * pn + q for z in range(zn)] for q in range(pn)]

    def outer_exchange(value):
        return lax.all_to_all(
            value,
            "expert",
            split_axis=0,
            concat_axis=0,
            axis_index_groups=columns,
            tiled=True,
        )

    def outer_gather(value):
        return outer_exchange(jnp.broadcast_to(value[None], (zn,) + value.shape))

    meta = outer_gather(own)
    sels = call(
        functools.partial(select_kernel, **fixed, picks=picks, cap=cap),
        [shape(pn * part_rows, zc * tokens)] * CHUNKS,
        [info, meta],
        [SMEM, VMEM],
        name="select",
    )
    dma = pltpu.SemaphoreType.DMA
    sizes = dict(nt=nt, pn=pn, rows=part_rows, cols=cols)

    def pack(gathered):
        return call(
            functools.partial(pack_kernel, **fixed, rows=part_rows),
            [shape(part_rows, cols)] * pn,
            [info, sels[0], gathered],
            [SMEM, VMEM, HBM],
            scratch=[pltpu.VMEM((zn * tokens, cols), BF16), dma((zn,))],
            name="pack",
        )

    def pack_gates(parts):
        return call(
            functools.partial(pack_gates_kernel, **fixed, picks=picks, rows=part_rows),
            [shape(part_rows + TAIL, cols)] * pn,
            [info, meta, *sels, *parts[:zc]],
            [SMEM] + [VMEM] * (1 + CHUNKS) + [HBM] * zc,
            scratch=[pltpu.VMEM((zc * tokens, cols), BF16), dma((zc,))],
            name="pack_gates",
        )

    zr = zn // RETURNS
    half = zr * cap

    def send_back(parts, first):
        return [outer_send(part, -(first + local)) for local, part in enumerate(parts)]

    def combine(backs):
        parts = call(
            functools.partial(combine_kernel, **fixed, rows=half),
            [shape(zn, tokens, cols)],
            [info, *chosen, *backs],
            [SMEM] + [VMEM] * RETURNS + [HBM] * pn,
            scratch=[pltpu.VMEM((RETURNS, pn * half, cols), BF16), dma((RETURNS * pn,))],
            name="combine",
        )
        return outer_exchange(parts[0])

    def combine_far(backs):
        *parts, gates = call(
            functools.partial(combine_far_kernel, **fixed, rows=half),
            [shape(tokens + TAIL, cols)] * zr + [shape(TAIL, zn * tokens)],
            [info, meta, sels[0], chosen[RETURNS - 1], *backs],
            [SMEM] + [VMEM] * 3 + [HBM] * pn,
            scratch=[pltpu.VMEM((pn * half, cols), BF16), pltpu.VMEM((pn, TAIL, cols), BF16)]
            + [dma((2 * pn,))],
            name="combine_far",
        )
        return send_back(parts, zn - zr), gates

    def combine_near(gates, backs):
        parts = call(
            functools.partial(combine_near_kernel, pn=pn, tokens=tokens, rows=half),
            [shape(tokens + TAIL, cols)] * zr,
            [gates, chosen[0], *backs],
            [VMEM] * 2 + [HBM] * pn,
            scratch=[pltpu.VMEM((pn * half, cols), BF16), dma((pn,))],
            name="combine_near",
        )
        return send_back(parts, 0)

    def swapped(chunks):
        return [tensor_send(piece, j) for j in range(nt) for pieces in chunks for piece in pieces]

    def core_sum(arrays, spans=(slice(None),)):
        sums = [[] for _ in spans]
        for q in range(pn):
            parts = [tensor_send(arrays[j * pn + q], j) for j in range(nt)]
            for at, span in enumerate(spans):
                total = sum(part[span].astype(F32) for part in parts)
                sums[at].append(total.astype(BF16))
        return sums

    x_parts = [outer_send(first_half, s) for s in range(zn)]
    x_packed = pack_gates(x_parts)
    x_here = inner_exchange(x_packed)
    gathered = outer_gather(after(second_grad, *x_parts[1:]))
    chosen = call(
        functools.partial(route_kernel, **fixed, picks=picks, cap=cap),
        [shape(zr * tokens, pn * half)] * RETURNS,
        [info, after(meta, *x_packed)],
        [SMEM, VMEM],
        name="route",
    )
    c_packed = pack(after(gathered, *chosen))
    c_here = inner_exchange(c_packed)

    xs = swapped(([after(piece, gathered) for piece in x_here],))
    pieces = nt * CHUNKS * pn
    forward = call(
        functools.partial(forward_kernel, **sizes),
        [shape(rows, cols)] * (nt * pn) + [shape(slots, hid_n)] * 4,
        [after(info, *c_packed), *xs, expert_in, expert_out],
        [SMEM] + [HBM] * (pieces + 2),
        out_specs=[HBM] * (nt * pn) + [VMEM] * 4,
        scratch=[pltpu.VMEM((slots, nt * cols), BF16), pltpu.VMEM((pn, TAIL, cols), BF16)]
        + [pltpu.VMEM((hid_n, nt * cols), BF16)] * 3
        + [pltpu.VMEM((nt, pn, rows, cols), BF16), dma((3 * nt + pieces + pn,))]
        + [dma((nt * pn,))],
        name="expert_forward",
    )
    outs, (hs, hid, a1, a2) = forward[: nt * pn], forward[nt * pn :]
    cs = swapped(([after(piece, hid) for piece in c_here],))
    out_here = core_sum(outs)[0]
    out_back = inner_exchange(out_here)

    backward = call(
        functools.partial(backward_kernel, **sizes),
        [shape(rows + TAIL, cols)] * (nt * pn) + [shape(slots, hid_n)] * 2,
        [info, *cs, expert_in, expert_out, after(hid, *out_here), a1, a2],
        [SMEM] + [HBM] * (pieces + 5),
        out_specs=[HBM] * (nt * pn) + [VMEM] * 2,
        scratch=[pltpu.VMEM((slots, nt * cols), BF16)]
        + [pltpu.VMEM((slots, hid_n), BF16)] * 3
        + [pltpu.VMEM((hid_n, nt * cols), BF16)] * 3
        + [pltpu.VMEM((nt, pn, rows + TAIL, cols), BF16), dma((3 * nt + pieces + 3,))]
        + [dma((nt * pn,))],
        name="expert_backward",
    )
    grads, (gg, ug) = backward[: nt * pn], backward[nt * pn :]
    spans = (slice(half, rows + TAIL), slice(0, half))
    far_here, near_here = core_sum([after(part, *out_back) for part in grads], spans)
    far_back = inner_exchange(far_here)
    near_back = inner_exchange(near_here)
    out_parts = combine([after(piece, *near_here) for piece in out_back])

    grad_in, grad_out = call(
        functools.partial(weights_kernel, **sizes),
        [shape(*expert_in.shape), shape(*expert_out.shape)],
        [after(info, *near_here), *xs, *cs, gg, ug, hs],
        [SMEM] + [HBM] * (2 * pieces + 3),
        out_specs=[HBM, HBM],
        scratch=[
            pltpu.VMEM((3, slots, hid_n), BF16),
            pltpu.VMEM((2, nt, slots, cols), BF16),
            pltpu.VMEM((nt, 3, hid_n, cols), BF16),
            dma((3 + 2 * pieces,)),
            dma((3 * nt,)),
        ],
        name="expert_weights",
    )

    far_parts, gate_parts = combine_far([after(piece, grad_in) for piece in far_back])
    grad_parts = combine_near(gate_parts, near_back) + far_parts
    branch = jnp.sum(out_parts.astype(F32), axis=0)
    input_sum = sum(part[:tokens].astype(F32) for part in grad_parts)
    gate_sum = sum(part[tokens : tokens + picks, :tokens].astype(F32) for part in grad_parts)
    restored = (second_half.astype(F32) - branch).astype(BF16)
    carried_grad = (first_grad.astype(F32) + input_sum).astype(BF16)
    return (restored, carried_grad, gate_sum.T, grad_in, grad_out)


def solution(mesh):
    in_specs = (
        P("expert", "tensor"),
        P("expert", "tensor"),
        P("expert", "tensor"),
        P("expert", "tensor"),
        P("expert", None),
        P("expert", None),
        P("expert", None, "tensor", None),
        P("expert", "tensor", None),
    )
    out_specs = (
        P("expert", "tensor"),
        P("expert", "tensor"),
        P("expert", None),
        P("expert", None, "tensor", None),
        P("expert", "tensor", None),
    )
    return jax.shard_map(body, mesh=mesh, in_specs=in_specs, out_specs=out_specs, check_vma=False)
```

```python
import functools

import jax
import jax.numpy as jnp
from jax import lax
from jax.experimental import pallas as pl
from jax.experimental.pallas import tpu as pltpu
from jax.sharding import PartitionSpec as P

PLANE = 4
CHUNKS = 1
RETURNS = 2
TAIL = 16
VMEM_LIMIT = 48 * 1024 * 1024
F32 = jnp.float32
BF16 = jnp.bfloat16


def dot_nn(a, b):
    return lax.dot_general(a, b, (((1,), (0,)), ((), ())), preferred_element_type=F32)


def dot_nt(a, b):
    return lax.dot_general(a, b, (((1,), (1,)), ((), ())), preferred_element_type=F32)


def dot_tn(a, b):
    return lax.dot_general(a, b, (((0,), (0,)), ((), ())), preferred_element_type=F32)


def iota(shape, axis):
    return lax.broadcasted_iota(jnp.int32, shape, axis)


SMEM = pl.BlockSpec(memory_space=pltpu.SMEM)
VMEM = pl.BlockSpec(memory_space=pltpu.VMEM)
HBM = pl.BlockSpec(memory_space=pl.ANY)


def call(kernel, outs, args, specs, out_specs=None, scratch=(), name=None):
    return pl.pallas_call(
        kernel,
        out_shape=outs,
        in_specs=specs,
        out_specs=out_specs if out_specs is not None else [VMEM] * len(outs),
        scratch_shapes=list(scratch),
        compiler_params=pltpu.CompilerParams(vmem_limit_bytes=VMEM_LIMIT),
        cost_estimate=pl.CostEstimate(flops=1024, bytes_accessed=1024, transcendentals=0),
        name=name,
    )(*args)


def shape(*dims, dtype=BF16):
    return jax.ShapeDtypeStruct(dims, dtype)


def outer_meta(info, meta, s, zn):
    return meta[lax.rem(info[3] - s + zn, zn)]


def select_kernel(info, meta, *sels, zn, pn, tokens, picks, cap):
    zc = zn // CHUNKS
    rows = zc * cap
    partner = iota((8, 1), 0)
    experts = jnp.where(partner < pn, info[0] + (partner ^ info[1]), -2).astype(F32)
    before = (iota((tokens, tokens), 0) < iota((tokens, tokens), 1)).astype(F32).astype(BF16)
    slot = iota((rows, tokens), 0).astype(F32)
    for s in range(zn):
        g, local = divmod(s, zc)
        ids = outer_meta(info, meta, s, zn)
        named = jnp.zeros((8, tokens), F32)
        for k in range(picks):
            named += (ids[k : k + 1, :] == experts).astype(F32)
        dest = dot_nn(named.astype(BF16), before) + local * cap
        dest = jnp.where(named > 0, dest, -1.0)
        for q in range(pn):
            sels[g][q * rows : (q + 1) * rows, local * tokens : (local + 1) * tokens] = (
                (slot == dest[q : q + 1, :]).astype(F32).astype(BF16)
            )


def route_kernel(info, meta, *chosen, zn, pn, tokens, picks, cap):
    zr = zn // RETURNS
    rows = zr * cap
    partner = iota((1, 8), 1)
    experts = jnp.where(partner < pn, info[0] + (partner ^ info[1]), -2).astype(F32)
    after = (iota((tokens, tokens), 1) < iota((tokens, tokens), 0)).astype(F32).astype(BF16)
    eye = (iota((16, 16), 0) == iota((16, 16), 1)).astype(F32).astype(BF16)
    lane = iota((tokens, pn * rows), 1).astype(F32)
    for s in range(zn):
        g, local = divmod(s, zr)
        columned = dot_tn(outer_meta(info, meta, s, zn).astype(BF16), eye)
        named = jnp.zeros((tokens, 8), F32)
        for k in range(picks):
            named += (columned[:, k : k + 1] == experts).astype(F32)
        dest = dot_nn(after, named.astype(BF16)) + local * cap
        dest = jnp.where(named > 0, dest + rows * partner.astype(F32), -1.0)
        picked = jnp.zeros((tokens, pn * rows), F32)
        for q in range(pn):
            picked += (lane == dest[:, q : q + 1]).astype(F32)
        chosen[g][local * tokens : (local + 1) * tokens, :] = picked.astype(BF16)


def tail_lanes(rows):
    return -(-rows // 128) * 128


class Loads:
    def __init__(self, sems):
        self.sems, self.copies, self.waited = sems, {}, set()

    def add(self, key, source, target):
        self.copies[key] = pltpu.make_async_copy(source, target, self.sems.at[len(self.copies)])
        self.copies[key].start()

    def need(self, *keys):
        for key in keys:
            if key not in self.waited:
                self.waited.add(key)
                self.copies[key].wait()

    def finish(self):
        self.need(*self.copies)


def pack_kernel(info, sel, source, *refs, zn, pn, tokens, rows):
    outs, whole, sems = refs[:pn], refs[-2], refs[-1]
    loads = Loads(sems)
    for s in range(zn):
        place = lax.rem(info[3] - s + zn, zn)
        loads.add(s, source.at[place], whole.at[pl.ds(s * tokens, tokens)])
    loads.finish()
    for q in range(pn):
        outs[q][...] = dot_nn(sel[q * rows : (q + 1) * rows, :], whole[...]).astype(BF16)


def pack_gates_kernel(info, meta, *refs, zn, pn, tokens, picks, rows):
    zc = zn // CHUNKS
    sels, sources = refs[:CHUNKS], refs[CHUNKS : CHUNKS + zc]
    outs, whole, sems = refs[CHUNKS + zc : CHUNKS + zc + pn], refs[-2], refs[-1]
    loads = Loads(sems)
    for s in range(zc):
        loads.add(s, sources[s], whole.at[pl.ds(s * tokens, tokens)])
    for q in range(pn):
        expert = (info[0] + (info[1] ^ q)).astype(F32)
        outs[q][rows : rows + TAIL, :] = jnp.zeros((TAIL, outs[q].shape[1]), BF16)
        for g in range(CHUNKS):
            tail = jnp.zeros((TAIL, rows), F32)
            for local in range(zc):
                known = outer_meta(info, meta, g * zc + local, zn)
                gate = jnp.zeros((1, tokens), F32)
                for k in range(picks):
                    gate += jnp.where(known[k : k + 1, :] == expert, known[8 + k : 9 + k, :], 0.0)
                gate = jnp.broadcast_to(gate, (TAIL, tokens)).astype(BF16)
                here = slice(local * tokens, (local + 1) * tokens)
                tail += dot_nt(gate, sels[g][q * rows : (q + 1) * rows, here])
            at = g * tail_lanes(rows)
            outs[q][rows : rows + TAIL, at : at + rows] = tail.astype(BF16)
    loads.finish()
    for q in range(pn):
        chosen = sels[0][q * rows : (q + 1) * rows, :]
        outs[q][0:rows, :] = dot_nn(chosen, whole[...]).astype(BF16)


def combine_kernel(info, *refs, zn, pn, tokens, rows):
    zr = zn // RETURNS
    chosen, backs = refs[:RETURNS], refs[RETURNS : RETURNS + pn]
    out, whole, sems = refs[RETURNS + pn :]
    loads = Loads(sems)
    for g in range(RETURNS):
        for q in range(pn):
            to = whole.at[g, pl.ds(q * rows, rows)]
            loads.add((g, q), backs[q].at[pl.ds(g * rows, rows)], to)
    for g in range(RETURNS):
        loads.need(*((g, q) for q in range(pn)))
        part = dot_nn(chosen[g][...], whole[g]).astype(BF16)
        for local in range(zr):
            place = lax.rem(info[3] - (g * zr + local) + zn, zn)
            out[place] = part[local * tokens : (local + 1) * tokens, :]


def combine_far_kernel(info, meta, sel, chosen, *refs, zn, pn, tokens, rows):
    zr, slots = zn // RETURNS, RETURNS * rows
    backs, outs, (gates, whole, tails, sems) = refs[:pn], refs[pn:-4], refs[-4:]
    loads = Loads(sems)
    for q in range(pn):
        loads.add(("t", q), backs[q].at[pl.ds(rows, TAIL)], tails.at[q])
        loads.add(q, backs[q].at[pl.ds(0, rows)], whole.at[pl.ds(q * rows, rows)])
    spreads = []
    for q in range(pn):
        loads.need(("t", q))
        spreads.append(dot_nn(tails[q, :, 0:slots], sel[q * slots : (q + 1) * slots, :])[0:8, :])
    for s in range(zn):
        ids = outer_meta(info, meta, s, zn)[0:8, :]
        total = jnp.zeros((8, tokens), F32)
        for q in range(pn):
            expert = (info[0] + (info[1] ^ q)).astype(F32)
            total += jnp.where(ids == expert, spreads[q][:, s * tokens : (s + 1) * tokens], 0.0)
        total = jnp.concatenate([total, jnp.zeros((TAIL - 8, tokens), F32)], axis=0)
        gates[:, s * tokens : (s + 1) * tokens] = total.astype(BF16)
    loads.finish()
    finish_combine(chosen, whole, gates, outs, zn - zr, tokens)


def combine_near_kernel(gates, chosen, *refs, pn, tokens, rows):
    backs, outs, (whole, sems) = refs[:pn], refs[pn:-2], refs[-2:]
    loads = Loads(sems)
    for q in range(pn):
        loads.add(q, backs[q], whole.at[pl.ds(q * rows, rows)])
    loads.finish()
    finish_combine(chosen, whole, gates, outs, 0, tokens)


def finish_combine(chosen, whole, gates, outs, first, tokens):
    part = dot_nn(chosen[...], whole[...]).astype(BF16)
    for local, out in enumerate(outs):
        at = first + local
        out[0:tokens, :] = part[local * tokens : (local + 1) * tokens, :]
        out[tokens : tokens + TAIL, :] = jnp.zeros((TAIL, part.shape[1]), BF16)
        out[tokens : tokens + TAIL, 0:tokens] = gates[:, at * tokens : (at + 1) * tokens]


def column_block(info, j, nt, cols):
    block = lax.rem(info[2] - j + nt, nt)
    return pl.ds(pl.multiple_of(block * cols, 128), cols)


def load_weight(loads, info, kind, source, target, blocks, nt, cols):
    for at, j in enumerate(blocks):
        block = source.at[:, column_block(info, j, nt, cols)]
        loads.add((kind, j), block, target.at[:, pl.ds(at * cols, cols)])


def by_core(refs, nt, pn):
    return [refs[j * pn : (j + 1) * pn] for j in range(nt)]


def load_chunk(loads, sources, target, g, pn, rows, cols):
    for j, pieces in enumerate(sources):
        for q in range(pn):
            to = target.at[pl.ds((g * pn + q) * rows, rows), pl.ds(j * cols, cols)]
            loads.add(("r", g, j, q), pieces[g * pn + q].at[pl.ds(0, rows)], to)


def halves(pn):
    units = [(g, q) for g in range(CHUNKS) for q in range(pn)]
    return units[: len(units) // 2], units[len(units) // 2 :]


def forward_kernel(info, *refs, nt, pn, rows, cols):
    n = CHUNKS * pn
    xs, refs = by_core(refs, nt, n), refs[nt * n :]
    (win, wout), outs, refs = refs[:2], by_core(refs[2:], nt, pn), refs[2 + nt * pn :]
    hs, hid, a1, a2, x, tails, wg, wu, wd, stage, in_sems, out_sems = refs
    loads, stores = Loads(in_sems), Loads(out_sems)
    every = range(nt)
    load_chunk(loads, xs, x, 0, pn, rows, cols)
    load_weight(loads, info, "g", win.at[0, 0], wg, every, nt, cols)
    load_weight(loads, info, "u", win.at[0, 1], wu, every, nt, cols)
    for q in range(pn):
        loads.add(("t", q), xs[0][q].at[pl.ds(rows, TAIL)], tails.at[q])
    for g in range(1, CHUNKS):
        load_chunk(loads, xs, x, g, pn, rows, cols)
    load_weight(loads, info, "d", wout.at[0], wd, every, nt, cols)
    same = iota((rows, rows), 0) == iota((rows, rows), 1)
    tail_step = tail_lanes(rows)
    for b, units in enumerate(halves(pn)):
        here = slice(b * len(units) * rows, (b + 1) * len(units) * rows)
        loads.need(*(("r", g, j, q) for j in every for g, q in units))
        loads.need(*(("g", j) for j in every))
        gate = dot_nt(x[here, :], wg[...])
        loads.need(*(("u", j) for j in every), *(("t", q) for q in range(pn)))
        up = dot_nt(x[here, :], wu[...])
        columns = []
        for g, q in units:
            row = tails[q, :, g * tail_step : g * tail_step + rows].astype(F32)[0:1, :]
            columns.append(jnp.sum(jnp.where(same, row, 0.0), axis=1, keepdims=True))
        weight = jnp.concatenate(columns, axis=0)
        sigma = jax.nn.sigmoid(gate)
        active = gate * sigma
        hidden = active * up
        scaled = (weight * hidden).astype(BF16)
        hs[here, :] = scaled
        hid[here, :] = hidden.astype(BF16)
        a1[here, :] = (weight * (up * sigma * (1.0 + gate * (1.0 - sigma)))).astype(BF16)
        a2[here, :] = (weight * active).astype(BF16)
        loads.need(*(("d", j) for j in every))
        part = dot_nn(scaled, wd[...]).astype(BF16)
        for j in reversed(every):
            w = (nt - j) % nt
            for u, (g, q) in enumerate(units):
                block = part[u * rows : (u + 1) * rows, w * cols : (w + 1) * cols]
                stage[j, q, g * rows : (g + 1) * rows, :] = block
                if g == CHUNKS - 1:
                    stores.add((j, q), stage.at[j, q], outs[j][q])
    loads.finish()
    stores.finish()


def backward_kernel(info, *refs, nt, pn, rows, cols):
    n = CHUNKS * pn
    cs, refs = by_core(refs, nt, n), refs[nt * n :]
    n_out = RETURNS * nt * pn
    (win, wout, hid, a1, a2), outs, refs = refs[:5], refs[5 : 5 + n_out], refs[5 + n_out :]
    outs = [by_core(outs[r * nt * pn :], nt, pn) for r in range(RETURNS)]
    half = CHUNKS * rows // RETURNS
    gg, ug, c, h, b1, b2, wg, wu, wd, stage, in_sems, out_sems = refs
    loads, stores = Loads(in_sems), Loads(out_sems)
    every = range(nt)
    load_chunk(loads, cs, c, 0, pn, rows, cols)
    load_weight(loads, info, "d", wout.at[0], wd, every, nt, cols)
    for key, source, target in (("h", hid, h), ("1", a1, b1), ("2", a2, b2)):
        loads.add(key, source, target)
    load_weight(loads, info, "g", win.at[0, 0], wg, every, nt, cols)
    load_weight(loads, info, "u", win.at[0, 1], wu, every, nt, cols)
    for g in range(1, CHUNKS):
        load_chunk(loads, cs, c, g, pn, rows, cols)
    same = iota((rows, rows), 0) == iota((rows, rows), 1)
    tail_step = tail_lanes(rows)
    bottom = slice(CHUNKS * rows, CHUNKS * rows + TAIL)
    for b, units in enumerate(halves(pn)):
        here = slice(b * len(units) * rows, (b + 1) * len(units) * rows)
        loads.need(*(("r", g, j, q) for j in every for g, q in units))
        loads.need(*(("d", j) for j in every))
        grad = dot_nt(c[here, :], wd[...])
        loads.need("h", "1", "2")
        piece = jnp.sum(grad * h[here, :].astype(F32), axis=1, keepdims=True)
        gate_grad = (grad * b1[here, :].astype(F32)).astype(BF16)
        up_grad = (grad * b2[here, :].astype(F32)).astype(BF16)
        gg[here, :] = gate_grad
        ug[here, :] = up_grad
        for u, (g, q) in enumerate(units):
            part = piece[u * rows : (u + 1) * rows, :]
            part = jnp.sum(jnp.where(same, part, 0.0), axis=0, keepdims=True)
            part = jnp.broadcast_to(part, (TAIL, rows)).astype(BF16)
            for j in every:
                if g == 0:
                    stage[j, q, bottom, :] = jnp.zeros((TAIL, cols), BF16)
                stage[j, q, bottom, g * tail_step : g * tail_step + rows] = part
        loads.need(*((k, j) for k in "gu" for j in every))
        part = (dot_nn(gate_grad, wg[...]) + dot_nn(up_grad, wu[...])).astype(BF16)
        for j in reversed(every):
            w = (nt - j) % nt
            for u, (g, q) in enumerate(units):
                block = part[u * rows : (u + 1) * rows, w * cols : (w + 1) * cols]
                stage[j, q, g * rows : (g + 1) * rows, :] = block
                for r in reversed(range(RETURNS if g == CHUNKS - 1 else 0)):
                    span = pl.ds(r * half, half + TAIL if r == RETURNS - 1 else half)
                    stores.add((j, q, r), stage.at[j, q, span], outs[r][j][q])
    loads.finish()
    stores.finish()


def weights_kernel(info, *refs, nt, pn, rows, cols):
    n = CHUNKS * pn
    xs, cs, refs = by_core(refs, nt, n), by_core(refs[nt * n :], nt, n), refs[2 * nt * n :]
    lefts, (gin, gout, left, right, stage, in_sems, out_sems) = refs[:3], refs[3:]
    loads, stores = Loads(in_sems), Loads(out_sems)
    order = ((0, 0, xs), (1, 0, xs), (2, 1, cs))
    for w, side, sources in order:
        loads.add(("l", w), lefts[w], left.at[w])
        if w == 1:
            continue
        for j in range(nt):
            for q in range(n):
                target = right.at[side, j, pl.ds(q * rows, rows)]
                loads.add((side, j, q), sources[j][q].at[pl.ds(0, rows)], target)
    for w, side, _ in order:
        loads.need(("l", w))
        for j in range(nt):
            loads.need(*((side, j, q) for q in range(n)))
            at = column_block(info, j, nt, cols)
            stage[j, w] = dot_tn(left[w], right[side, j]).astype(BF16)
            target = gout.at[0, :, at] if w == 2 else gin.at[0, w, :, at]
            stores.add((j, w), stage.at[j, w], target)
    loads.finish()
    stores.finish()


def after(value, *others):
    return lax.optimization_barrier((value, *others))[0]


def body(
    first_half,
    second_half,
    first_grad,
    second_grad,
    expert_ids,
    gate_weights,
    expert_in,
    expert_out,
):
    tokens, picks = expert_ids.shape
    groups = lax.axis_size("expert")
    nt = lax.axis_size("tensor")
    pn = PLANE
    zn = groups // pn
    cap = tokens * picks * 7 // (6 * groups)
    zc = zn // CHUNKS
    part_rows = zc * cap
    rows = CHUNKS * part_rows
    slots = pn * rows
    cols = first_half.shape[1]
    hid_n = expert_out.shape[1]
    me = lax.axis_index("expert")
    info = jnp.stack([(me // pn) * pn, me % pn, lax.axis_index("tensor"), me // pn]).astype(jnp.int32)

    def outer_send(value, s):
        if s % zn == 0:
            return value
        return lax.ppermute(
            value, "expert", [(e, ((e // pn + s) % zn) * pn + e % pn) for e in range(groups)]
        )

    def inner_send(value, q):
        if q == 0:
            return value
        return lax.ppermute(value, "expert", [(e, e ^ q) for e in range(groups)])

    def inner_exchange(pieces):
        return [inner_send(piece, q) for q, piece in enumerate(pieces)]

    def tensor_send(value, j):
        if j == 0:
            return value
        return lax.ppermute(value, "tensor", [(c, (c + j) % nt) for c in range(nt)])

    fixed = dict(zn=zn, pn=pn, tokens=tokens)

    own = jnp.concatenate(
        [
            jnp.pad(expert_ids.T.astype(F32), ((0, 8 - picks), (0, 0)), constant_values=-1.0),
            jnp.pad(gate_weights.T.astype(F32), ((0, 8 - picks), (0, 0))),
        ],
        axis=0,
    )
    columns = [[z * pn + q for z in range(zn)] for q in range(pn)]

    def outer_exchange(value):
        return lax.all_to_all(
            value,
            "expert",
            split_axis=0,
            concat_axis=0,
            axis_index_groups=columns,
            tiled=True,
        )

    def copies(value):
        return jnp.broadcast_to(value[None], (zn,) + value.shape)

    meta = outer_exchange(copies(own))
    sels = call(
        functools.partial(select_kernel, **fixed, picks=picks, cap=cap),
        [shape(pn * part_rows, zc * tokens)] * CHUNKS,
        [info, meta],
        [SMEM, VMEM],
        name="select",
    )
    dma = pltpu.SemaphoreType.DMA
    sizes = dict(nt=nt, pn=pn, rows=part_rows, cols=cols)

    def pack(gathered):
        return call(
            functools.partial(pack_kernel, **fixed, rows=part_rows),
            [shape(part_rows, cols)] * pn,
            [info, sels[0], gathered],
            [SMEM, VMEM, HBM],
            scratch=[pltpu.VMEM((zn * tokens, cols), BF16), dma((zn,))],
            name="pack",
        )

    def pack_gates(parts):
        return call(
            functools.partial(pack_gates_kernel, **fixed, picks=picks, rows=part_rows),
            [shape(part_rows + TAIL, cols)] * pn,
            [info, meta, *sels, *parts[:zc]],
            [SMEM] + [VMEM] * (1 + CHUNKS) + [HBM] * zc,
            scratch=[pltpu.VMEM((zc * tokens, cols), BF16), dma((zc,))],
            name="pack_gates",
        )

    zr = zn // RETURNS
    half = zr * cap

    def send_back(parts, first):
        return [outer_send(part, -(first + local)) for local, part in enumerate(parts)]

    def combine(backs):
        parts = call(
            functools.partial(combine_kernel, **fixed, rows=half),
            [shape(zn, tokens, cols)],
            [info, *chosen, *backs],
            [SMEM] + [VMEM] * RETURNS + [HBM] * pn,
            scratch=[pltpu.VMEM((RETURNS, pn * half, cols), BF16), dma((RETURNS * pn,))],
            name="combine",
        )
        return outer_exchange(parts[0])

    def combine_far(backs):
        *parts, gates = call(
            functools.partial(combine_far_kernel, **fixed, rows=half),
            [shape(tokens + TAIL, cols)] * zr + [shape(TAIL, zn * tokens)],
            [info, meta, sels[0], chosen[RETURNS - 1], *backs],
            [SMEM] + [VMEM] * 3 + [HBM] * pn,
            scratch=[pltpu.VMEM((pn * half, cols), BF16), pltpu.VMEM((pn, TAIL, cols), BF16)]
            + [dma((2 * pn,))],
            name="combine_far",
        )
        return send_back(parts, zn - zr), gates

    def combine_near(gates, backs):
        parts = call(
            functools.partial(combine_near_kernel, pn=pn, tokens=tokens, rows=half),
            [shape(tokens + TAIL, cols)] * zr,
            [gates, chosen[0], *backs],
            [VMEM] * 2 + [HBM] * pn,
            scratch=[pltpu.VMEM((pn * half, cols), BF16), dma((pn,))],
            name="combine_near",
        )
        return send_back(parts, 0)

    def swapped(chunks):
        return [tensor_send(piece, j) for j in range(nt) for pieces in chunks for piece in pieces]

    def core_sum(arrays):
        sums = []
        for q in range(pn):
            total = sum(tensor_send(arrays[j * pn + q], j).astype(F32) for j in range(nt))
            sums.append(total.astype(BF16))
        return sums

    x_parts = [outer_send(first_half, s) for s in range(zn)]
    x_packed = pack_gates(x_parts)
    x_here = inner_exchange(x_packed)
    gathered = outer_exchange(after(copies(second_grad), *x_parts[1:]))
    chosen = call(
        functools.partial(route_kernel, **fixed, picks=picks, cap=cap),
        [shape(zr * tokens, pn * half)] * RETURNS,
        [info, after(meta, *x_packed)],
        [SMEM, VMEM],
        name="route",
    )
    c_packed = pack(after(gathered, *chosen))
    c_here = inner_exchange(c_packed)

    xs = swapped(([after(piece, *c_packed) for piece in x_here],))
    pieces = nt * CHUNKS * pn
    forward = call(
        functools.partial(forward_kernel, **sizes),
        [shape(rows, cols)] * (nt * pn) + [shape(slots, hid_n)] * 4,
        [after(info, *c_packed), *xs, expert_in, expert_out],
        [SMEM] + [HBM] * (pieces + 2),
        out_specs=[HBM] * (nt * pn) + [VMEM] * 4,
        scratch=[pltpu.VMEM((slots, nt * cols), BF16), pltpu.VMEM((pn, TAIL, cols), BF16)]
        + [pltpu.VMEM((hid_n, nt * cols), BF16)] * 3
        + [pltpu.VMEM((nt, pn, rows, cols), BF16), dma((3 * nt + pieces + pn,))]
        + [dma((nt * pn,))],
        name="expert_forward",
    )
    outs, (hs, hid, a1, a2) = forward[: nt * pn], forward[nt * pn :]
    cs = swapped(([after(piece, hid) for piece in c_here],))
    out_here = core_sum(outs)
    out_back = inner_exchange(out_here)

    backward = call(
        functools.partial(backward_kernel, **sizes),
        [
            shape(half + TAIL if r == RETURNS - 1 else half, cols)
            for r in range(RETURNS)
            for _ in range(nt * pn)
        ]
        + [shape(slots, hid_n)] * 2,
        [info, *cs, expert_in, expert_out, after(hid, *out_here), a1, a2],
        [SMEM] + [HBM] * (pieces + 5),
        out_specs=[HBM] * (RETURNS * nt * pn) + [VMEM] * 2,
        scratch=[pltpu.VMEM((slots, nt * cols), BF16)]
        + [pltpu.VMEM((slots, hid_n), BF16)] * 3
        + [pltpu.VMEM((hid_n, nt * cols), BF16)] * 3
        + [pltpu.VMEM((nt, pn, rows + TAIL, cols), BF16), dma((3 * nt + pieces + 3,))]
        + [dma((RETURNS * nt * pn,))],
        name="expert_backward",
    )
    grads, (gg, ug) = backward[: RETURNS * nt * pn], backward[RETURNS * nt * pn :]
    near, far = grads[: nt * pn], grads[nt * pn :]
    far_here = core_sum([after(part, *out_back) for part in far])
    far_back = inner_exchange(far_here)
    near_here = core_sum([after(part, far_back[1]) for part in near])
    near_back = inner_exchange(near_here)
    out_parts = combine([after(piece, *far_here) for piece in out_back])

    grad_in, grad_out = call(
        functools.partial(weights_kernel, **sizes),
        [shape(*expert_in.shape), shape(*expert_out.shape)],
        [after(info, *near_here), *xs, *cs, gg, ug, hs],
        [SMEM] + [HBM] * (2 * pieces + 3),
        out_specs=[HBM, HBM],
        scratch=[
            pltpu.VMEM((3, slots, hid_n), BF16),
            pltpu.VMEM((2, nt, slots, cols), BF16),
            pltpu.VMEM((nt, 3, hid_n, cols), BF16),
            dma((3 + 2 * pieces,)),
            dma((3 * nt,)),
        ],
        name="expert_weights",
    )

    far_parts, gate_parts = combine_far([after(piece, grad_in) for piece in far_back])
    grad_parts = combine_near(gate_parts, near_back) + far_parts
    branch = jnp.sum(out_parts.astype(F32), axis=0)
    input_sum = sum(part[:tokens].astype(F32) for part in grad_parts)
    gate_sum = sum(part[tokens : tokens + picks, :tokens].astype(F32) for part in grad_parts)
    restored = (second_half.astype(F32) - branch).astype(BF16)
    carried_grad = (first_grad.astype(F32) + input_sum).astype(BF16)
    return (restored, carried_grad, gate_sum.T, grad_in, grad_out)


def solution(mesh):
    in_specs = (
        P("expert", "tensor"),
        P("expert", "tensor"),
        P("expert", "tensor"),
        P("expert", "tensor"),
        P("expert", None),
        P("expert", None),
        P("expert", None, "tensor", None),
        P("expert", "tensor", None),
    )
    out_specs = (
        P("expert", "tensor"),
        P("expert", "tensor"),
        P("expert", None),
        P("expert", None, "tensor", None),
        P("expert", "tensor", None),
    )
    return jax.shard_map(body, mesh=mesh, in_specs=in_specs, out_specs=out_specs, check_vma=False)
```

```python
import functools

import jax
import jax.numpy as jnp
from jax import lax
from jax.experimental import pallas as pl
from jax.experimental.pallas import tpu as pltpu
from jax.sharding import PartitionSpec as P

PLANE = 4
CHUNKS = 1
RETURNS = 2
TAIL = 16
VMEM_LIMIT = 48 * 1024 * 1024
F32 = jnp.float32
BF16 = jnp.bfloat16


def dot_nn(a, b):
    return lax.dot_general(a, b, (((1,), (0,)), ((), ())), preferred_element_type=F32)


def dot_nt(a, b):
    return lax.dot_general(a, b, (((1,), (1,)), ((), ())), preferred_element_type=F32)


def dot_tn(a, b):
    return lax.dot_general(a, b, (((0,), (0,)), ((), ())), preferred_element_type=F32)


def iota(shape, axis):
    return lax.broadcasted_iota(jnp.int32, shape, axis)


SMEM = pl.BlockSpec(memory_space=pltpu.SMEM)
VMEM = pl.BlockSpec(memory_space=pltpu.VMEM)
HBM = pl.BlockSpec(memory_space=pl.ANY)


def call(kernel, outs, args, specs, out_specs=None, scratch=(), name=None):
    return pl.pallas_call(
        kernel,
        out_shape=outs,
        in_specs=specs,
        out_specs=out_specs if out_specs is not None else [VMEM] * len(outs),
        scratch_shapes=list(scratch),
        compiler_params=pltpu.CompilerParams(vmem_limit_bytes=VMEM_LIMIT),
        cost_estimate=pl.CostEstimate(flops=1024, bytes_accessed=1024, transcendentals=0),
        name=name,
    )(*args)


def shape(*dims, dtype=BF16):
    return jax.ShapeDtypeStruct(dims, dtype)


def outer_meta(info, meta, s, zn):
    return meta[lax.rem(info[3] - s + zn, zn)]


def select(info, meta, sels, zn, pn, tokens, picks, rows):
    zc = zn // CHUNKS
    cap = rows // zc
    partner = iota((8, 1), 0)
    experts = jnp.where(partner < pn, info[0] + (partner ^ info[1]), -2).astype(F32)
    before = (iota((tokens, tokens), 0) < iota((tokens, tokens), 1)).astype(F32).astype(BF16)
    slot = iota((rows, tokens), 0).astype(F32)
    for s in range(zn):
        g, local = divmod(s, zc)
        ids = outer_meta(info, meta, s, zn)
        named = jnp.zeros((8, tokens), F32)
        for k in range(picks):
            named += (ids[k : k + 1, :] == experts).astype(F32)
        dest = dot_nn(named.astype(BF16), before) + local * cap
        dest = jnp.where(named > 0, dest, -1.0)
        for q in range(pn):
            sels[g][q * rows : (q + 1) * rows, local * tokens : (local + 1) * tokens] = (
                (slot == dest[q : q + 1, :]).astype(F32).astype(BF16)
            )


def route_kernel(info, meta, *chosen, zn, pn, tokens, picks, cap):
    zr = zn // RETURNS
    rows = zr * cap
    partner = iota((1, 8), 1)
    experts = jnp.where(partner < pn, info[0] + (partner ^ info[1]), -2).astype(F32)
    after = (iota((tokens, tokens), 1) < iota((tokens, tokens), 0)).astype(F32).astype(BF16)
    eye = (iota((16, 16), 0) == iota((16, 16), 1)).astype(F32).astype(BF16)
    lane = iota((tokens, pn * rows), 1).astype(F32)
    for s in range(zn):
        g, local = divmod(s, zr)
        columned = dot_tn(outer_meta(info, meta, s, zn).astype(BF16), eye)
        named = jnp.zeros((tokens, 8), F32)
        for k in range(picks):
            named += (columned[:, k : k + 1] == experts).astype(F32)
        dest = dot_nn(after, named.astype(BF16)) + local * cap
        dest = jnp.where(named > 0, dest + rows * partner.astype(F32), -1.0)
        picked = jnp.zeros((tokens, pn * rows), F32)
        for q in range(pn):
            picked += (lane == dest[:, q : q + 1]).astype(F32)
        chosen[g][local * tokens : (local + 1) * tokens, :] = picked.astype(BF16)


def tail_lanes(rows):
    return -(-rows // 128) * 128


class Loads:
    def __init__(self, sems):
        self.sems, self.copies, self.waited = sems, {}, set()

    def add(self, key, source, target):
        assert key not in self.copies
        self.copies[key] = pltpu.make_async_copy(source, target, self.sems.at[len(self.copies)])
        self.copies[key].start()

    def need(self, *keys):
        for key in keys:
            if key not in self.waited:
                self.waited.add(key)
                self.copies[key].wait()

    def finish(self):
        self.need(*self.copies)


def pack_kernel(info, sel, source, *refs, zn, pn, tokens, rows):
    outs, whole, sems = refs[:pn], refs[-2], refs[-1]
    loads = Loads(sems)
    for s in range(zn):
        place = lax.rem(info[3] - s + zn, zn)
        loads.add(s, source.at[place], whole.at[pl.ds(s * tokens, tokens)])
    loads.finish()
    for q in range(pn):
        outs[q][...] = dot_nn(sel[q * rows : (q + 1) * rows, :], whole[...]).astype(BF16)


def pack_gates_kernel(info, meta, *refs, zn, pn, tokens, picks, rows):
    zc = zn // CHUNKS
    sources, outs, refs = refs[:zc], refs[zc : zc + pn], refs[zc + pn :]
    sels, (whole, sems) = refs[:CHUNKS], refs[CHUNKS:]
    loads = Loads(sems)
    for s in range(zc):
        loads.add(s, sources[s], whole.at[pl.ds(s * tokens, tokens)])
    select(info, meta, sels, zn, pn, tokens, picks, rows)
    for q in range(pn):
        expert = (info[0] + (info[1] ^ q)).astype(F32)
        outs[q][rows : rows + TAIL, :] = jnp.zeros((TAIL, outs[q].shape[1]), BF16)
        for g in range(CHUNKS):
            tail = jnp.zeros((TAIL, rows), F32)
            for local in range(zc):
                known = outer_meta(info, meta, g * zc + local, zn)
                gate = jnp.zeros((1, tokens), F32)
                for k in range(picks):
                    gate += jnp.where(known[k : k + 1, :] == expert, known[8 + k : 9 + k, :], 0.0)
                gate = jnp.broadcast_to(gate, (TAIL, tokens)).astype(BF16)
                here = slice(local * tokens, (local + 1) * tokens)
                tail += dot_nt(gate, sels[g][q * rows : (q + 1) * rows, here])
            at = g * tail_lanes(rows)
            outs[q][rows : rows + TAIL, at : at + rows] = tail.astype(BF16)
    loads.finish()
    for q in range(pn):
        chosen = sels[0][q * rows : (q + 1) * rows, :]
        outs[q][0:rows, :] = dot_nn(chosen, whole[...]).astype(BF16)


def combine_kernel(info, *refs, zn, pn, tokens, rows):
    zr = zn // RETURNS
    chosen, backs = refs[:RETURNS], refs[RETURNS : RETURNS + pn]
    out, whole, sems = refs[RETURNS + pn :]
    loads = Loads(sems)
    for g in range(RETURNS):
        for q in range(pn):
            to = whole.at[g, pl.ds(q * rows, rows)]
            loads.add((g, q), backs[q].at[pl.ds(g * rows, rows)], to)
    for g in range(RETURNS):
        loads.need(*((g, q) for q in range(pn)))
        part = dot_nn(chosen[g][...], whole[g]).astype(BF16)
        for local in range(zr):
            place = lax.rem(info[3] - (g * zr + local) + zn, zn)
            out[place] = part[local * tokens : (local + 1) * tokens, :]


def combine_far_kernel(info, meta, sel, chosen, *refs, zn, pn, tokens, rows):
    zr, slots = zn // RETURNS, RETURNS * rows
    backs, outs, (gates, whole, tails, sems) = refs[:pn], refs[pn:-4], refs[-4:]
    loads = Loads(sems)
    for q in range(pn):
        loads.add(("t", q), backs[q].at[pl.ds(rows, TAIL)], tails.at[q])
        loads.add(q, backs[q].at[pl.ds(0, rows)], whole.at[pl.ds(q * rows, rows)])
    spreads = []
    for q in range(pn):
        loads.need(("t", q))
        spreads.append(dot_nn(tails[q, :, 0:slots], sel[q * slots : (q + 1) * slots, :])[0:8, :])
    for s in range(zn):
        ids = outer_meta(info, meta, s, zn)[0:8, :]
        total = jnp.zeros((8, tokens), F32)
        for q in range(pn):
            expert = (info[0] + (info[1] ^ q)).astype(F32)
            total += jnp.where(ids == expert, spreads[q][:, s * tokens : (s + 1) * tokens], 0.0)
        total = jnp.concatenate([total, jnp.zeros((TAIL - 8, tokens), F32)], axis=0)
        gates[:, s * tokens : (s + 1) * tokens] = total.astype(BF16)
    loads.finish()
    finish_combine(chosen, whole, gates, outs, zn - zr, tokens)


def combine_near_kernel(gates, chosen, *refs, pn, tokens, rows):
    backs, outs, (whole, sems) = refs[:pn], refs[pn:-2], refs[-2:]
    loads = Loads(sems)
    for q in range(pn):
        loads.add(q, backs[q], whole.at[pl.ds(q * rows, rows)])
    loads.finish()
    finish_combine(chosen, whole, gates, outs, 0, tokens)


def finish_combine(chosen, whole, gates, outs, first, tokens):
    part = dot_nn(chosen[...], whole[...]).astype(BF16)
    for local, out in enumerate(outs):
        at = first + local
        out[0:tokens, :] = part[local * tokens : (local + 1) * tokens, :]
        out[tokens : tokens + TAIL, :] = jnp.zeros((TAIL, part.shape[1]), BF16)
        out[tokens : tokens + TAIL, 0:tokens] = gates[:, at * tokens : (at + 1) * tokens]


def column_block(info, j, nt, cols):
    block = lax.rem(info[2] - j + nt, nt)
    return pl.ds(pl.multiple_of(block * cols, 128), cols)


def load_weight(loads, info, kind, source, target, blocks, nt, cols):
    for at, j in enumerate(blocks):
        block = source.at[:, column_block(info, j, nt, cols)]
        loads.add((kind, j), block, target.at[:, pl.ds(at * cols, cols)])


def by_core(refs, nt, pn):
    return [refs[j * pn : (j + 1) * pn] for j in range(nt)]


def load_chunk(loads, sources, target, g, pn, rows, cols):
    for j, pieces in enumerate(sources):
        for q in range(pn):
            to = target.at[pl.ds((g * pn + q) * rows, rows), pl.ds(j * cols, cols)]
            loads.add(("r", g, j, q), pieces[g * pn + q].at[pl.ds(0, rows)], to)


def halves(pn):
    units = [(g, q) for g in range(CHUNKS) for q in range(pn)]
    return units[: len(units) // 2], units[len(units) // 2 :]


def forward_kernel(info, *refs, nt, pn, rows, cols):
    n = CHUNKS * pn
    xs, refs = by_core(refs, nt, n), refs[nt * n :]
    (win, wout), outs, refs = refs[:2], by_core(refs[2:], nt, pn), refs[2 + nt * pn :]
    results, (x, tails, wg, wu, wd, kept, stage, in_sems, out_sems) = refs[:4], refs[4:]
    hs, hid, a1, a2 = (kept.at[i] for i in range(4))
    loads, stores = Loads(in_sems), Loads(out_sems)
    every = range(nt)
    load_chunk(loads, xs, x, 0, pn, rows, cols)
    load_weight(loads, info, "g", win.at[0, 0], wg, every, nt, cols)
    load_weight(loads, info, "u", win.at[0, 1], wu, every, nt, cols)
    for q in range(pn):
        loads.add(("t", q), xs[0][q].at[pl.ds(rows, TAIL)], tails.at[q])
    for g in range(1, CHUNKS):
        load_chunk(loads, xs, x, g, pn, rows, cols)
    load_weight(loads, info, "d", wout.at[0], wd, every, nt, cols)
    same = iota((rows, rows), 0) == iota((rows, rows), 1)
    tail_step = tail_lanes(rows)
    for b, units in enumerate(halves(pn)):
        here = slice(b * len(units) * rows, (b + 1) * len(units) * rows)
        loads.need(*(("r", g, j, q) for j in every for g, q in units))
        loads.need(*(("g", j) for j in every))
        gate = dot_nt(x[here, :], wg[...])
        loads.need(*(("u", j) for j in every), *(("t", q) for q in range(pn)))
        up = dot_nt(x[here, :], wu[...])
        columns = []
        for g, q in units:
            row = tails[q, :, g * tail_step : g * tail_step + rows].astype(F32)[0:1, :]
            columns.append(jnp.sum(jnp.where(same, row, 0.0), axis=1, keepdims=True))
        weight = jnp.concatenate(columns, axis=0)
        sigma = 0.5 * jnp.tanh(0.5 * gate) + 0.5
        active = gate * sigma
        hidden = active * up
        scaled = (weight * hidden).astype(BF16)
        hs[here, :] = scaled
        hid[here, :] = hidden.astype(BF16)
        a1[here, :] = (weight * (up * sigma * (1.0 + gate * (1.0 - sigma)))).astype(BF16)
        a2[here, :] = (weight * active).astype(BF16)
        span = pl.ds(b * len(units) * rows, len(units) * rows)
        for i, result in enumerate(results):
            stores.add(("kept", b, i), kept.at[i, span], result.at[span])
        loads.need(*(("d", j) for j in every))
        part = dot_nn(scaled, wd[...]).astype(BF16)
        for j in reversed(every):
            w = (nt - j) % nt
            for u, (g, q) in enumerate(units):
                block = part[u * rows : (u + 1) * rows, w * cols : (w + 1) * cols]
                stage[j, q, g * rows : (g + 1) * rows, :] = block
                if g == CHUNKS - 1:
                    stores.add((j, q), stage.at[j, q], outs[j][q])
    loads.finish()
    stores.finish()


def backward_kernel(info, *refs, nt, pn, rows, cols):
    n = CHUNKS * pn
    cs, refs = by_core(refs, nt, n), refs[nt * n :]
    n_out = RETURNS * nt * pn
    (win, wout, hid, a1, a2), outs, refs = refs[:5], refs[5 : 5 + n_out], refs[5 + n_out :]
    outs = [by_core(outs[r * nt * pn :], nt, pn) for r in range(RETURNS)]
    half = CHUNKS * rows // RETURNS
    results, (c, h, b1, b2, wg, wu, wd, kept, stage, in_sems, out_sems) = refs[:2], refs[2:]
    gg, ug = kept.at[0], kept.at[1]
    loads, stores = Loads(in_sems), Loads(out_sems)
    every = range(nt)
    load_chunk(loads, cs, c, 0, pn, rows, cols)
    load_weight(loads, info, "d", wout.at[0], wd, every, nt, cols)
    for key, source, target in (("h", hid, h), ("1", a1, b1), ("2", a2, b2)):
        loads.add(key, source, target)
    load_weight(loads, info, "g", win.at[0, 0], wg, every, nt, cols)
    load_weight(loads, info, "u", win.at[0, 1], wu, every, nt, cols)
    for g in range(1, CHUNKS):
        load_chunk(loads, cs, c, g, pn, rows, cols)
    same = iota((rows, rows), 0) == iota((rows, rows), 1)
    tail_step = tail_lanes(rows)
    bottom = slice(CHUNKS * rows, CHUNKS * rows + TAIL)
    for b, units in enumerate(halves(pn)):
        here = slice(b * len(units) * rows, (b + 1) * len(units) * rows)
        loads.need(*(("r", g, j, q) for j in every for g, q in units))
        loads.need(*(("d", j) for j in every))
        grad = dot_nt(c[here, :], wd[...])
        loads.need("h", "1", "2")
        piece = jnp.sum(grad * h[here, :].astype(F32), axis=1, keepdims=True)
        gate_grad = (grad * b1[here, :].astype(F32)).astype(BF16)
        up_grad = (grad * b2[here, :].astype(F32)).astype(BF16)
        gg[here, :] = gate_grad
        ug[here, :] = up_grad
        span = pl.ds(b * len(units) * rows, len(units) * rows)
        for i, result in enumerate(results):
            stores.add(("kept", b, i), kept.at[i, span], result.at[span])
        for u, (g, q) in enumerate(units):
            part = piece[u * rows : (u + 1) * rows, :]
            part = jnp.sum(jnp.where(same, part, 0.0), axis=0, keepdims=True)
            part = jnp.broadcast_to(part, (TAIL, rows)).astype(BF16)
            for j in every:
                if g == 0:
                    stage[j, q, bottom, :] = jnp.zeros((TAIL, cols), BF16)
                stage[j, q, bottom, g * tail_step : g * tail_step + rows] = part
        loads.need(*((k, j) for k in "gu" for j in every))
        part = (dot_nn(gate_grad, wg[...]) + dot_nn(up_grad, wu[...])).astype(BF16)
        for j in reversed(every):
            w = (nt - j) % nt
            for u, (g, q) in enumerate(units):
                block = part[u * rows : (u + 1) * rows, w * cols : (w + 1) * cols]
                stage[j, q, g * rows : (g + 1) * rows, :] = block
                for r in reversed(range(RETURNS if g == CHUNKS - 1 else 0)):
                    span = pl.ds(r * half, half + TAIL if r == RETURNS - 1 else half)
                    stores.add((j, q, r), stage.at[j, q, span], outs[r][j][q])
    loads.finish()
    stores.finish()


def weights_kernel(info, *refs, nt, pn, rows, cols):
    n = CHUNKS * pn
    xs, cs, refs = by_core(refs, nt, n), by_core(refs[nt * n :], nt, n), refs[2 * nt * n :]
    lefts, (gin, gout, left, right, stage, in_sems, out_sems) = refs[:3], refs[3:]
    loads, stores = Loads(in_sems), Loads(out_sems)
    order = ((0, 0, xs), (1, 0, xs), (2, 1, cs))
    for w, side, sources in order:
        loads.add(("l", w), lefts[w], left.at[w])
        if w == 1:
            continue
        for j in range(nt):
            for q in range(n):
                target = right.at[side, j, pl.ds(q * rows, rows)]
                loads.add((side, j, q), sources[j][q].at[pl.ds(0, rows)], target)
    for w, side, _ in order:
        loads.need(("l", w))
        for j in range(nt):
            loads.need(*((side, j, q) for q in range(n)))
            at = column_block(info, j, nt, cols)
            stage[j, w] = dot_tn(left[w], right[side, j]).astype(BF16)
            target = gout.at[0, :, at] if w == 2 else gin.at[0, w, :, at]
            stores.add((j, w), stage.at[j, w], target)
    loads.finish()
    stores.finish()


def after(value, *others):
    return lax.optimization_barrier((value, *others))[0]


def body(
    first_half,
    second_half,
    first_grad,
    second_grad,
    expert_ids,
    gate_weights,
    expert_in,
    expert_out,
):
    tokens, picks = expert_ids.shape
    groups = lax.axis_size("expert")
    nt = lax.axis_size("tensor")
    pn = PLANE
    zn = groups // pn
    cap = tokens * picks * 7 // (6 * groups)
    zc = zn // CHUNKS
    part_rows = zc * cap
    rows = CHUNKS * part_rows
    slots = pn * rows
    cols = first_half.shape[1]
    hid_n = expert_out.shape[1]
    me = lax.axis_index("expert")
    info = jnp.stack([(me // pn) * pn, me % pn, lax.axis_index("tensor"), me // pn]).astype(jnp.int32)

    def outer_send(value, s):
        if s % zn == 0:
            return value
        return lax.ppermute(
            value, "expert", [(e, ((e // pn + s) % zn) * pn + e % pn) for e in range(groups)]
        )

    def inner_send(value, q):
        if q == 0:
            return value
        return lax.ppermute(value, "expert", [(e, e ^ q) for e in range(groups)])

    def inner_exchange(pieces):
        return [inner_send(piece, q) for q, piece in enumerate(pieces)]

    def tensor_send(value, j):
        if j == 0:
            return value
        return lax.ppermute(value, "tensor", [(c, (c + j) % nt) for c in range(nt)])

    fixed = dict(zn=zn, pn=pn, tokens=tokens)

    own = jnp.concatenate(
        [
            jnp.pad(expert_ids.T.astype(F32), ((0, 8 - picks), (0, 0)), constant_values=-1.0),
            jnp.pad(gate_weights.T.astype(F32), ((0, 8 - picks), (0, 0))),
        ],
        axis=0,
    )
    columns = [[z * pn + q for z in range(zn)] for q in range(pn)]

    def outer_exchange(value):
        return lax.all_to_all(
            value,
            "expert",
            split_axis=0,
            concat_axis=0,
            axis_index_groups=columns,
            tiled=True,
        )

    def copies(value):
        return jnp.broadcast_to(value[None], (zn,) + value.shape)

    grad_copies = copies(second_grad)
    meta = outer_exchange(after(copies(own), grad_copies))
    dma = pltpu.SemaphoreType.DMA
    sizes = dict(nt=nt, pn=pn, rows=part_rows, cols=cols)

    def pack(gathered):
        return call(
            functools.partial(pack_kernel, **fixed, rows=part_rows),
            [shape(part_rows, cols)] * pn,
            [info, sels[0], gathered],
            [SMEM, VMEM, HBM],
            scratch=[pltpu.VMEM((zn * tokens, cols), BF16), dma((zn,))],
            name="pack",
        )

    def pack_gates(parts):
        return call(
            functools.partial(pack_gates_kernel, **fixed, picks=picks, rows=part_rows),
            [shape(part_rows + TAIL, cols)] * pn
            + [shape(pn * part_rows, zc * tokens)] * CHUNKS,
            [info, meta, *parts[:zc]],
            [SMEM, VMEM] + [HBM] * zc,
            scratch=[pltpu.VMEM((zc * tokens, cols), BF16), dma((zc,))],
            name="pack_gates",
        )

    zr = zn // RETURNS
    half = zr * cap

    def send_back(parts, first):
        return [outer_send(part, -(first + local)) for local, part in enumerate(parts)]

    def combine(backs):
        parts = call(
            functools.partial(combine_kernel, **fixed, rows=half),
            [shape(zn, tokens, cols)],
            [info, *chosen, *backs],
            [SMEM] + [VMEM] * RETURNS + [HBM] * pn,
            scratch=[pltpu.VMEM((RETURNS, pn * half, cols), BF16), dma((RETURNS * pn,))],
            name="combine",
        )
        return outer_exchange(parts[0])

    def combine_far(backs):
        *parts, gates = call(
            functools.partial(combine_far_kernel, **fixed, rows=half),
            [shape(tokens + TAIL, cols)] * zr + [shape(TAIL, zn * tokens)],
            [info, meta, sels[0], chosen[RETURNS - 1], *backs],
            [SMEM] + [VMEM] * 3 + [HBM] * pn,
            scratch=[pltpu.VMEM((pn * half, cols), BF16), pltpu.VMEM((pn, TAIL, cols), BF16)]
            + [dma((2 * pn,))],
            name="combine_far",
        )
        return send_back(parts, zn - zr), gates

    def combine_near(gates, backs):
        parts = call(
            functools.partial(combine_near_kernel, pn=pn, tokens=tokens, rows=half),
            [shape(tokens + TAIL, cols)] * zr,
            [gates, chosen[0], *backs],
            [VMEM] * 2 + [HBM] * pn,
            scratch=[pltpu.VMEM((pn * half, cols), BF16), dma((pn,))],
            name="combine_near",
        )
        return send_back(parts, 0)

    def swapped(chunks):
        return [tensor_send(piece, j) for j in range(nt) for pieces in chunks for piece in pieces]

    def core_sum(arrays):
        sums = []
        for q in range(pn):
            total = sum(tensor_send(arrays[j * pn + q], j).astype(F32) for j in range(nt))
            sums.append(total.astype(BF16))
        return sums

    x_parts = [outer_send(first_half, s) for s in range(zn)]
    x_packed = pack_gates(x_parts)
    x_packed, sels = x_packed[:pn], x_packed[pn:]
    x_here = inner_exchange(x_packed)
    gathered = outer_exchange(after(grad_copies, *x_parts[1:]))
    chosen = call(
        functools.partial(route_kernel, **fixed, picks=picks, cap=cap),
        [shape(zr * tokens, pn * half)] * RETURNS,
        [info, after(meta, *x_packed)],
        [SMEM, VMEM],
        name="route",
    )
    c_packed = pack(after(gathered, *chosen))
    c_here = inner_exchange(c_packed)

    xs = swapped(([after(piece, *c_packed) for piece in x_here],))
    pieces = nt * CHUNKS * pn
    forward = call(
        functools.partial(forward_kernel, **sizes),
        [shape(rows, cols)] * (nt * pn) + [shape(slots, hid_n)] * 4,
        [after(info, *c_packed), *xs, expert_in, expert_out],
        [SMEM] + [HBM] * (pieces + 2),
        out_specs=[HBM] * (nt * pn + 4),
        scratch=[pltpu.VMEM((slots, nt * cols), BF16), pltpu.VMEM((pn, TAIL, cols), BF16)]
        + [pltpu.VMEM((hid_n, nt * cols), BF16)] * 3
        + [pltpu.VMEM((4, slots, hid_n), BF16)]
        + [pltpu.VMEM((nt, pn, rows, cols), BF16), dma((3 * nt + pieces + pn,))]
        + [dma((nt * pn + 8,))],
        name="expert_forward",
    )
    outs, (hs, hid, a1, a2) = forward[: nt * pn], forward[nt * pn :]
    cs = swapped(([after(piece, hid) for piece in c_here],))
    out_here = core_sum(outs)
    out_back = inner_exchange(out_here)

    backward = call(
        functools.partial(backward_kernel, **sizes),
        [
            shape(half + TAIL if r == RETURNS - 1 else half, cols)
            for r in range(RETURNS)
            for _ in range(nt * pn)
        ]
        + [shape(slots, hid_n)] * 2,
        [info, *cs, expert_in, expert_out, after(hid, *out_here), a1, a2],
        [SMEM] + [HBM] * (pieces + 5),
        out_specs=[HBM] * (RETURNS * nt * pn + 2),
        scratch=[pltpu.VMEM((slots, nt * cols), BF16)]
        + [pltpu.VMEM((slots, hid_n), BF16)] * 3
        + [pltpu.VMEM((hid_n, nt * cols), BF16)] * 3
        + [pltpu.VMEM((2, slots, hid_n), BF16)]
        + [pltpu.VMEM((nt, pn, rows + TAIL, cols), BF16), dma((3 * nt + pieces + 3,))]
        + [dma((RETURNS * nt * pn + 4,))],
        name="expert_backward",
    )
    grads, (gg, ug) = backward[: RETURNS * nt * pn], backward[RETURNS * nt * pn :]
    near, far = grads[: nt * pn], grads[nt * pn :]
    far_here = core_sum([after(part, *out_back) for part in far])
    far_back = inner_exchange(far_here)
    near_here = core_sum([after(part, far_back[1]) for part in near])
    near_back = inner_exchange(near_here)
    out_parts = combine([after(piece, *far_here) for piece in out_back])

    far_parts, gate_parts = combine_far([after(piece, *near_here) for piece in far_back])
    grad_parts = combine_near(gate_parts, near_back) + far_parts

    grad_in, grad_out = call(
        functools.partial(weights_kernel, **sizes),
        [shape(*expert_in.shape), shape(*expert_out.shape)],
        [after(info, grad_parts[0]), *xs, *cs, gg, ug, hs],
        [SMEM] + [HBM] * (2 * pieces + 3),
        out_specs=[HBM, HBM],
        scratch=[
            pltpu.VMEM((3, slots, hid_n), BF16),
            pltpu.VMEM((2, nt, slots, cols), BF16),
            pltpu.VMEM((nt, 3, hid_n, cols), BF16),
            dma((3 + 2 * pieces,)),
            dma((3 * nt,)),
        ],
        name="expert_weights",
    )

    branch = jnp.sum(after(out_parts, grad_in).astype(F32), axis=0)
    input_sum = sum(part[:tokens].astype(F32) for part in grad_parts)
    gate_sum = sum(part[tokens : tokens + picks, :tokens].astype(F32) for part in grad_parts)
    restored = (second_half.astype(F32) - branch).astype(BF16)
    carried_grad = (first_grad.astype(F32) + input_sum).astype(BF16)
    return (restored, carried_grad, gate_sum.T, grad_in, grad_out)


def solution(mesh):
    in_specs = (
        P("expert", "tensor"),
        P("expert", "tensor"),
        P("expert", "tensor"),
        P("expert", "tensor"),
        P("expert", None),
        P("expert", None),
        P("expert", None, "tensor", None),
        P("expert", "tensor", None),
    )
    out_specs = (
        P("expert", "tensor"),
        P("expert", "tensor"),
        P("expert", None),
        P("expert", None, "tensor", None),
        P("expert", "tensor", None),
    )
    return jax.shard_map(body, mesh=mesh, in_specs=in_specs, out_specs=out_specs, check_vma=False)
```

```python
import functools

import jax
import jax.numpy as jnp
from jax import lax
from jax.experimental import pallas as pl
from jax.experimental.pallas import tpu as pltpu
from jax.sharding import PartitionSpec as P

PLANE = 4
CHUNKS = 1
RETURNS = 2
TAIL = 16
VMEM_LIMIT = 56 * 1024 * 1024
F32 = jnp.float32
BF16 = jnp.bfloat16


def dot_nn(a, b):
    return lax.dot_general(a, b, (((1,), (0,)), ((), ())), preferred_element_type=F32)


def dot_nt(a, b):
    return lax.dot_general(a, b, (((1,), (1,)), ((), ())), preferred_element_type=F32)


def dot_tn(a, b):
    return lax.dot_general(a, b, (((0,), (0,)), ((), ())), preferred_element_type=F32)


def iota(shape, axis):
    return lax.broadcasted_iota(jnp.int32, shape, axis)


SMEM = pl.BlockSpec(memory_space=pltpu.SMEM)
VMEM = pl.BlockSpec(memory_space=pltpu.VMEM)
HBM = pl.BlockSpec(memory_space=pl.ANY)


def call(kernel, outs, args, specs, out_specs=None, scratch=(), name=None):
    return pl.pallas_call(
        kernel,
        out_shape=outs,
        in_specs=specs,
        out_specs=out_specs if out_specs is not None else [VMEM] * len(outs),
        scratch_shapes=list(scratch),
        compiler_params=pltpu.CompilerParams(vmem_limit_bytes=VMEM_LIMIT),
        cost_estimate=pl.CostEstimate(flops=1024, bytes_accessed=1024, transcendentals=0),
        name=name,
    )(*args)


def shape(*dims, dtype=BF16):
    return jax.ShapeDtypeStruct(dims, dtype)


def outer_meta(info, meta, s, zn):
    return meta[lax.rem(info[3] - s + zn, zn)]


def select(info, meta, sels, zn, pn, tokens, picks, rows):
    zc = zn // CHUNKS
    cap = rows // zc
    partner = iota((8, 1), 0)
    experts = jnp.where(partner < pn, info[0] + (partner ^ info[1]), -2).astype(F32)
    before = (iota((tokens, tokens), 0) < iota((tokens, tokens), 1)).astype(F32).astype(BF16)
    slot = iota((rows, tokens), 0).astype(F32)
    for s in range(zn):
        g, local = divmod(s, zc)
        ids = outer_meta(info, meta, s, zn)
        named = jnp.zeros((8, tokens), F32)
        for k in range(picks):
            named += (ids[k : k + 1, :] == experts).astype(F32)
        dest = dot_nn(named.astype(BF16), before) + local * cap
        dest = jnp.where(named > 0, dest, -1.0)
        for q in range(pn):
            sels[g][q * rows : (q + 1) * rows, local * tokens : (local + 1) * tokens] = (
                (slot == dest[q : q + 1, :]).astype(F32).astype(BF16)
            )


def route_kernel(info, meta, *chosen, zn, pn, tokens, picks, cap):
    zr = zn // RETURNS
    rows = zr * cap
    partner = iota((1, 8), 1)
    experts = jnp.where(partner < pn, info[0] + (partner ^ info[1]), -2).astype(F32)
    after = (iota((tokens, tokens), 1) < iota((tokens, tokens), 0)).astype(F32).astype(BF16)
    eye = (iota((16, 16), 0) == iota((16, 16), 1)).astype(F32).astype(BF16)
    lane = iota((tokens, pn * rows), 1).astype(F32)
    for s in range(zn):
        g, local = divmod(s, zr)
        columned = dot_tn(outer_meta(info, meta, s, zn).astype(BF16), eye)
        named = jnp.zeros((tokens, 8), F32)
        for k in range(picks):
            named += (columned[:, k : k + 1] == experts).astype(F32)
        dest = dot_nn(after, named.astype(BF16)) + local * cap
        dest = jnp.where(named > 0, dest + rows * partner.astype(F32), -1.0)
        picked = jnp.zeros((tokens, pn * rows), F32)
        for q in range(pn):
            picked += (lane == dest[:, q : q + 1]).astype(F32)
        chosen[g][local * tokens : (local + 1) * tokens, :] = picked.astype(BF16)


def tail_lanes(rows):
    return -(-rows // 128) * 128


class Loads:
    def __init__(self, sems):
        self.sems, self.copies, self.waited = sems, {}, set()

    def add(self, key, source, target):
        assert key not in self.copies
        self.copies[key] = pltpu.make_async_copy(source, target, self.sems.at[len(self.copies)])
        self.copies[key].start()

    def need(self, *keys):
        for key in keys:
            if key not in self.waited:
                self.waited.add(key)
                self.copies[key].wait()

    def finish(self):
        self.need(*self.copies)


def pack_kernel(info, sel, source, *refs, zn, pn, tokens, rows):
    outs, whole, sems = refs[:pn], refs[-2], refs[-1]
    loads = Loads(sems)
    for s in range(zn):
        place = lax.rem(info[3] - s + zn, zn)
        loads.add(s, source.at[place], whole.at[pl.ds(s * tokens, tokens)])
    loads.finish()
    for q in range(pn):
        outs[q][...] = dot_nn(sel[q * rows : (q + 1) * rows, :], whole[...]).astype(BF16)


def pack_gates_kernel(info, meta, *refs, zn, pn, tokens, picks, rows):
    zc = zn // CHUNKS
    sources, outs, refs = refs[:zc], refs[zc : zc + pn], refs[zc + pn :]
    sels, (whole, sems) = refs[:CHUNKS], refs[CHUNKS:]
    loads = Loads(sems)
    for s in range(zc):
        loads.add(s, sources[s], whole.at[pl.ds(s * tokens, tokens)])
    select(info, meta, sels, zn, pn, tokens, picks, rows)
    for q in range(pn):
        expert = (info[0] + (info[1] ^ q)).astype(F32)
        outs[q][rows : rows + TAIL, :] = jnp.zeros((TAIL, outs[q].shape[1]), BF16)
        for g in range(CHUNKS):
            tail = jnp.zeros((TAIL, rows), F32)
            for local in range(zc):
                known = outer_meta(info, meta, g * zc + local, zn)
                gate = jnp.zeros((1, tokens), F32)
                for k in range(picks):
                    gate += jnp.where(known[k : k + 1, :] == expert, known[8 + k : 9 + k, :], 0.0)
                gate = jnp.broadcast_to(gate, (TAIL, tokens)).astype(BF16)
                here = slice(local * tokens, (local + 1) * tokens)
                tail += dot_nt(gate, sels[g][q * rows : (q + 1) * rows, here])
            at = g * tail_lanes(rows)
            outs[q][rows : rows + TAIL, at : at + rows] = tail.astype(BF16)
    loads.finish()
    for q in range(pn):
        chosen = sels[0][q * rows : (q + 1) * rows, :]
        outs[q][0:rows, :] = dot_nn(chosen, whole[...]).astype(BF16)


def combine_kernel(info, *refs, zn, pn, tokens, rows):
    zr = zn // RETURNS
    chosen, backs = refs[:RETURNS], refs[RETURNS : RETURNS + pn]
    out, whole, sems = refs[RETURNS + pn :]
    loads = Loads(sems)
    for g in range(RETURNS):
        for q in range(pn):
            to = whole.at[g, pl.ds(q * rows, rows)]
            loads.add((g, q), backs[q].at[pl.ds(g * rows, rows)], to)
    for g in range(RETURNS):
        loads.need(*((g, q) for q in range(pn)))
        part = dot_nn(chosen[g][...], whole[g]).astype(BF16)
        for local in range(zr):
            place = lax.rem(info[3] - (g * zr + local) + zn, zn)
            out[place] = part[local * tokens : (local + 1) * tokens, :]


def combine_far_kernel(info, meta, sel, chosen, *refs, zn, pn, tokens, rows):
    zr, slots = zn // RETURNS, RETURNS * rows
    backs, outs, (gates, whole, tails, sems) = refs[:pn], refs[pn:-4], refs[-4:]
    loads = Loads(sems)
    for q in range(pn):
        loads.add(("t", q), backs[q].at[pl.ds(rows, TAIL)], tails.at[q])
        loads.add(q, backs[q].at[pl.ds(0, rows)], whole.at[pl.ds(q * rows, rows)])
    spreads = []
    for q in range(pn):
        loads.need(("t", q))
        spreads.append(dot_nn(tails[q, :, 0:slots], sel[q * slots : (q + 1) * slots, :])[0:8, :])
    for s in range(zn):
        ids = outer_meta(info, meta, s, zn)[0:8, :]
        total = jnp.zeros((8, tokens), F32)
        for q in range(pn):
            expert = (info[0] + (info[1] ^ q)).astype(F32)
            total += jnp.where(ids == expert, spreads[q][:, s * tokens : (s + 1) * tokens], 0.0)
        total = jnp.concatenate([total, jnp.zeros((TAIL - 8, tokens), F32)], axis=0)
        gates[:, s * tokens : (s + 1) * tokens] = total.astype(BF16)
    loads.finish()
    finish_combine(chosen, whole, gates, outs, zn - zr, tokens)


def combine_near_kernel(gates, chosen, *refs, pn, tokens, rows):
    backs, outs, (whole, sems) = refs[:pn], refs[pn:-2], refs[-2:]
    loads = Loads(sems)
    for q in range(pn):
        loads.add(q, backs[q], whole.at[pl.ds(q * rows, rows)])
    loads.finish()
    finish_combine(chosen, whole, gates, outs, 0, tokens)


def finish_combine(chosen, whole, gates, outs, first, tokens):
    part = dot_nn(chosen[...], whole[...]).astype(BF16)
    for local, out in enumerate(outs):
        at = first + local
        out[0:tokens, :] = part[local * tokens : (local + 1) * tokens, :]
        out[tokens : tokens + TAIL, :] = jnp.zeros((TAIL, part.shape[1]), BF16)
        out[tokens : tokens + TAIL, 0:tokens] = gates[:, at * tokens : (at + 1) * tokens]


def column_block(info, j, nt, cols):
    block = lax.rem(info[2] - j + nt, nt)
    return pl.ds(pl.multiple_of(block * cols, 128), cols)


def load_weight(loads, info, kind, source, target, blocks, nt, cols):
    for at, j in enumerate(blocks):
        block = source.at[:, column_block(info, j, nt, cols)]
        loads.add((kind, j), block, target.at[:, pl.ds(at * cols, cols)])


def by_core(refs, nt, pn):
    return [refs[j * pn : (j + 1) * pn] for j in range(nt)]


def load_chunk(loads, sources, target, g, pn, rows, cols):
    for j, pieces in enumerate(sources):
        for q in range(pn):
            to = target.at[pl.ds((g * pn + q) * rows, rows), pl.ds(j * cols, cols)]
            loads.add(("r", g, j, q), pieces[g * pn + q].at[pl.ds(0, rows)], to)


def halves(pn):
    units = [(g, q) for g in range(CHUNKS) for q in range(pn)]
    return units[: len(units) // 2], units[len(units) // 2 :]


def forward_kernel(info, *refs, nt, pn, rows, cols):
    n = CHUNKS * pn
    xs, refs = by_core(refs, nt, n), refs[nt * n :]
    (win, wout), outs, refs = refs[:2], by_core(refs[2:], nt, pn), refs[2 + nt * pn :]
    results, (x, tails, wg, wu, wd, kept, stage, in_sems, out_sems) = refs[:4], refs[4:]
    hs, hid, a1, a2 = (kept.at[i] for i in range(4))
    loads, stores = Loads(in_sems), Loads(out_sems)
    every = range(nt)
    load_chunk(loads, xs, x, 0, pn, rows, cols)
    load_weight(loads, info, "g", win.at[0, 0], wg, every, nt, cols)
    load_weight(loads, info, "u", win.at[0, 1], wu, every, nt, cols)
    for q in range(pn):
        loads.add(("t", q), xs[0][q].at[pl.ds(rows, TAIL)], tails.at[q])
    for g in range(1, CHUNKS):
        load_chunk(loads, xs, x, g, pn, rows, cols)
    load_weight(loads, info, "d", wout.at[0], wd, every, nt, cols)
    same = iota((rows, rows), 0) == iota((rows, rows), 1)
    tail_step = tail_lanes(rows)
    for b, units in enumerate(halves(pn)):
        here = slice(b * len(units) * rows, (b + 1) * len(units) * rows)
        loads.need(*(("r", g, j, q) for j in every for g, q in units))
        loads.need(*(("g", j) for j in every))
        gate = dot_nt(x[here, :], wg[...])
        loads.need(*(("u", j) for j in every), *(("t", q) for q in range(pn)))
        up = dot_nt(x[here, :], wu[...])
        columns = []
        for g, q in units:
            row = tails[q, :, g * tail_step : g * tail_step + rows].astype(F32)[0:1, :]
            columns.append(jnp.sum(jnp.where(same, row, 0.0), axis=1, keepdims=True))
        weight = jnp.concatenate(columns, axis=0)
        sigma = 0.5 * jnp.tanh(0.5 * gate) + 0.5
        active = gate * sigma
        hidden = active * up
        scaled = (weight * hidden).astype(BF16)
        hs[here, :] = scaled
        hid[here, :] = hidden.astype(BF16)
        a1[here, :] = (weight * (up * sigma * (1.0 + gate * (1.0 - sigma)))).astype(BF16)
        a2[here, :] = (weight * active).astype(BF16)
        span = pl.ds(b * len(units) * rows, len(units) * rows)
        for i, result in enumerate(results):
            stores.add(("kept", b, i), kept.at[i, span], result.at[span])
        loads.need(*(("d", j) for j in every))
        part = dot_nn(scaled, wd[...]).astype(BF16)
        for j in reversed(every):
            w = (nt - j) % nt
            for u, (g, q) in enumerate(units):
                block = part[u * rows : (u + 1) * rows, w * cols : (w + 1) * cols]
                stage[j, q, g * rows : (g + 1) * rows, :] = block
                if g == CHUNKS - 1:
                    stores.add((j, q), stage.at[j, q], outs[j][q])
    loads.finish()
    stores.finish()


def backward_kernel(info, *refs, nt, pn, rows, cols):
    n = CHUNKS * pn
    cs, refs = by_core(refs, nt, n), refs[nt * n :]
    n_out = RETURNS * nt * pn
    (win, wout, hid, a1, a2), outs, refs = refs[:5], refs[5 : 5 + n_out], refs[5 + n_out :]
    outs = [by_core(outs[r * nt * pn :], nt, pn) for r in range(RETURNS)]
    half = CHUNKS * rows // RETURNS
    results, (c, h, b1, b2, wg, wu, wd, kept, stage, in_sems, out_sems) = refs[:2], refs[2:]
    gg, ug = kept.at[0], kept.at[1]
    loads, stores = Loads(in_sems), Loads(out_sems)
    every = range(nt)
    load_chunk(loads, cs, c, 0, pn, rows, cols)
    load_weight(loads, info, "d", wout.at[0], wd, every, nt, cols)
    for key, source, target in (("h", hid, h), ("1", a1, b1), ("2", a2, b2)):
        loads.add(key, source, target)
    load_weight(loads, info, "g", win.at[0, 0], wg, every, nt, cols)
    load_weight(loads, info, "u", win.at[0, 1], wu, every, nt, cols)
    for g in range(1, CHUNKS):
        load_chunk(loads, cs, c, g, pn, rows, cols)
    same = iota((rows, rows), 0) == iota((rows, rows), 1)
    tail_step = tail_lanes(rows)
    bottom = slice(CHUNKS * rows, CHUNKS * rows + TAIL)
    for b, units in enumerate(halves(pn)):
        here = slice(b * len(units) * rows, (b + 1) * len(units) * rows)
        loads.need(*(("r", g, j, q) for j in every for g, q in units))
        loads.need(*(("d", j) for j in every))
        grad = dot_nt(c[here, :], wd[...])
        loads.need("h", "1", "2")
        piece = jnp.sum(grad * h[here, :].astype(F32), axis=1, keepdims=True)
        gate_grad = (grad * b1[here, :].astype(F32)).astype(BF16)
        up_grad = (grad * b2[here, :].astype(F32)).astype(BF16)
        gg[here, :] = gate_grad
        ug[here, :] = up_grad
        span = pl.ds(b * len(units) * rows, len(units) * rows)
        for i, result in enumerate(results):
            stores.add(("kept", b, i), kept.at[i, span], result.at[span])
        for u, (g, q) in enumerate(units):
            part = piece[u * rows : (u + 1) * rows, :]
            part = jnp.sum(jnp.where(same, part, 0.0), axis=0, keepdims=True)
            part = jnp.broadcast_to(part, (TAIL, rows)).astype(BF16)
            for j in every:
                if g == 0:
                    stage[j, q, bottom, :] = jnp.zeros((TAIL, cols), BF16)
                stage[j, q, bottom, g * tail_step : g * tail_step + rows] = part
        loads.need(*((k, j) for k in "gu" for j in every))
        part = (dot_nn(gate_grad, wg[...]) + dot_nn(up_grad, wu[...])).astype(BF16)
        for j in reversed(every):
            w = (nt - j) % nt
            for u, (g, q) in enumerate(units):
                block = part[u * rows : (u + 1) * rows, w * cols : (w + 1) * cols]
                stage[j, q, g * rows : (g + 1) * rows, :] = block
                for r in reversed(range(RETURNS if g == CHUNKS - 1 else 0)):
                    span = pl.ds(r * half, half + TAIL if r == RETURNS - 1 else half)
                    stores.add((j, q, r), stage.at[j, q, span], outs[r][j][q])
    loads.finish()
    stores.finish()


def weights_kernel(info, *refs, nt, pn, rows, cols):
    n = CHUNKS * pn
    xs, cs, refs = by_core(refs, nt, n), by_core(refs[nt * n :], nt, n), refs[2 * nt * n :]
    lefts, (gin, gout, left, right, stage, in_sems, out_sems) = refs[:3], refs[3:]
    loads, stores = Loads(in_sems), Loads(out_sems)
    order = ((0, 0, xs), (1, 0, xs), (2, 1, cs))
    for w, side, sources in order:
        loads.add(("l", w), lefts[w], left.at[w])
        if w == 1:
            continue
        for j in range(nt):
            for q in range(n):
                target = right.at[side, j, pl.ds(q * rows, rows)]
                loads.add((side, j, q), sources[j][q].at[pl.ds(0, rows)], target)
    for w, side, _ in order:
        loads.need(("l", w))
        for j in range(nt):
            loads.need(*((side, j, q) for q in range(n)))
            at = column_block(info, j, nt, cols)
            stage[j, w] = dot_tn(left[w], right[side, j]).astype(BF16)
            target = gout.at[0, :, at] if w == 2 else gin.at[0, w, :, at]
            stores.add((j, w), stage.at[j, w], target)
    loads.finish()
    stores.finish()


def after(value, *others):
    return lax.optimization_barrier((value, *others))[0]


def body(
    first_half,
    second_half,
    first_grad,
    second_grad,
    expert_ids,
    gate_weights,
    expert_in,
    expert_out,
):
    tokens, picks = expert_ids.shape
    groups = lax.axis_size("expert")
    nt = lax.axis_size("tensor")
    pn = PLANE
    zn = groups // pn
    cap = tokens * picks * 7 // (6 * groups)
    zc = zn // CHUNKS
    part_rows = zc * cap
    rows = CHUNKS * part_rows
    slots = pn * rows
    cols = first_half.shape[1]
    hid_n = expert_out.shape[1]
    me = lax.axis_index("expert")
    info = jnp.stack([(me // pn) * pn, me % pn, lax.axis_index("tensor"), me // pn]).astype(jnp.int32)

    def outer_send(value, s):
        if s % zn == 0:
            return value
        return lax.ppermute(
            value, "expert", [(e, ((e // pn + s) % zn) * pn + e % pn) for e in range(groups)]
        )

    def inner_send(value, q):
        if q == 0:
            return value
        return lax.ppermute(value, "expert", [(e, e ^ q) for e in range(groups)])

    def inner_exchange(pieces):
        return [inner_send(piece, q) for q, piece in enumerate(pieces)]

    def tensor_send(value, j):
        if j == 0:
            return value
        return lax.ppermute(value, "tensor", [(c, (c + j) % nt) for c in range(nt)])

    fixed = dict(zn=zn, pn=pn, tokens=tokens)

    own = jnp.concatenate(
        [
            jnp.pad(expert_ids.T.astype(F32), ((0, 8 - picks), (0, 0)), constant_values=-1.0),
            jnp.pad(gate_weights.T.astype(F32), ((0, 8 - picks), (0, 0))),
        ],
        axis=0,
    )
    columns = [[z * pn + q for z in range(zn)] for q in range(pn)]

    def outer_exchange(value):
        return lax.all_to_all(
            value,
            "expert",
            split_axis=0,
            concat_axis=0,
            axis_index_groups=columns,
            tiled=True,
        )

    def copies(value):
        return jnp.broadcast_to(value[None], (zn,) + value.shape)

    grad_copies = copies(second_grad)
    meta = outer_exchange(after(copies(own), grad_copies))
    dma = pltpu.SemaphoreType.DMA
    sizes = dict(nt=nt, pn=pn, rows=part_rows, cols=cols)

    def pack(gathered):
        return call(
            functools.partial(pack_kernel, **fixed, rows=part_rows),
            [shape(part_rows, cols)] * pn,
            [info, sels[0], gathered],
            [SMEM, VMEM, HBM],
            scratch=[pltpu.VMEM((zn * tokens, cols), BF16), dma((zn,))],
            name="pack",
        )

    def pack_gates(parts):
        return call(
            functools.partial(pack_gates_kernel, **fixed, picks=picks, rows=part_rows),
            [shape(part_rows + TAIL, cols)] * pn
            + [shape(pn * part_rows, zc * tokens)] * CHUNKS,
            [info, meta, *parts[:zc]],
            [SMEM, VMEM] + [HBM] * zc,
            scratch=[pltpu.VMEM((zc * tokens, cols), BF16), dma((zc,))],
            name="pack_gates",
        )

    zr = zn // RETURNS
    half = zr * cap

    def send_back(parts, first):
        return [outer_send(part, -(first + local)) for local, part in enumerate(parts)]

    def combine(backs):
        parts = call(
            functools.partial(combine_kernel, **fixed, rows=half),
            [shape(zn, tokens, cols)],
            [info, *chosen, *backs],
            [SMEM] + [VMEM] * RETURNS + [HBM] * pn,
            scratch=[pltpu.VMEM((RETURNS, pn * half, cols), BF16), dma((RETURNS * pn,))],
            name="combine",
        )
        return parts[0]

    def combine_far(backs):
        *parts, gates = call(
            functools.partial(combine_far_kernel, **fixed, rows=half),
            [shape(tokens + TAIL, cols)] * zr + [shape(TAIL, zn * tokens)],
            [info, meta, sels[0], chosen[RETURNS - 1], *backs],
            [SMEM] + [VMEM] * 3 + [HBM] * pn,
            scratch=[pltpu.VMEM((pn * half, cols), BF16), pltpu.VMEM((pn, TAIL, cols), BF16)]
            + [dma((2 * pn,))],
            name="combine_far",
        )
        return send_back(parts, zn - zr), gates

    def combine_near(gates, backs):
        parts = call(
            functools.partial(combine_near_kernel, pn=pn, tokens=tokens, rows=half),
            [shape(tokens + TAIL, cols)] * zr,
            [gates, chosen[0], *backs],
            [VMEM] * 2 + [HBM] * pn,
            scratch=[pltpu.VMEM((pn * half, cols), BF16), dma((pn,))],
            name="combine_near",
        )
        return send_back(parts, 0)

    def swapped(chunks):
        return [tensor_send(piece, j) for j in range(nt) for pieces in chunks for piece in pieces]

    def core_sum(arrays):
        sums = []
        for q in range(pn):
            total = sum(tensor_send(arrays[j * pn + q], j).astype(F32) for j in range(nt))
            sums.append(total.astype(BF16))
        return sums

    x_parts = [outer_send(first_half, s) for s in range(zn)]
    x_packed = pack_gates(x_parts)
    x_packed, sels = x_packed[:pn], x_packed[pn:]
    x_here = inner_exchange(x_packed)
    gathered = outer_exchange(after(grad_copies, *x_parts[1:]))
    chosen = call(
        functools.partial(route_kernel, **fixed, picks=picks, cap=cap),
        [shape(zr * tokens, pn * half)] * RETURNS,
        [info, after(meta, *x_packed)],
        [SMEM, VMEM],
        name="route",
    )
    c_packed = pack(after(gathered, *chosen))
    c_here = inner_exchange(c_packed)

    xs = swapped(([after(piece, *c_packed) for piece in x_here],))
    pieces = nt * CHUNKS * pn
    forward = call(
        functools.partial(forward_kernel, **sizes),
        [shape(rows, cols)] * (nt * pn) + [shape(slots, hid_n)] * 4,
        [after(info, *c_packed), *xs, expert_in, expert_out],
        [SMEM] + [HBM] * (pieces + 2),
        out_specs=[HBM] * (nt * pn + 4),
        scratch=[pltpu.VMEM((slots, nt * cols), BF16), pltpu.VMEM((pn, TAIL, cols), BF16)]
        + [pltpu.VMEM((hid_n, nt * cols), BF16)] * 3
        + [pltpu.VMEM((4, slots, hid_n), BF16)]
        + [pltpu.VMEM((nt, pn, rows, cols), BF16), dma((3 * nt + pieces + pn,))]
        + [dma((nt * pn + 8,))],
        name="expert_forward",
    )
    outs, (hs, hid, a1, a2) = forward[: nt * pn], forward[nt * pn :]
    cs = swapped(([after(piece, hid) for piece in c_here],))
    out_here = core_sum(outs)
    out_back = inner_exchange(out_here)

    backward = call(
        functools.partial(backward_kernel, **sizes),
        [
            shape(half + TAIL if r == RETURNS - 1 else half, cols)
            for r in range(RETURNS)
            for _ in range(nt * pn)
        ]
        + [shape(slots, hid_n)] * 2,
        [info, *cs, expert_in, expert_out, after(hid, *out_here), a1, a2],
        [SMEM] + [HBM] * (pieces + 5),
        out_specs=[HBM] * (RETURNS * nt * pn + 2),
        scratch=[pltpu.VMEM((slots, nt * cols), BF16)]
        + [pltpu.VMEM((slots, hid_n), BF16)] * 3
        + [pltpu.VMEM((hid_n, nt * cols), BF16)] * 3
        + [pltpu.VMEM((2, slots, hid_n), BF16)]
        + [pltpu.VMEM((nt, pn, rows + TAIL, cols), BF16), dma((3 * nt + pieces + 3,))]
        + [dma((RETURNS * nt * pn + 4,))],
        name="expert_backward",
    )
    grads, (gg, ug) = backward[: RETURNS * nt * pn], backward[RETURNS * nt * pn :]
    near, far = grads[: nt * pn], grads[nt * pn :]
    out_combined = combine(out_back)
    out_parts = outer_exchange(out_combined)
    far = [after(part, *out_back) for part in far]
    far_here = core_sum([after(part, out_combined) for part in far[:pn]] + far[pn:])
    far_back = inner_exchange(far_here)
    near_here = core_sum([after(part, far_back[1]) for part in near])
    near_back = inner_exchange(near_here)

    far_parts, gate_parts = combine_far([after(piece, *near_here) for piece in far_back])
    grad_parts = combine_near(gate_parts, near_back) + far_parts

    grad_in, grad_out = call(
        functools.partial(weights_kernel, **sizes),
        [shape(*expert_in.shape), shape(*expert_out.shape)],
        [after(info, grad_parts[0]), *xs, *cs, gg, ug, hs],
        [SMEM] + [HBM] * (2 * pieces + 3),
        out_specs=[HBM, HBM],
        scratch=[
            pltpu.VMEM((3, slots, hid_n), BF16),
            pltpu.VMEM((2, nt, slots, cols), BF16),
            pltpu.VMEM((nt, 3, hid_n, cols), BF16),
            dma((3 + 2 * pieces,)),
            dma((3 * nt,)),
        ],
        name="expert_weights",
    )

    branch = jnp.sum(after(out_parts, grad_in).astype(F32), axis=0)
    input_sum = sum(part[:tokens].astype(F32) for part in grad_parts)
    gate_sum = sum(part[tokens : tokens + picks, :tokens].astype(F32) for part in grad_parts)
    restored = (second_half.astype(F32) - branch).astype(BF16)
    carried_grad = (first_grad.astype(F32) + input_sum).astype(BF16)
    return (restored, carried_grad, gate_sum.T, grad_in, grad_out)


def solution(mesh):
    in_specs = (
        P("expert", "tensor"),
        P("expert", "tensor"),
        P("expert", "tensor"),
        P("expert", "tensor"),
        P("expert", None),
        P("expert", None),
        P("expert", None, "tensor", None),
        P("expert", "tensor", None),
    )
    out_specs = (
        P("expert", "tensor"),
        P("expert", "tensor"),
        P("expert", None),
        P("expert", None, "tensor", None),
        P("expert", "tensor", None),
    )
    return jax.shard_map(body, mesh=mesh, in_specs=in_specs, out_specs=out_specs, check_vma=False)
```

```python
import functools

import jax
import jax.numpy as jnp
from jax import lax
from jax.experimental import pallas as pl
from jax.experimental.pallas import tpu as pltpu
from jax.sharding import PartitionSpec as P

PLANE = 4
CHUNKS = 1
RETURNS = 2
TAIL = 16
VMEM_LIMIT = 56 * 1024 * 1024
SMALL_LIMIT = 16 * 1024 * 1024
F32 = jnp.float32
BF16 = jnp.bfloat16


def dot_nn(a, b):
    return lax.dot_general(a, b, (((1,), (0,)), ((), ())), preferred_element_type=F32)


def dot_nt(a, b):
    return lax.dot_general(a, b, (((1,), (1,)), ((), ())), preferred_element_type=F32)


def dot_tn(a, b):
    return lax.dot_general(a, b, (((0,), (0,)), ((), ())), preferred_element_type=F32)


def iota(shape, axis):
    return lax.broadcasted_iota(jnp.int32, shape, axis)


SMEM = pl.BlockSpec(memory_space=pltpu.SMEM)
VMEM = pl.BlockSpec(memory_space=pltpu.VMEM)
HBM = pl.BlockSpec(memory_space=pl.ANY)


def call(kernel, outs, args, specs, out_specs=None, scratch=(), name=None, limit=SMALL_LIMIT):
    return pl.pallas_call(
        kernel,
        out_shape=outs,
        in_specs=specs,
        out_specs=out_specs if out_specs is not None else [VMEM] * len(outs),
        scratch_shapes=list(scratch),
        compiler_params=pltpu.CompilerParams(vmem_limit_bytes=limit),
        cost_estimate=pl.CostEstimate(flops=1024, bytes_accessed=1024, transcendentals=0),
        name=name,
    )(*args)


def shape(*dims, dtype=BF16):
    return jax.ShapeDtypeStruct(dims, dtype)


def outer_meta(info, meta, s, zn):
    return meta[lax.rem(info[3] - s + zn, zn)]


def select(info, meta, sels, zn, pn, tokens, picks, rows):
    zc = zn // CHUNKS
    cap = rows // zc
    partner = iota((8, 1), 0)
    experts = jnp.where(partner < pn, info[0] + (partner ^ info[1]), -2).astype(F32)
    before = (iota((tokens, tokens), 0) < iota((tokens, tokens), 1)).astype(F32).astype(BF16)
    slot = iota((rows, tokens), 0).astype(F32)
    for s in range(zn):
        g, local = divmod(s, zc)
        ids = outer_meta(info, meta, s, zn)
        named = jnp.zeros((8, tokens), F32)
        for k in range(picks):
            named += (ids[k : k + 1, :] == experts).astype(F32)
        dest = dot_nn(named.astype(BF16), before) + local * cap
        dest = jnp.where(named > 0, dest, -1.0)
        for q in range(pn):
            sels[g][q * rows : (q + 1) * rows, local * tokens : (local + 1) * tokens] = (
                (slot == dest[q : q + 1, :]).astype(F32).astype(BF16)
            )


def route_kernel(info, meta, *chosen, zn, pn, tokens, picks, cap):
    zr = zn // RETURNS
    rows = zr * cap
    partner = iota((1, 8), 1)
    experts = jnp.where(partner < pn, info[0] + (partner ^ info[1]), -2).astype(F32)
    after = (iota((tokens, tokens), 1) < iota((tokens, tokens), 0)).astype(F32).astype(BF16)
    eye = (iota((16, 16), 0) == iota((16, 16), 1)).astype(F32).astype(BF16)
    lane = iota((tokens, pn * rows), 1).astype(F32)
    for s in range(zn):
        g, local = divmod(s, zr)
        columned = dot_tn(outer_meta(info, meta, s, zn).astype(BF16), eye)
        named = jnp.zeros((tokens, 8), F32)
        for k in range(picks):
            named += (columned[:, k : k + 1] == experts).astype(F32)
        dest = dot_nn(after, named.astype(BF16)) + local * cap
        dest = jnp.where(named > 0, dest + rows * partner.astype(F32), -1.0)
        picked = jnp.zeros((tokens, pn * rows), F32)
        for q in range(pn):
            picked += (lane == dest[:, q : q + 1]).astype(F32)
        chosen[g][local * tokens : (local + 1) * tokens, :] = picked.astype(BF16)


def tail_lanes(rows):
    return -(-rows // 128) * 128


class Loads:
    def __init__(self, sems):
        self.sems, self.copies, self.waited = sems, {}, set()

    def add(self, key, source, target):
        assert key not in self.copies
        self.copies[key] = pltpu.make_async_copy(source, target, self.sems.at[len(self.copies)])
        self.copies[key].start()

    def need(self, *keys):
        for key in keys:
            if key not in self.waited:
                self.waited.add(key)
                self.copies[key].wait()

    def finish(self):
        self.need(*self.copies)


def pack_kernel(info, sel, source, *refs, zn, pn, tokens, rows):
    outs, whole, sems = refs[:pn], refs[-2], refs[-1]
    loads = Loads(sems)
    for s in range(zn):
        place = lax.rem(info[3] - s + zn, zn)
        loads.add(s, source.at[place], whole.at[pl.ds(s * tokens, tokens)])
    loads.finish()
    for q in range(pn):
        outs[q][...] = dot_nn(sel[q * rows : (q + 1) * rows, :], whole[...]).astype(BF16)


def pack_gates_kernel(info, meta, *refs, zn, pn, tokens, picks, rows):
    zc = zn // CHUNKS
    sources, outs, refs = refs[:zc], refs[zc : zc + pn], refs[zc + pn :]
    sels, (whole, sems) = refs[:CHUNKS], refs[CHUNKS:]
    loads = Loads(sems)
    for s in range(zc):
        loads.add(s, sources[s], whole.at[pl.ds(s * tokens, tokens)])
    select(info, meta, sels, zn, pn, tokens, picks, rows)
    for q in range(pn):
        expert = (info[0] + (info[1] ^ q)).astype(F32)
        outs[q][rows : rows + TAIL, :] = jnp.zeros((TAIL, outs[q].shape[1]), BF16)
        for g in range(CHUNKS):
            tail = jnp.zeros((TAIL, rows), F32)
            for local in range(zc):
                known = outer_meta(info, meta, g * zc + local, zn)
                gate = jnp.zeros((1, tokens), F32)
                for k in range(picks):
                    gate += jnp.where(known[k : k + 1, :] == expert, known[8 + k : 9 + k, :], 0.0)
                gate = jnp.broadcast_to(gate, (TAIL, tokens)).astype(BF16)
                here = slice(local * tokens, (local + 1) * tokens)
                tail += dot_nt(gate, sels[g][q * rows : (q + 1) * rows, here])
            at = g * tail_lanes(rows)
            outs[q][rows : rows + TAIL, at : at + rows] = tail.astype(BF16)
    loads.finish()
    for q in range(pn):
        chosen = sels[0][q * rows : (q + 1) * rows, :]
        outs[q][0:rows, :] = dot_nn(chosen, whole[...]).astype(BF16)


def combine_kernel(info, *refs, zn, pn, tokens, rows):
    zr = zn // RETURNS
    chosen, backs = refs[:RETURNS], refs[RETURNS : RETURNS + pn]
    out, whole, sems = refs[RETURNS + pn :]
    loads = Loads(sems)
    for g in range(RETURNS):
        for q in range(pn):
            to = whole.at[g, pl.ds(q * rows, rows)]
            loads.add((g, q), backs[q].at[pl.ds(g * rows, rows)], to)
    for g in range(RETURNS):
        loads.need(*((g, q) for q in range(pn)))
        part = dot_nn(chosen[g][...], whole[g]).astype(BF16)
        for local in range(zr):
            place = lax.rem(info[3] - (g * zr + local) + zn, zn)
            out[place] = part[local * tokens : (local + 1) * tokens, :]


def combine_far_kernel(info, meta, sel, chosen, *refs, zn, pn, tokens, rows):
    zr, slots = zn // RETURNS, RETURNS * rows
    backs, outs, (gates, whole, tails, sems) = refs[:pn], refs[pn:-4], refs[-4:]
    loads = Loads(sems)
    for q in range(pn):
        loads.add(("t", q), backs[q].at[pl.ds(rows, TAIL)], tails.at[q])
        loads.add(q, backs[q].at[pl.ds(0, rows)], whole.at[pl.ds(q * rows, rows)])
    spreads = []
    for q in range(pn):
        loads.need(("t", q))
        spreads.append(dot_nn(tails[q, :, 0:slots], sel[q * slots : (q + 1) * slots, :])[0:8, :])
    for s in range(zn):
        ids = outer_meta(info, meta, s, zn)[0:8, :]
        total = jnp.zeros((8, tokens), F32)
        for q in range(pn):
            expert = (info[0] + (info[1] ^ q)).astype(F32)
            total += jnp.where(ids == expert, spreads[q][:, s * tokens : (s + 1) * tokens], 0.0)
        total = jnp.concatenate([total, jnp.zeros((TAIL - 8, tokens), F32)], axis=0)
        gates[:, s * tokens : (s + 1) * tokens] = total.astype(BF16)
    loads.finish()
    finish_combine(chosen, whole, gates, outs, zn - zr, tokens)


def combine_near_kernel(gates, chosen, *refs, pn, tokens, rows):
    backs, outs, (whole, sems) = refs[:pn], refs[pn:-2], refs[-2:]
    loads = Loads(sems)
    for q in range(pn):
        loads.add(q, backs[q], whole.at[pl.ds(q * rows, rows)])
    loads.finish()
    finish_combine(chosen, whole, gates, outs, 0, tokens)


def finish_combine(chosen, whole, gates, outs, first, tokens):
    part = dot_nn(chosen[...], whole[...]).astype(BF16)
    for local, out in enumerate(outs):
        at = first + local
        out[0:tokens, :] = part[local * tokens : (local + 1) * tokens, :]
        out[tokens : tokens + TAIL, :] = jnp.zeros((TAIL, part.shape[1]), BF16)
        out[tokens : tokens + TAIL, 0:tokens] = gates[:, at * tokens : (at + 1) * tokens]


def column_block(info, j, nt, cols):
    block = lax.rem(info[2] - j + nt, nt)
    return pl.ds(pl.multiple_of(block * cols, 128), cols)


def load_weight(loads, info, kind, source, target, blocks, nt, cols):
    for at, j in enumerate(blocks):
        block = source.at[:, column_block(info, j, nt, cols)]
        loads.add((kind, j), block, target.at[:, pl.ds(at * cols, cols)])


def by_core(refs, nt, pn):
    return [refs[j * pn : (j + 1) * pn] for j in range(nt)]


def load_chunk(loads, sources, target, g, pn, rows, cols):
    for j, pieces in enumerate(sources):
        for q in range(pn):
            to = target.at[pl.ds((g * pn + q) * rows, rows), pl.ds(j * cols, cols)]
            loads.add(("r", g, j, q), pieces[g * pn + q].at[pl.ds(0, rows)], to)


def halves(pn):
    units = [(g, q) for g in range(CHUNKS) for q in range(pn)]
    return units[: len(units) // 2], units[len(units) // 2 :]


def forward_kernel(info, *refs, nt, pn, rows, cols):
    n = CHUNKS * pn
    xs, refs = by_core(refs, nt, n), refs[nt * n :]
    (win, wout), outs, refs = refs[:2], by_core(refs[2:], nt, pn), refs[2 + nt * pn :]
    results, (x, tails, wg, wu, wd, kept, stage, in_sems, out_sems) = refs[:4], refs[4:]
    hs, hid, a1, a2 = (kept.at[i] for i in range(4))
    loads, stores = Loads(in_sems), Loads(out_sems)
    every = range(nt)
    load_chunk(loads, xs, x, 0, pn, rows, cols)
    load_weight(loads, info, "g", win.at[0, 0], wg, every, nt, cols)
    load_weight(loads, info, "u", win.at[0, 1], wu, every, nt, cols)
    for q in range(pn):
        loads.add(("t", q), xs[0][q].at[pl.ds(rows, TAIL)], tails.at[q])
    for g in range(1, CHUNKS):
        load_chunk(loads, xs, x, g, pn, rows, cols)
    load_weight(loads, info, "d", wout.at[0], wd, every, nt, cols)
    same = iota((rows, rows), 0) == iota((rows, rows), 1)
    tail_step = tail_lanes(rows)
    for b, units in enumerate(halves(pn)):
        here = slice(b * len(units) * rows, (b + 1) * len(units) * rows)
        loads.need(*(("r", g, j, q) for j in every for g, q in units))
        loads.need(*(("g", j) for j in every))
        gate = dot_nt(x[here, :], wg[...])
        loads.need(*(("u", j) for j in every), *(("t", q) for q in range(pn)))
        up = dot_nt(x[here, :], wu[...])
        columns = []
        for g, q in units:
            row = tails[q, :, g * tail_step : g * tail_step + rows].astype(F32)[0:1, :]
            columns.append(jnp.sum(jnp.where(same, row, 0.0), axis=1, keepdims=True))
        weight = jnp.concatenate(columns, axis=0)
        sigma = 0.5 * jnp.tanh(0.5 * gate) + 0.5
        active = gate * sigma
        hidden = active * up
        scaled = (weight * hidden).astype(BF16)
        hs[here, :] = scaled
        hid[here, :] = hidden.astype(BF16)
        a1[here, :] = (weight * (up * sigma * (1.0 + gate * (1.0 - sigma)))).astype(BF16)
        a2[here, :] = (weight * active).astype(BF16)
        span = pl.ds(b * len(units) * rows, len(units) * rows)
        for i, result in enumerate(results):
            stores.add(("kept", b, i), kept.at[i, span], result.at[span])
        loads.need(*(("d", j) for j in every))
        part = dot_nn(scaled, wd[...]).astype(BF16)
        for j in reversed(every):
            w = (nt - j) % nt
            for u, (g, q) in enumerate(units):
                block = part[u * rows : (u + 1) * rows, w * cols : (w + 1) * cols]
                stage[j, q, g * rows : (g + 1) * rows, :] = block
                if g == CHUNKS - 1:
                    stores.add((j, q), stage.at[j, q], outs[j][q])
    loads.finish()
    stores.finish()


def backward_kernel(info, *refs, nt, pn, rows, cols):
    n = CHUNKS * pn
    cs, refs = by_core(refs, nt, n), refs[nt * n :]
    n_out = RETURNS * nt * pn
    (win, wout, hid, a1, a2), outs, refs = refs[:5], refs[5 : 5 + n_out], refs[5 + n_out :]
    outs = [by_core(outs[r * nt * pn :], nt, pn) for r in range(RETURNS)]
    half = CHUNKS * rows // RETURNS
    results, (c, h, b1, b2, wg, wu, wd, kept, stage, in_sems, out_sems) = refs[:2], refs[2:]
    gg, ug = kept.at[0], kept.at[1]
    loads, stores = Loads(in_sems), Loads(out_sems)
    every = range(nt)
    load_chunk(loads, cs, c, 0, pn, rows, cols)
    load_weight(loads, info, "d", wout.at[0], wd, every, nt, cols)
    for key, source, target in (("h", hid, h), ("1", a1, b1), ("2", a2, b2)):
        loads.add(key, source, target)
    load_weight(loads, info, "g", win.at[0, 0], wg, every, nt, cols)
    load_weight(loads, info, "u", win.at[0, 1], wu, every, nt, cols)
    for g in range(1, CHUNKS):
        load_chunk(loads, cs, c, g, pn, rows, cols)
    same = iota((rows, rows), 0) == iota((rows, rows), 1)
    tail_step = tail_lanes(rows)
    bottom = slice(CHUNKS * rows, CHUNKS * rows + TAIL)
    for b, units in enumerate(halves(pn)):
        here = slice(b * len(units) * rows, (b + 1) * len(units) * rows)
        loads.need(*(("r", g, j, q) for j in every for g, q in units))
        loads.need(*(("d", j) for j in every))
        grad = dot_nt(c[here, :], wd[...])
        loads.need("h", "1", "2")
        piece = jnp.sum(grad * h[here, :].astype(F32), axis=1, keepdims=True)
        gate_grad = (grad * b1[here, :].astype(F32)).astype(BF16)
        up_grad = (grad * b2[here, :].astype(F32)).astype(BF16)
        gg[here, :] = gate_grad
        ug[here, :] = up_grad
        span = pl.ds(b * len(units) * rows, len(units) * rows)
        for i, result in enumerate(results):
            stores.add(("kept", b, i), kept.at[i, span], result.at[span])
        for u, (g, q) in enumerate(units):
            part = piece[u * rows : (u + 1) * rows, :]
            part = jnp.sum(jnp.where(same, part, 0.0), axis=0, keepdims=True)
            part = jnp.broadcast_to(part, (TAIL, rows)).astype(BF16)
            for j in every:
                if g == 0:
                    stage[j, q, bottom, :] = jnp.zeros((TAIL, cols), BF16)
                stage[j, q, bottom, g * tail_step : g * tail_step + rows] = part
        loads.need(*((k, j) for k in "gu" for j in every))
        part = (dot_nn(gate_grad, wg[...]) + dot_nn(up_grad, wu[...])).astype(BF16)
        for j in reversed(every):
            w = (nt - j) % nt
            for u, (g, q) in enumerate(units):
                block = part[u * rows : (u + 1) * rows, w * cols : (w + 1) * cols]
                stage[j, q, g * rows : (g + 1) * rows, :] = block
                for r in reversed(range(RETURNS if g == CHUNKS - 1 else 0)):
                    span = pl.ds(r * half, half + TAIL if r == RETURNS - 1 else half)
                    stores.add((j, q, r), stage.at[j, q, span], outs[r][j][q])
    loads.finish()
    stores.finish()


def weights_kernel(info, *refs, nt, pn, rows, cols, kinds):
    n = CHUNKS * pn
    sources, refs = by_core(refs, nt, n), refs[nt * n :]
    lefts, out, (left, right, stage, in_sems, out_sems) = refs[:kinds], refs[kinds], refs[kinds + 1 :]
    loads, stores = Loads(in_sems), Loads(out_sems)
    loads.add(("l", 0), lefts[0], left.at[0])
    for j in range(nt):
        for q in range(n):
            target = right.at[j, pl.ds(q * rows, rows)]
            loads.add((j, q), sources[j][q].at[pl.ds(0, rows)], target)
    for w in range(1, kinds):
        loads.add(("l", w), lefts[w], left.at[w])
    for w in range(kinds):
        loads.need(("l", w))
        for j in range(nt):
            loads.need(*((j, q) for q in range(n)))
            at = column_block(info, j, nt, cols)
            stage[j, w] = dot_tn(left[w], right[j]).astype(BF16)
            target = out.at[0, w, :, at] if kinds > 1 else out.at[0, :, at]
            stores.add((j, w), stage.at[j, w], target)
    loads.finish()
    stores.finish()


def after(value, *others):
    return lax.optimization_barrier((value, *others))[0]


def body(
    first_half,
    second_half,
    first_grad,
    second_grad,
    expert_ids,
    gate_weights,
    expert_in,
    expert_out,
):
    tokens, picks = expert_ids.shape
    groups = lax.axis_size("expert")
    nt = lax.axis_size("tensor")
    pn = PLANE
    zn = groups // pn
    cap = tokens * picks * 7 // (6 * groups)
    zc = zn // CHUNKS
    part_rows = zc * cap
    rows = CHUNKS * part_rows
    slots = pn * rows
    cols = first_half.shape[1]
    hid_n = expert_out.shape[1]
    me = lax.axis_index("expert")
    info = jnp.stack([(me // pn) * pn, me % pn, lax.axis_index("tensor"), me // pn]).astype(jnp.int32)

    def outer_send(value, s):
        if s % zn == 0:
            return value
        return lax.ppermute(
            value, "expert", [(e, ((e // pn + s) % zn) * pn + e % pn) for e in range(groups)]
        )

    def inner_send(value, q):
        if q == 0:
            return value
        return lax.ppermute(value, "expert", [(e, e ^ q) for e in range(groups)])

    def inner_exchange(pieces):
        return [inner_send(piece, q) for q, piece in enumerate(pieces)]

    def tensor_send(value, j):
        if j == 0:
            return value
        return lax.ppermute(value, "tensor", [(c, (c + j) % nt) for c in range(nt)])

    fixed = dict(zn=zn, pn=pn, tokens=tokens)

    own = jnp.concatenate(
        [
            jnp.pad(expert_ids.T.astype(F32), ((0, 8 - picks), (0, 0)), constant_values=-1.0),
            jnp.pad(gate_weights.T.astype(F32), ((0, 8 - picks), (0, 0))),
        ],
        axis=0,
    )
    columns = [[z * pn + q for z in range(zn)] for q in range(pn)]

    def outer_exchange(value):
        return lax.all_to_all(
            value,
            "expert",
            split_axis=0,
            concat_axis=0,
            axis_index_groups=columns,
            tiled=True,
        )

    def copies(value):
        return jnp.broadcast_to(value[None], (zn,) + value.shape)

    grad_copies = copies(second_grad)
    meta = outer_exchange(after(copies(own), grad_copies, info))
    dma = pltpu.SemaphoreType.DMA
    sizes = dict(nt=nt, pn=pn, rows=part_rows, cols=cols)

    def pack(gathered):
        return call(
            functools.partial(pack_kernel, **fixed, rows=part_rows),
            [shape(part_rows, cols)] * pn,
            [info, sels[0], gathered],
            [SMEM, VMEM, HBM],
            scratch=[pltpu.VMEM((zn * tokens, cols), BF16), dma((zn,))],
            name="pack",
        )

    def pack_gates(parts):
        return call(
            functools.partial(pack_gates_kernel, **fixed, picks=picks, rows=part_rows),
            [shape(part_rows + TAIL, cols)] * pn
            + [shape(pn * part_rows, zc * tokens)] * CHUNKS,
            [info, meta, *parts[:zc]],
            [SMEM, VMEM] + [HBM] * zc,
            scratch=[pltpu.VMEM((zc * tokens, cols), BF16), dma((zc,))],
            name="pack_gates",
        )

    zr = zn // RETURNS
    half = zr * cap

    def send_back(parts, first):
        return [outer_send(part, -(first + local)) for local, part in enumerate(parts)]

    def combine(backs):
        parts = call(
            functools.partial(combine_kernel, **fixed, rows=half),
            [shape(zn, tokens, cols)],
            [info, *chosen, *backs],
            [SMEM] + [VMEM] * RETURNS + [HBM] * pn,
            scratch=[pltpu.VMEM((RETURNS, pn * half, cols), BF16), dma((RETURNS * pn,))],
            name="combine",
        )
        return parts[0]

    def combine_far(backs):
        *parts, gates = call(
            functools.partial(combine_far_kernel, **fixed, rows=half),
            [shape(tokens + TAIL, cols)] * zr + [shape(TAIL, zn * tokens)],
            [info, meta, sels[0], chosen[RETURNS - 1], *backs],
            [SMEM] + [VMEM] * 3 + [HBM] * pn,
            scratch=[pltpu.VMEM((pn * half, cols), BF16), pltpu.VMEM((pn, TAIL, cols), BF16)]
            + [dma((2 * pn,))],
            name="combine_far",
        )
        return send_back(parts, zn - zr), gates

    def combine_near(gates, backs):
        parts = call(
            functools.partial(combine_near_kernel, pn=pn, tokens=tokens, rows=half),
            [shape(tokens + TAIL, cols)] * zr,
            [gates, chosen[0], *backs],
            [VMEM] * 2 + [HBM] * pn,
            scratch=[pltpu.VMEM((pn * half, cols), BF16), dma((pn,))],
            name="combine_near",
        )
        return send_back(parts, 0)

    def swapped(chunks):
        return [tensor_send(piece, j) for j in range(nt) for pieces in chunks for piece in pieces]

    def core_sum(arrays):
        sums = []
        for q in range(pn):
            total = sum(tensor_send(arrays[j * pn + q], j).astype(F32) for j in range(nt))
            sums.append(total.astype(BF16))
        return sums

    x_parts = [outer_send(first_half, s) for s in range(zn)]
    x_packed = pack_gates(x_parts)
    x_packed, sels = x_packed[:pn], x_packed[pn:]
    x_here = inner_exchange(x_packed)
    gathered = outer_exchange(after(grad_copies, *x_parts[1:]))
    chosen = call(
        functools.partial(route_kernel, **fixed, picks=picks, cap=cap),
        [shape(zr * tokens, pn * half)] * RETURNS,
        [info, after(meta, *x_packed)],
        [SMEM, VMEM],
        name="route",
    )
    c_packed = pack(after(gathered, *chosen))
    c_here = inner_exchange(c_packed)

    def weight_grad(like, info, sources, lefts):
        kinds = len(lefts)
        return call(
            functools.partial(weights_kernel, **sizes, kinds=kinds),
            [shape(*like.shape)],
            [info, *sources, *lefts],
            [SMEM] + [HBM] * (pieces + kinds),
            out_specs=[HBM],
            scratch=[
                pltpu.VMEM((kinds, slots, hid_n), BF16),
                pltpu.VMEM((nt, slots, cols), BF16),
                pltpu.VMEM((nt, kinds, hid_n, cols), BF16),
                dma((kinds + pieces,)),
                dma((kinds * nt,)),
            ],
            name="expert_weights",
            limit=VMEM_LIMIT,
        )[0]

    pieces = nt * CHUNKS * pn
    xs = swapped(([after(piece, *c_packed) for piece in x_here],))
    forward = call(
        functools.partial(forward_kernel, **sizes),
        [shape(rows, cols)] * (nt * pn) + [shape(slots, hid_n)] * 4,
        [after(info, *c_packed), *xs, expert_in, expert_out],
        [SMEM] + [HBM] * (pieces + 2),
        out_specs=[HBM] * (nt * pn + 4),
        scratch=[pltpu.VMEM((slots, nt * cols), BF16), pltpu.VMEM((pn, TAIL, cols), BF16)]
        + [pltpu.VMEM((hid_n, nt * cols), BF16)] * 3
        + [pltpu.VMEM((4, slots, hid_n), BF16)]
        + [pltpu.VMEM((nt, pn, rows, cols), BF16), dma((3 * nt + pieces + pn,))]
        + [dma((nt * pn + 8,))],
        name="expert_forward",
        limit=VMEM_LIMIT,
    )
    outs, (hs, hid, a1, a2) = forward[: nt * pn], forward[nt * pn :]
    cs = swapped(([after(piece, hid) for piece in c_here],))
    out_here = core_sum(outs)
    out_back = inner_exchange(out_here)

    backward = call(
        functools.partial(backward_kernel, **sizes),
        [
            shape(half + TAIL if r == RETURNS - 1 else half, cols)
            for r in range(RETURNS)
            for _ in range(nt * pn)
        ]
        + [shape(slots, hid_n)] * 2,
        [info, *cs, expert_in, expert_out, after(hid, *out_here), a1, a2],
        [SMEM] + [HBM] * (pieces + 5),
        out_specs=[HBM] * (RETURNS * nt * pn + 2),
        scratch=[pltpu.VMEM((slots, nt * cols), BF16)]
        + [pltpu.VMEM((slots, hid_n), BF16)] * 3
        + [pltpu.VMEM((hid_n, nt * cols), BF16)] * 3
        + [pltpu.VMEM((2, slots, hid_n), BF16)]
        + [pltpu.VMEM((nt, pn, rows + TAIL, cols), BF16), dma((3 * nt + pieces + 3,))]
        + [dma((RETURNS * nt * pn + 4,))],
        name="expert_backward",
        limit=VMEM_LIMIT,
    )
    grads, (gg, ug) = backward[: RETURNS * nt * pn], backward[RETURNS * nt * pn :]
    near, far = grads[: nt * pn], grads[nt * pn :]
    out_combined = combine(out_back)
    out_parts = outer_exchange(out_combined)
    far = [after(part, *out_back) for part in far]
    far_here = core_sum([after(part, out_combined) for part in far[:pn]] + far[pn:])
    far_back = inner_exchange(far_here)
    near_here = core_sum([after(part, far_back[1]) for part in near])
    near_back = inner_exchange(near_here)
    grad_out = weight_grad(expert_out, after(info, *near_here), cs, (hs,))

    far_parts, gate_parts = combine_far([after(piece, *near_here, grad_out) for piece in far_back])
    grad_parts = combine_near(gate_parts, near_back) + far_parts

    grad_in = weight_grad(expert_in, after(info, grad_parts[0]), xs, (gg, ug))

    branch = jnp.sum(after(out_parts, grad_in).astype(F32), axis=0)
    input_sum = sum(part[:tokens].astype(F32) for part in grad_parts)
    gate_sum = sum(part[tokens : tokens + picks, :tokens].astype(F32) for part in grad_parts)
    restored = (second_half.astype(F32) - branch).astype(BF16)
    carried_grad = (first_grad.astype(F32) + input_sum).astype(BF16)
    return (restored, carried_grad, gate_sum.T, grad_in, grad_out)


def solution(mesh):
    in_specs = (
        P("expert", "tensor"),
        P("expert", "tensor"),
        P("expert", "tensor"),
        P("expert", "tensor"),
        P("expert", None),
        P("expert", None),
        P("expert", None, "tensor", None),
        P("expert", "tensor", None),
    )
    out_specs = (
        P("expert", "tensor"),
        P("expert", "tensor"),
        P("expert", None),
        P("expert", None, "tensor", None),
        P("expert", "tensor", None),
    )
    return jax.shard_map(body, mesh=mesh, in_specs=in_specs, out_specs=out_specs, check_vma=False)
```

```python
import functools

import jax
import jax.numpy as jnp
from jax import lax
from jax.experimental import pallas as pl
from jax.experimental.pallas import tpu as pltpu
from jax.sharding import PartitionSpec as P

PLANE = 4
CHUNKS = 1
RETURNS = 2
BLOCKS = 1
TAIL = 16
VMEM_LIMIT = 56 * 1024 * 1024
SMALL_LIMIT = 16 * 1024 * 1024
F32 = jnp.float32
BF16 = jnp.bfloat16


def dot_nn(a, b):
    return lax.dot_general(a, b, (((1,), (0,)), ((), ())), preferred_element_type=F32)


def dot_nt(a, b):
    return lax.dot_general(a, b, (((1,), (1,)), ((), ())), preferred_element_type=F32)


def dot_tn(a, b):
    return lax.dot_general(a, b, (((0,), (0,)), ((), ())), preferred_element_type=F32)


def iota(shape, axis):
    return lax.broadcasted_iota(jnp.int32, shape, axis)


SMEM = pl.BlockSpec(memory_space=pltpu.SMEM)
VMEM = pl.BlockSpec(memory_space=pltpu.VMEM)
HBM = pl.BlockSpec(memory_space=pl.ANY)


def call(kernel, outs, args, specs, out_specs=None, scratch=(), name=None, limit=SMALL_LIMIT):
    return pl.pallas_call(
        kernel,
        out_shape=outs,
        in_specs=specs,
        out_specs=out_specs if out_specs is not None else [VMEM] * len(outs),
        scratch_shapes=list(scratch),
        compiler_params=pltpu.CompilerParams(vmem_limit_bytes=limit),
        cost_estimate=pl.CostEstimate(flops=1024, bytes_accessed=1024, transcendentals=0),
        name=name,
    )(*args)


def shape(*dims, dtype=BF16):
    return jax.ShapeDtypeStruct(dims, dtype)


def outer_meta(info, meta, s, zn):
    return meta[lax.rem(info[3] - s + zn, zn)]


def select(info, meta, sels, zn, pn, tokens, picks, rows):
    zc = zn // CHUNKS
    cap = rows // zc
    partner = iota((8, 1), 0)
    experts = jnp.where(partner < pn, info[0] + (partner ^ info[1]), -2).astype(F32)
    before = (iota((tokens, tokens), 0) < iota((tokens, tokens), 1)).astype(F32).astype(BF16)
    slot = iota((rows, tokens), 0).astype(F32)
    for s in range(zn):
        g, local = divmod(s, zc)
        ids = outer_meta(info, meta, s, zn)
        named = jnp.zeros((8, tokens), F32)
        for k in range(picks):
            named += (ids[k : k + 1, :] == experts).astype(F32)
        dest = dot_nn(named.astype(BF16), before) + local * cap
        dest = jnp.where(named > 0, dest, -1.0)
        for q in range(pn):
            sels[g][q * rows : (q + 1) * rows, local * tokens : (local + 1) * tokens] = (
                (slot == dest[q : q + 1, :]).astype(F32).astype(BF16)
            )


def route_kernel(info, meta, *chosen, zn, pn, tokens, picks, cap):
    zr = zn // RETURNS
    rows = zr * cap
    partner = iota((1, 8), 1)
    experts = jnp.where(partner < pn, info[0] + (partner ^ info[1]), -2).astype(F32)
    after = (iota((tokens, tokens), 1) < iota((tokens, tokens), 0)).astype(F32).astype(BF16)
    eye = (iota((16, 16), 0) == iota((16, 16), 1)).astype(F32).astype(BF16)
    lane = iota((tokens, pn * rows), 1).astype(F32)
    for s in range(zn):
        g, local = divmod(s, zr)
        columned = dot_tn(outer_meta(info, meta, s, zn).astype(BF16), eye)
        named = jnp.zeros((tokens, 8), F32)
        for k in range(picks):
            named += (columned[:, k : k + 1] == experts).astype(F32)
        dest = dot_nn(after, named.astype(BF16)) + local * cap
        dest = jnp.where(named > 0, dest + rows * partner.astype(F32), -1.0)
        picked = jnp.zeros((tokens, pn * rows), F32)
        for q in range(pn):
            picked += (lane == dest[:, q : q + 1]).astype(F32)
        chosen[g][local * tokens : (local + 1) * tokens, :] = picked.astype(BF16)


def tail_lanes(rows):
    return -(-rows // 128) * 128


class Loads:
    def __init__(self, sems):
        self.sems, self.copies, self.waited = sems, {}, set()

    def add(self, key, source, target):
        assert key not in self.copies
        self.copies[key] = pltpu.make_async_copy(source, target, self.sems.at[len(self.copies)])
        self.copies[key].start()

    def need(self, *keys):
        for key in keys:
            if key not in self.waited:
                self.waited.add(key)
                self.copies[key].wait()

    def finish(self):
        self.need(*self.copies)


def pack_kernel(info, sel, source, *refs, zn, pn, tokens, rows):
    outs, whole, sems = refs[:pn], refs[-2], refs[-1]
    loads = Loads(sems)
    for s in range(zn):
        place = lax.rem(info[3] - s + zn, zn)
        loads.add(s, source.at[place], whole.at[pl.ds(s * tokens, tokens)])
    loads.finish()
    for q in range(pn):
        outs[q][...] = dot_nn(sel[q * rows : (q + 1) * rows, :], whole[...]).astype(BF16)


def pack_gates_kernel(info, meta, *refs, zn, pn, tokens, picks, rows):
    zc = zn // CHUNKS
    sources, outs, refs = refs[:zc], refs[zc : zc + pn], refs[zc + pn :]
    sels, (whole, sems) = refs[:CHUNKS], refs[CHUNKS:]
    loads = Loads(sems)
    for s in range(zc):
        loads.add(s, sources[s], whole.at[pl.ds(s * tokens, tokens)])
    select(info, meta, sels, zn, pn, tokens, picks, rows)
    for q in range(pn):
        expert = (info[0] + (info[1] ^ q)).astype(F32)
        outs[q][rows : rows + TAIL, :] = jnp.zeros((TAIL, outs[q].shape[1]), BF16)
        for g in range(CHUNKS):
            tail = jnp.zeros((TAIL, rows), F32)
            for local in range(zc):
                known = outer_meta(info, meta, g * zc + local, zn)
                gate = jnp.zeros((1, tokens), F32)
                for k in range(picks):
                    gate += jnp.where(known[k : k + 1, :] == expert, known[8 + k : 9 + k, :], 0.0)
                gate = jnp.broadcast_to(gate, (TAIL, tokens)).astype(BF16)
                here = slice(local * tokens, (local + 1) * tokens)
                tail += dot_nt(gate, sels[g][q * rows : (q + 1) * rows, here])
            at = g * tail_lanes(rows)
            outs[q][rows : rows + TAIL, at : at + rows] = tail.astype(BF16)
    loads.finish()
    for q in range(pn):
        chosen = sels[0][q * rows : (q + 1) * rows, :]
        outs[q][0:rows, :] = dot_nn(chosen, whole[...]).astype(BF16)


def combine_kernel(info, *refs, zn, pn, tokens, rows):
    zr = zn // RETURNS
    chosen, backs = refs[:RETURNS], refs[RETURNS : RETURNS + pn]
    out, whole, sems = refs[RETURNS + pn :]
    loads = Loads(sems)
    for g in range(RETURNS):
        for q in range(pn):
            to = whole.at[g, pl.ds(q * rows, rows)]
            loads.add((g, q), backs[q].at[pl.ds(g * rows, rows)], to)
    for g in range(RETURNS):
        loads.need(*((g, q) for q in range(pn)))
        part = dot_nn(chosen[g][...], whole[g]).astype(BF16)
        for local in range(zr):
            place = lax.rem(info[3] - (g * zr + local) + zn, zn)
            out[place] = part[local * tokens : (local + 1) * tokens, :]


def combine_far_kernel(info, meta, sel, chosen, *refs, zn, pn, tokens, rows):
    zr, slots = zn // RETURNS, RETURNS * rows
    backs, outs, (gates, whole, tails, sems) = refs[:pn], refs[pn:-4], refs[-4:]
    loads = Loads(sems)
    for q in range(pn):
        loads.add(("t", q), backs[q].at[pl.ds(rows, TAIL)], tails.at[q])
        loads.add(q, backs[q].at[pl.ds(0, rows)], whole.at[pl.ds(q * rows, rows)])
    spreads = []
    for q in range(pn):
        loads.need(("t", q))
        spreads.append(dot_nn(tails[q, :, 0:slots], sel[q * slots : (q + 1) * slots, :])[0:8, :])
    for s in range(zn):
        ids = outer_meta(info, meta, s, zn)[0:8, :]
        total = jnp.zeros((8, tokens), F32)
        for q in range(pn):
            expert = (info[0] + (info[1] ^ q)).astype(F32)
            total += jnp.where(ids == expert, spreads[q][:, s * tokens : (s + 1) * tokens], 0.0)
        total = jnp.concatenate([total, jnp.zeros((TAIL - 8, tokens), F32)], axis=0)
        gates[:, s * tokens : (s + 1) * tokens] = total.astype(BF16)
    loads.finish()
    finish_combine(chosen, whole, gates, outs, zn - zr, tokens)


def combine_near_kernel(gates, chosen, *refs, pn, tokens, rows):
    backs, outs, (whole, sems) = refs[:pn], refs[pn:-2], refs[-2:]
    loads = Loads(sems)
    for q in range(pn):
        loads.add(q, backs[q], whole.at[pl.ds(q * rows, rows)])
    loads.finish()
    finish_combine(chosen, whole, gates, outs, 0, tokens)


def finish_combine(chosen, whole, gates, outs, first, tokens):
    part = dot_nn(chosen[...], whole[...]).astype(BF16)
    for local, out in enumerate(outs):
        at = first + local
        out[0:tokens, :] = part[local * tokens : (local + 1) * tokens, :]
        out[tokens : tokens + TAIL, :] = jnp.zeros((TAIL, part.shape[1]), BF16)
        out[tokens : tokens + TAIL, 0:tokens] = gates[:, at * tokens : (at + 1) * tokens]


def column_block(info, j, nt, cols):
    block = lax.rem(info[2] - j + nt, nt)
    return pl.ds(pl.multiple_of(block * cols, 128), cols)


def load_weight(loads, info, kind, source, target, blocks, nt, cols):
    for at, j in enumerate(blocks):
        block = source.at[:, column_block(info, j, nt, cols)]
        loads.add((kind, j), block, target.at[:, pl.ds(at * cols, cols)])


def by_core(refs, nt, pn):
    return [refs[j * pn : (j + 1) * pn] for j in range(nt)]


def load_chunk(loads, sources, target, g, pn, rows, cols):
    for j, pieces in enumerate(sources):
        for q in range(pn):
            to = target.at[pl.ds((g * pn + q) * rows, rows), pl.ds(j * cols, cols)]
            loads.add(("r", g, j, q), pieces[g * pn + q].at[pl.ds(0, rows)], to)


def blocks(pn):
    units = [(g, q) for g in range(CHUNKS) for q in range(pn)]
    size = len(units) // BLOCKS
    return [units[b * size : (b + 1) * size] for b in range(BLOCKS)]


def forward_kernel(info, *refs, nt, pn, rows, cols):
    n = CHUNKS * pn
    xs, refs = by_core(refs, nt, n), refs[nt * n :]
    (win, wout), outs, refs = refs[:2], by_core(refs[2:], nt, pn), refs[2 + nt * pn :]
    results, (x, tails, wg, wu, wd, kept, stage, in_sems, out_sems) = refs[:4], refs[4:]
    hs, hid, a1, a2 = (kept.at[i] for i in range(4))
    loads, stores = Loads(in_sems), Loads(out_sems)
    every = range(nt)
    load_chunk(loads, xs, x, 0, pn, rows, cols)
    load_weight(loads, info, "g", win.at[0, 0], wg, every, nt, cols)
    load_weight(loads, info, "u", win.at[0, 1], wu, every, nt, cols)
    for q in range(pn):
        loads.add(("t", q), xs[0][q].at[pl.ds(rows, TAIL)], tails.at[q])
    for g in range(1, CHUNKS):
        load_chunk(loads, xs, x, g, pn, rows, cols)
    load_weight(loads, info, "d", wout.at[0], wd, every, nt, cols)
    same = iota((rows, rows), 0) == iota((rows, rows), 1)
    tail_step = tail_lanes(rows)
    for b, units in enumerate(blocks(pn)):
        here = slice(b * len(units) * rows, (b + 1) * len(units) * rows)
        loads.need(*(("r", g, j, q) for j in every for g, q in units))
        loads.need(*(("g", j) for j in every))
        gate = dot_nt(x[here, :], wg[...])
        loads.need(*(("u", j) for j in every), *(("t", q) for q in range(pn)))
        up = dot_nt(x[here, :], wu[...])
        columns = []
        for g, q in units:
            row = tails[q, :, g * tail_step : g * tail_step + rows].astype(F32)[0:1, :]
            columns.append(jnp.sum(jnp.where(same, row, 0.0), axis=1, keepdims=True))
        weight = jnp.concatenate(columns, axis=0)
        sigma = 0.5 * jnp.tanh(0.5 * gate) + 0.5
        active = gate * sigma
        hidden = active * up
        scaled = (weight * hidden).astype(BF16)
        hs[here, :] = scaled
        hid[here, :] = hidden.astype(BF16)
        a1[here, :] = (weight * (up * sigma * (1.0 + gate * (1.0 - sigma)))).astype(BF16)
        a2[here, :] = (weight * active).astype(BF16)
        span = pl.ds(b * len(units) * rows, len(units) * rows)
        for i, result in enumerate(results):
            stores.add(("kept", b, i), kept.at[i, span], result.at[span])
        loads.need(*(("d", j) for j in every))
        part = dot_nn(scaled, wd[...]).astype(BF16)
        for j in reversed(every):
            w = (nt - j) % nt
            for u, (g, q) in enumerate(units):
                block = part[u * rows : (u + 1) * rows, w * cols : (w + 1) * cols]
                stage[j, q, g * rows : (g + 1) * rows, :] = block
                if g == CHUNKS - 1:
                    stores.add((j, q), stage.at[j, q], outs[j][q])
    loads.finish()
    stores.finish()


def backward_kernel(info, *refs, nt, pn, rows, cols):
    n = CHUNKS * pn
    cs, refs = by_core(refs, nt, n), refs[nt * n :]
    n_out = RETURNS * nt * pn
    (win, wout, hid, a1, a2), outs, refs = refs[:5], refs[5 : 5 + n_out], refs[5 + n_out :]
    outs = [by_core(outs[r * nt * pn :], nt, pn) for r in range(RETURNS)]
    half = CHUNKS * rows // RETURNS
    results, (c, h, b1, b2, wg, wu, wd, kept, stage, in_sems, out_sems) = refs[:2], refs[2:]
    gg, ug = kept.at[0], kept.at[1]
    loads, stores = Loads(in_sems), Loads(out_sems)
    every = range(nt)
    load_chunk(loads, cs, c, 0, pn, rows, cols)
    load_weight(loads, info, "d", wout.at[0], wd, every, nt, cols)
    for key, source, target in (("h", hid, h), ("1", a1, b1), ("2", a2, b2)):
        loads.add(key, source, target)
    load_weight(loads, info, "g", win.at[0, 0], wg, every, nt, cols)
    load_weight(loads, info, "u", win.at[0, 1], wu, every, nt, cols)
    for g in range(1, CHUNKS):
        load_chunk(loads, cs, c, g, pn, rows, cols)
    same = iota((rows, rows), 0) == iota((rows, rows), 1)
    tail_step = tail_lanes(rows)
    bottom = slice(CHUNKS * rows, CHUNKS * rows + TAIL)
    for b, units in enumerate(blocks(pn)):
        here = slice(b * len(units) * rows, (b + 1) * len(units) * rows)
        loads.need(*(("r", g, j, q) for j in every for g, q in units))
        loads.need(*(("d", j) for j in every))
        grad = dot_nt(c[here, :], wd[...])
        loads.need("h", "1", "2")
        piece = jnp.sum(grad * h[here, :].astype(F32), axis=1, keepdims=True)
        gate_grad = (grad * b1[here, :].astype(F32)).astype(BF16)
        up_grad = (grad * b2[here, :].astype(F32)).astype(BF16)
        gg[here, :] = gate_grad
        ug[here, :] = up_grad
        span = pl.ds(b * len(units) * rows, len(units) * rows)
        for i, result in enumerate(results):
            stores.add(("kept", b, i), kept.at[i, span], result.at[span])
        for u, (g, q) in enumerate(units):
            part = piece[u * rows : (u + 1) * rows, :]
            part = jnp.sum(jnp.where(same, part, 0.0), axis=0, keepdims=True)
            part = jnp.broadcast_to(part, (TAIL, rows)).astype(BF16)
            for j in every:
                if g == 0:
                    stage[j, q, bottom, :] = jnp.zeros((TAIL, cols), BF16)
                stage[j, q, bottom, g * tail_step : g * tail_step + rows] = part
        loads.need(*((k, j) for k in "gu" for j in every))
        part = (dot_nn(gate_grad, wg[...]) + dot_nn(up_grad, wu[...])).astype(BF16)
        for j in reversed(every):
            w = (nt - j) % nt
            for u, (g, q) in enumerate(units):
                block = part[u * rows : (u + 1) * rows, w * cols : (w + 1) * cols]
                stage[j, q, g * rows : (g + 1) * rows, :] = block
                for r in reversed(range(RETURNS if g == CHUNKS - 1 else 0)):
                    span = pl.ds(r * half, half + TAIL if r == RETURNS - 1 else half)
                    stores.add((j, q, r), stage.at[j, q, span], outs[r][j][q])
    loads.finish()
    stores.finish()


def weights_kernel(info, *refs, nt, pn, rows, cols):
    n = CHUNKS * pn
    xs, cs, refs = by_core(refs, nt, n), by_core(refs[nt * n :], nt, n), refs[2 * nt * n :]
    lefts, (gin, gout, left, right, stage, in_sems, out_sems) = refs[:3], refs[3:]
    loads, stores = Loads(in_sems), Loads(out_sems)
    order = ((0, 0, xs), (1, 0, xs), (2, 1, cs))
    for w, side, sources in order:
        loads.add(("l", w), lefts[w], left.at[w])
        if w == 1:
            continue
        for j in range(nt):
            for q in range(n):
                target = right.at[side, j, pl.ds(q * rows, rows)]
                loads.add((side, j, q), sources[j][q].at[pl.ds(0, rows)], target)
    for w, side, _ in order:
        loads.need(("l", w))
        for j in range(nt):
            loads.need(*((side, j, q) for q in range(n)))
            at = column_block(info, j, nt, cols)
            stage[j, w] = dot_tn(left[w], right[side, j]).astype(BF16)
            target = gout.at[0, :, at] if w == 2 else gin.at[0, w, :, at]
            stores.add((j, w), stage.at[j, w], target)
    loads.finish()
    stores.finish()


def after(value, *others):
    return lax.optimization_barrier((value, *others))[0]


def body(
    first_half,
    second_half,
    first_grad,
    second_grad,
    expert_ids,
    gate_weights,
    expert_in,
    expert_out,
):
    tokens, picks = expert_ids.shape
    groups = lax.axis_size("expert")
    nt = lax.axis_size("tensor")
    pn = PLANE
    zn = groups // pn
    cap = tokens * picks * 7 // (6 * groups)
    zc = zn // CHUNKS
    part_rows = zc * cap
    rows = CHUNKS * part_rows
    slots = pn * rows
    cols = first_half.shape[1]
    hid_n = expert_out.shape[1]
    me = lax.axis_index("expert")
    info = jnp.stack([(me // pn) * pn, me % pn, lax.axis_index("tensor"), me // pn]).astype(jnp.int32)

    def outer_send(value, s):
        if s % zn == 0:
            return value
        return lax.ppermute(
            value, "expert", [(e, ((e // pn + s) % zn) * pn + e % pn) for e in range(groups)]
        )

    def inner_send(value, q):
        if q == 0:
            return value
        return lax.ppermute(value, "expert", [(e, e ^ q) for e in range(groups)])

    def inner_exchange(pieces):
        return [inner_send(piece, q) for q, piece in enumerate(pieces)]

    def tensor_send(value, j):
        if j == 0:
            return value
        return lax.ppermute(value, "tensor", [(c, (c + j) % nt) for c in range(nt)])

    fixed = dict(zn=zn, pn=pn, tokens=tokens)

    own = jnp.concatenate(
        [
            jnp.pad(expert_ids.T.astype(F32), ((0, 8 - picks), (0, 0)), constant_values=-1.0),
            jnp.pad(gate_weights.T.astype(F32), ((0, 8 - picks), (0, 0))),
        ],
        axis=0,
    )
    columns = [[z * pn + q for z in range(zn)] for q in range(pn)]

    def outer_exchange(value):
        return lax.all_to_all(
            value,
            "expert",
            split_axis=0,
            concat_axis=0,
            axis_index_groups=columns,
            tiled=True,
        )

    def copies(value):
        return jnp.broadcast_to(value[None], (zn,) + value.shape)

    grad_copies = copies(second_grad)
    meta = outer_exchange(after(copies(own), grad_copies, info))
    dma = pltpu.SemaphoreType.DMA
    sizes = dict(nt=nt, pn=pn, rows=part_rows, cols=cols)

    def pack(gathered):
        return call(
            functools.partial(pack_kernel, **fixed, rows=part_rows),
            [shape(part_rows, cols)] * pn,
            [info, sels[0], gathered],
            [SMEM, VMEM, HBM],
            scratch=[pltpu.VMEM((zn * tokens, cols), BF16), dma((zn,))],
            name="pack",
        )

    def pack_gates(parts):
        return call(
            functools.partial(pack_gates_kernel, **fixed, picks=picks, rows=part_rows),
            [shape(part_rows + TAIL, cols)] * pn
            + [shape(pn * part_rows, zc * tokens)] * CHUNKS,
            [info, meta, *parts[:zc]],
            [SMEM, VMEM] + [HBM] * zc,
            scratch=[pltpu.VMEM((zc * tokens, cols), BF16), dma((zc,))],
            name="pack_gates",
        )

    zr = zn // RETURNS
    half = zr * cap

    def send_back(parts, first):
        return [outer_send(part, -(first + local)) for local, part in enumerate(parts)]

    def combine(backs):
        parts = call(
            functools.partial(combine_kernel, **fixed, rows=half),
            [shape(zn, tokens, cols)],
            [info, *chosen, *backs],
            [SMEM] + [VMEM] * RETURNS + [HBM] * pn,
            scratch=[pltpu.VMEM((RETURNS, pn * half, cols), BF16), dma((RETURNS * pn,))],
            name="combine",
        )
        return parts[0]

    def combine_far(backs):
        *parts, gates = call(
            functools.partial(combine_far_kernel, **fixed, rows=half),
            [shape(tokens + TAIL, cols)] * zr + [shape(TAIL, zn * tokens)],
            [info, meta, sels[0], chosen[RETURNS - 1], *backs],
            [SMEM] + [VMEM] * 3 + [HBM] * pn,
            scratch=[pltpu.VMEM((pn * half, cols), BF16), pltpu.VMEM((pn, TAIL, cols), BF16)]
            + [dma((2 * pn,))],
            name="combine_far",
        )
        return send_back(parts, zn - zr), gates

    def combine_near(gates, backs):
        parts = call(
            functools.partial(combine_near_kernel, pn=pn, tokens=tokens, rows=half),
            [shape(tokens + TAIL, cols)] * zr,
            [gates, chosen[0], *backs],
            [VMEM] * 2 + [HBM] * pn,
            scratch=[pltpu.VMEM((pn * half, cols), BF16), dma((pn,))],
            name="combine_near",
        )
        return send_back(parts, 0)

    def swapped(chunks):
        return [tensor_send(piece, j) for j in range(nt) for pieces in chunks for piece in pieces]

    def core_sum(arrays):
        sums = []
        for q in range(pn):
            total = sum(tensor_send(arrays[j * pn + q], j).astype(F32) for j in range(nt))
            sums.append(total.astype(BF16))
        return sums

    x_parts = [outer_send(first_half, s) for s in range(zn)]
    x_packed = pack_gates(x_parts)
    x_packed, sels = x_packed[:pn], x_packed[pn:]
    x_here = inner_exchange(x_packed)
    gathered = outer_exchange(after(grad_copies, *x_parts[1:]))
    chosen = call(
        functools.partial(route_kernel, **fixed, picks=picks, cap=cap),
        [shape(zr * tokens, pn * half)] * RETURNS,
        [info, after(meta, *x_packed)],
        [SMEM, VMEM],
        name="route",
    )
    c_packed = pack(after(gathered, *chosen))
    c_here = inner_exchange(c_packed)

    pieces = nt * CHUNKS * pn
    xs = swapped(([after(piece, *c_packed) for piece in x_here],))
    forward = call(
        functools.partial(forward_kernel, **sizes),
        [shape(rows, cols)] * (nt * pn) + [shape(slots, hid_n)] * 4,
        [after(info, *c_packed), *xs, expert_in, expert_out],
        [SMEM] + [HBM] * (pieces + 2),
        out_specs=[HBM] * (nt * pn + 4),
        scratch=[pltpu.VMEM((slots, nt * cols), BF16), pltpu.VMEM((pn, TAIL, cols), BF16)]
        + [pltpu.VMEM((hid_n, nt * cols), BF16)] * 3
        + [pltpu.VMEM((4, slots, hid_n), BF16)]
        + [pltpu.VMEM((nt, pn, rows, cols), BF16), dma((3 * nt + pieces + pn,))]
        + [dma((nt * pn + 4 * BLOCKS,))],
        name="expert_forward",
        limit=VMEM_LIMIT,
    )
    outs, (hs, hid, a1, a2) = forward[: nt * pn], forward[nt * pn :]
    cs = swapped(([after(piece, hid) for piece in c_here],))
    out_here = core_sum(outs)
    out_back = inner_exchange(out_here)

    backward = call(
        functools.partial(backward_kernel, **sizes),
        [
            shape(half + TAIL if r == RETURNS - 1 else half, cols)
            for r in range(RETURNS)
            for _ in range(nt * pn)
        ]
        + [shape(slots, hid_n)] * 2,
        [info, *cs, expert_in, expert_out, after(hid, *out_here), a1, a2],
        [SMEM] + [HBM] * (pieces + 5),
        out_specs=[HBM] * (RETURNS * nt * pn + 2),
        scratch=[pltpu.VMEM((slots, nt * cols), BF16)]
        + [pltpu.VMEM((slots, hid_n), BF16)] * 3
        + [pltpu.VMEM((hid_n, nt * cols), BF16)] * 3
        + [pltpu.VMEM((2, slots, hid_n), BF16)]
        + [pltpu.VMEM((nt, pn, rows + TAIL, cols), BF16), dma((3 * nt + pieces + 3,))]
        + [dma((RETURNS * nt * pn + 2 * BLOCKS,))],
        name="expert_backward",
        limit=VMEM_LIMIT,
    )
    grads, (gg, ug) = backward[: RETURNS * nt * pn], backward[RETURNS * nt * pn :]
    near, far = grads[: nt * pn], grads[nt * pn :]
    out_combined = combine(out_back)
    out_parts = outer_exchange(out_combined)
    far = [after(part, *out_back) for part in far]
    far_here = core_sum([after(part, out_combined) for part in far[:pn]] + far[pn:])
    far_back = inner_exchange(far_here)
    near_here = core_sum([after(part, far_back[pn - 1]) for part in near])
    near_back = inner_exchange(near_here)

    far_parts, gate_parts = combine_far([after(piece, *near_here) for piece in far_back])
    grad_parts = combine_near(gate_parts, near_back) + far_parts

    grad_in, grad_out = call(
        functools.partial(weights_kernel, **sizes),
        [shape(*expert_in.shape), shape(*expert_out.shape)],
        [after(info, grad_parts[0]), *xs, *cs, gg, ug, hs],
        [SMEM] + [HBM] * (2 * pieces + 3),
        out_specs=[HBM, HBM],
        scratch=[
            pltpu.VMEM((3, slots, hid_n), BF16),
            pltpu.VMEM((2, nt, slots, cols), BF16),
            pltpu.VMEM((nt, 3, hid_n, cols), BF16),
            dma((3 + 2 * pieces,)),
            dma((3 * nt,)),
        ],
        name="expert_weights",
        limit=VMEM_LIMIT,
    )

    branch = jnp.sum(after(out_parts, grad_in).astype(F32), axis=0)
    input_sum = sum(part[:tokens].astype(F32) for part in grad_parts)
    gate_sum = sum(part[tokens : tokens + picks, :tokens].astype(F32) for part in grad_parts)
    restored = (second_half.astype(F32) - branch).astype(BF16)
    carried_grad = (first_grad.astype(F32) + input_sum).astype(BF16)
    return (restored, carried_grad, gate_sum.T, grad_in, grad_out)


def solution(mesh):
    in_specs = (
        P("expert", "tensor"),
        P("expert", "tensor"),
        P("expert", "tensor"),
        P("expert", "tensor"),
        P("expert", None),
        P("expert", None),
        P("expert", None, "tensor", None),
        P("expert", "tensor", None),
    )
    out_specs = (
        P("expert", "tensor"),
        P("expert", "tensor"),
        P("expert", None),
        P("expert", None, "tensor", None),
        P("expert", "tensor", None),
    )
    return jax.shard_map(body, mesh=mesh, in_specs=in_specs, out_specs=out_specs, check_vma=False)
```

```python
import functools

import jax
import jax.numpy as jnp
from jax import lax
from jax.experimental import pallas as pl
from jax.experimental.pallas import tpu as pltpu
from jax.sharding import PartitionSpec as P

PLANE = 4
CHUNKS = 1
RETURNS = 2
BLOCKS = 2
TAIL = 16
VMEM_LIMIT = 56 * 1024 * 1024
EXPERT_LIMIT = 48 * 1024 * 1024
SMALL_LIMIT = 16 * 1024 * 1024
F32 = jnp.float32
BF16 = jnp.bfloat16


def dot_nn(a, b):
    return lax.dot_general(a, b, (((1,), (0,)), ((), ())), preferred_element_type=F32)


def dot_nt(a, b):
    return lax.dot_general(a, b, (((1,), (1,)), ((), ())), preferred_element_type=F32)


def dot_tn(a, b):
    return lax.dot_general(a, b, (((0,), (0,)), ((), ())), preferred_element_type=F32)


def iota(shape, axis):
    return lax.broadcasted_iota(jnp.int32, shape, axis)


SMEM = pl.BlockSpec(memory_space=pltpu.SMEM)
VMEM = pl.BlockSpec(memory_space=pltpu.VMEM)
HBM = pl.BlockSpec(memory_space=pl.ANY)


def call(kernel, outs, args, specs, out_specs=None, scratch=(), name=None, limit=SMALL_LIMIT):
    return pl.pallas_call(
        kernel,
        out_shape=outs,
        in_specs=specs,
        out_specs=out_specs if out_specs is not None else [VMEM] * len(outs),
        scratch_shapes=list(scratch),
        compiler_params=pltpu.CompilerParams(vmem_limit_bytes=limit),
        cost_estimate=pl.CostEstimate(flops=1024, bytes_accessed=1024, transcendentals=0),
        name=name,
    )(*args)


def shape(*dims, dtype=BF16):
    return jax.ShapeDtypeStruct(dims, dtype)


def outer_meta(info, meta, s, zn):
    return meta[lax.rem(info[3] - s + zn, zn)]


def select(info, meta, sels, zn, pn, tokens, picks, rows):
    zc = zn // CHUNKS
    cap = rows // zc
    partner = iota((8, 1), 0)
    experts = jnp.where(partner < pn, info[0] + (partner ^ info[1]), -2).astype(F32)
    before = (iota((tokens, tokens), 0) < iota((tokens, tokens), 1)).astype(F32).astype(BF16)
    slot = iota((rows, tokens), 0).astype(F32)
    for s in range(zn):
        g, local = divmod(s, zc)
        ids = outer_meta(info, meta, s, zn)
        named = jnp.zeros((8, tokens), F32)
        for k in range(picks):
            named += (ids[k : k + 1, :] == experts).astype(F32)
        dest = dot_nn(named.astype(BF16), before) + local * cap
        dest = jnp.where(named > 0, dest, -1.0)
        for q in range(pn):
            sels[g][q * rows : (q + 1) * rows, local * tokens : (local + 1) * tokens] = (
                (slot == dest[q : q + 1, :]).astype(F32).astype(BF16)
            )


def route_kernel(info, meta, *chosen, zn, pn, tokens, picks, cap):
    zr = zn // RETURNS
    rows = zr * cap
    partner = iota((1, 8), 1)
    experts = jnp.where(partner < pn, info[0] + (partner ^ info[1]), -2).astype(F32)
    after = (iota((tokens, tokens), 1) < iota((tokens, tokens), 0)).astype(F32).astype(BF16)
    eye = (iota((16, 16), 0) == iota((16, 16), 1)).astype(F32).astype(BF16)
    lane = iota((tokens, pn * rows), 1).astype(F32)
    for s in range(zn):
        g, local = divmod(s, zr)
        columned = dot_tn(outer_meta(info, meta, s, zn).astype(BF16), eye)
        named = jnp.zeros((tokens, 8), F32)
        for k in range(picks):
            named += (columned[:, k : k + 1] == experts).astype(F32)
        dest = dot_nn(after, named.astype(BF16)) + local * cap
        dest = jnp.where(named > 0, dest + rows * partner.astype(F32), -1.0)
        picked = jnp.zeros((tokens, pn * rows), F32)
        for q in range(pn):
            picked += (lane == dest[:, q : q + 1]).astype(F32)
        chosen[g][local * tokens : (local + 1) * tokens, :] = picked.astype(BF16)


def tail_lanes(rows):
    return -(-rows // 128) * 128


class Loads:
    def __init__(self, sems):
        self.sems, self.copies, self.waited = sems, {}, set()

    def add(self, key, source, target):
        assert key not in self.copies
        self.copies[key] = pltpu.make_async_copy(source, target, self.sems.at[len(self.copies)])
        self.copies[key].start()

    def need(self, *keys):
        for key in keys:
            if key not in self.waited:
                self.waited.add(key)
                self.copies[key].wait()

    def finish(self):
        self.need(*self.copies)


def pack_kernel(info, sel, source, *refs, zn, pn, tokens, rows):
    outs, whole, sems = refs[:pn], refs[-2], refs[-1]
    loads = Loads(sems)
    for s in range(zn):
        place = lax.rem(info[3] - s + zn, zn)
        loads.add(s, source.at[place], whole.at[pl.ds(s * tokens, tokens)])
    loads.finish()
    for q in range(pn):
        outs[q][...] = dot_nn(sel[q * rows : (q + 1) * rows, :], whole[...]).astype(BF16)


def pack_gates_kernel(info, meta, *refs, zn, pn, tokens, picks, rows):
    zc = zn // CHUNKS
    sources, outs, refs = refs[:zc], refs[zc : zc + pn], refs[zc + pn :]
    sels, (whole, sems) = refs[:CHUNKS], refs[CHUNKS:]
    loads = Loads(sems)
    for s in range(zc):
        loads.add(s, sources[s], whole.at[pl.ds(s * tokens, tokens)])
    select(info, meta, sels, zn, pn, tokens, picks, rows)
    for q in range(pn):
        expert = (info[0] + (info[1] ^ q)).astype(F32)
        outs[q][rows : rows + TAIL, :] = jnp.zeros((TAIL, outs[q].shape[1]), BF16)
        for g in range(CHUNKS):
            tail = jnp.zeros((TAIL, rows), F32)
            for local in range(zc):
                known = outer_meta(info, meta, g * zc + local, zn)
                gate = jnp.zeros((1, tokens), F32)
                for k in range(picks):
                    gate += jnp.where(known[k : k + 1, :] == expert, known[8 + k : 9 + k, :], 0.0)
                gate = jnp.broadcast_to(gate, (TAIL, tokens)).astype(BF16)
                here = slice(local * tokens, (local + 1) * tokens)
                tail += dot_nt(gate, sels[g][q * rows : (q + 1) * rows, here])
            at = g * tail_lanes(rows)
            outs[q][rows : rows + TAIL, at : at + rows] = tail.astype(BF16)
    loads.finish()
    for q in range(pn):
        chosen = sels[0][q * rows : (q + 1) * rows, :]
        outs[q][0:rows, :] = dot_nn(chosen, whole[...]).astype(BF16)


def combine_kernel(info, *refs, zn, pn, tokens, rows):
    zr = zn // RETURNS
    chosen, backs = refs[:RETURNS], refs[RETURNS : RETURNS + pn]
    out, whole, sems = refs[RETURNS + pn :]
    loads = Loads(sems)
    for g in range(RETURNS):
        for q in range(pn):
            to = whole.at[g, pl.ds(q * rows, rows)]
            loads.add((g, q), backs[q].at[pl.ds(g * rows, rows)], to)
    for g in range(RETURNS):
        loads.need(*((g, q) for q in range(pn)))
        part = dot_nn(chosen[g][...], whole[g]).astype(BF16)
        for local in range(zr):
            place = lax.rem(info[3] - (g * zr + local) + zn, zn)
            out[place] = part[local * tokens : (local + 1) * tokens, :]


def combine_far_kernel(info, meta, sel, chosen, *refs, zn, pn, tokens, rows):
    zr, slots = zn // RETURNS, RETURNS * rows
    backs, outs, (gates, whole, tails, sems) = refs[:pn], refs[pn:-4], refs[-4:]
    loads = Loads(sems)
    for q in range(pn):
        loads.add(("t", q), backs[q].at[pl.ds(rows, TAIL)], tails.at[q])
        loads.add(q, backs[q].at[pl.ds(0, rows)], whole.at[pl.ds(q * rows, rows)])
    spreads = []
    for q in range(pn):
        loads.need(("t", q))
        spreads.append(dot_nn(tails[q, :, 0:slots], sel[q * slots : (q + 1) * slots, :])[0:8, :])
    for s in range(zn):
        ids = outer_meta(info, meta, s, zn)[0:8, :]
        total = jnp.zeros((8, tokens), F32)
        for q in range(pn):
            expert = (info[0] + (info[1] ^ q)).astype(F32)
            total += jnp.where(ids == expert, spreads[q][:, s * tokens : (s + 1) * tokens], 0.0)
        total = jnp.concatenate([total, jnp.zeros((TAIL - 8, tokens), F32)], axis=0)
        gates[:, s * tokens : (s + 1) * tokens] = total.astype(BF16)
    loads.finish()
    finish_combine(chosen, whole, gates, outs, zn - zr, tokens)


def combine_near_kernel(gates, chosen, *refs, pn, tokens, rows):
    backs, outs, (whole, sems) = refs[:pn], refs[pn:-2], refs[-2:]
    loads = Loads(sems)
    for q in range(pn):
        loads.add(q, backs[q], whole.at[pl.ds(q * rows, rows)])
    loads.finish()
    finish_combine(chosen, whole, gates, outs, 0, tokens)


def finish_combine(chosen, whole, gates, outs, first, tokens):
    part = dot_nn(chosen[...], whole[...]).astype(BF16)
    for local, out in enumerate(outs):
        at = first + local
        out[0:tokens, :] = part[local * tokens : (local + 1) * tokens, :]
        out[tokens : tokens + TAIL, :] = jnp.zeros((TAIL, part.shape[1]), BF16)
        out[tokens : tokens + TAIL, 0:tokens] = gates[:, at * tokens : (at + 1) * tokens]


def column_block(info, j, nt, cols):
    block = lax.rem(info[2] - j + nt, nt)
    return pl.ds(pl.multiple_of(block * cols, 128), cols)


def load_weight(loads, info, kind, source, target, blocks, nt, cols):
    for at, j in enumerate(blocks):
        block = source.at[:, column_block(info, j, nt, cols)]
        loads.add((kind, j), block, target.at[:, pl.ds(at * cols, cols)])


def by_core(refs, nt, pn):
    return [refs[j * pn : (j + 1) * pn] for j in range(nt)]


def load_chunk(loads, sources, target, g, pn, rows, cols):
    for j, pieces in enumerate(sources):
        for q in range(pn):
            to = target.at[pl.ds((g * pn + q) * rows, rows), pl.ds(j * cols, cols)]
            loads.add(("r", g, j, q), pieces[g * pn + q].at[pl.ds(0, rows)], to)


def blocks(pn):
    units = [(g, q) for g in range(CHUNKS) for q in range(pn)]
    size = len(units) // BLOCKS
    return [units[b * size : (b + 1) * size] for b in range(BLOCKS)]


def forward_kernel(info, *refs, nt, pn, rows, cols):
    n = CHUNKS * pn
    xs, refs = by_core(refs, nt, n), refs[nt * n :]
    (win, wout), outs, refs = refs[:2], by_core(refs[2:], nt, pn), refs[2 + nt * pn :]
    results, (x, tails, wg, wu, wd, kept, stage, in_sems, out_sems) = refs[:4], refs[4:]
    hs, hid, a1, a2 = (kept.at[i] for i in range(4))
    loads, stores = Loads(in_sems), Loads(out_sems)
    every = range(nt)
    load_chunk(loads, xs, x, 0, pn, rows, cols)
    load_weight(loads, info, "g", win.at[0, 0], wg, every, nt, cols)
    load_weight(loads, info, "u", win.at[0, 1], wu, every, nt, cols)
    for q in range(pn):
        loads.add(("t", q), xs[0][q].at[pl.ds(rows, TAIL)], tails.at[q])
    for g in range(1, CHUNKS):
        load_chunk(loads, xs, x, g, pn, rows, cols)
    load_weight(loads, info, "d", wout.at[0], wd, every, nt, cols)
    same = iota((rows, rows), 0) == iota((rows, rows), 1)
    tail_step = tail_lanes(rows)
    for b, units in enumerate(blocks(pn)):
        here = slice(b * len(units) * rows, (b + 1) * len(units) * rows)
        loads.need(*(("r", g, j, q) for j in every for g, q in units))
        loads.need(*(("g", j) for j in every))
        gate = dot_nt(x[here, :], wg[...])
        loads.need(*(("u", j) for j in every), *(("t", q) for q in range(pn)))
        up = dot_nt(x[here, :], wu[...])
        columns = []
        for g, q in units:
            row = tails[q, :, g * tail_step : g * tail_step + rows].astype(F32)[0:1, :]
            columns.append(jnp.sum(jnp.where(same, row, 0.0), axis=1, keepdims=True))
        weight = jnp.concatenate(columns, axis=0)
        sigma = 0.5 * jnp.tanh(0.5 * gate) + 0.5
        active = gate * sigma
        hidden = active * up
        scaled = (weight * hidden).astype(BF16)
        hs[here, :] = scaled
        hid[here, :] = hidden.astype(BF16)
        a1[here, :] = (weight * (up * sigma * (1.0 + gate * (1.0 - sigma)))).astype(BF16)
        a2[here, :] = (weight * active).astype(BF16)
        span = pl.ds(b * len(units) * rows, len(units) * rows)
        for i, result in enumerate(results):
            stores.add(("kept", b, i), kept.at[i, span], result.at[span])
        loads.need(*(("d", j) for j in every))
        part = dot_nn(scaled, wd[...]).astype(BF16)
        for j in reversed(every):
            w = (nt - j) % nt
            for u, (g, q) in enumerate(units):
                block = part[u * rows : (u + 1) * rows, w * cols : (w + 1) * cols]
                stage[j, q, g * rows : (g + 1) * rows, :] = block
                if g == CHUNKS - 1:
                    stores.add((j, q), stage.at[j, q], outs[j][q])
    loads.finish()
    stores.finish()


def backward_kernel(info, *refs, nt, pn, rows, cols):
    n = CHUNKS * pn
    cs, refs = by_core(refs, nt, n), refs[nt * n :]
    n_out = RETURNS * nt * pn
    (win, wout, hid, a1, a2), outs, refs = refs[:5], refs[5 : 5 + n_out], refs[5 + n_out :]
    outs = [by_core(outs[r * nt * pn :], nt, pn) for r in range(RETURNS)]
    half = CHUNKS * rows // RETURNS
    results, (c, h, b1, b2, wg, wu, wd, kept, stage, in_sems, out_sems) = refs[:2], refs[2:]
    gg, ug = kept.at[0], kept.at[1]
    loads, stores = Loads(in_sems), Loads(out_sems)
    every = range(nt)
    load_chunk(loads, cs, c, 0, pn, rows, cols)
    load_weight(loads, info, "d", wout.at[0], wd, every, nt, cols)
    for key, source, target in (("h", hid, h), ("1", a1, b1), ("2", a2, b2)):
        loads.add(key, source, target)
    load_weight(loads, info, "g", win.at[0, 0], wg, every, nt, cols)
    load_weight(loads, info, "u", win.at[0, 1], wu, every, nt, cols)
    for g in range(1, CHUNKS):
        load_chunk(loads, cs, c, g, pn, rows, cols)
    same = iota((rows, rows), 0) == iota((rows, rows), 1)
    tail_step = tail_lanes(rows)
    bottom = slice(CHUNKS * rows, CHUNKS * rows + TAIL)
    for b, units in enumerate(blocks(pn)):
        here = slice(b * len(units) * rows, (b + 1) * len(units) * rows)
        loads.need(*(("r", g, j, q) for j in every for g, q in units))
        loads.need(*(("d", j) for j in every))
        grad = dot_nt(c[here, :], wd[...])
        loads.need("h", "1", "2")
        piece = jnp.sum(grad * h[here, :].astype(F32), axis=1, keepdims=True)
        gate_grad = (grad * b1[here, :].astype(F32)).astype(BF16)
        up_grad = (grad * b2[here, :].astype(F32)).astype(BF16)
        gg[here, :] = gate_grad
        ug[here, :] = up_grad
        span = pl.ds(b * len(units) * rows, len(units) * rows)
        for i, result in enumerate(results):
            stores.add(("kept", b, i), kept.at[i, span], result.at[span])
        for u, (g, q) in enumerate(units):
            part = piece[u * rows : (u + 1) * rows, :]
            part = jnp.sum(jnp.where(same, part, 0.0), axis=0, keepdims=True)
            part = jnp.broadcast_to(part, (TAIL, rows)).astype(BF16)
            for j in every:
                if g == 0:
                    stage[j, q, bottom, :] = jnp.zeros((TAIL, cols), BF16)
                stage[j, q, bottom, g * tail_step : g * tail_step + rows] = part
        loads.need(*((k, j) for k in "gu" for j in every))
        part = (dot_nn(gate_grad, wg[...]) + dot_nn(up_grad, wu[...])).astype(BF16)
        for j in reversed(every):
            w = (nt - j) % nt
            for u, (g, q) in enumerate(units):
                block = part[u * rows : (u + 1) * rows, w * cols : (w + 1) * cols]
                stage[j, q, g * rows : (g + 1) * rows, :] = block
                for r in reversed(range(RETURNS if g == CHUNKS - 1 else 0)):
                    span = pl.ds(r * half, half + TAIL if r == RETURNS - 1 else half)
                    stores.add((j, q, r), stage.at[j, q, span], outs[r][j][q])
    loads.finish()
    stores.finish()


def weights_kernel(info, *refs, nt, pn, rows, cols):
    n = CHUNKS * pn
    xs, cs, refs = by_core(refs, nt, n), by_core(refs[nt * n :], nt, n), refs[2 * nt * n :]
    lefts, (gin, gout, left, right, stage, in_sems, out_sems) = refs[:3], refs[3:]
    loads, stores = Loads(in_sems), Loads(out_sems)
    order = ((0, 0, xs), (1, 0, xs), (2, 1, cs))
    for w, side, sources in order:
        loads.add(("l", w), lefts[w], left.at[w])
        if w == 1:
            continue
        for j in range(nt):
            for q in range(n):
                target = right.at[side, j, pl.ds(q * rows, rows)]
                loads.add((side, j, q), sources[j][q].at[pl.ds(0, rows)], target)
    for w, side, _ in order:
        loads.need(("l", w))
        for j in range(nt):
            loads.need(*((side, j, q) for q in range(n)))
            at = column_block(info, j, nt, cols)
            stage[j, w] = dot_tn(left[w], right[side, j]).astype(BF16)
            target = gout.at[0, :, at] if w == 2 else gin.at[0, w, :, at]
            stores.add((j, w), stage.at[j, w], target)
    loads.finish()
    stores.finish()


def after(value, *others):
    return lax.optimization_barrier((value, *others))[0]


def body(
    first_half,
    second_half,
    first_grad,
    second_grad,
    expert_ids,
    gate_weights,
    expert_in,
    expert_out,
):
    tokens, picks = expert_ids.shape
    groups = lax.axis_size("expert")
    nt = lax.axis_size("tensor")
    pn = PLANE
    zn = groups // pn
    cap = tokens * picks * 7 // (6 * groups)
    zc = zn // CHUNKS
    part_rows = zc * cap
    rows = CHUNKS * part_rows
    slots = pn * rows
    cols = first_half.shape[1]
    hid_n = expert_out.shape[1]
    me = lax.axis_index("expert")
    info = jnp.stack([(me // pn) * pn, me % pn, lax.axis_index("tensor"), me // pn]).astype(jnp.int32)

    def outer_send(value, s):
        if s % zn == 0:
            return value
        return lax.ppermute(
            value, "expert", [(e, ((e // pn + s) % zn) * pn + e % pn) for e in range(groups)]
        )

    def inner_send(value, q):
        if q == 0:
            return value
        return lax.ppermute(value, "expert", [(e, e ^ q) for e in range(groups)])

    def inner_exchange(pieces):
        return [inner_send(piece, q) for q, piece in enumerate(pieces)]

    def tensor_send(value, j):
        if j == 0:
            return value
        return lax.ppermute(value, "tensor", [(c, (c + j) % nt) for c in range(nt)])

    fixed = dict(zn=zn, pn=pn, tokens=tokens)

    own = jnp.concatenate(
        [
            jnp.pad(expert_ids.T.astype(F32), ((0, 8 - picks), (0, 0)), constant_values=-1.0),
            jnp.pad(gate_weights.T.astype(F32), ((0, 8 - picks), (0, 0))),
        ],
        axis=0,
    )
    columns = [[z * pn + q for z in range(zn)] for q in range(pn)]

    def outer_exchange(value):
        return lax.all_to_all(
            value,
            "expert",
            split_axis=0,
            concat_axis=0,
            axis_index_groups=columns,
            tiled=True,
        )

    def copies(value):
        return jnp.broadcast_to(value[None], (zn,) + value.shape)

    grad_copies = copies(second_grad)
    meta = outer_exchange(after(copies(own), grad_copies, info))
    dma = pltpu.SemaphoreType.DMA
    sizes = dict(nt=nt, pn=pn, rows=part_rows, cols=cols)

    def pack(gathered):
        return call(
            functools.partial(pack_kernel, **fixed, rows=part_rows),
            [shape(part_rows, cols)] * pn,
            [info, sels[0], gathered],
            [SMEM, VMEM, HBM],
            scratch=[pltpu.VMEM((zn * tokens, cols), BF16), dma((zn,))],
            name="pack",
        )

    def pack_gates(parts):
        return call(
            functools.partial(pack_gates_kernel, **fixed, picks=picks, rows=part_rows),
            [shape(part_rows + TAIL, cols)] * pn
            + [shape(pn * part_rows, zc * tokens)] * CHUNKS,
            [info, meta, *parts[:zc]],
            [SMEM, VMEM] + [HBM] * zc,
            scratch=[pltpu.VMEM((zc * tokens, cols), BF16), dma((zc,))],
            name="pack_gates",
        )

    zr = zn // RETURNS
    half = zr * cap

    def send_back(parts, first):
        return [outer_send(part, -(first + local)) for local, part in enumerate(parts)]

    def combine(backs):
        parts = call(
            functools.partial(combine_kernel, **fixed, rows=half),
            [shape(zn, tokens, cols)],
            [info, *chosen, *backs],
            [SMEM] + [VMEM] * RETURNS + [HBM] * pn,
            scratch=[pltpu.VMEM((RETURNS, pn * half, cols), BF16), dma((RETURNS * pn,))],
            name="combine",
        )
        return parts[0]

    def combine_far(backs):
        *parts, gates = call(
            functools.partial(combine_far_kernel, **fixed, rows=half),
            [shape(tokens + TAIL, cols)] * zr + [shape(TAIL, zn * tokens)],
            [info, meta, sels[0], chosen[RETURNS - 1], *backs],
            [SMEM] + [VMEM] * 3 + [HBM] * pn,
            scratch=[pltpu.VMEM((pn * half, cols), BF16), pltpu.VMEM((pn, TAIL, cols), BF16)]
            + [dma((2 * pn,))],
            name="combine_far",
        )
        return send_back(parts, zn - zr), gates

    def combine_near(gates, backs):
        parts = call(
            functools.partial(combine_near_kernel, pn=pn, tokens=tokens, rows=half),
            [shape(tokens + TAIL, cols)] * zr,
            [gates, chosen[0], *backs],
            [VMEM] * 2 + [HBM] * pn,
            scratch=[pltpu.VMEM((pn * half, cols), BF16), dma((pn,))],
            name="combine_near",
        )
        return send_back(parts, 0)

    def swapped(chunks):
        return [tensor_send(piece, j) for j in range(nt) for pieces in chunks for piece in pieces]

    def core_sum(arrays):
        sums = []
        for q in range(pn):
            total = sum(tensor_send(arrays[j * pn + q], j).astype(F32) for j in range(nt))
            sums.append(total.astype(BF16))
        return sums

    x_parts = [outer_send(first_half, s) for s in range(zn)]
    x_packed = pack_gates(x_parts)
    x_packed, sels = x_packed[:pn], x_packed[pn:]
    x_here = inner_exchange(x_packed)
    gathered = outer_exchange(after(grad_copies, *x_parts[1:]))
    chosen = call(
        functools.partial(route_kernel, **fixed, picks=picks, cap=cap),
        [shape(zr * tokens, pn * half)] * RETURNS,
        [info, after(meta, *x_packed)],
        [SMEM, VMEM],
        name="route",
    )
    c_packed = pack(after(gathered, *chosen))
    c_here = inner_exchange(c_packed)

    pieces = nt * CHUNKS * pn
    xs = swapped(([after(piece, *c_packed) for piece in x_here],))
    forward = call(
        functools.partial(forward_kernel, **sizes),
        [shape(rows, cols)] * (nt * pn) + [shape(slots, hid_n)] * 4,
        [after(info, *c_packed), *xs, expert_in, expert_out],
        [SMEM] + [HBM] * (pieces + 2),
        out_specs=[HBM] * (nt * pn + 4),
        scratch=[pltpu.VMEM((slots, nt * cols), BF16), pltpu.VMEM((pn, TAIL, cols), BF16)]
        + [pltpu.VMEM((hid_n, nt * cols), BF16)] * 3
        + [pltpu.VMEM((4, slots, hid_n), BF16)]
        + [pltpu.VMEM((nt, pn, rows, cols), BF16), dma((3 * nt + pieces + pn,))]
        + [dma((nt * pn + 4 * BLOCKS,))],
        name="expert_forward",
        limit=EXPERT_LIMIT,
    )
    outs, (hs, hid, a1, a2) = forward[: nt * pn], forward[nt * pn :]
    cs = swapped(([after(piece, hid) for piece in c_here],))
    out_here = core_sum(outs)
    out_back = inner_exchange(out_here)

    backward = call(
        functools.partial(backward_kernel, **sizes),
        [
            shape(half + TAIL if r == RETURNS - 1 else half, cols)
            for r in range(RETURNS)
            for _ in range(nt * pn)
        ]
        + [shape(slots, hid_n)] * 2,
        [info, *cs, expert_in, expert_out, after(hid, *out_here), a1, a2],
        [SMEM] + [HBM] * (pieces + 5),
        out_specs=[HBM] * (RETURNS * nt * pn + 2),
        scratch=[pltpu.VMEM((slots, nt * cols), BF16)]
        + [pltpu.VMEM((slots, hid_n), BF16)] * 3
        + [pltpu.VMEM((hid_n, nt * cols), BF16)] * 3
        + [pltpu.VMEM((2, slots, hid_n), BF16)]
        + [pltpu.VMEM((nt, pn, rows + TAIL, cols), BF16), dma((3 * nt + pieces + 3,))]
        + [dma((RETURNS * nt * pn + 2 * BLOCKS,))],
        name="expert_backward",
        limit=EXPERT_LIMIT,
    )
    grads, (gg, ug) = backward[: RETURNS * nt * pn], backward[RETURNS * nt * pn :]
    near, far = grads[: nt * pn], grads[nt * pn :]
    out_combined = combine(out_back)
    out_parts = outer_exchange(out_combined)
    far = [after(part, *out_back) for part in far]
    far_here = core_sum([after(part, out_combined) for part in far[:pn]] + far[pn:])
    far_back = inner_exchange(far_here)
    near_here = core_sum([after(part, far_back[pn - 1]) for part in near])
    near_back = inner_exchange(near_here)

    far_parts, gate_parts = combine_far([after(piece, *near_here) for piece in far_back])
    grad_parts = combine_near(gate_parts, near_back) + far_parts

    grad_in, grad_out = call(
        functools.partial(weights_kernel, **sizes),
        [shape(*expert_in.shape), shape(*expert_out.shape)],
        [after(info, grad_parts[0]), *xs, *cs, gg, ug, hs],
        [SMEM] + [HBM] * (2 * pieces + 3),
        out_specs=[HBM, HBM],
        scratch=[
            pltpu.VMEM((3, slots, hid_n), BF16),
            pltpu.VMEM((2, nt, slots, cols), BF16),
            pltpu.VMEM((nt, 3, hid_n, cols), BF16),
            dma((3 + 2 * pieces,)),
            dma((3 * nt,)),
        ],
        name="expert_weights",
        limit=VMEM_LIMIT,
    )

    branch = jnp.sum(after(out_parts, grad_in).astype(F32), axis=0)
    input_sum = sum(part[:tokens].astype(F32) for part in grad_parts)
    gate_sum = sum(part[tokens : tokens + picks, :tokens].astype(F32) for part in grad_parts)
    restored = (second_half.astype(F32) - branch).astype(BF16)
    carried_grad = (first_grad.astype(F32) + input_sum).astype(BF16)
    return (restored, carried_grad, gate_sum.T, grad_in, grad_out)


def solution(mesh):
    in_specs = (
        P("expert", "tensor"),
        P("expert", "tensor"),
        P("expert", "tensor"),
        P("expert", "tensor"),
        P("expert", None),
        P("expert", None),
        P("expert", None, "tensor", None),
        P("expert", "tensor", None),
    )
    out_specs = (
        P("expert", "tensor"),
        P("expert", "tensor"),
        P("expert", None),
        P("expert", None, "tensor", None),
        P("expert", "tensor", None),
    )
    return jax.shard_map(body, mesh=mesh, in_specs=in_specs, out_specs=out_specs, check_vma=False)
```

```python
import functools

import jax
import jax.numpy as jnp
from jax import lax
from jax.experimental import pallas as pl
from jax.experimental.pallas import tpu as pltpu
from jax.sharding import PartitionSpec as P

PLANE = 4
CHUNKS = 1
RETURNS = 2
BLOCKS = 2
TAIL = 16
VMEM_LIMIT = 62 * 1024 * 1024
SMALL_LIMIT = 16 * 1024 * 1024
F32 = jnp.float32
BF16 = jnp.bfloat16


def dot_nn(a, b):
    return lax.dot_general(a, b, (((1,), (0,)), ((), ())), preferred_element_type=F32)


def dot_nt(a, b):
    return lax.dot_general(a, b, (((1,), (1,)), ((), ())), preferred_element_type=F32)


def dot_tn(a, b):
    return lax.dot_general(a, b, (((0,), (0,)), ((), ())), preferred_element_type=F32)


def iota(shape, axis):
    return lax.broadcasted_iota(jnp.int32, shape, axis)


SMEM = pl.BlockSpec(memory_space=pltpu.SMEM)
VMEM = pl.BlockSpec(memory_space=pltpu.VMEM)
HBM = pl.BlockSpec(memory_space=pl.ANY)


def call(kernel, outs, args, specs, out_specs=None, scratch=(), name=None, limit=SMALL_LIMIT):
    return pl.pallas_call(
        kernel,
        out_shape=outs,
        in_specs=specs,
        out_specs=out_specs if out_specs is not None else [VMEM] * len(outs),
        scratch_shapes=list(scratch),
        compiler_params=pltpu.CompilerParams(vmem_limit_bytes=limit),
        cost_estimate=pl.CostEstimate(flops=1024, bytes_accessed=1024, transcendentals=0),
        name=name,
    )(*args)


def shape(*dims, dtype=BF16):
    return jax.ShapeDtypeStruct(dims, dtype)


def outer_meta(info, meta, s, zn):
    return meta[lax.rem(info[3] - s + zn, zn)]


def select(info, meta, sels, zn, pn, tokens, picks, rows):
    zc = zn // CHUNKS
    cap = rows // zc
    partner = iota((8, 1), 0)
    experts = jnp.where(partner < pn, info[0] + (partner ^ info[1]), -2).astype(F32)
    before = (iota((tokens, tokens), 0) < iota((tokens, tokens), 1)).astype(F32).astype(BF16)
    slot = iota((rows, tokens), 0).astype(F32)
    for s in range(zn):
        g, local = divmod(s, zc)
        ids = outer_meta(info, meta, s, zn)
        named = jnp.zeros((8, tokens), F32)
        for k in range(picks):
            named += (ids[k : k + 1, :] == experts).astype(F32)
        dest = dot_nn(named.astype(BF16), before) + local * cap
        dest = jnp.where(named > 0, dest, -1.0)
        for q in range(pn):
            sels[g][q * rows : (q + 1) * rows, local * tokens : (local + 1) * tokens] = (
                (slot == dest[q : q + 1, :]).astype(F32).astype(BF16)
            )


def route_kernel(info, meta, *chosen, zn, pn, tokens, picks, cap):
    zr = zn // RETURNS
    rows = zr * cap
    partner = iota((1, 8), 1)
    experts = jnp.where(partner < pn, info[0] + (partner ^ info[1]), -2).astype(F32)
    after = (iota((tokens, tokens), 1) < iota((tokens, tokens), 0)).astype(F32).astype(BF16)
    eye = (iota((16, 16), 0) == iota((16, 16), 1)).astype(F32).astype(BF16)
    lane = iota((tokens, pn * rows), 1).astype(F32)
    for s in range(zn):
        g, local = divmod(s, zr)
        columned = dot_tn(outer_meta(info, meta, s, zn).astype(BF16), eye)
        named = jnp.zeros((tokens, 8), F32)
        for k in range(picks):
            named += (columned[:, k : k + 1] == experts).astype(F32)
        dest = dot_nn(after, named.astype(BF16)) + local * cap
        dest = jnp.where(named > 0, dest + rows * partner.astype(F32), -1.0)
        picked = jnp.zeros((tokens, pn * rows), F32)
        for q in range(pn):
            picked += (lane == dest[:, q : q + 1]).astype(F32)
        chosen[g][local * tokens : (local + 1) * tokens, :] = picked.astype(BF16)


def tail_lanes(rows):
    return -(-rows // 128) * 128


class Loads:
    def __init__(self, sems):
        self.sems, self.copies, self.waited = sems, {}, set()

    def add(self, key, source, target):
        assert key not in self.copies
        self.copies[key] = pltpu.make_async_copy(source, target, self.sems.at[len(self.copies)])
        self.copies[key].start()

    def need(self, *keys):
        for key in keys:
            if key not in self.waited:
                self.waited.add(key)
                self.copies[key].wait()

    def finish(self):
        self.need(*self.copies)


def pack_kernel(info, sel, source, *refs, zn, pn, tokens, rows):
    outs, whole, sems = refs[:pn], refs[-2], refs[-1]
    loads = Loads(sems)
    for s in range(zn):
        place = lax.rem(info[3] - s + zn, zn)
        loads.add(s, source.at[place], whole.at[pl.ds(s * tokens, tokens)])
    loads.finish()
    for q in range(pn):
        outs[q][...] = dot_nn(sel[q * rows : (q + 1) * rows, :], whole[...]).astype(BF16)


def pack_gates_kernel(info, meta_hbm, *refs, zn, pn, tokens, picks, rows):
    zc = zn // CHUNKS
    sources, outs, refs = refs[:zc], refs[zc : zc + pn], refs[zc + pn :]
    sels, (meta, whole, sems) = refs[:CHUNKS], refs[CHUNKS:]
    loads = Loads(sems)
    loads.add("meta", meta_hbm, meta)
    for s in range(zc):
        loads.add(s, sources[s], whole.at[pl.ds(s * tokens, tokens)])
    loads.need("meta")
    select(info, meta, sels, zn, pn, tokens, picks, rows)
    for q in range(pn):
        expert = (info[0] + (info[1] ^ q)).astype(F32)
        outs[q][rows : rows + TAIL, :] = jnp.zeros((TAIL, outs[q].shape[1]), BF16)
        for g in range(CHUNKS):
            tail = jnp.zeros((TAIL, rows), F32)
            for local in range(zc):
                known = outer_meta(info, meta, g * zc + local, zn)
                gate = jnp.zeros((1, tokens), F32)
                for k in range(picks):
                    gate += jnp.where(known[k : k + 1, :] == expert, known[8 + k : 9 + k, :], 0.0)
                gate = jnp.broadcast_to(gate, (TAIL, tokens)).astype(BF16)
                here = slice(local * tokens, (local + 1) * tokens)
                tail += dot_nt(gate, sels[g][q * rows : (q + 1) * rows, here])
            at = g * tail_lanes(rows)
            outs[q][rows : rows + TAIL, at : at + rows] = tail.astype(BF16)
    loads.finish()
    for q in range(pn):
        chosen = sels[0][q * rows : (q + 1) * rows, :]
        outs[q][0:rows, :] = dot_nn(chosen, whole[...]).astype(BF16)


def combine_kernel(info, *refs, zn, pn, tokens, rows):
    zr = zn // RETURNS
    chosen, backs = refs[:RETURNS], refs[RETURNS : RETURNS + pn]
    out, whole, sems = refs[RETURNS + pn :]
    loads = Loads(sems)
    for g in range(RETURNS):
        for q in range(pn):
            to = whole.at[g, pl.ds(q * rows, rows)]
            loads.add((g, q), backs[q].at[pl.ds(g * rows, rows)], to)
    for g in range(RETURNS):
        loads.need(*((g, q) for q in range(pn)))
        part = dot_nn(chosen[g][...], whole[g]).astype(BF16)
        for local in range(zr):
            place = lax.rem(info[3] - (g * zr + local) + zn, zn)
            out[place] = part[local * tokens : (local + 1) * tokens, :]


def combine_far_kernel(info, meta, sel, chosen, *refs, zn, pn, tokens, rows):
    zr, slots = zn // RETURNS, RETURNS * rows
    backs, outs, (gates, whole, tails, sems) = refs[:pn], refs[pn:-4], refs[-4:]
    loads = Loads(sems)
    for q in range(pn):
        loads.add(("t", q), backs[q].at[pl.ds(rows, TAIL)], tails.at[q])
        loads.add(q, backs[q].at[pl.ds(0, rows)], whole.at[pl.ds(q * rows, rows)])
    spreads = []
    for q in range(pn):
        loads.need(("t", q))
        spreads.append(dot_nn(tails[q, :, 0:slots], sel[q * slots : (q + 1) * slots, :])[0:8, :])
    for s in range(zn):
        ids = outer_meta(info, meta, s, zn)[0:8, :]
        total = jnp.zeros((8, tokens), F32)
        for q in range(pn):
            expert = (info[0] + (info[1] ^ q)).astype(F32)
            total += jnp.where(ids == expert, spreads[q][:, s * tokens : (s + 1) * tokens], 0.0)
        total = jnp.concatenate([total, jnp.zeros((TAIL - 8, tokens), F32)], axis=0)
        gates[:, s * tokens : (s + 1) * tokens] = total.astype(BF16)
    loads.finish()
    finish_combine(chosen, whole, gates, outs, zn - zr, tokens)


def combine_near_kernel(gates, chosen, *refs, pn, tokens, rows):
    backs, outs, (whole, sems) = refs[:pn], refs[pn:-2], refs[-2:]
    loads = Loads(sems)
    for q in range(pn):
        loads.add(q, backs[q], whole.at[pl.ds(q * rows, rows)])
    loads.finish()
    finish_combine(chosen, whole, gates, outs, 0, tokens)


def finish_combine(chosen, whole, gates, outs, first, tokens):
    part = dot_nn(chosen[...], whole[...]).astype(BF16)
    for local, out in enumerate(outs):
        at = first + local
        out[0:tokens, :] = part[local * tokens : (local + 1) * tokens, :]
        out[tokens : tokens + TAIL, :] = jnp.zeros((TAIL, part.shape[1]), BF16)
        out[tokens : tokens + TAIL, 0:tokens] = gates[:, at * tokens : (at + 1) * tokens]


def column_block(info, j, nt, cols):
    block = lax.rem(info[2] - j + nt, nt)
    return pl.ds(pl.multiple_of(block * cols, 128), cols)


def load_weight(loads, info, kind, source, target, blocks, nt, cols):
    for at, j in enumerate(blocks):
        block = source.at[:, column_block(info, j, nt, cols)]
        loads.add((kind, j), block, target.at[:, pl.ds(at * cols, cols)])


def by_core(refs, nt, pn):
    return [refs[j * pn : (j + 1) * pn] for j in range(nt)]


def load_chunk(loads, sources, target, g, pn, rows, cols):
    for j, pieces in enumerate(sources):
        for q in range(pn):
            to = target.at[pl.ds((g * pn + q) * rows, rows), pl.ds(j * cols, cols)]
            loads.add(("r", g, j, q), pieces[g * pn + q].at[pl.ds(0, rows)], to)


def blocks(pn):
    units = [(g, q) for g in range(CHUNKS) for q in range(pn)]
    size = len(units) // BLOCKS
    return [units[b * size : (b + 1) * size] for b in range(BLOCKS)]


def forward_kernel(info, *refs, nt, pn, rows, cols):
    n = CHUNKS * pn
    xs, refs = by_core(refs, nt, n), refs[nt * n :]
    (win, wout), outs, refs = refs[:2], by_core(refs[2:], nt, pn), refs[2 + nt * pn :]
    results, (x, tails, wg, wu, wd, kept, stage, in_sems, out_sems) = refs[:4], refs[4:]
    hs, hid, a1, a2 = (kept.at[i] for i in range(4))
    loads, stores = Loads(in_sems), Loads(out_sems)
    every = range(nt)
    load_chunk(loads, xs, x, 0, pn, rows, cols)
    load_weight(loads, info, "g", win.at[0, 0], wg, every, nt, cols)
    load_weight(loads, info, "u", win.at[0, 1], wu, every, nt, cols)
    for q in range(pn):
        loads.add(("t", q), xs[0][q].at[pl.ds(rows, TAIL)], tails.at[q])
    for g in range(1, CHUNKS):
        load_chunk(loads, xs, x, g, pn, rows, cols)
    load_weight(loads, info, "d", wout.at[0], wd, every, nt, cols)
    same = iota((rows, rows), 0) == iota((rows, rows), 1)
    tail_step = tail_lanes(rows)
    for b, units in enumerate(blocks(pn)):
        here = slice(b * len(units) * rows, (b + 1) * len(units) * rows)
        loads.need(*(("r", g, j, q) for j in every for g, q in units))
        loads.need(*(("g", j) for j in every))
        gate = dot_nt(x[here, :], wg[...])
        loads.need(*(("u", j) for j in every), *(("t", q) for q in range(pn)))
        up = dot_nt(x[here, :], wu[...])
        columns = []
        for g, q in units:
            row = tails[q, :, g * tail_step : g * tail_step + rows].astype(F32)[0:1, :]
            columns.append(jnp.sum(jnp.where(same, row, 0.0), axis=1, keepdims=True))
        weight = jnp.concatenate(columns, axis=0)
        sigma = 0.5 * jnp.tanh(0.5 * gate) + 0.5
        active = gate * sigma
        hidden = active * up
        scaled = (weight * hidden).astype(BF16)
        hs[here, :] = scaled
        hid[here, :] = hidden.astype(BF16)
        a1[here, :] = (weight * (up * sigma * (1.0 + gate * (1.0 - sigma)))).astype(BF16)
        a2[here, :] = (weight * active).astype(BF16)
        span = pl.ds(b * len(units) * rows, len(units) * rows)
        for i, result in enumerate(results):
            stores.add(("kept", b, i), kept.at[i, span], result.at[span])
        loads.need(*(("d", j) for j in every))
        part = dot_nn(scaled, wd[...]).astype(BF16)
        for j in reversed(every):
            w = (nt - j) % nt
            for u, (g, q) in enumerate(units):
                block = part[u * rows : (u + 1) * rows, w * cols : (w + 1) * cols]
                stage[j, q, g * rows : (g + 1) * rows, :] = block
                if g == CHUNKS - 1:
                    stores.add((j, q), stage.at[j, q], outs[j][q])
    loads.finish()
    stores.finish()


def backward_kernel(info, *refs, nt, pn, rows, cols):
    n = CHUNKS * pn
    cs, refs = by_core(refs, nt, n), refs[nt * n :]
    n_out = RETURNS * nt * pn
    (win, wout, hid, a1, a2), outs, refs = refs[:5], refs[5 : 5 + n_out], refs[5 + n_out :]
    outs = [by_core(outs[r * nt * pn :], nt, pn) for r in range(RETURNS)]
    half = CHUNKS * rows // RETURNS
    results, (c, h, b1, b2, wg, wu, wd, kept, stage, in_sems, out_sems) = refs[:2], refs[2:]
    gg, ug = kept.at[0], kept.at[1]
    loads, stores = Loads(in_sems), Loads(out_sems)
    every = range(nt)
    load_chunk(loads, cs, c, 0, pn, rows, cols)
    load_weight(loads, info, "d", wout.at[0], wd, every, nt, cols)
    for key, source, target in (("h", hid, h), ("1", a1, b1), ("2", a2, b2)):
        loads.add(key, source, target)
    load_weight(loads, info, "g", win.at[0, 0], wg, every, nt, cols)
    load_weight(loads, info, "u", win.at[0, 1], wu, every, nt, cols)
    for g in range(1, CHUNKS):
        load_chunk(loads, cs, c, g, pn, rows, cols)
    same = iota((rows, rows), 0) == iota((rows, rows), 1)
    tail_step = tail_lanes(rows)
    bottom = slice(CHUNKS * rows, CHUNKS * rows + TAIL)
    for b, units in enumerate(blocks(pn)):
        here = slice(b * len(units) * rows, (b + 1) * len(units) * rows)
        loads.need(*(("r", g, j, q) for j in every for g, q in units))
        loads.need(*(("d", j) for j in every))
        grad = dot_nt(c[here, :], wd[...])
        loads.need("h", "1", "2")
        piece = jnp.sum(grad * h[here, :].astype(F32), axis=1, keepdims=True)
        gate_grad = (grad * b1[here, :].astype(F32)).astype(BF16)
        up_grad = (grad * b2[here, :].astype(F32)).astype(BF16)
        gg[here, :] = gate_grad
        ug[here, :] = up_grad
        span = pl.ds(b * len(units) * rows, len(units) * rows)
        for i, result in enumerate(results):
            stores.add(("kept", b, i), kept.at[i, span], result.at[span])
        for u, (g, q) in enumerate(units):
            part = piece[u * rows : (u + 1) * rows, :]
            part = jnp.sum(jnp.where(same, part, 0.0), axis=0, keepdims=True)
            part = jnp.broadcast_to(part, (TAIL, rows)).astype(BF16)
            for j in every:
                if g == 0:
                    stage[j, q, bottom, :] = jnp.zeros((TAIL, cols), BF16)
                stage[j, q, bottom, g * tail_step : g * tail_step + rows] = part
        loads.need(*((k, j) for k in "gu" for j in every))
        part = (dot_nn(gate_grad, wg[...]) + dot_nn(up_grad, wu[...])).astype(BF16)
        for j in reversed(every):
            w = (nt - j) % nt
            for u, (g, q) in enumerate(units):
                block = part[u * rows : (u + 1) * rows, w * cols : (w + 1) * cols]
                stage[j, q, g * rows : (g + 1) * rows, :] = block
                for r in reversed(range(RETURNS if g == CHUNKS - 1 else 0)):
                    span = pl.ds(r * half, half + TAIL if r == RETURNS - 1 else half)
                    stores.add((j, q, r), stage.at[j, q, span], outs[r][j][q])
    loads.finish()
    stores.finish()


def weights_kernel(info, *refs, nt, pn, rows, cols):
    n = CHUNKS * pn
    xs, cs, refs = by_core(refs, nt, n), by_core(refs[nt * n :], nt, n), refs[2 * nt * n :]
    lefts, (gin, gout, left, right, stage, in_sems, out_sems) = refs[:3], refs[3:]
    loads, stores = Loads(in_sems), Loads(out_sems)
    order = ((0, 0, xs), (1, 0, xs), (2, 1, cs))
    for w, side, sources in order:
        loads.add(("l", w), lefts[w], left.at[w])
        if w == 1:
            continue
        for j in range(nt):
            for q in range(n):
                target = right.at[side, j, pl.ds(q * rows, rows)]
                loads.add((side, j, q), sources[j][q].at[pl.ds(0, rows)], target)
    for w, side, _ in order:
        loads.need(("l", w))
        for j in range(nt):
            loads.need(*((side, j, q) for q in range(n)))
            at = column_block(info, j, nt, cols)
            stage[j, w] = dot_tn(left[w], right[side, j]).astype(BF16)
            target = gout.at[0, :, at] if w == 2 else gin.at[0, w, :, at]
            stores.add((j, w), stage.at[j, w], target)
    loads.finish()
    stores.finish()


def after(value, *others):
    return lax.optimization_barrier((value, *others))[0]


def body(
    first_half,
    second_half,
    first_grad,
    second_grad,
    expert_ids,
    gate_weights,
    expert_in,
    expert_out,
):
    tokens, picks = expert_ids.shape
    groups = lax.axis_size("expert")
    nt = lax.axis_size("tensor")
    pn = PLANE
    zn = groups // pn
    cap = tokens * picks * 7 // (6 * groups)
    zc = zn // CHUNKS
    part_rows = zc * cap
    rows = CHUNKS * part_rows
    slots = pn * rows
    cols = first_half.shape[1]
    hid_n = expert_out.shape[1]
    me = lax.axis_index("expert")
    info = jnp.stack([(me // pn) * pn, me % pn, lax.axis_index("tensor"), me // pn]).astype(jnp.int32)

    def outer_send(value, s):
        if s % zn == 0:
            return value
        return lax.ppermute(
            value, "expert", [(e, ((e // pn + s) % zn) * pn + e % pn) for e in range(groups)]
        )

    def inner_send(value, q):
        if q == 0:
            return value
        return lax.ppermute(value, "expert", [(e, e ^ q) for e in range(groups)])

    def inner_exchange(pieces):
        return [inner_send(piece, q) for q, piece in enumerate(pieces)]

    def tensor_send(value, j):
        if j == 0:
            return value
        return lax.ppermute(value, "tensor", [(c, (c + j) % nt) for c in range(nt)])

    fixed = dict(zn=zn, pn=pn, tokens=tokens)

    own = jnp.concatenate(
        [
            jnp.pad(expert_ids.T.astype(F32), ((0, 8 - picks), (0, 0)), constant_values=-1.0),
            jnp.pad(gate_weights.T.astype(F32), ((0, 8 - picks), (0, 0))),
        ],
        axis=0,
    )
    columns = [[z * pn + q for z in range(zn)] for q in range(pn)]

    def outer_exchange(value):
        return lax.all_to_all(
            value,
            "expert",
            split_axis=0,
            concat_axis=0,
            axis_index_groups=columns,
            tiled=True,
        )

    def copies(value):
        return jnp.broadcast_to(value[None], (zn,) + value.shape)

    grad_copies = copies(second_grad)
    meta = outer_exchange(after(copies(own), grad_copies, info))
    dma = pltpu.SemaphoreType.DMA
    sizes = dict(nt=nt, pn=pn, rows=part_rows, cols=cols)

    def pack(gathered):
        return call(
            functools.partial(pack_kernel, **fixed, rows=part_rows),
            [shape(part_rows, cols)] * pn,
            [info, sels[0], gathered],
            [SMEM, VMEM, HBM],
            scratch=[pltpu.VMEM((zn * tokens, cols), BF16), dma((zn,))],
            name="pack",
        )

    def pack_gates(parts):
        return call(
            functools.partial(pack_gates_kernel, **fixed, picks=picks, rows=part_rows),
            [shape(part_rows + TAIL, cols)] * pn
            + [shape(pn * part_rows, zc * tokens)] * CHUNKS,
            [info, meta, *parts[:zc]],
            [SMEM, HBM] + [HBM] * zc,
            scratch=[pltpu.VMEM(meta.shape, F32), pltpu.VMEM((zc * tokens, cols), BF16)]
            + [dma((zc + 1,))],
            name="pack_gates",
        )

    zr = zn // RETURNS
    half = zr * cap

    def send_back(parts, first):
        return [outer_send(part, -(first + local)) for local, part in enumerate(parts)]

    def combine(backs):
        parts = call(
            functools.partial(combine_kernel, **fixed, rows=half),
            [shape(zn, tokens, cols)],
            [info, *chosen, *backs],
            [SMEM] + [VMEM] * RETURNS + [HBM] * pn,
            scratch=[pltpu.VMEM((RETURNS, pn * half, cols), BF16), dma((RETURNS * pn,))],
            name="combine",
        )
        return parts[0]

    def combine_far(backs):
        *parts, gates = call(
            functools.partial(combine_far_kernel, **fixed, rows=half),
            [shape(tokens + TAIL, cols)] * zr + [shape(TAIL, zn * tokens)],
            [info, meta, sels[0], chosen[RETURNS - 1], *backs],
            [SMEM] + [VMEM] * 3 + [HBM] * pn,
            scratch=[pltpu.VMEM((pn * half, cols), BF16), pltpu.VMEM((pn, TAIL, cols), BF16)]
            + [dma((2 * pn,))],
            name="combine_far",
        )
        return send_back(parts, zn - zr), gates

    def combine_near(gates, backs):
        parts = call(
            functools.partial(combine_near_kernel, pn=pn, tokens=tokens, rows=half),
            [shape(tokens + TAIL, cols)] * zr,
            [gates, chosen[0], *backs],
            [VMEM] * 2 + [HBM] * pn,
            scratch=[pltpu.VMEM((pn * half, cols), BF16), dma((pn,))],
            name="combine_near",
        )
        return send_back(parts, 0)

    def swapped(chunks):
        return [tensor_send(piece, j) for j in range(nt) for pieces in chunks for piece in pieces]

    def core_sum(arrays):
        sums = []
        for q in range(pn):
            total = sum(tensor_send(arrays[j * pn + q], j).astype(F32) for j in range(nt))
            sums.append(total.astype(BF16))
        return sums

    x_parts = [outer_send(first_half, s) for s in range(zn)]
    x_packed = pack_gates(x_parts)
    x_packed, sels = x_packed[:pn], x_packed[pn:]
    x_here = inner_exchange(x_packed)
    gathered = outer_exchange(after(grad_copies, *x_parts[1:]))
    chosen = call(
        functools.partial(route_kernel, **fixed, picks=picks, cap=cap),
        [shape(zr * tokens, pn * half)] * RETURNS,
        [info, after(meta, *x_packed)],
        [SMEM, VMEM],
        name="route",
    )
    c_packed = pack(after(gathered, *chosen))
    c_here = inner_exchange(c_packed)

    pieces = nt * CHUNKS * pn
    xs = swapped(([after(piece, *c_packed) for piece in x_here],))
    forward = call(
        functools.partial(forward_kernel, **sizes),
        [shape(rows, cols)] * (nt * pn) + [shape(slots, hid_n)] * 4,
        [after(info, *c_packed), *xs, expert_in, expert_out],
        [SMEM] + [HBM] * (pieces + 2),
        out_specs=[HBM] * (nt * pn + 4),
        scratch=[pltpu.VMEM((slots, nt * cols), BF16), pltpu.VMEM((pn, TAIL, cols), BF16)]
        + [pltpu.VMEM((hid_n, nt * cols), BF16)] * 3
        + [pltpu.VMEM((4, slots, hid_n), BF16)]
        + [pltpu.VMEM((nt, pn, rows, cols), BF16), dma((3 * nt + pieces + pn,))]
        + [dma((nt * pn + 4 * BLOCKS,))],
        name="expert_forward",
        limit=VMEM_LIMIT,
    )
    outs, (hs, hid, a1, a2) = forward[: nt * pn], forward[nt * pn :]
    cs = swapped(([after(piece, hid) for piece in c_here],))
    out_here = core_sum(outs)
    out_back = inner_exchange(out_here)

    backward = call(
        functools.partial(backward_kernel, **sizes),
        [
            shape(half + TAIL if r == RETURNS - 1 else half, cols)
            for r in range(RETURNS)
            for _ in range(nt * pn)
        ]
        + [shape(slots, hid_n)] * 2,
        [info, *cs, expert_in, expert_out, after(hid, *out_here), a1, a2],
        [SMEM] + [HBM] * (pieces + 5),
        out_specs=[HBM] * (RETURNS * nt * pn + 2),
        scratch=[pltpu.VMEM((slots, nt * cols), BF16)]
        + [pltpu.VMEM((slots, hid_n), BF16)] * 3
        + [pltpu.VMEM((hid_n, nt * cols), BF16)] * 3
        + [pltpu.VMEM((2, slots, hid_n), BF16)]
        + [pltpu.VMEM((nt, pn, rows + TAIL, cols), BF16), dma((3 * nt + pieces + 3,))]
        + [dma((RETURNS * nt * pn + 2 * BLOCKS,))],
        name="expert_backward",
        limit=VMEM_LIMIT,
    )
    grads, (gg, ug) = backward[: RETURNS * nt * pn], backward[RETURNS * nt * pn :]
    near, far = grads[: nt * pn], grads[nt * pn :]
    out_combined = combine(out_back)
    out_parts = outer_exchange(out_combined)
    far = [after(part, *out_back) for part in far]
    far_here = core_sum([after(part, out_combined) for part in far[:pn]] + far[pn:])
    far_back = inner_exchange(far_here)
    near_here = core_sum([after(part, far_back[pn - 1]) for part in near])
    near_back = inner_exchange(near_here)

    far_parts, gate_parts = combine_far([after(piece, *near_here) for piece in far_back])
    grad_parts = combine_near(gate_parts, near_back) + far_parts

    grad_in, grad_out = call(
        functools.partial(weights_kernel, **sizes),
        [shape(*expert_in.shape), shape(*expert_out.shape)],
        [after(info, grad_parts[0]), *xs, *cs, gg, ug, hs],
        [SMEM] + [HBM] * (2 * pieces + 3),
        out_specs=[HBM, HBM],
        scratch=[
            pltpu.VMEM((3, slots, hid_n), BF16),
            pltpu.VMEM((2, nt, slots, cols), BF16),
            pltpu.VMEM((nt, 3, hid_n, cols), BF16),
            dma((3 + 2 * pieces,)),
            dma((3 * nt,)),
        ],
        name="expert_weights",
        limit=VMEM_LIMIT,
    )

    branch = jnp.sum(after(out_parts, grad_in).astype(F32), axis=0)
    input_sum = sum(part[:tokens].astype(F32) for part in grad_parts)
    gate_sum = sum(part[tokens : tokens + picks, :tokens].astype(F32) for part in grad_parts)
    restored = (second_half.astype(F32) - branch).astype(BF16)
    carried_grad = (first_grad.astype(F32) + input_sum).astype(BF16)
    return (restored, carried_grad, gate_sum.T, grad_in, grad_out)


def solution(mesh):
    in_specs = (
        P("expert", "tensor"),
        P("expert", "tensor"),
        P("expert", "tensor"),
        P("expert", "tensor"),
        P("expert", None),
        P("expert", None),
        P("expert", None, "tensor", None),
        P("expert", "tensor", None),
    )
    out_specs = (
        P("expert", "tensor"),
        P("expert", "tensor"),
        P("expert", None),
        P("expert", None, "tensor", None),
        P("expert", "tensor", None),
    )
    return jax.shard_map(body, mesh=mesh, in_specs=in_specs, out_specs=out_specs, check_vma=False)
```

```python
import functools

import jax
import jax.numpy as jnp
from jax import lax
from jax.experimental import pallas as pl
from jax.experimental.pallas import tpu as pltpu
from jax.sharding import PartitionSpec as P

PLANE = 4
CHUNKS = 1
RETURNS = 2
BLOCKS = 2
TAIL = 16
VMEM_LIMIT = 56 * 1024 * 1024
SMALL_LIMIT = 16 * 1024 * 1024
F32 = jnp.float32
BF16 = jnp.bfloat16


def dot_nn(a, b):
    return lax.dot_general(a, b, (((1,), (0,)), ((), ())), preferred_element_type=F32)


def dot_nt(a, b):
    return lax.dot_general(a, b, (((1,), (1,)), ((), ())), preferred_element_type=F32)


def dot_tn(a, b):
    return lax.dot_general(a, b, (((0,), (0,)), ((), ())), preferred_element_type=F32)


def iota(shape, axis):
    return lax.broadcasted_iota(jnp.int32, shape, axis)


SMEM = pl.BlockSpec(memory_space=pltpu.SMEM)
VMEM = pl.BlockSpec(memory_space=pltpu.VMEM)
HBM = pl.BlockSpec(memory_space=pl.ANY)


def call(kernel, outs, args, specs, out_specs=None, scratch=(), name=None, limit=SMALL_LIMIT):
    return pl.pallas_call(
        kernel,
        out_shape=outs,
        in_specs=specs,
        out_specs=out_specs if out_specs is not None else [VMEM] * len(outs),
        scratch_shapes=list(scratch),
        compiler_params=pltpu.CompilerParams(vmem_limit_bytes=limit),
        cost_estimate=pl.CostEstimate(flops=1024, bytes_accessed=1024, transcendentals=0),
        name=name,
    )(*args)


def shape(*dims, dtype=BF16):
    return jax.ShapeDtypeStruct(dims, dtype)


def outer_meta(info, meta, s, zn):
    return meta[lax.rem(info[3] - s + zn, zn)]


def select(info, meta, sels, zn, pn, tokens, picks, rows):
    zc = zn // CHUNKS
    cap = rows // zc
    partner = iota((8, 1), 0)
    experts = jnp.where(partner < pn, info[0] + (partner ^ info[1]), -2).astype(F32)
    before = (iota((tokens, tokens), 0) < iota((tokens, tokens), 1)).astype(F32).astype(BF16)
    slot = iota((rows, tokens), 0).astype(F32)
    for s in range(zn):
        g, local = divmod(s, zc)
        ids = outer_meta(info, meta, s, zn)
        named = jnp.zeros((8, tokens), F32)
        for k in range(picks):
            named += (ids[k : k + 1, :] == experts).astype(F32)
        dest = dot_nn(named.astype(BF16), before) + local * cap
        dest = jnp.where(named > 0, dest, -1.0)
        for q in range(pn):
            sels[g][q * rows : (q + 1) * rows, local * tokens : (local + 1) * tokens] = (
                (slot == dest[q : q + 1, :]).astype(F32).astype(BF16)
            )


def route_kernel(info, meta, *chosen, zn, pn, tokens, picks, cap):
    zr = zn // RETURNS
    rows = zr * cap
    partner = iota((1, 8), 1)
    experts = jnp.where(partner < pn, info[0] + (partner ^ info[1]), -2).astype(F32)
    after = (iota((tokens, tokens), 1) < iota((tokens, tokens), 0)).astype(F32).astype(BF16)
    eye = (iota((16, 16), 0) == iota((16, 16), 1)).astype(F32).astype(BF16)
    lane = iota((tokens, pn * rows), 1).astype(F32)
    for s in range(zn):
        g, local = divmod(s, zr)
        columned = dot_tn(outer_meta(info, meta, s, zn).astype(BF16), eye)
        named = jnp.zeros((tokens, 8), F32)
        for k in range(picks):
            named += (columned[:, k : k + 1] == experts).astype(F32)
        dest = dot_nn(after, named.astype(BF16)) + local * cap
        dest = jnp.where(named > 0, dest + rows * partner.astype(F32), -1.0)
        picked = jnp.zeros((tokens, pn * rows), F32)
        for q in range(pn):
            picked += (lane == dest[:, q : q + 1]).astype(F32)
        chosen[g][local * tokens : (local + 1) * tokens, :] = picked.astype(BF16)


def tail_lanes(rows):
    return -(-rows // 128) * 128


class Loads:
    def __init__(self, sems):
        self.sems, self.copies, self.waited = sems, {}, set()

    def add(self, key, source, target):
        assert key not in self.copies
        self.copies[key] = pltpu.make_async_copy(source, target, self.sems.at[len(self.copies)])
        self.copies[key].start()

    def need(self, *keys):
        for key in keys:
            if key not in self.waited:
                self.waited.add(key)
                self.copies[key].wait()

    def finish(self):
        self.need(*self.copies)


def pack_kernel(info, sel, source, *refs, zn, pn, tokens, rows):
    outs, whole, sems = refs[:pn], refs[-2], refs[-1]
    loads = Loads(sems)
    for s in range(zn):
        place = lax.rem(info[3] - s + zn, zn)
        loads.add(s, source.at[place], whole.at[pl.ds(s * tokens, tokens)])
    loads.finish()
    for q in range(pn):
        outs[q][...] = dot_nn(sel[q * rows : (q + 1) * rows, :], whole[...]).astype(BF16)


def pack_gates_kernel(info, meta, *refs, zn, pn, tokens, picks, rows):
    zc = zn // CHUNKS
    sources, outs, refs = refs[:zc], refs[zc : zc + pn], refs[zc + pn :]
    sels, (whole, sems) = refs[:CHUNKS], refs[CHUNKS:]
    loads = Loads(sems)
    for s in range(zc):
        loads.add(s, sources[s], whole.at[pl.ds(s * tokens, tokens)])
    select(info, meta, sels, zn, pn, tokens, picks, rows)
    for q in range(pn):
        expert = (info[0] + (info[1] ^ q)).astype(F32)
        outs[q][rows : rows + TAIL, :] = jnp.zeros((TAIL, outs[q].shape[1]), BF16)
        for g in range(CHUNKS):
            tail = jnp.zeros((TAIL, rows), F32)
            for local in range(zc):
                known = outer_meta(info, meta, g * zc + local, zn)
                gate = jnp.zeros((1, tokens), F32)
                for k in range(picks):
                    gate += jnp.where(known[k : k + 1, :] == expert, known[8 + k : 9 + k, :], 0.0)
                gate = jnp.broadcast_to(gate, (TAIL, tokens)).astype(BF16)
                here = slice(local * tokens, (local + 1) * tokens)
                tail += dot_nt(gate, sels[g][q * rows : (q + 1) * rows, here])
            at = g * tail_lanes(rows)
            outs[q][rows : rows + TAIL, at : at + rows] = tail.astype(BF16)
    loads.finish()
    for q in range(pn):
        chosen = sels[0][q * rows : (q + 1) * rows, :]
        outs[q][0:rows, :] = dot_nn(chosen, whole[...]).astype(BF16)


def combine_kernel(info, *refs, zn, pn, tokens, rows):
    zr = zn // RETURNS
    chosen, backs = refs[:RETURNS], refs[RETURNS : RETURNS + pn]
    out, whole, sems = refs[RETURNS + pn :]
    loads = Loads(sems)
    for g in range(RETURNS):
        for q in range(pn):
            to = whole.at[g, pl.ds(q * rows, rows)]
            loads.add((g, q), backs[q].at[pl.ds(g * rows, rows)], to)
    for g in range(RETURNS):
        loads.need(*((g, q) for q in range(pn)))
        part = dot_nn(chosen[g][...], whole[g]).astype(BF16)
        for local in range(zr):
            place = lax.rem(info[3] - (g * zr + local) + zn, zn)
            out[place] = part[local * tokens : (local + 1) * tokens, :]


def combine_far_kernel(info, meta, sel, chosen, *refs, zn, pn, tokens, rows):
    zr, slots = zn // RETURNS, RETURNS * rows
    backs, outs, (gates, whole, tails, sems) = refs[:pn], refs[pn:-4], refs[-4:]
    loads = Loads(sems)
    for q in range(pn):
        loads.add(("t", q), backs[q].at[pl.ds(rows, TAIL)], tails.at[q])
        loads.add(q, backs[q].at[pl.ds(0, rows)], whole.at[pl.ds(q * rows, rows)])
    spreads = []
    for q in range(pn):
        loads.need(("t", q))
        spreads.append(dot_nn(tails[q, :, 0:slots], sel[q * slots : (q + 1) * slots, :])[0:8, :])
    for s in range(zn):
        ids = outer_meta(info, meta, s, zn)[0:8, :]
        total = jnp.zeros((8, tokens), F32)
        for q in range(pn):
            expert = (info[0] + (info[1] ^ q)).astype(F32)
            total += jnp.where(ids == expert, spreads[q][:, s * tokens : (s + 1) * tokens], 0.0)
        total = jnp.concatenate([total, jnp.zeros((TAIL - 8, tokens), F32)], axis=0)
        gates[:, s * tokens : (s + 1) * tokens] = total.astype(BF16)
    loads.finish()
    finish_combine(chosen, whole, gates, outs, zn - zr, tokens)


def combine_near_kernel(gates, chosen, *refs, pn, tokens, rows):
    backs, outs, (whole, sems) = refs[:pn], refs[pn:-2], refs[-2:]
    loads = Loads(sems)
    for q in range(pn):
        loads.add(q, backs[q], whole.at[pl.ds(q * rows, rows)])
    loads.finish()
    finish_combine(chosen, whole, gates, outs, 0, tokens)


def finish_combine(chosen, whole, gates, outs, first, tokens):
    part = dot_nn(chosen[...], whole[...]).astype(BF16)
    for local, out in enumerate(outs):
        at = first + local
        out[0:tokens, :] = part[local * tokens : (local + 1) * tokens, :]
        out[tokens : tokens + TAIL, :] = jnp.zeros((TAIL, part.shape[1]), BF16)
        out[tokens : tokens + TAIL, 0:tokens] = gates[:, at * tokens : (at + 1) * tokens]


def column_block(info, j, nt, cols):
    block = lax.rem(info[2] - j + nt, nt)
    return pl.ds(pl.multiple_of(block * cols, 128), cols)


def load_weight(loads, info, kind, source, target, blocks, nt, cols):
    for at, j in enumerate(blocks):
        block = source.at[:, column_block(info, j, nt, cols)]
        loads.add((kind, j), block, target.at[:, pl.ds(at * cols, cols)])


def by_core(refs, nt, pn):
    return [refs[j * pn : (j + 1) * pn] for j in range(nt)]


def load_chunk(loads, sources, target, g, pn, rows, cols):
    for j, pieces in enumerate(sources):
        for q in range(pn):
            to = target.at[pl.ds((g * pn + q) * rows, rows), pl.ds(j * cols, cols)]
            loads.add(("r", g, j, q), pieces[g * pn + q].at[pl.ds(0, rows)], to)


def blocks(pn):
    units = [(g, q) for g in range(CHUNKS) for q in range(pn)]
    size = len(units) // BLOCKS
    return [units[b * size : (b + 1) * size] for b in range(BLOCKS)]


def forward_kernel(info, *refs, nt, pn, rows, cols):
    n = CHUNKS * pn
    xs, refs = by_core(refs, nt, n), refs[nt * n :]
    (win, wout), outs, refs = refs[:2], by_core(refs[2:], nt, pn), refs[2 + nt * pn :]
    results, (x, tails, wg, wu, wd, kept, stage, in_sems, out_sems) = refs[:4], refs[4:]
    hs, hid, a1, a2 = (kept.at[i] for i in range(4))
    loads, stores = Loads(in_sems), Loads(out_sems)
    every = range(nt)
    load_chunk(loads, xs, x, 0, pn, rows, cols)
    load_weight(loads, info, "g", win.at[0, 0], wg, every, nt, cols)
    load_weight(loads, info, "u", win.at[0, 1], wu, every, nt, cols)
    for q in range(pn):
        loads.add(("t", q), xs[0][q].at[pl.ds(rows, TAIL)], tails.at[q])
    for g in range(1, CHUNKS):
        load_chunk(loads, xs, x, g, pn, rows, cols)
    load_weight(loads, info, "d", wout.at[0], wd, every, nt, cols)
    same = iota((rows, rows), 0) == iota((rows, rows), 1)
    tail_step = tail_lanes(rows)
    for b, units in enumerate(blocks(pn)):
        here = slice(b * len(units) * rows, (b + 1) * len(units) * rows)
        loads.need(*(("r", g, j, q) for j in every for g, q in units))
        loads.need(*(("g", j) for j in every))
        gate = dot_nt(x[here, :], wg[...])
        loads.need(*(("u", j) for j in every), *(("t", q) for q in range(pn)))
        up = dot_nt(x[here, :], wu[...])
        columns = []
        for g, q in units:
            row = tails[q, :, g * tail_step : g * tail_step + rows].astype(F32)[0:1, :]
            columns.append(jnp.sum(jnp.where(same, row, 0.0), axis=1, keepdims=True))
        weight = jnp.concatenate(columns, axis=0)
        sigma = 0.5 * jnp.tanh(0.5 * gate) + 0.5
        active = gate * sigma
        hidden = active * up
        scaled = (weight * hidden).astype(BF16)
        hs[here, :] = scaled
        hid[here, :] = hidden.astype(BF16)
        a1[here, :] = (weight * (up * sigma * (1.0 + gate * (1.0 - sigma)))).astype(BF16)
        a2[here, :] = (weight * active).astype(BF16)
        span = pl.ds(b * len(units) * rows, len(units) * rows)
        for i, result in enumerate(results):
            stores.add(("kept", b, i), kept.at[i, span], result.at[span])
        loads.need(*(("d", j) for j in every))
        part = dot_nn(scaled, wd[...]).astype(BF16)
        for j in reversed(every):
            w = (nt - j) % nt
            for u, (g, q) in enumerate(units):
                block = part[u * rows : (u + 1) * rows, w * cols : (w + 1) * cols]
                stage[j, q, g * rows : (g + 1) * rows, :] = block
                if g == CHUNKS - 1:
                    stores.add((j, q), stage.at[j, q], outs[j][q])
    loads.finish()
    stores.finish()


def backward_kernel(info, *refs, nt, pn, rows, cols):
    n = CHUNKS * pn
    cs, refs = by_core(refs, nt, n), refs[nt * n :]
    n_out = RETURNS * nt * pn
    (win, wout, hid, a1, a2), outs, refs = refs[:5], refs[5 : 5 + n_out], refs[5 + n_out :]
    outs = [by_core(outs[r * nt * pn :], nt, pn) for r in range(RETURNS)]
    half = CHUNKS * rows // RETURNS
    results, (c, h, b1, b2, wg, wu, wd, kept, stage, in_sems, out_sems) = refs[:2], refs[2:]
    gg, ug = kept.at[0], kept.at[1]
    loads, stores = Loads(in_sems), Loads(out_sems)
    every = range(nt)
    load_chunk(loads, cs, c, 0, pn, rows, cols)
    load_weight(loads, info, "d", wout.at[0], wd, every, nt, cols)
    for key, source, target in (("h", hid, h), ("1", a1, b1), ("2", a2, b2)):
        loads.add(key, source, target)
    load_weight(loads, info, "g", win.at[0, 0], wg, every, nt, cols)
    load_weight(loads, info, "u", win.at[0, 1], wu, every, nt, cols)
    for g in range(1, CHUNKS):
        load_chunk(loads, cs, c, g, pn, rows, cols)
    same = iota((rows, rows), 0) == iota((rows, rows), 1)
    tail_step = tail_lanes(rows)
    bottom = slice(CHUNKS * rows, CHUNKS * rows + TAIL)
    for b, units in enumerate(blocks(pn)):
        here = slice(b * len(units) * rows, (b + 1) * len(units) * rows)
        loads.need(*(("r", g, j, q) for j in every for g, q in units))
        loads.need(*(("d", j) for j in every))
        grad = dot_nt(c[here, :], wd[...])
        loads.need("h", "1", "2")
        piece = jnp.sum(grad * h[here, :].astype(F32), axis=1, keepdims=True)
        gate_grad = (grad * b1[here, :].astype(F32)).astype(BF16)
        up_grad = (grad * b2[here, :].astype(F32)).astype(BF16)
        gg[here, :] = gate_grad
        ug[here, :] = up_grad
        span = pl.ds(b * len(units) * rows, len(units) * rows)
        for i, result in enumerate(results):
            stores.add(("kept", b, i), kept.at[i, span], result.at[span])
        for u, (g, q) in enumerate(units):
            part = piece[u * rows : (u + 1) * rows, :]
            part = jnp.sum(jnp.where(same, part, 0.0), axis=0, keepdims=True)
            part = jnp.broadcast_to(part, (TAIL, rows)).astype(BF16)
            for j in every:
                if g == 0:
                    stage[j, q, bottom, :] = jnp.zeros((TAIL, cols), BF16)
                stage[j, q, bottom, g * tail_step : g * tail_step + rows] = part
        loads.need(*((k, j) for k in "gu" for j in every))
        part = (dot_nn(gate_grad, wg[...]) + dot_nn(up_grad, wu[...])).astype(BF16)
        for j in reversed(every):
            w = (nt - j) % nt
            for u, (g, q) in enumerate(units):
                block = part[u * rows : (u + 1) * rows, w * cols : (w + 1) * cols]
                stage[j, q, g * rows : (g + 1) * rows, :] = block
                for r in reversed(range(RETURNS if g == CHUNKS - 1 else 0)):
                    span = pl.ds(r * half, half + TAIL if r == RETURNS - 1 else half)
                    stores.add((j, q, r), stage.at[j, q, span], outs[r][j][q])
    loads.finish()
    stores.finish()


def weights_kernel(info, *refs, nt, pn, rows, cols):
    n = CHUNKS * pn
    xs, cs, refs = by_core(refs, nt, n), by_core(refs[nt * n :], nt, n), refs[2 * nt * n :]
    lefts, (gin, gout, left, right, stage, in_sems, out_sems) = refs[:3], refs[3:]
    loads, stores = Loads(in_sems), Loads(out_sems)
    order = ((0, 0, xs), (1, 0, xs), (2, 1, cs))
    for w, side, sources in order:
        loads.add(("l", w), lefts[w], left.at[w])
        if w == 1:
            continue
        for j in range(nt):
            for q in range(n):
                target = right.at[side, j, pl.ds(q * rows, rows)]
                loads.add((side, j, q), sources[j][q].at[pl.ds(0, rows)], target)
    for w, side, _ in order:
        loads.need(("l", w))
        for j in range(nt):
            loads.need(*((side, j, q) for q in range(n)))
            at = column_block(info, j, nt, cols)
            stage[j, w] = dot_tn(left[w], right[side, j]).astype(BF16)
            target = gout.at[0, :, at] if w == 2 else gin.at[0, w, :, at]
            stores.add((j, w), stage.at[j, w], target)
    loads.finish()
    stores.finish()


def after(value, *others):
    return lax.optimization_barrier((value, *others))[0]


def body(
    first_half,
    second_half,
    first_grad,
    second_grad,
    expert_ids,
    gate_weights,
    expert_in,
    expert_out,
):
    tokens, picks = expert_ids.shape
    groups = lax.axis_size("expert")
    nt = lax.axis_size("tensor")
    pn = PLANE
    zn = groups // pn
    cap = tokens * picks * 7 // (6 * groups)
    zc = zn // CHUNKS
    part_rows = zc * cap
    rows = CHUNKS * part_rows
    slots = pn * rows
    cols = first_half.shape[1]
    hid_n = expert_out.shape[1]
    me = lax.axis_index("expert")
    info = jnp.stack([(me // pn) * pn, me % pn, lax.axis_index("tensor"), me // pn]).astype(jnp.int32)

    def outer_send(value, s):
        if s % zn == 0:
            return value
        return lax.ppermute(
            value, "expert", [(e, ((e // pn + s) % zn) * pn + e % pn) for e in range(groups)]
        )

    def inner_send(value, q):
        if q == 0:
            return value
        return lax.ppermute(value, "expert", [(e, e ^ q) for e in range(groups)])

    def inner_exchange(pieces):
        return [inner_send(piece, q) for q, piece in enumerate(pieces)]

    def tensor_send(value, j):
        if j == 0:
            return value
        return lax.ppermute(value, "tensor", [(c, (c + j) % nt) for c in range(nt)])

    fixed = dict(zn=zn, pn=pn, tokens=tokens)

    own = jnp.concatenate(
        [
            jnp.pad(expert_ids.T.astype(F32), ((0, 8 - picks), (0, 0)), constant_values=-1.0),
            jnp.pad(gate_weights.T.astype(F32), ((0, 8 - picks), (0, 0))),
        ],
        axis=0,
    )
    columns = [[z * pn + q for z in range(zn)] for q in range(pn)]

    def outer_exchange(value):
        return lax.all_to_all(
            value,
            "expert",
            split_axis=0,
            concat_axis=0,
            axis_index_groups=columns,
            tiled=True,
        )

    def copies(value):
        return jnp.broadcast_to(value[None], (zn,) + value.shape)

    grad_copies = copies(second_grad)
    meta = outer_exchange(after(copies(own), grad_copies, info))
    dma = pltpu.SemaphoreType.DMA
    sizes = dict(nt=nt, pn=pn, rows=part_rows, cols=cols)

    def pack(gathered):
        return call(
            functools.partial(pack_kernel, **fixed, rows=part_rows),
            [shape(part_rows, cols)] * pn,
            [info, sels[0], gathered],
            [SMEM, VMEM, HBM],
            scratch=[pltpu.VMEM((zn * tokens, cols), BF16), dma((zn,))],
            name="pack",
        )

    def pack_gates(parts):
        return call(
            functools.partial(pack_gates_kernel, **fixed, picks=picks, rows=part_rows),
            [shape(part_rows + TAIL, cols)] * pn
            + [shape(pn * part_rows, zc * tokens)] * CHUNKS,
            [info, meta, *parts[:zc]],
            [SMEM, VMEM] + [HBM] * zc,
            scratch=[pltpu.VMEM((zc * tokens, cols), BF16), dma((zc,))],
            name="pack_gates",
        )

    zr = zn // RETURNS
    half = zr * cap

    def send_back(parts, first):
        return [outer_send(part, -(first + local)) for local, part in enumerate(parts)]

    def combine(backs):
        parts = call(
            functools.partial(combine_kernel, **fixed, rows=half),
            [shape(zn, tokens, cols)],
            [info, *chosen, *backs],
            [SMEM] + [VMEM] * RETURNS + [HBM] * pn,
            scratch=[pltpu.VMEM((RETURNS, pn * half, cols), BF16), dma((RETURNS * pn,))],
            name="combine",
        )
        return parts[0]

    def combine_far(backs):
        *parts, gates = call(
            functools.partial(combine_far_kernel, **fixed, rows=half),
            [shape(tokens + TAIL, cols)] * zr + [shape(TAIL, zn * tokens)],
            [info, meta, sels[0], chosen[RETURNS - 1], *backs],
            [SMEM] + [VMEM] * 3 + [HBM] * pn,
            scratch=[pltpu.VMEM((pn * half, cols), BF16), pltpu.VMEM((pn, TAIL, cols), BF16)]
            + [dma((2 * pn,))],
            name="combine_far",
        )
        return send_back(parts, zn - zr), gates

    def combine_near(gates, backs):
        parts = call(
            functools.partial(combine_near_kernel, pn=pn, tokens=tokens, rows=half),
            [shape(tokens + TAIL, cols)] * zr,
            [gates, chosen[0], *backs],
            [VMEM] * 2 + [HBM] * pn,
            scratch=[pltpu.VMEM((pn * half, cols), BF16), dma((pn,))],
            name="combine_near",
        )
        return send_back(parts, 0)

    def swapped(chunks):
        return [tensor_send(piece, j) for j in range(nt) for pieces in chunks for piece in pieces]

    def core_sum(arrays):
        sums = []
        for q in range(pn):
            total = sum(tensor_send(arrays[j * pn + q], j).astype(F32) for j in range(nt))
            sums.append(total.astype(BF16))
        return sums

    x_parts = [outer_send(first_half, s) for s in range(zn)]
    x_packed = pack_gates(x_parts)
    x_packed, sels = x_packed[:pn], x_packed[pn:]
    x_here = inner_exchange(x_packed)
    gathered = outer_exchange(after(grad_copies, *x_parts[1:]))
    chosen = call(
        functools.partial(route_kernel, **fixed, picks=picks, cap=cap),
        [shape(zr * tokens, pn * half)] * RETURNS,
        [info, after(meta, *x_packed)],
        [SMEM, VMEM],
        name="route",
    )
    c_packed = pack(after(gathered, *chosen))
    c_here = inner_exchange(c_packed)

    pieces = nt * CHUNKS * pn
    xs = swapped(([after(piece, *c_packed) for piece in x_here],))
    forward = call(
        functools.partial(forward_kernel, **sizes),
        [shape(rows, cols)] * (nt * pn) + [shape(slots, hid_n)] * 4,
        [after(info, *c_packed), *xs, expert_in, expert_out],
        [SMEM] + [HBM] * (pieces + 2),
        out_specs=[HBM] * (nt * pn + 4),
        scratch=[pltpu.VMEM((slots, nt * cols), BF16), pltpu.VMEM((pn, TAIL, cols), BF16)]
        + [pltpu.VMEM((hid_n, nt * cols), BF16)] * 3
        + [pltpu.VMEM((4, slots, hid_n), BF16)]
        + [pltpu.VMEM((nt, pn, rows, cols), BF16), dma((3 * nt + pieces + pn,))]
        + [dma((nt * pn + 4 * BLOCKS,))],
        name="expert_forward",
        limit=VMEM_LIMIT,
    )
    outs, (hs, hid, a1, a2) = forward[: nt * pn], forward[nt * pn :]
    cs = swapped(([after(piece, hid) for piece in c_here],))
    out_here = core_sum(outs)
    out_back = inner_exchange(out_here)

    backward = call(
        functools.partial(backward_kernel, **sizes),
        [
            shape(half + TAIL if r == RETURNS - 1 else half, cols)
            for r in range(RETURNS)
            for _ in range(nt * pn)
        ]
        + [shape(slots, hid_n)] * 2,
        [info, *cs, expert_in, expert_out, after(hid, *out_here), a1, a2],
        [SMEM] + [HBM] * (pieces + 5),
        out_specs=[HBM] * (RETURNS * nt * pn + 2),
        scratch=[pltpu.VMEM((slots, nt * cols), BF16)]
        + [pltpu.VMEM((slots, hid_n), BF16)] * 3
        + [pltpu.VMEM((hid_n, nt * cols), BF16)] * 3
        + [pltpu.VMEM((2, slots, hid_n), BF16)]
        + [pltpu.VMEM((nt, pn, rows + TAIL, cols), BF16), dma((3 * nt + pieces + 3,))]
        + [dma((RETURNS * nt * pn + 2 * BLOCKS,))],
        name="expert_backward",
        limit=VMEM_LIMIT,
    )
    grads, (gg, ug) = backward[: RETURNS * nt * pn], backward[RETURNS * nt * pn :]
    near, far = grads[: nt * pn], grads[nt * pn :]
    out_combined = combine(out_back)
    out_parts = outer_exchange(out_combined)
    far = [after(part, *out_back) for part in far]
    far_here = core_sum([after(part, out_combined) for part in far[:pn]] + far[pn:])
    far_back = inner_exchange(far_here)
    near_here = core_sum([after(part, far_back[pn - 1]) for part in near])
    near_back = inner_exchange(near_here)

    far_parts, gate_parts = combine_far([after(piece, *near_here) for piece in far_back])
    grad_parts = combine_near(gate_parts, near_back) + far_parts

    grad_in, grad_out = call(
        functools.partial(weights_kernel, **sizes),
        [shape(*expert_in.shape), shape(*expert_out.shape)],
        [after(info, grad_parts[0]), *xs, *cs, gg, ug, hs],
        [SMEM] + [HBM] * (2 * pieces + 3),
        out_specs=[HBM, HBM],
        scratch=[
            pltpu.VMEM((3, slots, hid_n), BF16),
            pltpu.VMEM((2, nt, slots, cols), BF16),
            pltpu.VMEM((nt, 3, hid_n, cols), BF16),
            dma((3 + 2 * pieces,)),
            dma((3 * nt,)),
        ],
        name="expert_weights",
        limit=VMEM_LIMIT,
    )

    branch = jnp.sum(after(out_parts, grad_in).astype(F32), axis=0)
    input_sum = sum(part[:tokens].astype(F32) for part in grad_parts)
    gate_sum = sum(part[tokens : tokens + picks, :tokens].astype(F32) for part in grad_parts)
    restored = (second_half.astype(F32) - branch).astype(BF16)
    carried_grad = (first_grad.astype(F32) + input_sum).astype(BF16)
    return (restored, carried_grad, gate_sum.T, grad_in, grad_out)


def solution(mesh):
    in_specs = (
        P("expert", "tensor"),
        P("expert", "tensor"),
        P("expert", "tensor"),
        P("expert", "tensor"),
        P("expert", None),
        P("expert", None),
        P("expert", None, "tensor", None),
        P("expert", "tensor", None),
    )
    out_specs = (
        P("expert", "tensor"),
        P("expert", "tensor"),
        P("expert", None),
        P("expert", None, "tensor", None),
        P("expert", "tensor", None),
    )
    return jax.shard_map(body, mesh=mesh, in_specs=in_specs, out_specs=out_specs, check_vma=False)
```

```python
import functools

import jax
import jax.numpy as jnp
from jax import lax
from jax.experimental import pallas as pl
from jax.experimental.pallas import tpu as pltpu
from jax.sharding import PartitionSpec as P

PLANE = 4
CHUNKS = 1
RETURNS = 2
BLOCKS = 4
TAIL = 16
VMEM_LIMIT = 56 * 1024 * 1024
SMALL_LIMIT = 16 * 1024 * 1024
F32 = jnp.float32
BF16 = jnp.bfloat16


def dot_nn(a, b):
    return lax.dot_general(a, b, (((1,), (0,)), ((), ())), preferred_element_type=F32)


def dot_nt(a, b):
    return lax.dot_general(a, b, (((1,), (1,)), ((), ())), preferred_element_type=F32)


def dot_tn(a, b):
    return lax.dot_general(a, b, (((0,), (0,)), ((), ())), preferred_element_type=F32)


def iota(shape, axis):
    return lax.broadcasted_iota(jnp.int32, shape, axis)


SMEM = pl.BlockSpec(memory_space=pltpu.SMEM)
VMEM = pl.BlockSpec(memory_space=pltpu.VMEM)
HBM = pl.BlockSpec(memory_space=pl.ANY)


def call(kernel, outs, args, specs, out_specs=None, scratch=(), name=None, limit=SMALL_LIMIT):
    return pl.pallas_call(
        kernel,
        out_shape=outs,
        in_specs=specs,
        out_specs=out_specs if out_specs is not None else [VMEM] * len(outs),
        scratch_shapes=list(scratch),
        compiler_params=pltpu.CompilerParams(vmem_limit_bytes=limit),
        cost_estimate=pl.CostEstimate(flops=1024, bytes_accessed=1024, transcendentals=0),
        name=name,
    )(*args)


def shape(*dims, dtype=BF16):
    return jax.ShapeDtypeStruct(dims, dtype)


def outer_meta(info, meta, s, zn):
    return meta[lax.rem(info[3] - s + zn, zn)]


def select(info, meta, sels, zn, pn, tokens, picks, rows):
    zc = zn // CHUNKS
    cap = rows // zc
    partner = iota((8, 1), 0)
    experts = jnp.where(partner < pn, info[0] + (partner ^ info[1]), -2).astype(F32)
    before = (iota((tokens, tokens), 0) < iota((tokens, tokens), 1)).astype(F32).astype(BF16)
    slot = iota((rows, tokens), 0).astype(F32)
    for s in range(zn):
        g, local = divmod(s, zc)
        ids = outer_meta(info, meta, s, zn)
        named = jnp.zeros((8, tokens), F32)
        for k in range(picks):
            named += (ids[k : k + 1, :] == experts).astype(F32)
        dest = dot_nn(named.astype(BF16), before) + local * cap
        dest = jnp.where(named > 0, dest, -1.0)
        for q in range(pn):
            sels[g][q * rows : (q + 1) * rows, local * tokens : (local + 1) * tokens] = (
                (slot == dest[q : q + 1, :]).astype(F32).astype(BF16)
            )


def route_kernel(info, meta, *chosen, zn, pn, tokens, picks, cap):
    zr = zn // RETURNS
    rows = zr * cap
    partner = iota((1, 8), 1)
    experts = jnp.where(partner < pn, info[0] + (partner ^ info[1]), -2).astype(F32)
    after = (iota((tokens, tokens), 1) < iota((tokens, tokens), 0)).astype(F32).astype(BF16)
    eye = (iota((16, 16), 0) == iota((16, 16), 1)).astype(F32).astype(BF16)
    lane = iota((tokens, pn * rows), 1).astype(F32)
    for s in range(zn):
        g, local = divmod(s, zr)
        columned = dot_tn(outer_meta(info, meta, s, zn).astype(BF16), eye)
        named = jnp.zeros((tokens, 8), F32)
        for k in range(picks):
            named += (columned[:, k : k + 1] == experts).astype(F32)
        dest = dot_nn(after, named.astype(BF16)) + local * cap
        dest = jnp.where(named > 0, dest + rows * partner.astype(F32), -1.0)
        picked = jnp.zeros((tokens, pn * rows), F32)
        for q in range(pn):
            picked += (lane == dest[:, q : q + 1]).astype(F32)
        chosen[g][local * tokens : (local + 1) * tokens, :] = picked.astype(BF16)


def tail_lanes(rows):
    return -(-rows // 128) * 128


class Loads:
    def __init__(self, sems):
        self.sems, self.copies, self.waited = sems, {}, set()

    def add(self, key, source, target):
        assert key not in self.copies
        self.copies[key] = pltpu.make_async_copy(source, target, self.sems.at[len(self.copies)])
        self.copies[key].start()

    def need(self, *keys):
        for key in keys:
            if key not in self.waited:
                self.waited.add(key)
                self.copies[key].wait()

    def finish(self):
        self.need(*self.copies)


def pack_kernel(info, sel, source, *refs, zn, pn, tokens, rows):
    outs, whole, sems = refs[:pn], refs[-2], refs[-1]
    loads = Loads(sems)
    for s in range(zn):
        place = lax.rem(info[3] - s + zn, zn)
        loads.add(s, source.at[place], whole.at[pl.ds(s * tokens, tokens)])
    loads.finish()
    for q in range(pn):
        outs[q][...] = dot_nn(sel[q * rows : (q + 1) * rows, :], whole[...]).astype(BF16)


def pack_gates_kernel(info, meta, *refs, zn, pn, tokens, picks, rows):
    zc = zn // CHUNKS
    sources, outs, refs = refs[:zc], refs[zc : zc + pn], refs[zc + pn :]
    sels, (whole, sems) = refs[:CHUNKS], refs[CHUNKS:]
    loads = Loads(sems)
    for s in range(zc):
        loads.add(s, sources[s], whole.at[pl.ds(s * tokens, tokens)])
    select(info, meta, sels, zn, pn, tokens, picks, rows)
    for q in range(pn):
        expert = (info[0] + (info[1] ^ q)).astype(F32)
        outs[q][rows : rows + TAIL, :] = jnp.zeros((TAIL, outs[q].shape[1]), BF16)
        for g in range(CHUNKS):
            tail = jnp.zeros((TAIL, rows), F32)
            for local in range(zc):
                known = outer_meta(info, meta, g * zc + local, zn)
                gate = jnp.zeros((1, tokens), F32)
                for k in range(picks):
                    gate += jnp.where(known[k : k + 1, :] == expert, known[8 + k : 9 + k, :], 0.0)
                gate = jnp.broadcast_to(gate, (TAIL, tokens)).astype(BF16)
                here = slice(local * tokens, (local + 1) * tokens)
                tail += dot_nt(gate, sels[g][q * rows : (q + 1) * rows, here])
            at = g * tail_lanes(rows)
            outs[q][rows : rows + TAIL, at : at + rows] = tail.astype(BF16)
    loads.finish()
    for q in range(pn):
        chosen = sels[0][q * rows : (q + 1) * rows, :]
        outs[q][0:rows, :] = dot_nn(chosen, whole[...]).astype(BF16)


def combine_kernel(info, *refs, zn, pn, tokens, rows):
    zr = zn // RETURNS
    chosen, backs = refs[:RETURNS], refs[RETURNS : RETURNS + pn]
    out, whole, sems = refs[RETURNS + pn :]
    loads = Loads(sems)
    for g in range(RETURNS):
        for q in range(pn):
            to = whole.at[g, pl.ds(q * rows, rows)]
            loads.add((g, q), backs[q].at[pl.ds(g * rows, rows)], to)
    for g in range(RETURNS):
        loads.need(*((g, q) for q in range(pn)))
        part = dot_nn(chosen[g][...], whole[g]).astype(BF16)
        for local in range(zr):
            place = lax.rem(info[3] - (g * zr + local) + zn, zn)
            out[place] = part[local * tokens : (local + 1) * tokens, :]


def combine_far_kernel(info, meta, sel, chosen, *refs, zn, pn, tokens, rows):
    zr, slots = zn // RETURNS, RETURNS * rows
    backs, outs, (gates, whole, tails, sems) = refs[:pn], refs[pn:-4], refs[-4:]
    loads = Loads(sems)
    for q in range(pn):
        loads.add(("t", q), backs[q].at[pl.ds(rows, TAIL)], tails.at[q])
        loads.add(q, backs[q].at[pl.ds(0, rows)], whole.at[pl.ds(q * rows, rows)])
    spreads = []
    for q in range(pn):
        loads.need(("t", q))
        spreads.append(dot_nn(tails[q, :, 0:slots], sel[q * slots : (q + 1) * slots, :])[0:8, :])
    for s in range(zn):
        ids = outer_meta(info, meta, s, zn)[0:8, :]
        total = jnp.zeros((8, tokens), F32)
        for q in range(pn):
            expert = (info[0] + (info[1] ^ q)).astype(F32)
            total += jnp.where(ids == expert, spreads[q][:, s * tokens : (s + 1) * tokens], 0.0)
        total = jnp.concatenate([total, jnp.zeros((TAIL - 8, tokens), F32)], axis=0)
        gates[:, s * tokens : (s + 1) * tokens] = total.astype(BF16)
    loads.finish()
    finish_combine(chosen, whole, gates, outs, zn - zr, tokens)


def combine_near_kernel(gates, chosen, *refs, pn, tokens, rows):
    backs, outs, (whole, sems) = refs[:pn], refs[pn:-2], refs[-2:]
    loads = Loads(sems)
    for q in range(pn):
        loads.add(q, backs[q], whole.at[pl.ds(q * rows, rows)])
    loads.finish()
    finish_combine(chosen, whole, gates, outs, 0, tokens)


def finish_combine(chosen, whole, gates, outs, first, tokens):
    part = dot_nn(chosen[...], whole[...]).astype(BF16)
    for local, out in enumerate(outs):
        at = first + local
        out[0:tokens, :] = part[local * tokens : (local + 1) * tokens, :]
        out[tokens : tokens + TAIL, :] = jnp.zeros((TAIL, part.shape[1]), BF16)
        out[tokens : tokens + TAIL, 0:tokens] = gates[:, at * tokens : (at + 1) * tokens]


def column_block(info, j, nt, cols):
    block = lax.rem(info[2] - j + nt, nt)
    return pl.ds(pl.multiple_of(block * cols, 128), cols)


def load_weight(loads, info, kind, source, target, blocks, nt, cols):
    for at, j in enumerate(blocks):
        block = source.at[:, column_block(info, j, nt, cols)]
        loads.add((kind, j), block, target.at[:, pl.ds(at * cols, cols)])


def by_core(refs, nt, pn):
    return [refs[j * pn : (j + 1) * pn] for j in range(nt)]


def load_chunk(loads, sources, target, g, pn, rows, cols):
    for j, pieces in enumerate(sources):
        for q in range(pn):
            to = target.at[pl.ds((g * pn + q) * rows, rows), pl.ds(j * cols, cols)]
            loads.add(("r", g, j, q), pieces[g * pn + q].at[pl.ds(0, rows)], to)


def blocks(pn):
    units = [(g, q) for g in range(CHUNKS) for q in range(pn)]
    size = len(units) // BLOCKS
    return [units[b * size : (b + 1) * size] for b in range(BLOCKS)]


def forward_kernel(info, *refs, nt, pn, rows, cols):
    n = CHUNKS * pn
    xs, refs = by_core(refs, nt, n), refs[nt * n :]
    (win, wout), outs, refs = refs[:2], by_core(refs[2:], nt, pn), refs[2 + nt * pn :]
    results, (x, tails, wg, wu, wd, kept, stage, in_sems, out_sems) = refs[:4], refs[4:]
    hs, hid, a1, a2 = (kept.at[i] for i in range(4))
    loads, stores = Loads(in_sems), Loads(out_sems)
    every = range(nt)
    load_chunk(loads, xs, x, 0, pn, rows, cols)
    load_weight(loads, info, "g", win.at[0, 0], wg, every, nt, cols)
    load_weight(loads, info, "u", win.at[0, 1], wu, every, nt, cols)
    for q in range(pn):
        loads.add(("t", q), xs[0][q].at[pl.ds(rows, TAIL)], tails.at[q])
    for g in range(1, CHUNKS):
        load_chunk(loads, xs, x, g, pn, rows, cols)
    load_weight(loads, info, "d", wout.at[0], wd, every, nt, cols)
    same = iota((rows, rows), 0) == iota((rows, rows), 1)
    tail_step = tail_lanes(rows)
    for b, units in enumerate(blocks(pn)):
        here = slice(b * len(units) * rows, (b + 1) * len(units) * rows)
        loads.need(*(("r", g, j, q) for j in every for g, q in units))
        loads.need(*(("g", j) for j in every))
        gate = dot_nt(x[here, :], wg[...])
        loads.need(*(("u", j) for j in every), *(("t", q) for q in range(pn)))
        up = dot_nt(x[here, :], wu[...])
        columns = []
        for g, q in units:
            row = tails[q, :, g * tail_step : g * tail_step + rows].astype(F32)[0:1, :]
            columns.append(jnp.sum(jnp.where(same, row, 0.0), axis=1, keepdims=True))
        weight = jnp.concatenate(columns, axis=0)
        sigma = 0.5 * jnp.tanh(0.5 * gate) + 0.5
        active = gate * sigma
        hidden = active * up
        scaled = (weight * hidden).astype(BF16)
        hs[here, :] = scaled
        hid[here, :] = hidden.astype(BF16)
        a1[here, :] = (weight * (up * sigma * (1.0 + gate * (1.0 - sigma)))).astype(BF16)
        a2[here, :] = (weight * active).astype(BF16)
        span = pl.ds(b * len(units) * rows, len(units) * rows)
        for i, result in enumerate(results):
            stores.add(("kept", b, i), kept.at[i, span], result.at[span])
        loads.need(*(("d", j) for j in every))
        part = dot_nn(scaled, wd[...]).astype(BF16)
        for j in reversed(every):
            w = (nt - j) % nt
            for u, (g, q) in enumerate(units):
                block = part[u * rows : (u + 1) * rows, w * cols : (w + 1) * cols]
                stage[j, q, g * rows : (g + 1) * rows, :] = block
                if g == CHUNKS - 1:
                    stores.add((j, q), stage.at[j, q], outs[j][q])
    loads.finish()
    stores.finish()


def backward_kernel(info, *refs, nt, pn, rows, cols):
    n = CHUNKS * pn
    cs, refs = by_core(refs, nt, n), refs[nt * n :]
    n_out = RETURNS * nt * pn
    (win, wout, hid, a1, a2), outs, refs = refs[:5], refs[5 : 5 + n_out], refs[5 + n_out :]
    outs = [by_core(outs[r * nt * pn :], nt, pn) for r in range(RETURNS)]
    half = CHUNKS * rows // RETURNS
    results, (c, h, b1, b2, wg, wu, wd, kept, stage, in_sems, out_sems) = refs[:2], refs[2:]
    gg, ug = kept.at[0], kept.at[1]
    loads, stores = Loads(in_sems), Loads(out_sems)
    every = range(nt)
    load_chunk(loads, cs, c, 0, pn, rows, cols)
    load_weight(loads, info, "d", wout.at[0], wd, every, nt, cols)
    for key, source, target in (("h", hid, h), ("1", a1, b1), ("2", a2, b2)):
        loads.add(key, source, target)
    load_weight(loads, info, "g", win.at[0, 0], wg, every, nt, cols)
    load_weight(loads, info, "u", win.at[0, 1], wu, every, nt, cols)
    for g in range(1, CHUNKS):
        load_chunk(loads, cs, c, g, pn, rows, cols)
    same = iota((rows, rows), 0) == iota((rows, rows), 1)
    tail_step = tail_lanes(rows)
    bottom = slice(CHUNKS * rows, CHUNKS * rows + TAIL)
    for b, units in enumerate(blocks(pn)):
        here = slice(b * len(units) * rows, (b + 1) * len(units) * rows)
        loads.need(*(("r", g, j, q) for j in every for g, q in units))
        loads.need(*(("d", j) for j in every))
        grad = dot_nt(c[here, :], wd[...])
        loads.need("h", "1", "2")
        piece = jnp.sum(grad * h[here, :].astype(F32), axis=1, keepdims=True)
        gate_grad = (grad * b1[here, :].astype(F32)).astype(BF16)
        up_grad = (grad * b2[here, :].astype(F32)).astype(BF16)
        gg[here, :] = gate_grad
        ug[here, :] = up_grad
        span = pl.ds(b * len(units) * rows, len(units) * rows)
        for i, result in enumerate(results):
            stores.add(("kept", b, i), kept.at[i, span], result.at[span])
        for u, (g, q) in enumerate(units):
            part = piece[u * rows : (u + 1) * rows, :]
            part = jnp.sum(jnp.where(same, part, 0.0), axis=0, keepdims=True)
            part = jnp.broadcast_to(part, (TAIL, rows)).astype(BF16)
            for j in every:
                if g == 0:
                    stage[j, q, bottom, :] = jnp.zeros((TAIL, cols), BF16)
                stage[j, q, bottom, g * tail_step : g * tail_step + rows] = part
        loads.need(*((k, j) for k in "gu" for j in every))
        part = (dot_nn(gate_grad, wg[...]) + dot_nn(up_grad, wu[...])).astype(BF16)
        for j in reversed(every):
            w = (nt - j) % nt
            for u, (g, q) in enumerate(units):
                block = part[u * rows : (u + 1) * rows, w * cols : (w + 1) * cols]
                stage[j, q, g * rows : (g + 1) * rows, :] = block
                for r in reversed(range(RETURNS if g == CHUNKS - 1 else 0)):
                    span = pl.ds(r * half, half + TAIL if r == RETURNS - 1 else half)
                    stores.add((j, q, r), stage.at[j, q, span], outs[r][j][q])
    loads.finish()
    stores.finish()


def weights_kernel(info, *refs, nt, pn, rows, cols):
    n = CHUNKS * pn
    xs, cs, refs = by_core(refs, nt, n), by_core(refs[nt * n :], nt, n), refs[2 * nt * n :]
    lefts, (gin, gout, left, right, stage, in_sems, out_sems) = refs[:3], refs[3:]
    loads, stores = Loads(in_sems), Loads(out_sems)
    order = ((0, 0, xs), (1, 0, xs), (2, 1, cs))
    for w, side, sources in order:
        loads.add(("l", w), lefts[w], left.at[w])
        if w == 1:
            continue
        for j in range(nt):
            for q in range(n):
                target = right.at[side, j, pl.ds(q * rows, rows)]
                loads.add((side, j, q), sources[j][q].at[pl.ds(0, rows)], target)
    for w, side, _ in order:
        loads.need(("l", w))
        for j in range(nt):
            loads.need(*((side, j, q) for q in range(n)))
            at = column_block(info, j, nt, cols)
            stage[j, w] = dot_tn(left[w], right[side, j]).astype(BF16)
            target = gout.at[0, :, at] if w == 2 else gin.at[0, w, :, at]
            stores.add((j, w), stage.at[j, w], target)
    loads.finish()
    stores.finish()


def after(value, *others):
    return lax.optimization_barrier((value, *others))[0]


def body(
    first_half,
    second_half,
    first_grad,
    second_grad,
    expert_ids,
    gate_weights,
    expert_in,
    expert_out,
):
    tokens, picks = expert_ids.shape
    groups = lax.axis_size("expert")
    nt = lax.axis_size("tensor")
    pn = PLANE
    zn = groups // pn
    cap = tokens * picks * 7 // (6 * groups)
    zc = zn // CHUNKS
    part_rows = zc * cap
    rows = CHUNKS * part_rows
    slots = pn * rows
    cols = first_half.shape[1]
    hid_n = expert_out.shape[1]
    me = lax.axis_index("expert")
    info = jnp.stack([(me // pn) * pn, me % pn, lax.axis_index("tensor"), me // pn]).astype(jnp.int32)

    def outer_send(value, s):
        if s % zn == 0:
            return value
        return lax.ppermute(
            value, "expert", [(e, ((e // pn + s) % zn) * pn + e % pn) for e in range(groups)]
        )

    def inner_send(value, q):
        if q == 0:
            return value
        return lax.ppermute(value, "expert", [(e, e ^ q) for e in range(groups)])

    def inner_exchange(pieces):
        return [inner_send(piece, q) for q, piece in enumerate(pieces)]

    def tensor_send(value, j):
        if j == 0:
            return value
        return lax.ppermute(value, "tensor", [(c, (c + j) % nt) for c in range(nt)])

    fixed = dict(zn=zn, pn=pn, tokens=tokens)

    own = jnp.concatenate(
        [
            jnp.pad(expert_ids.T.astype(F32), ((0, 8 - picks), (0, 0)), constant_values=-1.0),
            jnp.pad(gate_weights.T.astype(F32), ((0, 8 - picks), (0, 0))),
        ],
        axis=0,
    )
    columns = [[z * pn + q for z in range(zn)] for q in range(pn)]

    def outer_exchange(value):
        return lax.all_to_all(
            value,
            "expert",
            split_axis=0,
            concat_axis=0,
            axis_index_groups=columns,
            tiled=True,
        )

    def copies(value):
        return jnp.broadcast_to(value[None], (zn,) + value.shape)

    grad_copies = copies(second_grad)
    meta = outer_exchange(after(copies(own), grad_copies, info))
    dma = pltpu.SemaphoreType.DMA
    sizes = dict(nt=nt, pn=pn, rows=part_rows, cols=cols)

    def pack(gathered):
        return call(
            functools.partial(pack_kernel, **fixed, rows=part_rows),
            [shape(part_rows, cols)] * pn,
            [info, sels[0], gathered],
            [SMEM, VMEM, HBM],
            scratch=[pltpu.VMEM((zn * tokens, cols), BF16), dma((zn,))],
            name="pack",
        )

    def pack_gates(parts):
        return call(
            functools.partial(pack_gates_kernel, **fixed, picks=picks, rows=part_rows),
            [shape(part_rows + TAIL, cols)] * pn
            + [shape(pn * part_rows, zc * tokens)] * CHUNKS,
            [info, meta, *parts[:zc]],
            [SMEM, VMEM] + [HBM] * zc,
            scratch=[pltpu.VMEM((zc * tokens, cols), BF16), dma((zc,))],
            name="pack_gates",
        )

    zr = zn // RETURNS
    half = zr * cap

    def send_back(parts, first):
        return [outer_send(part, -(first + local)) for local, part in enumerate(parts)]

    def combine(backs):
        parts = call(
            functools.partial(combine_kernel, **fixed, rows=half),
            [shape(zn, tokens, cols)],
            [info, *chosen, *backs],
            [SMEM] + [VMEM] * RETURNS + [HBM] * pn,
            scratch=[pltpu.VMEM((RETURNS, pn * half, cols), BF16), dma((RETURNS * pn,))],
            name="combine",
        )
        return parts[0]

    def combine_far(backs):
        *parts, gates = call(
            functools.partial(combine_far_kernel, **fixed, rows=half),
            [shape(tokens + TAIL, cols)] * zr + [shape(TAIL, zn * tokens)],
            [info, meta, sels[0], chosen[RETURNS - 1], *backs],
            [SMEM] + [VMEM] * 3 + [HBM] * pn,
            scratch=[pltpu.VMEM((pn * half, cols), BF16), pltpu.VMEM((pn, TAIL, cols), BF16)]
            + [dma((2 * pn,))],
            name="combine_far",
        )
        return send_back(parts, zn - zr), gates

    def combine_near(gates, backs):
        parts = call(
            functools.partial(combine_near_kernel, pn=pn, tokens=tokens, rows=half),
            [shape(tokens + TAIL, cols)] * zr,
            [gates, chosen[0], *backs],
            [VMEM] * 2 + [HBM] * pn,
            scratch=[pltpu.VMEM((pn * half, cols), BF16), dma((pn,))],
            name="combine_near",
        )
        return send_back(parts, 0)

    def swapped(chunks):
        return [tensor_send(piece, j) for j in range(nt) for pieces in chunks for piece in pieces]

    def core_sum(arrays):
        sums = []
        for q in range(pn):
            total = sum(tensor_send(arrays[j * pn + q], j).astype(F32) for j in range(nt))
            sums.append(total.astype(BF16))
        return sums

    x_parts = [outer_send(first_half, s) for s in range(zn)]
    x_packed = pack_gates(x_parts)
    x_packed, sels = x_packed[:pn], x_packed[pn:]
    x_here = inner_exchange(x_packed)
    gathered = outer_exchange(after(grad_copies, *x_parts[1:]))
    chosen = call(
        functools.partial(route_kernel, **fixed, picks=picks, cap=cap),
        [shape(zr * tokens, pn * half)] * RETURNS,
        [info, after(meta, *x_packed)],
        [SMEM, VMEM],
        name="route",
    )
    c_packed = pack(after(gathered, *chosen))
    c_here = inner_exchange(c_packed)

    pieces = nt * CHUNKS * pn
    xs = swapped(([after(piece, *c_packed) for piece in x_here],))
    forward = call(
        functools.partial(forward_kernel, **sizes),
        [shape(rows, cols)] * (nt * pn) + [shape(slots, hid_n)] * 4,
        [after(info, *c_packed), *xs, expert_in, expert_out],
        [SMEM] + [HBM] * (pieces + 2),
        out_specs=[HBM] * (nt * pn + 4),
        scratch=[pltpu.VMEM((slots, nt * cols), BF16), pltpu.VMEM((pn, TAIL, cols), BF16)]
        + [pltpu.VMEM((hid_n, nt * cols), BF16)] * 3
        + [pltpu.VMEM((4, slots, hid_n), BF16)]
        + [pltpu.VMEM((nt, pn, rows, cols), BF16), dma((3 * nt + pieces + pn,))]
        + [dma((nt * pn + 4 * BLOCKS,))],
        name="expert_forward",
        limit=VMEM_LIMIT,
    )
    outs, (hs, hid, a1, a2) = forward[: nt * pn], forward[nt * pn :]
    cs = swapped(([after(piece, hid) for piece in c_here],))
    out_here = core_sum(outs)
    out_back = inner_exchange(out_here)

    backward = call(
        functools.partial(backward_kernel, **sizes),
        [
            shape(half + TAIL if r == RETURNS - 1 else half, cols)
            for r in range(RETURNS)
            for _ in range(nt * pn)
        ]
        + [shape(slots, hid_n)] * 2,
        [info, *cs, expert_in, expert_out, after(hid, *out_here), a1, a2],
        [SMEM] + [HBM] * (pieces + 5),
        out_specs=[HBM] * (RETURNS * nt * pn + 2),
        scratch=[pltpu.VMEM((slots, nt * cols), BF16)]
        + [pltpu.VMEM((slots, hid_n), BF16)] * 3
        + [pltpu.VMEM((hid_n, nt * cols), BF16)] * 3
        + [pltpu.VMEM((2, slots, hid_n), BF16)]
        + [pltpu.VMEM((nt, pn, rows + TAIL, cols), BF16), dma((3 * nt + pieces + 3,))]
        + [dma((RETURNS * nt * pn + 2 * BLOCKS,))],
        name="expert_backward",
        limit=VMEM_LIMIT,
    )
    grads, (gg, ug) = backward[: RETURNS * nt * pn], backward[RETURNS * nt * pn :]
    near, far = grads[: nt * pn], grads[nt * pn :]
    out_combined = combine(out_back)
    out_parts = outer_exchange(out_combined)
    far = [after(part, *out_back) for part in far]
    far_here = core_sum([after(part, out_combined) for part in far[:pn]] + far[pn:])
    far_back = inner_exchange(far_here)
    near_here = core_sum([after(part, far_back[pn - 1]) for part in near])
    near_back = inner_exchange(near_here)

    far_parts, gate_parts = combine_far([after(piece, *near_here) for piece in far_back])
    grad_parts = combine_near(gate_parts, near_back) + far_parts

    grad_in, grad_out = call(
        functools.partial(weights_kernel, **sizes),
        [shape(*expert_in.shape), shape(*expert_out.shape)],
        [after(info, grad_parts[0]), *xs, *cs, gg, ug, hs],
        [SMEM] + [HBM] * (2 * pieces + 3),
        out_specs=[HBM, HBM],
        scratch=[
            pltpu.VMEM((3, slots, hid_n), BF16),
            pltpu.VMEM((2, nt, slots, cols), BF16),
            pltpu.VMEM((nt, 3, hid_n, cols), BF16),
            dma((3 + 2 * pieces,)),
            dma((3 * nt,)),
        ],
        name="expert_weights",
        limit=VMEM_LIMIT,
    )

    branch = jnp.sum(after(out_parts, grad_in).astype(F32), axis=0)
    input_sum = sum(part[:tokens].astype(F32) for part in grad_parts)
    gate_sum = sum(part[tokens : tokens + picks, :tokens].astype(F32) for part in grad_parts)
    restored = (second_half.astype(F32) - branch).astype(BF16)
    carried_grad = (first_grad.astype(F32) + input_sum).astype(BF16)
    return (restored, carried_grad, gate_sum.T, grad_in, grad_out)


def solution(mesh):
    in_specs = (
        P("expert", "tensor"),
        P("expert", "tensor"),
        P("expert", "tensor"),
        P("expert", "tensor"),
        P("expert", None),
        P("expert", None),
        P("expert", None, "tensor", None),
        P("expert", "tensor", None),
    )
    out_specs = (
        P("expert", "tensor"),
        P("expert", "tensor"),
        P("expert", None),
        P("expert", None, "tensor", None),
        P("expert", "tensor", None),
    )
    return jax.shard_map(body, mesh=mesh, in_specs=in_specs, out_specs=out_specs, check_vma=False)
```
